32 devices in a mesh: dp: 8 (over z, core), tensor: 4 (over y, x).
Axes of the slice: x: 2, y: 2, z: 4, core: 2. Of those that a mesh axis runs over, the one named last changes fastest.
Arguments:
- inputs: bfloat16 [16384, 2048], P(('dp', 'tensor')), may hold values from -6 to 6
- segment_ids: int32 [16384], P('dp'), may hold values from 0 to 1, as said below
- attn_gain: bfloat16 [2048], P('dp'), may hold values from 0.099609375 to 1.8984375
- query_weight: bfloat16 [2048, 2048], P('dp', 'tensor'), may hold values from -0.125 to 0.125
- key_weight: bfloat16 [2048, 512], P('dp', 'tensor'), may hold values from -0.125 to 0.125
- value_weight: bfloat16 [2048, 512], P('dp', 'tensor'), may hold values from -0.125 to 0.125
- output_weight: bfloat16 [2048, 2048], P('tensor', 'dp'), may hold values from -0.75 to 0.75
- mlp_gain: bfloat16 [2048], P('dp'), may hold values from 0.099609375 to 1.8984375
- gate_weight: bfloat16 [2048, 8192], P('dp', 'tensor'), may hold values from -0.125 to 0.125
- up_weight: bfloat16 [2048, 8192], P('dp', 'tensor'), may hold values from -0.125 to 0.125
- down_weight: bfloat16 [8192, 2048], P('tensor', 'dp'), may hold values from -0.125 to 0.125
- cotangent: bfloat16 [16384, 2048], P(('dp', 'tensor')), may hold values from -6 to 6
Outputs:
- layer_out: bfloat16 [16384, 2048], P(('dp', 'tensor'))
- input_grad: bfloat16 [16384, 2048], P(('dp', 'tensor'))
- attn_gain_grad: float32 [2048], P('dp')
- query_weight_grad: float32 [2048, 2048], P('dp', 'tensor')
- key_weight_grad: float32 [2048, 512], P('dp', 'tensor')
- value_weight_grad: float32 [2048, 512], P('dp', 'tensor')
- output_weight_grad: float32 [2048, 2048], P('tensor', 'dp')
- mlp_gain_grad: float32 [2048], P('dp')
- gate_weight_grad: float32 [2048, 8192], P('dp', 'tensor')
- up_weight_grad: float32 [2048, 8192], P('dp', 'tensor')
- down_weight_grad: float32 [8192, 2048], P('tensor', 'dp')
The draws below stay inside these ranges and needn't reach their ends.
Inputs may be any that keep to these rules, and one draw needn't show every extreme that they name: `segment_ids`: in each aligned block of 2048 tokens the ids never fall and are 0 for the first sequence and 1 for a second one where the block holds two; every sequence has 1024 tokens or more; some block holds one sequence and some block two.
All inputs are finite; a program needn't handle non-finite values.
Results may differ from the reference program's by a relative error of at most 0.025.
Values may be sent and summed in bfloat16 or wider, within the bound.
No kernel may reach another device: no remote copies, remote signals or barrier semaphores. Data moves between devices by JAX's collectives and lax.ppermute only.
A program may use at most 256 MiB of HBM per device.

```python
import math
import jax
import jax.numpy as jnp
from jax import lax

D = 2048
H = 32
KV = 8
HD = 64
FF = 8192
TOK_DP = 2048
MIN_LEN = 1024
TOKENS = 16384
N_DP = 8


def draw_segment_ids(key, part):
    key = jax.random.fold_in(key, 11)
    shards = TOKENS // TOK_DP
    key_bound, key_flag, key_order = jax.random.split(key, 3)
    bounds = jax.random.randint(key_bound, (shards,), MIN_LEN, TOK_DP - MIN_LEN + 1)
    split_flags = jax.random.randint(key_flag, (shards,), 0, 2)
    ranking = jax.random.permutation(key_order, shards)
    split_flags = split_flags.at[ranking[0]].set(0).at[ranking[1]].set(1)
    places = jnp.arange(TOK_DP, dtype=jnp.int32)
    labels = (places[None, :] >= bounds[:, None]).astype(jnp.int32) * split_flags[:, None]
    return labels.reshape(TOKENS).astype(jnp.int32)


def strengthened(drawn, own_key, source, target, shards_of, factor):
    owner, partner = [(jnp.arange(drawn.shape[dim]) // (drawn.shape[dim] // shards_of)).reshape([-1 if axis == dim else 1 for axis in range(drawn.ndim)]) for dim in (source, target)]
    chosen = jax.random.permutation(own_key, shards_of)[partner]
    strong = (owner == chosen) | (owner == (partner + shards_of // 2) % shards_of)
    return jnp.where(strong, factor * drawn, drawn)


def steps_of(stream_key, extent, cuts, smallest, largest):
    def one(dim, blocks):
        steps = jax.random.uniform(jax.random.fold_in(jax.random.fold_in(stream_key, 6), dim), (blocks,), jnp.float32, smallest / len(cuts), largest / len(cuts))
        return jnp.repeat(jnp.exp(steps), extent[dim] // blocks).reshape((-1,) + (1,) * (len(extent) - dim - 1))

    gain = one(*cuts[0])
    for cut in cuts[1:]:
        gain = gain * one(*cut)
    return gain


def normal_values(key, extent, deviation, bound, cuts=(), held_as=jnp.bfloat16):
    values = jax.random.normal(key, extent, jnp.float32) * deviation
    if len(cuts) > 0:
        values = steps_of(key, extent, cuts, -0.22, 0.18) * values
    return jnp.clip(values, min=-bound, max=bound).astype(held_as)


def heavy_noise(stream_key, shape, spread, limit, cuts, heavy, kind=jnp.bfloat16):
    entries = spread * jax.random.normal(stream_key, shape, jnp.float32)
    if cuts:
        entries = entries * steps_of(stream_key, shape, cuts, -0.22, 0.18)
    return jnp.clip(strengthened(entries, jax.random.fold_in(stream_key, 3), *heavy), -limit, limit).astype(kind)


def setup_inputs(seed: int = 0) -> dict:
    keys = jax.random.split(jax.random.key(seed), 13)
    inputs = normal_values(keys[0], (TOKENS, D), 1.0, 6.0, ((0, 32),))
    segment_ids = draw_segment_ids(jax.random.fold_in(keys[12], 71), 0)
    attn_gain = jnp.clip(1.0 + 0.18 * jax.random.normal(keys[2], (D,), jnp.float32), 0.099609375, 1.8984375).astype(jnp.bfloat16)
    query_weight = normal_values(keys[3], (D, H * HD), D ** -0.5, 0.125, ((0, 8), (1, 4)))
    key_weight = normal_values(keys[4], (D, KV * HD), D ** -0.5, 0.125, ((0, 8), (1, 4)))
    value_weight = normal_values(keys[5], (D, KV * HD), D ** -0.5, 0.125, ((0, 8), (1, 4)))
    output_weight = normal_values(keys[6], (H * HD, D), (H * HD // 32) ** -0.5, 0.75, ((0, 4), (1, 8)))
    mlp_gain = jnp.clip(1.0 + 0.18 * jax.random.normal(keys[7], (D,), jnp.float32), 0.099609375, 1.8984375).astype(jnp.bfloat16)
    gate_weight = normal_values(keys[8], (D, FF), D ** -0.5, 0.125, ((0, 8), (1, 4)))
    up_weight = normal_values(keys[9], (D, FF), D ** -0.5, 0.125, ((0, 8), (1, 4)))
    down_weight = normal_values(keys[10], (FF, D), (FF // 4) ** -0.5, 0.125, ((0, 4), (1, 8)))
    cotangent = heavy_noise(keys[11], (TOKENS, D), 1.0, 6.0, ((0, 32),), (0, 1, 32, 2.75))
    return dict(inputs=inputs, segment_ids=segment_ids, attn_gain=attn_gain, query_weight=query_weight, key_weight=key_weight, value_weight=value_weight, output_weight=output_weight, mlp_gain=mlp_gain, gate_weight=gate_weight, up_weight=up_weight, down_weight=down_weight, cotangent=cotangent)


EPSILON = 1e-05
ROPE_BASE = 500000.0
MASKED = -1e+30

@jax.custom_vjp
def low(v):
    return lax.optimization_barrier(v.astype(jnp.bfloat16)).astype(jnp.float32)

@jax.custom_vjp
def low_back(v):
    return v

def low_keep(v):
    return (low(v), None)

def low_pass(kept, grad):
    return (grad,)

def back_keep(v):
    return (v, None)

def back_low(kept, grad):
    return (low(grad),)
low.defvjp(low_keep, low_pass)
low_back.defvjp(back_keep, back_low)

def product(left, right):
    return jnp.dot(left, right, precision=lax.Precision.HIGHEST)

def positions(segment):
    length = segment.shape[0]
    places = jnp.arange(length, dtype=jnp.int32)
    labels = jnp.arange(TOK_DP // MIN_LEN, dtype=jnp.int32)
    member = (segment[:, None] == labels[None, :]).astype(jnp.int32)
    counts = lax.optimization_barrier(jnp.sum(member, axis=0))
    before = (labels[None, :] < segment[:, None]).astype(jnp.int32)
    starts = lax.optimization_barrier(jnp.sum(before * counts[None, :], axis=1))
    return places - starts

def rope_tables(placed):
    half_dim = HD // 2
    freqs = jnp.exp(jnp.arange(half_dim, dtype=jnp.float32) * (-2.0 * math.log(ROPE_BASE) / HD))
    angles = placed.astype(jnp.float32)[:, None] * freqs[None, :]
    return (jnp.cos(angles), jnp.sin(angles))

def rotate(values, cosine, sine, direction):
    length = values.shape[0]
    head_count = values.shape[1] // HD
    parts = values.reshape(length, head_count, 2, HD // 2)
    former = parts[:, :, 0]
    latter = parts[:, :, 1]
    cos_b = cosine[:, None, :]
    sin_b = direction * sine[:, None, :]
    turned = jnp.stack([former * cos_b - latter * sin_b, latter * cos_b + former * sin_b], axis=2)
    return turned.reshape(length, head_count * HD)

def normalize(stream):
    scale_r = lax.rsqrt(lax.optimization_barrier(jnp.mean(stream * stream, axis=-1, keepdims=True)) + EPSILON)
    return stream * scale_r

def head_attention(query_rows, key_rows, value_rows, allowed):
    scores = low_back(product(query_rows, key_rows.T) * (1.0 / math.sqrt(HD)))
    scores = jnp.where(allowed, scores, MASKED)
    row_max = lax.optimization_barrier(jnp.max(scores, axis=-1, keepdims=True))
    powered = jnp.exp(scores - row_max)
    probability = low(powered / lax.optimization_barrier(jnp.sum(powered, axis=-1, keepdims=True)))
    return low(low_back(product(probability, value_rows)))

def shard_layer(stream, segment, attn_gain, query_weight, key_weight, value_weight, output_weight, mlp_gain, gate_weight, up_weight, down_weight):
    length = stream.shape[0]
    cosine, sine = rope_tables(positions(segment))
    normed_a = low(normalize(stream) * attn_gain)
    query_pre = low_back(product(normed_a, query_weight))
    key_pre = low_back(product(normed_a, key_weight))
    value_pre = low_back(product(normed_a, value_weight))
    queries = low(rotate(query_pre, cosine, sine, 1.0))
    key_rot = low(rotate(key_pre, cosine, sine, 1.0))
    value_low = low(value_pre)
    query_heads = queries.reshape(length, H, HD).transpose(1, 0, 2)
    key_heads = jnp.repeat(key_rot.reshape(length, KV, HD).transpose(1, 0, 2), H // KV, axis=0)
    value_heads = jnp.repeat(value_low.reshape(length, KV, HD).transpose(1, 0, 2), H // KV, axis=0)
    places = jnp.arange(length, dtype=jnp.int32)
    allowed = (segment[:, None] == segment[None, :]) & (places[None, :] <= places[:, None])
    head_step = jax.checkpoint(lambda triple: head_attention(triple[0], triple[1], triple[2], allowed))
    attended = lax.map(head_step, (query_heads, key_heads, value_heads))
    attended = attended.transpose(1, 0, 2).reshape(length, H * HD)
    stream_one = stream + low_back(product(attended, output_weight))
    normed_m = low(normalize(stream_one) * mlp_gain)
    gate_pre = low_back(product(normed_m, gate_weight))
    up_pre = low_back(product(normed_m, up_weight))
    hidden = low(jax.nn.silu(gate_pre) * up_pre)
    return stream_one + low_back(product(hidden, down_weight))

def reference(inputs, segment_ids, attn_gain, query_weight, key_weight, value_weight, output_weight, mlp_gain, gate_weight, up_weight, down_weight, cotangent):
    weights = tuple((array.astype(jnp.float32) for array in (attn_gain, query_weight, key_weight, value_weight, output_weight, mlp_gain, gate_weight, up_weight, down_weight)))
    stream = inputs.astype(jnp.float32).reshape(N_DP, TOK_DP, D)
    segments = segment_ids.reshape(N_DP, TOK_DP)
    layer_ckpt = jax.checkpoint(shard_layer)

    def forward(stream_all, params):
        return lax.map(lambda pair: layer_ckpt(pair[0], pair[1], *params), (stream_all, segments))
    outputs, pullback = jax.vjp(forward, stream, weights)
    stream_grad, grads = pullback(cotangent.astype(jnp.float32).reshape(N_DP, TOK_DP, D))
    return (outputs.reshape(TOKENS, D).astype(jnp.bfloat16), stream_grad.reshape(TOKENS, D).astype(jnp.bfloat16), grads[0], grads[1], grads[2], grads[3], grads[4], grads[5], grads[6], grads[7], grads[8])
```

```python
import functools
import math

import jax
import jax.numpy as jnp
from jax import lax
from jax.experimental import pallas as pl
from jax.experimental.pallas import tpu as pltpu
from jax.sharding import PartitionSpec as P

HD = 64
LANES = 128
EPSILON = 1e-05
ROPE_BASE = 500000.0
MASKED = -1e30
OVER_ROWS = (((0,), (0,)), ((), ()))
OVER_COLS = (((1,), (1,)), ((), ()))
VMEM_LIMIT = 56 * 2**20
F32 = jnp.float32
BF16 = jnp.bfloat16


def dot_cols(left, right):
    return lax.dot_general(left, right, OVER_COLS, preferred_element_type=F32)


def dot_rows(left, right):
    return lax.dot_general(left, right, OVER_ROWS, preferred_element_type=F32)


def dot(left, right):
    return jnp.dot(left, right, preferred_element_type=F32)


def pairs(size, bit):
    return [(index, index ^ bit) for index in range(size)]


def slots_of(size):
    if size == 4:
        return [lax.axis_index("tensor") ^ step for step in range(size)]
    return [jnp.int32(step) for step in range(size)]


def gather(shard, size):
    if size != 4:
        whole = lax.all_gather(shard, "tensor", axis=0)
        return [whole[step] for step in range(size)]
    half = shard.shape[0] // 2
    one = lax.ppermute(shard, "tensor", pairs(size, 1))
    two = lax.ppermute(shard, "tensor", pairs(size, 2))
    three_a = lax.ppermute(one[:half], "tensor", pairs(size, 2))
    three_b = lax.ppermute(two[half:], "tensor", pairs(size, 1))
    return [shard, one, two, jnp.concatenate([three_a, three_b], axis=0)]


def scatter(terms, size):
    if size != 4:
        low = jnp.concatenate([term.astype(BF16) for term in terms], axis=0)
        return lax.psum_scatter(low, "tensor", scatter_dimension=0, tiled=True).astype(F32)
    half = terms[0].shape[0] // 2
    three = terms[3].astype(BF16)
    into_two = lax.ppermute(three[:half], "tensor", pairs(size, 1))
    into_one = lax.ppermute(three[half:], "tensor", pairs(size, 2))
    one = jnp.concatenate([terms[1][:half], terms[1][half:] + into_one.astype(F32)], axis=0)
    two = jnp.concatenate([terms[2][:half] + into_two.astype(F32), terms[2][half:]], axis=0)
    from_one = lax.ppermute(one.astype(BF16), "tensor", pairs(size, 1))
    from_two = lax.ppermute(two.astype(BF16), "tensor", pairs(size, 2))
    return terms[0] + from_one.astype(F32) + from_two.astype(F32)


def rope_tables(segment):
    length = segment.shape[0]
    bound = jnp.sum((segment == 0).astype(jnp.int32))
    place = lax.broadcasted_iota(jnp.int32, (length, LANES), 0)
    place = place - jnp.where(place >= bound, bound, 0)
    lane = lax.broadcasted_iota(jnp.int32, (length, LANES), 1)
    freqs = jnp.exp(
        (lane % (HD // 2)).astype(F32) * (-2.0 * math.log(ROPE_BASE) / HD)
    )
    angles = place.astype(F32) * freqs
    sine = jnp.sin(angles)
    return bound, jnp.cos(angles), jnp.where(lane % HD < HD // 2, -sine, sine)


def swap_halves(values):
    lane = lax.broadcasted_iota(jnp.int32, values.shape, 1)
    after = pltpu.roll(values, LANES - HD // 2, 1)
    before = pltpu.roll(values, HD // 2, 1)
    return jnp.where(lane % HD < HD // 2, after, before)


def normalize(stream):
    scale_r = lax.rsqrt(jnp.mean(stream * stream, axis=-1, keepdims=True) + EPSILON)
    return (stream * scale_r, scale_r)


def project_kernel(slot_ref, x_ref, gain_ref, w_ref, cos_ref, sin_ref, *rest, heads, kv):
    h_ref, q_ref, kx_ref, vx_ref, kt_ref, vt_ref = rest[-6:]
    normed, _ = normalize(x_ref[...].astype(F32))
    low = (normed * gain_ref[...]).astype(BF16)
    h_ref[...] = low
    pre = dot(low, w_ref[...])
    cosine, sine = cos_ref[...], sin_ref[...]
    rows = pre.shape[0]
    lane = lax.broadcasted_iota(jnp.int32, (rows, LANES), 1)
    chunks = []
    for chunk in range(pre.shape[1] // LANES):
        part = pre[:, chunk * LANES : (chunk + 1) * LANES]
        turned = part * cosine + swap_halves(part) * sine
        first = 2 * chunk
        if first + 1 < heads + kv:
            chunks.append(turned)
        elif first < heads + kv:
            chunks.append(jnp.where(lane < HD, turned, part))
        else:
            chunks.append(part)
        if first < heads:
            q_ref[:, chunk * LANES : (chunk + 1) * LANES] = (
                chunks[chunk] * (1.0 / math.sqrt(HD))
            ).astype(BF16)
    flipped = {}
    for head in range(2 * kv):
        place = heads + head
        part = chunks[place // 2]
        moved = pltpu.roll(part, HD, 1)
        wide = [part, moved] if place % 2 == 0 else [moved, part]
        out = kx_ref if head < kv else vx_ref
        out[head % kv, 0] = jnp.where(lane < HD, wide[0], 0.0).astype(BF16)
        out[head % kv, 1] = jnp.where(lane < HD, 0.0, wide[1]).astype(BF16)
        if place // 2 not in flipped:
            flipped[place // 2] = part.T
        turn = flipped[place // 2][(place % 2) * HD : (place % 2 + 1) * HD]
        out_t = kt_ref if head < kv else vt_ref
        out_t[(head % kv) * HD : (head % kv + 1) * HD, :] = turn.astype(BF16)


def project(slot, block, gain, weight, cosine, sine, heads, kv, length, prev):
    rows, width = block.shape
    tile = min(256, rows)
    steps = rows // tile
    columns = (heads + 2 * kv) * HD

    def at(i, slot):
        return slot[0] * steps + i

    shapes = [
        jax.ShapeDtypeStruct((length, width), BF16),
        jax.ShapeDtypeStruct((length, heads * HD), BF16),
        jax.ShapeDtypeStruct((kv, 2, length, LANES), BF16),
        jax.ShapeDtypeStruct((kv, 2, length, LANES), BF16),
        jax.ShapeDtypeStruct((kv * HD, length), BF16),
        jax.ShapeDtypeStruct((kv * HD, length), BF16),
    ]
    out_specs = [
        pl.BlockSpec((tile, width), lambda i, s: (at(i, s), 0)),
        pl.BlockSpec((tile, heads * HD), lambda i, s: (at(i, s), 0)),
        pl.BlockSpec((kv, 2, tile, LANES), lambda i, s: (0, 0, at(i, s), 0)),
        pl.BlockSpec((kv, 2, tile, LANES), lambda i, s: (0, 0, at(i, s), 0)),
        pl.BlockSpec((kv * HD, tile), lambda i, s: (0, at(i, s))),
        pl.BlockSpec((kv * HD, tile), lambda i, s: (0, at(i, s))),
    ]
    in_specs = [
        pl.BlockSpec((tile, width), lambda i, s: (i, 0)),
        pl.BlockSpec((1, width), lambda i, s: (0, 0)),
        pl.BlockSpec((width, columns), lambda i, s: (0, 0)),
        pl.BlockSpec((tile, LANES), lambda i, s: (at(i, s), 0)),
        pl.BlockSpec((tile, LANES), lambda i, s: (at(i, s), 0)),
    ]
    operands = [slot.reshape(1), block, gain, weight, cosine, sine]
    aliases = {}
    if prev is not None:
        for index, array in enumerate(prev):
            aliases[len(operands)] = index
            operands.append(array)
            in_specs.append(pl.BlockSpec(memory_space=pl.ANY))
    return pl.pallas_call(
        functools.partial(project_kernel, heads=heads, kv=kv),
        grid_spec=pltpu.PrefetchScalarGridSpec(
            num_scalar_prefetch=1, grid=(steps,), in_specs=in_specs, out_specs=out_specs
        ),
        out_shape=shapes,
        input_output_aliases=aliases,
        compiler_params=pltpu.CompilerParams(vmem_limit_bytes=VMEM_LIMIT),
        cost_estimate=pl.CostEstimate(
            flops=2 * rows * width * columns,
            bytes_accessed=2 * (2 * rows * width + width * columns + 3 * rows * columns),
            transcendentals=0,
        ),
    )(*operands)


def causal(block):
    keys = lax.broadcasted_iota(jnp.int32, (block, block), 0)
    return keys <= lax.broadcasted_iota(jnp.int32, (block, block), 1)


def first_block(bound, offset, block):
    return jnp.where(offset >= bound, lax.div(bound, jnp.int32(block)), 0)


def attend_kernel(bound_ref, q_ref, kx_ref, vt_ref, out_ref, lse_ref, top_ref, acc_ref, *, block):
    length = q_ref.shape[0]
    kv = kx_ref.shape[0]
    per = q_ref.shape[1] // LANES // kv
    bound = bound_ref[0]
    ones = jnp.ones((16, block), BF16)
    for group in range(kv):

        def q_step(index, _):
            offset = pl.multiple_of(index * block, block)
            top_ref[...] = jnp.full(top_ref.shape, MASKED, F32)
            acc_ref[...] = jnp.zeros(acc_ref.shape, F32)

            def tile(step, diagonal):
                keys = pl.ds(pl.multiple_of(step * block, block), block)
                value_t = jnp.concatenate(
                    [vt_ref[group * HD : (group + 1) * HD, keys], ones], axis=0
                )
                for head in range(2 * per):
                    column = (group * per + head // 2) * LANES
                    query = q_ref[pl.ds(offset, block), column : column + LANES]
                    scores = dot_cols(kx_ref[group, head % 2, keys, :], query)
                    if diagonal:
                        scores = jnp.where(causal(block), scores, MASKED)
                    old = top_ref[head, 0:1, :]
                    top = jnp.maximum(old, jnp.max(scores, axis=0, keepdims=True))
                    powered = jnp.exp(scores - top).astype(BF16)
                    acc_ref[head] = acc_ref[head] * jnp.exp(old - top) + dot(value_t, powered)
                    top_ref[head, 0:1, :] = top

            def full_tile(step, carry):
                tile(step, False)
                return carry

            lax.fori_loop(first_block(bound, offset, block), index, full_tile, 0)
            tile(index, True)
            for pair in range(per):
                both = []
                for head in (2 * pair, 2 * pair + 1):
                    total = acc_ref[head, HD : HD + 1, :]
                    both.append(acc_ref[head, :HD, :] / total)
                    place = group * 2 * per + head
                    lse_ref[place : place + 1, pl.ds(offset, block)] = top_ref[
                        head, 0:1, :
                    ] + jnp.log(total)
                column = (group * per + pair) * LANES
                out_ref[pl.ds(offset, block), column : column + LANES] = (
                    jnp.concatenate(both, axis=0).T.astype(BF16)
                )
            return _

        lax.fori_loop(0, length // block, q_step, 0)


def attend(bound, queries, kx, vt, block):
    length, width = queries.shape
    heads = width // HD
    kv = kx.shape[0]
    per = heads // kv
    cells = heads * length * (length + block) // 2
    vmem = pl.BlockSpec(memory_space=pltpu.VMEM)
    return pl.pallas_call(
        functools.partial(attend_kernel, block=block),
        in_specs=[pl.BlockSpec(memory_space=pltpu.SMEM), vmem, vmem, vmem],
        out_specs=[vmem, vmem],
        out_shape=[
            jax.ShapeDtypeStruct((length, width), BF16),
            jax.ShapeDtypeStruct((heads, length), F32),
        ],
        scratch_shapes=[
            pltpu.VMEM((per, 8, block), F32),
            pltpu.VMEM((per, HD + 16, block), F32),
        ],
        compiler_params=pltpu.CompilerParams(vmem_limit_bytes=VMEM_LIMIT),
        cost_estimate=pl.CostEstimate(
            flops=2 * 4 * HD * 4 * cells, bytes_accessed=12 * length * width, transcendentals=cells
        ),
    )(bound.reshape(1), queries, kx, vt)


def attend_back_kernel(
    bound_ref, q_ref, kx_ref, vx_ref, kt_ref, lse_ref, out_ref, grad_ref, cos_ref, sin_ref,
    dqkv_ref, dk_ref, dv_ref, dq_ref, *, block
):
    length = q_ref.shape[0]
    kv = kx_ref.shape[0]
    heads = q_ref.shape[1] // HD
    per = heads // 2 // kv
    bound = bound_ref[0]
    dk_ref[...] = jnp.zeros(dk_ref.shape, F32)
    dv_ref[...] = jnp.zeros(dv_ref.shape, F32)
    lane = lax.broadcasted_iota(jnp.int32, (8, LANES), 1)
    row = lax.broadcasted_iota(jnp.int32, (8, LANES), 0)
    chosen = ((lane // HD) == row).astype(F32)

    def turn_back(values, rows):
        return values * cos_ref[rows, :] - swap_halves(values) * sin_ref[rows, :]

    for group in range(kv):

        def q_step(index, _):
            offset = pl.multiple_of(index * block, block)
            rows = pl.ds(offset, block)
            dq_ref[...] = jnp.zeros(dq_ref.shape, F32)
            deltas = []
            for pair in range(per):
                column = (group * per + pair) * LANES
                product = grad_ref[rows, column : column + LANES].astype(F32) * out_ref[
                    rows, column : column + LANES
                ].astype(F32)
                deltas.append(
                    lax.dot_general(
                        chosen, product, OVER_COLS, precision=lax.Precision.HIGHEST,
                        preferred_element_type=F32,
                    )
                )

            def tile(step, diagonal):
                keys = pl.ds(pl.multiple_of(step * block, block), block)
                key_t = kt_ref[group * HD : (group + 1) * HD, keys]
                for parity in range(2):
                    key_add, value_add = 0.0, 0.0
                    for pair in range(per):
                        head = 2 * pair + parity
                        place = group * 2 * per + head
                        column = (group * per + pair) * LANES
                        query = q_ref[rows, column : column + LANES]
                        grad = grad_ref[rows, column : column + LANES]
                        scores = dot_cols(kx_ref[group, parity, keys, :], query)
                        if diagonal:
                            scores = jnp.where(causal(block), scores, MASKED)
                        probs = jnp.exp(scores - lse_ref[place : place + 1, rows])
                        dprobs = dot_cols(vx_ref[group, parity, keys, :], grad)
                        dscores = (probs * (dprobs - deltas[pair][parity : parity + 1])).astype(BF16)
                        value_add = value_add + dot(probs.astype(BF16), grad)
                        key_add = key_add + dot(dscores, query)
                        dq_ref[head * HD : (head + 1) * HD, :] += dot(key_t, dscores)
                    dk_ref[group, parity, keys, :] += key_add
                    dv_ref[group, parity, keys, :] += value_add

            def full_tile(step, carry):
                tile(step, False)
                return carry

            lax.fori_loop(first_block(bound, offset, block), index, full_tile, 0)
            tile(index, True)
            for pair in range(per):
                column = (group * per + pair) * LANES
                grad_q = dq_ref[pair * LANES : (pair + 1) * LANES, :].T * (1.0 / math.sqrt(HD))
                dqkv_ref[rows, column : column + LANES] = turn_back(grad_q, rows).astype(BF16)
            return _

        lax.fori_loop(0, length // block, q_step, 0)

    def finish(index, _):
        rows = pl.ds(pl.multiple_of(index * block, block), block)
        lanes = lax.broadcasted_iota(jnp.int32, (block, LANES), 1)

        def placed(part, half):
            ref = dk_ref if part < kv else dv_ref
            even, odd = ref[part % kv, 0, rows, :], ref[part % kv, 1, rows, :]
            return even + pltpu.roll(odd, HD, 1) if half == 0 else pltpu.roll(even, HD, 1) + odd

        for chunk in range(kv):
            values = jnp.where(lanes < HD, placed(2 * chunk, 0), placed(2 * chunk + 1, 1))
            if 2 * chunk + 1 < kv:
                values = turn_back(values, rows)
            elif 2 * chunk < kv:
                values = jnp.where(lanes < HD, turn_back(values, rows), values)
            column = heads * HD + chunk * LANES
            dqkv_ref[rows, column : column + LANES] = values.astype(BF16)
        return _

    lax.fori_loop(0, length // block, finish, 0)


def attend_back(bound, queries, kx, vx, kt, log_sums, attended, grad, cosine, sine, block):
    length, width = queries.shape
    heads = width // HD
    kv = kx.shape[0]
    cells = heads * length * (length + block) // 2
    vmem = pl.BlockSpec(memory_space=pltpu.VMEM)
    return pl.pallas_call(
        functools.partial(attend_back_kernel, block=block),
        in_specs=[pl.BlockSpec(memory_space=pltpu.SMEM)] + [vmem] * 9,
        out_specs=vmem,
        out_shape=jax.ShapeDtypeStruct((length, width + 2 * kv * HD), BF16),
        scratch_shapes=[
            pltpu.VMEM((kv, 2, length, LANES), F32),
            pltpu.VMEM((kv, 2, length, LANES), F32),
            pltpu.VMEM((heads // kv * HD, block), F32),
        ],
        compiler_params=pltpu.CompilerParams(vmem_limit_bytes=VMEM_LIMIT),
        cost_estimate=pl.CostEstimate(
            flops=2 * 10 * HD * 4 * cells, bytes_accessed=20 * length * width, transcendentals=cells
        ),
    )(bound.reshape(1), queries, kx, vx, kt, log_sums, attended, grad, cosine, sine)


def local(
    inputs,
    segment_ids,
    attn_gain,
    query_weight,
    key_weight,
    value_weight,
    output_weight,
    mlp_gain,
    gate_weight,
    up_weight,
    down_weight,
    cotangent,
    *,
    size,
):
    rows = inputs.shape[0]
    length = segment_ids.shape[0]
    query_cols = query_weight.shape[1]
    key_cols = key_weight.shape[1]
    heads, kv = query_cols // HD, key_cols // HD
    columns = query_cols + 2 * key_cols
    slots = slots_of(size)

    gains = jnp.pad(jnp.stack([attn_gain, mlp_gain], axis=1), ((0, 0), (0, LANES - 2)))
    bundle = lax.all_gather(
        jnp.concatenate([query_weight, key_weight, value_weight, output_weight.T, gains], axis=1),
        "dp", axis=0, tiled=True,
    )
    gate_full = lax.all_gather(gate_weight, "dp", axis=0, tiled=True)
    up_full = lax.all_gather(up_weight, "dp", axis=0, tiled=True)
    down_full = lax.all_gather(down_weight, "dp", axis=1, tiled=True)
    qkv_weight = bundle[:, :columns]
    out_t = bundle[:, columns : columns + query_cols]
    scales = bundle[:, columns + query_cols : columns + query_cols + 2].T.astype(F32)
    attn_scale, mlp_scale = scales[0:1], scales[1:2]

    bound, cosine, sine = rope_tables(segment_ids)
    blocks = gather(inputs, size)
    arrays = None
    for slot, block in zip(slots, blocks):
        arrays = project(
            slot, block, attn_scale, bundle, cosine, sine, heads, kv, length, arrays
        )
    block_a, queries, kx, vx, kt, vt = arrays
    attended, log_sums = attend(bound, queries, kx, vt, rows)

    def of_slot(array, slot):
        return lax.dynamic_slice_in_dim(array, slot * rows, rows, 0)

    stream = inputs.astype(F32)
    attended_parts = [of_slot(attended, slot) for slot in slots]
    stream_one = stream + scatter([dot_cols(part, out_t) for part in attended_parts], size)
    normed_m, scale_m = normalize(stream_one)
    parts_m = gather((normed_m * mlp_scale).astype(BF16), size)
    block_m = jnp.concatenate(parts_m, axis=0)
    grad_block = jnp.concatenate(gather(cotangent, size), axis=0)

    gate_pre = dot(block_m, gate_full)
    up_pre = dot(block_m, up_full)
    hidden = (jax.nn.silu(gate_pre) * up_pre).astype(BF16)
    grad_hidden = dot_cols(grad_block, down_full)
    sigmoid_g = jax.nn.sigmoid(gate_pre)
    grad_gate = (grad_hidden * up_pre * sigmoid_g * (1.0 + gate_pre * (1.0 - sigmoid_g))).astype(BF16)
    grad_up = (grad_hidden * gate_pre * sigmoid_g).astype(BF16)

    def of_place(array, place):
        return array[place * rows : (place + 1) * rows]

    grad_normed_m = scatter(
        [
            dot_cols(of_place(grad_gate, place), gate_full)
            + dot_cols(of_place(grad_up, place), up_full)
            for place in range(size)
        ],
        size,
    )
    layer_out = (
        stream_one
        + scatter([dot(of_place(hidden, place), down_full) for place in range(size)], size)
    ).astype(BF16)

    def reduce_rows(term, dimension=0):
        return lax.psum_scatter(
            term.astype(BF16), "dp", scatter_dimension=dimension, tiled=True
        ).astype(F32)

    gate_sum = reduce_rows(dot_rows(block_m, grad_gate))
    up_sum = reduce_rows(dot_rows(block_m, grad_up))
    down_sum = reduce_rows(dot_rows(hidden, grad_block), 1)

    def norm_back(grad_in, normed, scale_r, gain):
        scaled = grad_in * gain
        return scale_r * (scaled - normed * jnp.mean(scaled * normed, axis=-1, keepdims=True))

    mlp_gain_term = jnp.sum(grad_normed_m * normed_m, axis=0)
    grad_stream_one = cotangent.astype(F32) + norm_back(grad_normed_m, normed_m, scale_m, mlp_scale)
    grad_parts = gather(grad_stream_one.astype(BF16), size)
    grad_attended = jnp.zeros((length, query_cols), BF16)
    for slot, part in zip(slots, grad_parts):
        grad_attended = lax.dynamic_update_slice_in_dim(
            grad_attended, dot(part, out_t).astype(BF16), slot * rows, 0
        )
    out_t_sum = reduce_rows(
        dot_rows(jnp.concatenate(grad_parts, axis=0), jnp.concatenate(attended_parts, axis=0))
    )
    grad_qkv = attend_back(
        bound, queries, kx, vx, kt, log_sums, attended, grad_attended, cosine, sine, rows
    )
    grad_normed_a = scatter(
        [dot_cols(of_slot(grad_qkv, slot), qkv_weight) for slot in slots], size
    )
    qkv_wgrad = dot_rows(block_a, grad_qkv)
    qkv_sum = reduce_rows(qkv_wgrad)
    attn_gain_term = jnp.sum(qkv_wgrad * qkv_weight.astype(F32), axis=1) / attn_scale[0]
    gain_totals = lax.psum(jnp.stack([attn_gain_term, mlp_gain_term]), ("dp", "tensor"))
    width = attn_gain.shape[0]
    gain_mine = lax.dynamic_slice_in_dim(gain_totals, lax.axis_index("dp") * width, width, 1)
    normed_a, scale_a = normalize(stream)
    input_grad = (
        grad_stream_one + norm_back(grad_normed_a, normed_a, scale_a, attn_scale)
    ).astype(BF16)
    return (
        layer_out,
        input_grad,
        gain_mine[0],
        qkv_sum[:, :query_cols],
        qkv_sum[:, query_cols : query_cols + key_cols],
        qkv_sum[:, query_cols + key_cols :],
        out_t_sum.T,
        gain_mine[1],
        gate_sum,
        up_sum,
        down_sum,
    )


def solution(mesh):
    tokens = P(("dp", "tensor"), None)
    in_specs = (
        tokens,
        P("dp"),
        P("dp"),
        P("dp", "tensor"),
        P("dp", "tensor"),
        P("dp", "tensor"),
        P("tensor", "dp"),
        P("dp"),
        P("dp", "tensor"),
        P("dp", "tensor"),
        P("tensor", "dp"),
        tokens,
    )
    out_specs = (
        tokens,
        tokens,
        P("dp"),
        P("dp", "tensor"),
        P("dp", "tensor"),
        P("dp", "tensor"),
        P("tensor", "dp"),
        P("dp"),
        P("dp", "tensor"),
        P("dp", "tensor"),
        P("tensor", "dp"),
    )
    return jax.shard_map(
        functools.partial(local, size=mesh.shape["tensor"]),
        mesh=mesh, in_specs=in_specs, out_specs=out_specs, check_vma=False,
    )
```

```python
import functools
import math

import jax
import jax.numpy as jnp
from jax import lax
from jax.experimental import pallas as pl
from jax.experimental.pallas import tpu as pltpu
from jax.sharding import PartitionSpec as P

HD = 64
LANES = 128
EPSILON = 1e-05
ROPE_BASE = 500000.0
MASKED = -1e30
OVER_ROWS = (((0,), (0,)), ((), ()))
OVER_COLS = (((1,), (1,)), ((), ()))
VMEM_LIMIT = 56 * 2**20
F32 = jnp.float32
BF16 = jnp.bfloat16


def dot_cols(left, right):
    return lax.dot_general(left, right, OVER_COLS, preferred_element_type=F32)


def dot_rows(left, right):
    return lax.dot_general(left, right, OVER_ROWS, preferred_element_type=F32)


def dot(left, right):
    return jnp.dot(left, right, preferred_element_type=F32)


def pairs(size, bit):
    return [(index, index ^ bit) for index in range(size)]


def slots_of(size):
    if size == 4:
        return [lax.axis_index("tensor") ^ step for step in range(size)]
    return [jnp.int32(step) for step in range(size)]


ANYWHERE = pl.BlockSpec(memory_space=pl.ANY)


def nothing_kernel(*refs):
    pass


def hold(value, *others):
    return pl.pallas_call(
        nothing_kernel,
        in_specs=[ANYWHERE] * (1 + len(others)),
        out_specs=ANYWHERE,
        out_shape=jax.ShapeDtypeStruct(value.shape, value.dtype),
        input_output_aliases={0: 0},
        cost_estimate=pl.CostEstimate(flops=0, bytes_accessed=0, transcendentals=0),
    )(value, *others)


def first_hop(shard, size):
    if size != 4:
        return None
    return [lax.ppermute(shard, "tensor", pairs(size, bit)) for bit in (1, 2)]


def second_hop(shard, hop, size):
    if size != 4:
        whole = lax.all_gather(shard, "tensor", axis=0)
        return [whole[step] for step in range(size)]
    half = shard.shape[0] // 2
    one, two = hop
    three_a = lax.ppermute(one[:half], "tensor", pairs(size, 2))
    three_b = lax.ppermute(two[half:], "tensor", pairs(size, 1))
    return [shard, one, two, jnp.concatenate([three_a, three_b], axis=0)]


def gather(shard, size):
    return second_hop(shard, first_hop(shard, size), size)


def send_half(three, size):
    half = three.shape[0] // 2
    into_two = lax.ppermute(three[:half], "tensor", pairs(size, 1))
    into_one = lax.ppermute(three[half:], "tensor", pairs(size, 2))
    return into_one, into_two


def scatter(term_of, size):
    if size != 4:
        whole = jnp.concatenate([term_of(step, None, False) for step in range(size)], axis=0)
        return [lax.psum_scatter(whole, "tensor", scatter_dimension=0, tiled=True)]
    into_one, into_two = send_half(term_of(3, None, False), size)
    from_one = lax.ppermute(term_of(1, into_one, False), "tensor", pairs(size, 1))
    from_two = lax.ppermute(term_of(2, into_two, True), "tensor", pairs(size, 2))
    return [term_of(0, None, False), from_one, from_two]


def total(parts):
    return functools.reduce(jnp.add, [part.astype(F32) for part in parts])


def both_cores(chips, step):
    return [(2 * chip + core, 2 * (chip + step) + core) for chip in chips for core in range(2)]


def line_gather(shard, size):
    if size != 8:
        return lax.all_gather(shard, "dp", axis=0, tiled=True), ()
    chips = size // 2
    me = lax.axis_index("dp")
    chip, core = me // 2, me % 2
    whole = jnp.zeros((chips, 2) + shard.shape, shard.dtype)
    right, left = [shard], [shard]
    for step in range(1, chips):
        right.append(lax.ppermute(right[-1], "dp", both_cores(range(step - 1, chips - 1), 1)))
        left.append(lax.ppermute(left[-1], "dp", both_cores(range(1, chips - step + 1), -1)))
    for step in range(chips):
        piece = shard if step == 0 else jnp.where(chip >= step, right[step], left[chips - step])
        other = lax.ppermute(piece, "dp", pairs(size, 1))
        source = (chip - step + chips) % chips
        start = (source, core, 0, 0)
        whole = lax.dynamic_update_slice(whole, piece[None, None], start)
        start = (source, 1 - core, 0, 0)
        whole = lax.dynamic_update_slice(whole, other[None, None], start)
    return whole.reshape((size * shard.shape[0],) + shard.shape[1:]), (right[1], left[1])


def line_scatter(term, size):
    if size != 8:
        return lax.psum_scatter(term, "dp", scatter_dimension=0, tiled=True).astype(F32)
    chips = size // 2
    me = lax.axis_index("dp")
    chip, core = me // 2, me % 2
    blocks = term.reshape((chips, 2, term.shape[0] // size) + term.shape[1:])
    theirs = lax.dynamic_index_in_dim(blocks, 1 - core, 1, keepdims=False)
    mine = lax.dynamic_index_in_dim(blocks, core, 1, keepdims=False)
    mine = (mine.astype(F32) + lax.ppermute(theirs, "dp", pairs(size, 1)).astype(F32)).astype(BF16)

    def block(index):
        return lax.dynamic_index_in_dim(mine, index, 0, keepdims=False)

    right = left = None
    for step in range(1, chips):
        to_right, to_left = block(chip + chips - step), block(chip - chips + step)
        if right is not None:
            to_right = (to_right.astype(F32) + right.astype(F32)).astype(BF16)
            to_left = (to_left.astype(F32) + left.astype(F32)).astype(BF16)
        right = lax.ppermute(to_right, "dp", both_cores(range(min(step, chips - 1)), 1))
        left = lax.ppermute(to_left, "dp", both_cores(range(chips - step, chips), -1))
    return total([block(chip), right, left])


def sum_everywhere(value, sizes):
    for axis, size in sizes.items():
        if size & (size - 1):
            value = lax.psum(value, axis)
            continue
        bit = 1
        while bit < size:
            value = value + lax.ppermute(value, axis, pairs(size, bit))
            bit *= 2
    return value


def rope_tables(segment):
    length = segment.shape[0]
    bound = jnp.sum((segment == 0).astype(jnp.int32))
    place = lax.broadcasted_iota(jnp.int32, (length, LANES), 0)
    place = place - jnp.where(place >= bound, bound, 0)
    lane = lax.broadcasted_iota(jnp.int32, (length, LANES), 1)
    freqs = jnp.exp(
        (lane % (HD // 2)).astype(F32) * (-2.0 * math.log(ROPE_BASE) / HD)
    )
    angles = place.astype(F32) * freqs
    sine = jnp.sin(angles)
    return bound, jnp.cos(angles), jnp.where(lane % HD < HD // 2, -sine, sine)


def swap_halves(values):
    lane = lax.broadcasted_iota(jnp.int32, values.shape, 1)
    after = pltpu.roll(values, LANES - HD // 2, 1)
    before = pltpu.roll(values, HD // 2, 1)
    return jnp.where(lane % HD < HD // 2, after, before)


def normalize(stream):
    scale_r = lax.rsqrt(jnp.mean(stream * stream, axis=-1, keepdims=True) + EPSILON)
    return (stream * scale_r, scale_r)


def project_kernel(slot_ref, x_ref, gain_ref, w_ref, cos_ref, sin_ref, *rest, heads, kv):
    h_ref, q_ref, kx_ref, vx_ref, kt_ref, vt_ref = rest[-6:]
    normed, _ = normalize(x_ref[...].astype(F32))
    low = (normed * gain_ref[...]).astype(BF16)
    h_ref[...] = low
    pre = dot(low, w_ref[...])
    cosine, sine = cos_ref[...], sin_ref[...]
    rows = pre.shape[0]
    lane = lax.broadcasted_iota(jnp.int32, (rows, LANES), 1)
    chunks = []
    for chunk in range(pre.shape[1] // LANES):
        part = pre[:, chunk * LANES : (chunk + 1) * LANES]
        turned = part * cosine + swap_halves(part) * sine
        first = 2 * chunk
        if first + 1 < heads + kv:
            chunks.append(turned)
        elif first < heads + kv:
            chunks.append(jnp.where(lane < HD, turned, part))
        else:
            chunks.append(part)
        if first < heads:
            q_ref[:, chunk * LANES : (chunk + 1) * LANES] = (
                chunks[chunk] * (1.0 / math.sqrt(HD))
            ).astype(BF16)
    flipped = {}
    for head in range(2 * kv):
        place = heads + head
        part = chunks[place // 2]
        moved = pltpu.roll(part, HD, 1)
        wide = [part, moved] if place % 2 == 0 else [moved, part]
        out = kx_ref if head < kv else vx_ref
        out[head % kv, 0] = jnp.where(lane < HD, wide[0], 0.0).astype(BF16)
        out[head % kv, 1] = jnp.where(lane < HD, 0.0, wide[1]).astype(BF16)
        if place // 2 not in flipped:
            flipped[place // 2] = part.T
        turn = flipped[place // 2][(place % 2) * HD : (place % 2 + 1) * HD]
        out_t = kt_ref if head < kv else vt_ref
        out_t[(head % kv) * HD : (head % kv + 1) * HD, :] = turn.astype(BF16)


def project(slot, block, gain, weight, cosine, sine, heads, kv, length, prev):
    rows, width = block.shape
    tile = min(128, rows)
    steps = rows // tile
    columns = (heads + 2 * kv) * HD

    def at(i, slot):
        return slot[0] * steps + i

    shapes = [
        jax.ShapeDtypeStruct((length, width), BF16),
        jax.ShapeDtypeStruct((length, heads * HD), BF16),
        jax.ShapeDtypeStruct((kv, 2, length, LANES), BF16),
        jax.ShapeDtypeStruct((kv, 2, length, LANES), BF16),
        jax.ShapeDtypeStruct((kv * HD, length), BF16),
        jax.ShapeDtypeStruct((kv * HD, length), BF16),
    ]
    out_specs = [
        pl.BlockSpec((tile, width), lambda i, s: (at(i, s), 0)),
        pl.BlockSpec((tile, heads * HD), lambda i, s: (at(i, s), 0)),
        pl.BlockSpec((kv, 2, tile, LANES), lambda i, s: (0, 0, at(i, s), 0)),
        pl.BlockSpec((kv, 2, tile, LANES), lambda i, s: (0, 0, at(i, s), 0)),
        pl.BlockSpec((kv * HD, tile), lambda i, s: (0, at(i, s))),
        pl.BlockSpec((kv * HD, tile), lambda i, s: (0, at(i, s))),
    ]
    in_specs = [
        pl.BlockSpec((tile, width), lambda i, s: (i, 0)),
        pl.BlockSpec((1, width), lambda i, s: (0, 0)),
        pl.BlockSpec((width, columns), lambda i, s: (0, 0)),
        pl.BlockSpec((tile, LANES), lambda i, s: (at(i, s), 0)),
        pl.BlockSpec((tile, LANES), lambda i, s: (at(i, s), 0)),
    ]
    operands = [slot.reshape(1), block, gain, weight, cosine, sine]
    aliases = {}
    if prev is not None:
        for index, array in enumerate(prev):
            aliases[len(operands)] = index
            operands.append(array)
            in_specs.append(ANYWHERE)
    return pl.pallas_call(
        functools.partial(project_kernel, heads=heads, kv=kv),
        grid_spec=pltpu.PrefetchScalarGridSpec(
            num_scalar_prefetch=1, grid=(steps,), in_specs=in_specs, out_specs=out_specs
        ),
        out_shape=shapes,
        input_output_aliases=aliases,
        compiler_params=pltpu.CompilerParams(vmem_limit_bytes=VMEM_LIMIT),
        cost_estimate=pl.CostEstimate(
            flops=2 * rows * width * columns,
            bytes_accessed=2 * (2 * rows * width + width * columns + 3 * rows * columns),
            transcendentals=0,
        ),
    )(*operands)


def feed_kernel(h_ref, grad_ref, gate_ref, up_ref, down_ref, *rest):
    hidden_ref, dgate_ref, dup_ref, h_out, grad_out = rest[-5:]
    wide = h_out.shape[1]
    lanes = pl.ds(pl.multiple_of(pl.program_id(0) * wide, wide), wide)
    gate = dot(h_ref[...], gate_ref[...])
    up = dot(h_ref[...], up_ref[...])
    sigmoid = jax.nn.sigmoid(gate)
    silu = gate * sigmoid
    hidden_ref[...] = (silu * up).astype(BF16)
    dhidden = dot(grad_ref[...], down_ref[...])
    dup_ref[...] = (dhidden * silu).astype(BF16)
    dgate_ref[...] = (dhidden * up * sigmoid * (1.0 + gate * (1.0 - sigmoid))).astype(BF16)
    h_out[...] = h_ref[:, lanes]
    grad_out[...] = grad_ref[:, lanes]


def feed(place, count, normed, grad, gate_w, up_w, down_t, prev, others):
    rows, width = normed.shape
    units = gate_w.shape[1]
    steps = 4
    tile, wide = units // steps, width // steps
    shapes = [jax.ShapeDtypeStruct((count * rows, units), BF16)] * 3
    shapes += [jax.ShapeDtypeStruct((count * rows, width), BF16)] * 2
    weight = pl.BlockSpec((width, tile), lambda i: (0, i))
    tokens = pl.BlockSpec((rows, width), lambda i: (0, 0))
    in_specs = [tokens, tokens, weight, weight, weight]
    out_specs = [pl.BlockSpec((rows, tile), lambda i: (place, i))] * 3
    out_specs += [pl.BlockSpec((rows, wide), lambda i: (place, i))] * 2
    operands = [normed, grad, gate_w, up_w, down_t]
    aliases = {}
    if prev is not None:
        for index, array in enumerate(prev):
            aliases[len(operands)] = index
            operands.append(array)
            in_specs.append(ANYWHERE)
    operands += others
    in_specs += [ANYWHERE] * len(others)
    return pl.pallas_call(
        feed_kernel,
        grid=(steps,),
        in_specs=in_specs,
        out_specs=out_specs,
        out_shape=shapes,
        input_output_aliases=aliases,
        compiler_params=pltpu.CompilerParams(vmem_limit_bytes=VMEM_LIMIT),
        cost_estimate=pl.CostEstimate(
            flops=6 * rows * width * units,
            bytes_accessed=2 * (3 * width * units + 3 * rows * units + 4 * rows * width),
            transcendentals=rows * units,
        ),
    )(*operands)


def back_kernel(slot_ref, *refs, terms, added, upper):
    out_ref = refs[-1]
    value = dot_cols(refs[0][...], refs[terms][...])
    for term in range(1, terms):
        value = value + dot_cols(refs[term][...], refs[terms + term][...])
    if not added:
        out_ref[...] = value.astype(out_ref.dtype)
        return
    half = value.shape[0] // 2
    into = refs[2 * terms][...].astype(F32)
    top, bottom = value[:half], value[half:]
    if upper:
        top = top + into
    else:
        bottom = bottom + into
    out_ref[:half, :] = top.astype(out_ref.dtype)
    out_ref[half:, :] = bottom.astype(out_ref.dtype)


def back(slot, rows, lefts, weights, into, upper, others=()):
    depth = lefts[0].shape[1]
    width = weights[0].shape[0]
    tile = min(512, width)
    terms = len(lefts)
    in_specs = [pl.BlockSpec((rows, depth), lambda i, s: (s[0], 0))] * terms
    in_specs += [pl.BlockSpec((tile, depth), lambda i, s: (i, 0))] * terms
    operands = [jnp.asarray(slot, jnp.int32).reshape(1), *lefts, *weights]
    if into is not None:
        in_specs.append(pl.BlockSpec((rows // 2, tile), lambda i, s: (0, i)))
        operands.append(into)
    operands += others
    in_specs += [ANYWHERE] * len(others)
    return pl.pallas_call(
        functools.partial(back_kernel, terms=terms, added=into is not None, upper=upper),
        grid_spec=pltpu.PrefetchScalarGridSpec(
            num_scalar_prefetch=1,
            grid=(width // tile,),
            in_specs=in_specs,
            out_specs=pl.BlockSpec((rows, tile), lambda i, s: (0, i)),
        ),
        out_shape=jax.ShapeDtypeStruct((rows, width), BF16),
        compiler_params=pltpu.CompilerParams(vmem_limit_bytes=VMEM_LIMIT),
        cost_estimate=pl.CostEstimate(
            flops=2 * terms * rows * width * depth,
            bytes_accessed=2 * (terms * (rows + width) * depth + 2 * rows * width),
            transcendentals=0,
        ),
    )(*operands)


def back_attended_kernel(slot_ref, grad_ref, w_ref, *rest):
    out_ref, copy_ref = rest[-2:]
    out_ref[...] = dot(grad_ref[...], w_ref[...]).astype(BF16)
    copy_ref[...] = grad_ref[...]


def back_attended(slot, grad, weight, length, prev):
    rows, width = grad.shape
    columns = weight.shape[1]
    tile = min(128, rows)
    steps = rows // tile
    in_specs = [
        pl.BlockSpec((tile, width), lambda i, s: (i, 0)),
        pl.BlockSpec((width, columns), lambda i, s: (0, 0)),
    ]
    operands = [slot.reshape(1), grad, weight]
    aliases = {}
    if prev is not None:
        for index, array in enumerate(prev):
            aliases[len(operands)] = index
            operands.append(array)
            in_specs.append(ANYWHERE)
    return pl.pallas_call(
        back_attended_kernel,
        grid_spec=pltpu.PrefetchScalarGridSpec(
            num_scalar_prefetch=1,
            grid=(steps,),
            in_specs=in_specs,
            out_specs=[
                pl.BlockSpec((tile, columns), lambda i, s: (s[0] * steps + i, 0)),
                pl.BlockSpec((tile, width), lambda i, s: (s[0] * steps + i, 0)),
            ],
        ),
        out_shape=[
            jax.ShapeDtypeStruct((length, columns), BF16),
            jax.ShapeDtypeStruct((length, width), BF16),
        ],
        input_output_aliases=aliases,
        compiler_params=pltpu.CompilerParams(vmem_limit_bytes=VMEM_LIMIT),
        cost_estimate=pl.CostEstimate(
            flops=2 * rows * width * columns,
            bytes_accessed=2 * (2 * rows * width + width * columns + rows * columns),
            transcendentals=0,
        ),
    )(*operands)


def causal(block):
    keys = lax.broadcasted_iota(jnp.int32, (block, block), 0)
    return keys <= lax.broadcasted_iota(jnp.int32, (block, block), 1)


def first_block(bound, offset, block):
    return jnp.where(offset >= bound, lax.div(bound, jnp.int32(block)), 0)


def attend_kernel(bound_ref, q_ref, kx_ref, vt_ref, out_ref, lse_ref, top_ref, acc_ref, *, block):
    length = q_ref.shape[0]
    kv = kx_ref.shape[0]
    per = q_ref.shape[1] // LANES // kv
    bound = bound_ref[0]
    ones = jnp.ones((16, block), BF16)
    for group in range(kv):

        def q_step(index, _):
            offset = pl.multiple_of(index * block, block)
            top_ref[...] = jnp.full(top_ref.shape, MASKED, F32)
            acc_ref[...] = jnp.zeros(acc_ref.shape, F32)

            def tile(step, diagonal):
                keys = pl.ds(pl.multiple_of(step * block, block), block)
                value_t = jnp.concatenate(
                    [vt_ref[group * HD : (group + 1) * HD, keys], ones], axis=0
                )
                for head in range(2 * per):
                    column = (group * per + head // 2) * LANES
                    query = q_ref[pl.ds(offset, block), column : column + LANES]
                    scores = dot_cols(kx_ref[group, head % 2, keys, :], query)
                    if diagonal:
                        scores = jnp.where(causal(block), scores, MASKED)
                    old = top_ref[head, 0:1, :]
                    top = jnp.maximum(old, jnp.max(scores, axis=0, keepdims=True))
                    powered = jnp.exp(scores - top).astype(BF16)
                    acc_ref[head] = acc_ref[head] * jnp.exp(old - top) + dot(value_t, powered)
                    top_ref[head, 0:1, :] = top

            def full_tile(step, carry):
                tile(step, False)
                return carry

            lax.fori_loop(first_block(bound, offset, block), index, full_tile, 0)
            tile(index, True)
            for pair in range(per):
                both = []
                for head in (2 * pair, 2 * pair + 1):
                    total = acc_ref[head, HD : HD + 1, :]
                    both.append(acc_ref[head, :HD, :] / total)
                    place = group * 2 * per + head
                    lse_ref[place : place + 1, pl.ds(offset, block)] = top_ref[
                        head, 0:1, :
                    ] + jnp.log(total)
                column = (group * per + pair) * LANES
                out_ref[pl.ds(offset, block), column : column + LANES] = (
                    jnp.concatenate(both, axis=0).T.astype(BF16)
                )
            return _

        lax.fori_loop(0, length // block, q_step, 0)


def attend(bound, queries, kx, vt, block):
    length, width = queries.shape
    heads = width // HD
    kv = kx.shape[0]
    per = heads // kv
    cells = heads * length * (length + block) // 2
    vmem = pl.BlockSpec(memory_space=pltpu.VMEM)
    return pl.pallas_call(
        functools.partial(attend_kernel, block=block),
        in_specs=[pl.BlockSpec(memory_space=pltpu.SMEM), vmem, vmem, vmem],
        out_specs=[vmem, vmem],
        out_shape=[
            jax.ShapeDtypeStruct((length, width), BF16),
            jax.ShapeDtypeStruct((heads, length), F32),
        ],
        scratch_shapes=[
            pltpu.VMEM((per, 8, block), F32),
            pltpu.VMEM((per, HD + 16, block), F32),
        ],
        compiler_params=pltpu.CompilerParams(vmem_limit_bytes=VMEM_LIMIT),
        cost_estimate=pl.CostEstimate(
            flops=2 * 4 * HD * 4 * cells, bytes_accessed=12 * length * width, transcendentals=cells
        ),
    )(bound.reshape(1), queries, kx, vt)


def attend_back_kernel(
    bound_ref, q_ref, kx_ref, vx_ref, kt_ref, lse_ref, out_ref, grad_ref, cos_ref, sin_ref,
    dqkv_ref, dk_ref, dv_ref, dq_ref, *, block
):
    length = q_ref.shape[0]
    kv = kx_ref.shape[0]
    heads = q_ref.shape[1] // HD
    per = heads // 2 // kv
    bound = bound_ref[0]
    dk_ref[...] = jnp.zeros(dk_ref.shape, F32)
    dv_ref[...] = jnp.zeros(dv_ref.shape, F32)
    lane = lax.broadcasted_iota(jnp.int32, (8, LANES), 1)
    row = lax.broadcasted_iota(jnp.int32, (8, LANES), 0)
    chosen = ((lane // HD) == row).astype(F32)

    def turn_back(values, rows):
        return values * cos_ref[rows, :] - swap_halves(values) * sin_ref[rows, :]

    for group in range(kv):

        def q_step(index, _):
            offset = pl.multiple_of(index * block, block)
            rows = pl.ds(offset, block)
            dq_ref[...] = jnp.zeros(dq_ref.shape, F32)
            deltas = []
            for pair in range(per):
                column = (group * per + pair) * LANES
                product = grad_ref[rows, column : column + LANES].astype(F32) * out_ref[
                    rows, column : column + LANES
                ].astype(F32)
                deltas.append(
                    lax.dot_general(
                        chosen, product, OVER_COLS, precision=lax.Precision.HIGHEST,
                        preferred_element_type=F32,
                    )
                )

            def tile(step, diagonal):
                keys = pl.ds(pl.multiple_of(step * block, block), block)
                key_t = kt_ref[group * HD : (group + 1) * HD, keys]
                for parity in range(2):
                    key_add, value_add = 0.0, 0.0
                    for pair in range(per):
                        head = 2 * pair + parity
                        place = group * 2 * per + head
                        column = (group * per + pair) * LANES
                        query = q_ref[rows, column : column + LANES]
                        grad = grad_ref[rows, column : column + LANES]
                        scores = dot_cols(kx_ref[group, parity, keys, :], query)
                        if diagonal:
                            scores = jnp.where(causal(block), scores, MASKED)
                        probs = jnp.exp(scores - lse_ref[place : place + 1, rows])
                        dprobs = dot_cols(vx_ref[group, parity, keys, :], grad)
                        dscores = (probs * (dprobs - deltas[pair][parity : parity + 1])).astype(BF16)
                        value_add = value_add + dot(probs.astype(BF16), grad)
                        key_add = key_add + dot(dscores, query)
                        dq_ref[head * HD : (head + 1) * HD, :] += dot(key_t, dscores)
                    dk_ref[group, parity, keys, :] += key_add
                    dv_ref[group, parity, keys, :] += value_add

            def full_tile(step, carry):
                tile(step, False)
                return carry

            lax.fori_loop(first_block(bound, offset, block), index, full_tile, 0)
            tile(index, True)
            for pair in range(per):
                column = (group * per + pair) * LANES
                grad_q = dq_ref[pair * LANES : (pair + 1) * LANES, :].T * (1.0 / math.sqrt(HD))
                dqkv_ref[rows, column : column + LANES] = turn_back(grad_q, rows).astype(BF16)
            return _

        lax.fori_loop(0, length // block, q_step, 0)

    def finish(index, _):
        rows = pl.ds(pl.multiple_of(index * block, block), block)
        lanes = lax.broadcasted_iota(jnp.int32, (block, LANES), 1)

        def placed(part, half):
            ref = dk_ref if part < kv else dv_ref
            even, odd = ref[part % kv, 0, rows, :], ref[part % kv, 1, rows, :]
            return even + pltpu.roll(odd, HD, 1) if half == 0 else pltpu.roll(even, HD, 1) + odd

        for chunk in range(kv):
            values = jnp.where(lanes < HD, placed(2 * chunk, 0), placed(2 * chunk + 1, 1))
            if 2 * chunk + 1 < kv:
                values = turn_back(values, rows)
            elif 2 * chunk < kv:
                values = jnp.where(lanes < HD, turn_back(values, rows), values)
            column = heads * HD + chunk * LANES
            dqkv_ref[rows, column : column + LANES] = values.astype(BF16)
        return _

    lax.fori_loop(0, length // block, finish, 0)


def attend_back(bound, queries, kx, vx, kt, log_sums, attended, grad, cosine, sine, block):
    length, width = queries.shape
    heads = width // HD
    kv = kx.shape[0]
    cells = heads * length * (length + block) // 2
    vmem = pl.BlockSpec(memory_space=pltpu.VMEM)
    return pl.pallas_call(
        functools.partial(attend_back_kernel, block=block),
        in_specs=[pl.BlockSpec(memory_space=pltpu.SMEM)] + [vmem] * 9,
        out_specs=vmem,
        out_shape=jax.ShapeDtypeStruct((length, width + 2 * kv * HD), BF16),
        scratch_shapes=[
            pltpu.VMEM((kv, 2, length, LANES), F32),
            pltpu.VMEM((kv, 2, length, LANES), F32),
            pltpu.VMEM((heads // kv * HD, block), F32),
        ],
        compiler_params=pltpu.CompilerParams(vmem_limit_bytes=VMEM_LIMIT),
        cost_estimate=pl.CostEstimate(
            flops=2 * 10 * HD * 4 * cells, bytes_accessed=20 * length * width, transcendentals=cells
        ),
    )(bound.reshape(1), queries, kx, vx, kt, log_sums, attended, grad, cosine, sine)


def local(
    inputs,
    segment_ids,
    attn_gain,
    query_weight,
    key_weight,
    value_weight,
    output_weight,
    mlp_gain,
    gate_weight,
    up_weight,
    down_weight,
    cotangent,
    *,
    sizes,
):
    rows = inputs.shape[0]
    length = segment_ids.shape[0]
    query_cols = query_weight.shape[1]
    key_cols = key_weight.shape[1]
    heads, kv = query_cols // HD, key_cols // HD
    columns = query_cols + 2 * key_cols
    slots = slots_of(sizes["tensor"])
    tensor, dp = sizes["tensor"], sizes["dp"]
    gains = jnp.pad(jnp.stack([attn_gain, mlp_gain], axis=1), ((0, 0), (0, LANES - 2)))
    bundle = lax.all_gather(
        jnp.concatenate([query_weight, key_weight, value_weight, output_weight.T, gains], axis=1),
        "dp", axis=0, tiled=True,
    )
    gate_full = lax.all_gather(gate_weight, "dp", axis=0, tiled=True)
    up_full = lax.all_gather(up_weight, "dp", axis=0, tiled=True)
    down_t, down_first = line_gather(hold(down_weight.T, bundle), dp)
    qkv_weight = bundle[:, :columns]
    out_t = bundle[:, columns : columns + query_cols]
    scales = bundle[:, columns + query_cols : columns + query_cols + 2].T.astype(F32)
    attn_scale, mlp_scale = scales[0:1], scales[1:2]

    bound, cosine, sine = rope_tables(segment_ids)
    blocks = gather(inputs, tensor)
    arrays = None
    for slot, block in zip(slots, blocks):
        arrays = project(
            slot, block, attn_scale, bundle, cosine, sine, heads, kv, length, arrays
        )
    block_a, queries, kx, vx, kt, vt = arrays
    cotangent_sent = hold(cotangent, blocks[-1])
    cotangent_hop = first_hop(cotangent_sent, tensor)
    attended, log_sums = attend(bound, queries, kx, vt, rows)

    stream = inputs.astype(F32)
    early = [*(cotangent_hop or ()), *down_first]
    stream_one = stream + total(
        scatter(
            lambda place, into, upper: back(
                slots[place], rows, [attended], [out_t], into, upper,
                early if place == tensor - 1 else (),
            ),
            tensor,
        )
    )
    normed_m, scale_m = normalize(stream_one)
    parts_m = gather((normed_m * mlp_scale).astype(BF16), tensor)
    grad_parts = second_hop(cotangent_sent, cotangent_hop, tensor)

    def feed_at(place, fed, others):
        return feed(
            place, tensor, parts_m[place], grad_parts[place], gate_full, up_full, down_t, fed, others
        )

    def back_m(place, fed, into=None, upper=False, others=()):
        return back(place, rows, fed[1:3], [gate_full, up_full], into, upper, others)

    def back_out(place, fed, into=None, upper=False, others=()):
        return back(place, rows, fed[0:1], [down_t], into, upper, others)

    if tensor == 4:
        fed = feed_at(3, None, ())
        three_m = back_m(3, fed)
        three_out = back_out(3, fed, others=[three_m])
        m_one, m_two = send_half(three_m, tensor)
        out_one, out_two = send_half(three_out, tensor)
        fed = feed_at(1, fed, [three_out])
        fed = feed_at(2, fed, ())
        one_m = back_m(1, fed, m_one, False)
        two_m = back_m(2, fed, m_two, True)
        fed = feed_at(0, fed, [one_m, two_m])
        grad_m_parts = [
            back_m(0, fed),
            lax.ppermute(one_m, "tensor", pairs(tensor, 1)),
            lax.ppermute(two_m, "tensor", pairs(tensor, 2)),
        ]
        out_terms = [
            back_out(0, fed),
            back_out(1, fed, out_one, False),
            back_out(2, fed, out_two, True),
        ]
    else:
        fed = None
        for place in range(tensor):
            fed = feed_at(place, fed, ())
        grad_m_parts = scatter(lambda place, into, upper: back_m(place, fed), tensor)
    hidden, grad_gate, grad_up, block_m, grad_block = fed

    def reduce_rows(term):
        return lax.psum_scatter(term, "dp", scatter_dimension=0, tiled=True).astype(F32)

    down_t_sum = line_scatter(dot_rows(grad_block, hidden).astype(BF16), dp)
    gate_sum = reduce_rows(dot_rows(block_m, grad_gate).astype(BF16))
    up_sum = reduce_rows(dot_rows(block_m, grad_up).astype(BF16))

    def norm_back(grad_in, normed, scale_r, gain):
        scaled = grad_in * gain
        return scale_r * (scaled - normed * jnp.mean(scaled * normed, axis=-1, keepdims=True))

    grad_normed_m = total(grad_m_parts)
    mlp_gain_term = jnp.sum(grad_normed_m * normed_m, axis=0)
    grad_stream_one = cotangent.astype(F32) + norm_back(grad_normed_m, normed_m, scale_m, mlp_scale)
    backs = None
    for slot, part in zip(slots, gather(grad_stream_one.astype(BF16), tensor)):
        backs = back_attended(slot, part, out_t, length, backs)
    grad_attended, grad_stream_block = backs
    out_t_sum = line_scatter(dot_rows(grad_stream_block, attended).astype(BF16), dp)
    grad_qkv = attend_back(
        bound, queries, kx, vx, kt, log_sums, attended, grad_attended, cosine, sine, rows
    )
    if tensor == 4:
        out_parts = [
            out_terms[0],
            lax.ppermute(hold(out_terms[1], grad_attended), "tensor", pairs(tensor, 1)),
            lax.ppermute(hold(out_terms[2], grad_attended), "tensor", pairs(tensor, 2)),
        ]
    else:
        out_parts = scatter(lambda place, into, upper: back_out(place, fed), tensor)
    layer_out = (stream_one + total(out_parts)).astype(BF16)
    grad_normed_a = total(
        scatter(
            lambda place, into, upper: back(
                slots[place], rows, [grad_qkv], [qkv_weight], into, upper,
                out_parts[1:] if place == tensor - 1 else (),
            ),
            tensor,
        )
    )
    qkv_wgrad = dot_rows(block_a, grad_qkv)
    qkv_sum = line_scatter(qkv_wgrad.astype(BF16), dp)
    attn_gain_term = jnp.sum(qkv_wgrad * qkv_weight.astype(F32), axis=1) / attn_scale[0]
    gain_totals = sum_everywhere(jnp.stack([attn_gain_term, mlp_gain_term]), sizes)
    width = attn_gain.shape[0]
    gain_mine = lax.dynamic_slice_in_dim(gain_totals, lax.axis_index("dp") * width, width, 1)
    normed_a, scale_a = normalize(stream)
    input_grad = (
        grad_stream_one + norm_back(grad_normed_a, normed_a, scale_a, attn_scale)
    ).astype(BF16)
    return (
        layer_out,
        input_grad,
        gain_mine[0],
        qkv_sum[:, :query_cols],
        qkv_sum[:, query_cols : query_cols + key_cols],
        qkv_sum[:, query_cols + key_cols :],
        out_t_sum.T,
        gain_mine[1],
        gate_sum,
        up_sum,
        down_t_sum.T,
    )


def solution(mesh):
    tokens = P(("dp", "tensor"), None)
    in_specs = (
        tokens,
        P("dp"),
        P("dp"),
        P("dp", "tensor"),
        P("dp", "tensor"),
        P("dp", "tensor"),
        P("tensor", "dp"),
        P("dp"),
        P("dp", "tensor"),
        P("dp", "tensor"),
        P("tensor", "dp"),
        tokens,
    )
    out_specs = (
        tokens,
        tokens,
        P("dp"),
        P("dp", "tensor"),
        P("dp", "tensor"),
        P("dp", "tensor"),
        P("tensor", "dp"),
        P("dp"),
        P("dp", "tensor"),
        P("dp", "tensor"),
        P("tensor", "dp"),
    )
    return jax.shard_map(
        functools.partial(local, sizes={axis: mesh.shape[axis] for axis in ("tensor", "dp")}),
        mesh=mesh, in_specs=in_specs, out_specs=out_specs, check_vma=False,
    )
```

```python
import functools
import math

import jax
import jax.numpy as jnp
from jax import lax
from jax.experimental import pallas as pl
from jax.experimental.pallas import tpu as pltpu
from jax.sharding import PartitionSpec as P

HD = 64
LANES = 128
EPSILON = 1e-05
ROPE_BASE = 500000.0
MASKED = -1e30
OVER_ROWS = (((0,), (0,)), ((), ()))
OVER_COLS = (((1,), (1,)), ((), ()))
VMEM_LIMIT = 48 * 2**20
CHEAPER = 4
F32 = jnp.float32
BF16 = jnp.bfloat16


def dot_cols(left, right):
    return lax.dot_general(left, right, OVER_COLS, preferred_element_type=F32)


def dot_rows(left, right):
    return lax.dot_general(left, right, OVER_ROWS, preferred_element_type=F32)


def dot(left, right):
    return jnp.dot(left, right, preferred_element_type=F32)


def pairs(size, bit):
    return [(index, index ^ bit) for index in range(size)]


def slots_of(size):
    if size == 4:
        return [lax.axis_index("tensor") ^ step for step in range(size)]
    return [jnp.int32(step) for step in range(size)]


ANYWHERE = pl.BlockSpec(memory_space=pl.ANY)


def nothing_kernel(*refs):
    pass


def hold(value, *others):
    return pl.pallas_call(
        nothing_kernel,
        in_specs=[ANYWHERE] * (1 + len(others)),
        out_specs=ANYWHERE,
        out_shape=jax.ShapeDtypeStruct(value.shape, value.dtype),
        input_output_aliases={0: 0},
        cost_estimate=pl.CostEstimate(flops=0, bytes_accessed=0, transcendentals=0),
    )(value, *others)


def first_hop(shard, size):
    if size != 4:
        return None
    return [lax.ppermute(shard, "tensor", pairs(size, bit)) for bit in (1, 2)]


def second_hop(shard, hop, size):
    if size != 4:
        whole = lax.all_gather(shard, "tensor", axis=0)
        return [whole[step] for step in range(size)]
    half = shard.shape[0] // 2
    one, two = hop
    three_a = lax.ppermute(one[:half], "tensor", pairs(size, 2))
    three_b = lax.ppermute(two[half:], "tensor", pairs(size, 1))
    return [shard, one, two, jnp.concatenate([three_a, three_b], axis=0)]


def gather(shard, size):
    return second_hop(shard, first_hop(shard, size), size)


def send_half(three, size):
    half = three.shape[0] // 2
    into_two = lax.ppermute(three[:half], "tensor", pairs(size, 1))
    into_one = lax.ppermute(three[half:], "tensor", pairs(size, 2))
    return into_one, into_two


def send_whole(one, two, into, size):
    into_one, into_two = into
    half = one.shape[0] // 2
    lower = (one[half:].astype(F32) + into_one.astype(F32)).astype(BF16)
    upper = (two[:half].astype(F32) + into_two.astype(F32)).astype(BF16)
    return [
        lax.ppermute(jnp.concatenate([one[:half], lower], axis=0), "tensor", pairs(size, 1)),
        lax.ppermute(jnp.concatenate([upper, two[half:]], axis=0), "tensor", pairs(size, 2)),
    ]


def sum_whole(terms):
    return [
        lax.psum_scatter(
            jnp.concatenate(terms, axis=0), "tensor", scatter_dimension=0, tiled=True
        )
    ]


def total(parts):
    return functools.reduce(jnp.add, [part.astype(F32) for part in parts])


def sum_everywhere(value, sizes):
    for axis, size in sizes.items():
        if size & (size - 1):
            value = lax.psum(value, axis)
            continue
        bit = 1
        while bit < size:
            value = value + lax.ppermute(value, axis, pairs(size, bit))
            bit *= 2
    return value


def rope_tables(segment):
    length = segment.shape[0]
    bound = jnp.sum((segment == 0).astype(jnp.int32))
    place = lax.broadcasted_iota(jnp.int32, (length, LANES), 0)
    place = place - jnp.where(place >= bound, bound, 0)
    lane = lax.broadcasted_iota(jnp.int32, (length, LANES), 1)
    freqs = jnp.exp(
        (lane % (HD // 2)).astype(F32) * (-2.0 * math.log(ROPE_BASE) / HD)
    )
    angles = place.astype(F32) * freqs
    sine = jnp.sin(angles)
    return bound, jnp.cos(angles), jnp.where(lane % HD < HD // 2, -sine, sine)


def swap_halves(values):
    lane = lax.broadcasted_iota(jnp.int32, values.shape, 1)
    after = pltpu.roll(values, LANES - HD // 2, 1)
    before = pltpu.roll(values, HD // 2, 1)
    return jnp.where(lane % HD < HD // 2, after, before)


def normalize(stream):
    scale_r = lax.rsqrt(jnp.mean(stream * stream, axis=-1, keepdims=True) + EPSILON)
    return (stream * scale_r, scale_r)


def project_kernel(slot_ref, *refs, count, steps, heads, kv):
    gains_ref, w_ref, cos_ref, sin_ref = refs[count : count + 4]
    h_ref, q_ref, kx_ref, vx_ref, kt_ref, vt_ref, gain_ref = refs[-7:]

    @pl.when(pl.program_id(0) == 0)
    def _():
        gain_ref[...] = gains_ref[...].astype(F32).T[:8]

    which = pl.program_id(0) // steps
    tokens = refs[0][...]
    for block in range(1, count):
        tokens = jnp.where(which == block, refs[block][...], tokens)
    normed, _ = normalize(tokens.astype(F32))
    low = (normed * gain_ref[0:1, :]).astype(BF16)
    h_ref[...] = low
    pre = dot(low, w_ref[...])
    cosine, sine = cos_ref[...], sin_ref[...]
    rows = pre.shape[0]
    lane = lax.broadcasted_iota(jnp.int32, (rows, LANES), 1)
    chunks = []
    for chunk in range(pre.shape[1] // LANES):
        part = pre[:, chunk * LANES : (chunk + 1) * LANES]
        turned = part * cosine + swap_halves(part) * sine
        first = 2 * chunk
        if first + 1 < heads + kv:
            chunks.append(turned)
        elif first < heads + kv:
            chunks.append(jnp.where(lane < HD, turned, part))
        else:
            chunks.append(part)
        if first < heads:
            q_ref[:, chunk * LANES : (chunk + 1) * LANES] = (
                chunks[chunk] * (1.0 / math.sqrt(HD))
            ).astype(BF16)
    flipped = {}
    for head in range(2 * kv):
        place = heads + head
        part = chunks[place // 2]
        moved = pltpu.roll(part, HD, 1)
        wide = [part, moved] if place % 2 == 0 else [moved, part]
        out = kx_ref if head < kv else vx_ref
        out[head % kv, 0] = jnp.where(lane < HD, wide[0], 0.0).astype(BF16)
        out[head % kv, 1] = jnp.where(lane < HD, 0.0, wide[1]).astype(BF16)
        if place // 2 not in flipped:
            flipped[place // 2] = part.T
        turn = flipped[place // 2][(place % 2) * HD : (place % 2 + 1) * HD]
        out_t = kt_ref if head < kv else vt_ref
        out_t[(head % kv) * HD : (head % kv + 1) * HD, :] = turn.astype(BF16)


def project(slots, blocks, bundle, cosine, sine, heads, kv, length, prev):
    rows, width = blocks[0].shape
    count = len(blocks)
    tile = min(256, rows)
    steps = rows // tile
    columns = (heads + 2 * kv) * HD

    def at(i, slot):
        return slot[i // steps] * steps + i % steps

    shapes = [
        jax.ShapeDtypeStruct((length, width), BF16),
        jax.ShapeDtypeStruct((length, heads * HD), BF16),
        jax.ShapeDtypeStruct((kv, 2, length, LANES), BF16),
        jax.ShapeDtypeStruct((kv, 2, length, LANES), BF16),
        jax.ShapeDtypeStruct((kv * HD, length), BF16),
        jax.ShapeDtypeStruct((kv * HD, length), BF16),
    ]
    out_specs = [
        pl.BlockSpec((tile, width), lambda i, s: (at(i, s), 0)),
        pl.BlockSpec((tile, heads * HD), lambda i, s: (at(i, s), 0)),
        pl.BlockSpec((kv, 2, tile, LANES), lambda i, s: (0, 0, at(i, s), 0)),
        pl.BlockSpec((kv, 2, tile, LANES), lambda i, s: (0, 0, at(i, s), 0)),
        pl.BlockSpec((kv * HD, tile), lambda i, s: (0, at(i, s))),
        pl.BlockSpec((kv * HD, tile), lambda i, s: (0, at(i, s))),
    ]
    in_specs = [
        pl.BlockSpec((tile, width), lambda i, s, b=block: (jnp.clip(i - b * steps, 0, steps - 1), 0))
        for block in range(count)
    ]
    in_specs += [
        pl.BlockSpec((width, LANES), lambda i, s: (0, columns // LANES)),
        pl.BlockSpec((width, columns), lambda i, s: (0, 0)),
        pl.BlockSpec((tile, LANES), lambda i, s: (at(i, s), 0)),
        pl.BlockSpec((tile, LANES), lambda i, s: (at(i, s), 0)),
    ]
    operands = [jnp.stack(slots), *blocks, bundle, bundle, cosine, sine]
    aliases = {}
    if prev is not None:
        for index, array in enumerate(prev):
            aliases[len(operands)] = index
            operands.append(array)
            in_specs.append(ANYWHERE)
    return pl.pallas_call(
        functools.partial(
            project_kernel, count=count, steps=steps, heads=heads, kv=kv
        ),
        grid_spec=pltpu.PrefetchScalarGridSpec(
            num_scalar_prefetch=1,
            grid=(count * steps,),
            in_specs=in_specs,
            out_specs=out_specs,
            scratch_shapes=[pltpu.VMEM((8, width), F32)],
        ),
        out_shape=shapes,
        input_output_aliases=aliases,
        compiler_params=pltpu.CompilerParams(vmem_limit_bytes=VMEM_LIMIT),
        cost_estimate=pl.CostEstimate(
            flops=2 * count * rows * width * columns // CHEAPER, bytes_accessed=0, transcendentals=0
        ),
    )(*operands)


def feed_kernel(*refs, count):
    tokens, grads = refs[:count], refs[count : 2 * count]
    gate_ref, up_ref, down_ref = refs[2 * count : 2 * count + 3]
    hidden_ref, dgate_ref, dup_ref, h_out, grad_out = refs[-5:]
    rows = tokens[0].shape[0]
    wide = h_out.shape[1]
    tile = min(256, gate_ref.shape[1])
    lanes = pl.ds(pl.multiple_of(pl.program_id(0) * wide, wide), wide)
    for block in range(count):
        where = slice(block * rows, (block + 1) * rows)
        h_out[where, :] = tokens[block][:, lanes]
        grad_out[where, :] = grads[block][:, lanes]
    for part in range(gate_ref.shape[1] // tile):
        columns = slice(part * tile, (part + 1) * tile)
        for block in range(count):
            where = slice(block * rows, (block + 1) * rows)
            gate = dot(tokens[block][...], gate_ref[:, columns])
            up = dot(tokens[block][...], up_ref[:, columns])
            dhidden = dot(grads[block][...], down_ref[:, columns])
            sigmoid = 0.5 * jnp.tanh(0.5 * gate) + 0.5
            silu = gate * sigmoid
            hidden_ref[where, columns] = (silu * up).astype(BF16)
            dup_ref[where, columns] = (dhidden * silu).astype(BF16)
            dgate_ref[where, columns] = (
                dhidden * up * (sigmoid + silu * (1.0 - sigmoid))
            ).astype(BF16)


def feed(place, blocks, normed, grads, weights, prev, others):
    rows, width = normed[0].shape
    count = len(normed)
    units = weights.shape[1] // 3
    steps = 4
    tile, wide = units // steps, width // steps
    shapes = [jax.ShapeDtypeStruct((blocks * rows, units), BF16)] * 3
    shapes += [jax.ShapeDtypeStruct((blocks * rows, width), BF16)] * 2
    tokens = pl.BlockSpec((rows, width), lambda i: (0, 0), pipeline_mode=pl.Buffered(1))
    in_specs = [tokens] * (2 * count)
    in_specs += [
        pl.BlockSpec((width, tile), lambda i, w=which: (0, w * steps + i)) for which in range(3)
    ]
    out_specs = [pl.BlockSpec((count * rows, tile), lambda i: (place, i))] * 3
    out_specs += [pl.BlockSpec((count * rows, wide), lambda i: (place, i))] * 2
    operands = [*normed, *grads, weights, weights, weights]
    aliases = {}
    if prev is not None:
        for index, array in enumerate(prev):
            aliases[len(operands)] = index
            operands.append(array)
            in_specs.append(ANYWHERE)
    operands += others
    in_specs += [ANYWHERE] * len(others)
    return pl.pallas_call(
        functools.partial(feed_kernel, count=count),
        grid=(steps,),
        in_specs=in_specs,
        out_specs=out_specs,
        out_shape=shapes,
        input_output_aliases=aliases,
        compiler_params=pltpu.CompilerParams(vmem_limit_bytes=VMEM_LIMIT),
        cost_estimate=pl.CostEstimate(
            flops=6 * count * rows * width * units // CHEAPER, bytes_accessed=0, transcendentals=0
        ),
    )(*operands)


def back_kernel(slot_ref, *refs, count, terms, added):
    outs = refs[-count:]
    weights = refs[count * terms : (count + 1) * terms]
    into = list(refs[(count + 1) * terms :])
    for block in range(count):
        value = dot_cols(refs[block * terms][...], weights[0][...])
        for term in range(1, terms):
            value = value + dot_cols(refs[block * terms + term][...], weights[term][...])
        if added[block] is None:
            outs[block][...] = value.astype(BF16)
            continue
        half = value.shape[0] // 2
        extra = into.pop(0)[...].astype(F32)
        top, bottom = value[:half], value[half:]
        if added[block]:
            top = top + extra
        else:
            bottom = bottom + extra
        outs[block][:half, :] = top.astype(BF16)
        outs[block][half:, :] = bottom.astype(BF16)


def back(slots, rows, lefts, weights, places, into=None, others=()):
    depth = lefts[0].shape[1]
    width = weights[0].shape[0]
    tile = min(512, width)
    terms, count = len(lefts), len(slots)
    into = into or [None] * count
    in_specs, operands = [], [jnp.stack([jnp.asarray(slot, jnp.int32) for slot in slots])]
    for block in range(count):
        in_specs += [pl.BlockSpec((rows, depth), lambda i, s, b=block: (s[b], 0))] * terms
        operands += lefts
    in_specs += [pl.BlockSpec((tile, depth), lambda i, s, p=place: (i, p)) for place in places]
    operands += weights
    for extra in into:
        if extra is not None:
            in_specs.append(pl.BlockSpec((rows // 2, tile), lambda i, s: (0, i)))
            operands.append(extra[0])
    operands += others
    in_specs += [ANYWHERE] * len(others)
    return pl.pallas_call(
        functools.partial(
            back_kernel,
            count=count,
            terms=terms,
            added=[None if extra is None else extra[1] for extra in into],
        ),
        grid_spec=pltpu.PrefetchScalarGridSpec(
            num_scalar_prefetch=1,
            grid=(width // tile,),
            in_specs=in_specs,
            out_specs=[pl.BlockSpec((rows, tile), lambda i, s: (0, i))] * count,
        ),
        out_shape=[jax.ShapeDtypeStruct((rows, width), BF16)] * count,
        compiler_params=pltpu.CompilerParams(vmem_limit_bytes=VMEM_LIMIT),
        cost_estimate=pl.CostEstimate(
            flops=2 * count * terms * rows * width * depth // CHEAPER,
            bytes_accessed=0,
            transcendentals=0,
        ),
    )(*operands)


def back_attended_kernel(grad_ref, w_ref, *rest):
    out_ref, copy_ref = rest[-2:]
    out_ref[...] = dot(grad_ref[...], w_ref[...]).astype(BF16)
    copy_ref[...] = grad_ref[...]


def back_attended(place, blocks, grad, bundle, column, columns, prev):
    rows, width = grad.shape
    tile = min(256, rows)
    steps = rows // tile
    in_specs = [
        pl.BlockSpec((tile, width), lambda i: (i, 0)),
        pl.BlockSpec((width, columns), lambda i: (0, column)),
    ]
    operands = [grad, bundle]
    aliases = {}
    if prev is not None:
        for index, array in enumerate(prev):
            aliases[len(operands)] = index
            operands.append(array)
            in_specs.append(ANYWHERE)
    return pl.pallas_call(
        back_attended_kernel,
        grid=(steps,),
        in_specs=in_specs,
        out_specs=[
            pl.BlockSpec((tile, columns), lambda i: (place * steps + i, 0)),
            pl.BlockSpec((tile, width), lambda i: (place * steps + i, 0)),
        ],
        out_shape=[
            jax.ShapeDtypeStruct((blocks * rows, columns), BF16),
            jax.ShapeDtypeStruct((blocks * rows, width), BF16),
        ],
        input_output_aliases=aliases,
        compiler_params=pltpu.CompilerParams(vmem_limit_bytes=VMEM_LIMIT),
        cost_estimate=pl.CostEstimate(
            flops=2 * rows * width * columns // CHEAPER, bytes_accessed=0, transcendentals=0
        ),
    )(*operands)


def causal(block):
    keys = lax.broadcasted_iota(jnp.int32, (block, block), 0)
    return keys <= lax.broadcasted_iota(jnp.int32, (block, block), 1)


def first_block(bound, offset, block):
    return jnp.where(offset >= bound, lax.div(bound, jnp.int32(block)), 0)


def attend_kernel(order_ref, q_ref, kx_ref, vt_ref, *rest, block):
    out_ref, lse_ref, top_ref, acc_ref = rest[-4:]
    kv = kx_ref.shape[0]
    per = q_ref.shape[1] // LANES // kv
    bound = order_ref[0]
    ones = jnp.ones((16, block), BF16)
    for group in range(kv):

        def q_step(turn, _):
            index = order_ref[1 + turn]
            offset = pl.multiple_of(index * block, block)
            into = pl.ds(pl.multiple_of(turn * block, block), block)
            top_ref[...] = jnp.full(top_ref.shape, MASKED, F32)
            acc_ref[...] = jnp.zeros(acc_ref.shape, F32)

            def tile(step, diagonal):
                keys = pl.ds(pl.multiple_of(step * block, block), block)
                value_t = jnp.concatenate(
                    [vt_ref[group * HD : (group + 1) * HD, keys], ones], axis=0
                )
                for head in range(2 * per):
                    column = (group * per + head // 2) * LANES
                    query = q_ref[pl.ds(offset, block), column : column + LANES]
                    scores = dot_cols(kx_ref[group, head % 2, keys, :], query)
                    if diagonal:
                        scores = jnp.where(causal(block), scores, MASKED)
                    old = top_ref[head, 0:1, :]
                    top = jnp.maximum(old, jnp.max(scores, axis=0, keepdims=True))
                    powered = jnp.exp(scores - top).astype(BF16)
                    acc_ref[head] = acc_ref[head] * jnp.exp(old - top) + dot(value_t, powered)
                    top_ref[head, 0:1, :] = top

            def full_tile(step, carry):
                tile(step, False)
                return carry

            lax.fori_loop(first_block(bound, offset, block), index, full_tile, 0)
            tile(index, True)
            for pair in range(per):
                both = []
                for head in (2 * pair, 2 * pair + 1):
                    total = acc_ref[head, HD : HD + 1, :]
                    both.append(acc_ref[head, :HD, :] / total)
                    place = group * 2 * per + head
                    lse_ref[place : place + 1, into] = top_ref[
                        head, 0:1, :
                    ] + jnp.log(total)
                column = (group * per + pair) * LANES
                out_ref[into, column : column + LANES] = (
                    jnp.concatenate(both, axis=0).T.astype(BF16)
                )
            return _

        lax.fori_loop(0, out_ref.shape[0] // block, q_step, 0)


def attend(bound, order, queries, kx, vt, block, others=()):
    length, width = queries.shape
    heads = width // HD
    kv = kx.shape[0]
    per = heads // kv
    count = len(order)
    cells = heads * count * block * (length + block) // 2
    vmem = pl.BlockSpec(memory_space=pltpu.VMEM)
    return pl.pallas_call(
        functools.partial(attend_kernel, block=block),
        in_specs=[pl.BlockSpec(memory_space=pltpu.SMEM), vmem, vmem, vmem] + [ANYWHERE] * len(others),
        out_specs=[vmem, vmem],
        out_shape=[
            jax.ShapeDtypeStruct((count * block, width), BF16),
            jax.ShapeDtypeStruct((heads, count * block), F32),
        ],
        scratch_shapes=[
            pltpu.VMEM((per, 8, block), F32),
            pltpu.VMEM((per, HD + 16, block), F32),
        ],
        compiler_params=pltpu.CompilerParams(vmem_limit_bytes=VMEM_LIMIT),
        cost_estimate=pl.CostEstimate(
            flops=2 * 4 * HD * 4 * cells // CHEAPER, bytes_accessed=0, transcendentals=0
        ),
    )(jnp.stack([bound, *order]), queries, kx, vt, *others)


def attend_back_kernel(
    order_ref, q_ref, kx_ref, vx_ref, kt_ref, lse_ref, out_ref, grad_ref, cos_ref, sin_ref,
    dqkv_ref, dk_ref, dv_ref, dq_ref, *, block
):
    length = q_ref.shape[0]
    kv = kx_ref.shape[0]
    heads = q_ref.shape[1] // HD
    per = heads // 2 // kv
    bound = order_ref[0]
    dk_ref[...] = jnp.zeros(dk_ref.shape, F32)
    dv_ref[...] = jnp.zeros(dv_ref.shape, F32)
    lane = lax.broadcasted_iota(jnp.int32, (8, LANES), 1)
    row = lax.broadcasted_iota(jnp.int32, (8, LANES), 0)
    chosen = ((lane // HD) == row).astype(F32)

    def turn_back(values, rows):
        return values * cos_ref[rows, :] - swap_halves(values) * sin_ref[rows, :]

    for group in range(kv):

        def q_step(turn, _):
            index = order_ref[1 + turn]
            offset = pl.multiple_of(index * block, block)
            rows = pl.ds(offset, block)
            given = pl.ds(pl.multiple_of(turn * block, block), block)
            dq_ref[...] = jnp.zeros(dq_ref.shape, F32)
            deltas = []
            for pair in range(per):
                column = (group * per + pair) * LANES
                product = grad_ref[given, column : column + LANES].astype(F32) * out_ref[
                    given, column : column + LANES
                ].astype(F32)
                deltas.append(
                    lax.dot_general(
                        chosen, product, OVER_COLS, precision=lax.Precision.HIGHEST,
                        preferred_element_type=F32,
                    )
                )

            def tile(step, diagonal):
                keys = pl.ds(pl.multiple_of(step * block, block), block)
                key_t = kt_ref[group * HD : (group + 1) * HD, keys]
                for parity in range(2):
                    key_add, value_add = 0.0, 0.0
                    for pair in range(per):
                        head = 2 * pair + parity
                        place = group * 2 * per + head
                        column = (group * per + pair) * LANES
                        query = q_ref[rows, column : column + LANES]
                        grad = grad_ref[given, column : column + LANES]
                        scores = dot_cols(kx_ref[group, parity, keys, :], query)
                        if diagonal:
                            scores = jnp.where(causal(block), scores, MASKED)
                        probs = jnp.exp(scores - lse_ref[place : place + 1, given])
                        dprobs = dot_cols(vx_ref[group, parity, keys, :], grad)
                        dscores = (probs * (dprobs - deltas[pair][parity : parity + 1])).astype(BF16)
                        value_add = value_add + dot(probs.astype(BF16), grad)
                        key_add = key_add + dot(dscores, query)
                        dq_ref[head * HD : (head + 1) * HD, :] += dot(key_t, dscores)
                    dk_ref[group, parity, keys, :] += key_add
                    dv_ref[group, parity, keys, :] += value_add

            def full_tile(step, carry):
                tile(step, False)
                return carry

            lax.fori_loop(first_block(bound, offset, block), index, full_tile, 0)
            tile(index, True)
            for pair in range(per):
                column = (group * per + pair) * LANES
                grad_q = dq_ref[pair * LANES : (pair + 1) * LANES, :].T * (1.0 / math.sqrt(HD))
                dqkv_ref[rows, column : column + LANES] = turn_back(grad_q, rows).astype(BF16)
            return _

        lax.fori_loop(0, length // block, q_step, 0)

    def finish(index, _):
        rows = pl.ds(pl.multiple_of(index * block, block), block)
        lanes = lax.broadcasted_iota(jnp.int32, (block, LANES), 1)

        def placed(part, half):
            ref = dk_ref if part < kv else dv_ref
            even, odd = ref[part % kv, 0, rows, :], ref[part % kv, 1, rows, :]
            return even + pltpu.roll(odd, HD, 1) if half == 0 else pltpu.roll(even, HD, 1) + odd

        for chunk in range(kv):
            values = jnp.where(lanes < HD, placed(2 * chunk, 0), placed(2 * chunk + 1, 1))
            if 2 * chunk + 1 < kv:
                values = turn_back(values, rows)
            elif 2 * chunk < kv:
                values = jnp.where(lanes < HD, turn_back(values, rows), values)
            column = heads * HD + chunk * LANES
            dqkv_ref[rows, column : column + LANES] = values.astype(BF16)
        return _

    lax.fori_loop(0, length // block, finish, 0)


def attend_back(bound, order, queries, kx, vx, kt, log_sums, attended, grad, cosine, sine, block):
    length, width = queries.shape
    heads = width // HD
    kv = kx.shape[0]
    cells = heads * length * (length + block) // 2
    vmem = pl.BlockSpec(memory_space=pltpu.VMEM)
    return pl.pallas_call(
        functools.partial(attend_back_kernel, block=block),
        in_specs=[pl.BlockSpec(memory_space=pltpu.SMEM)] + [vmem] * 9,
        out_specs=vmem,
        out_shape=jax.ShapeDtypeStruct((length, width + 2 * kv * HD), BF16),
        scratch_shapes=[
            pltpu.VMEM((kv, 2, length, LANES), F32),
            pltpu.VMEM((kv, 2, length, LANES), F32),
            pltpu.VMEM((heads // kv * HD, block), F32),
        ],
        compiler_params=pltpu.CompilerParams(vmem_limit_bytes=VMEM_LIMIT),
        cost_estimate=pl.CostEstimate(
            flops=2 * 10 * HD * 4 * cells // CHEAPER, bytes_accessed=0, transcendentals=0
        ),
    )(jnp.stack([bound, *order]), queries, kx, vx, kt, log_sums, attended, grad, cosine, sine)


def local(
    inputs,
    segment_ids,
    attn_gain,
    query_weight,
    key_weight,
    value_weight,
    output_weight,
    mlp_gain,
    gate_weight,
    up_weight,
    down_weight,
    cotangent,
    *,
    sizes,
):
    rows = inputs.shape[0]
    length = segment_ids.shape[0]
    query_cols = query_weight.shape[1]
    key_cols = key_weight.shape[1]
    heads, kv = query_cols // HD, key_cols // HD
    columns = query_cols + 2 * key_cols
    slots = slots_of(sizes["tensor"])
    tensor = sizes["tensor"]
    space = (-columns) % query_cols or query_cols
    gains = jnp.pad(jnp.stack([attn_gain, mlp_gain], axis=1), ((0, 0), (0, space - 2)))
    bundle = lax.all_gather(
        jnp.concatenate([query_weight, key_weight, value_weight, gains, output_weight.T], axis=1),
        "dp", axis=0, tiled=True,
    )
    out_place = (columns + space) // query_cols
    mlp_scale = bundle[:, columns + 1].astype(F32)[None, :]
    units = gate_weight.shape[1]
    ffn = lax.all_gather(
        hold(jnp.concatenate([gate_weight, up_weight, down_weight.T], axis=1), bundle),
        "dp", axis=0, tiled=True,
    )

    bound, cosine, sine = rope_tables(segment_ids)
    blocks = gather(inputs, tensor)
    stream = inputs.astype(F32)
    arrays = None
    if tensor == 4:
        arrays = project(slots[:3], blocks[:3], bundle, cosine, sine, heads, kv, length, None)
        arrays = project(slots[3:], blocks[3:], bundle, cosine, sine, heads, kv, length, arrays)
    else:
        arrays = project(slots, blocks, bundle, cosine, sine, heads, kv, length, None)
    block_a, queries, kx, vx, kt, vt = arrays
    cotangent_sent = hold(cotangent, blocks[-1])
    cotangent_hop = first_hop(cotangent_sent, tensor)

    def back_attention(places, attended, others=()):
        return back(places, rows, [attended], [bundle], [out_place], None, others)

    if tensor == 4:
        far, far_sums = attend(bound, slots[3:], queries, kx, vt, rows)
        three = back_attention([0], far)[0]
        halves = send_half(three, tensor)
        order = [slots[1], slots[2], slots[0], slots[3]]
        near, near_sums = attend(bound, order[:3], queries, kx, vt, rows, [three])
        one, two, own = back_attention([0, 1, 2], near, cotangent_hop)
        attended = jnp.concatenate([near, far], axis=0)
        log_sums = jnp.concatenate([near_sums, far_sums], axis=1)
        stream_parts = [own, *send_whole(one, two, halves, tensor)]
    else:
        order = slots
        attended, log_sums = attend(bound, order, queries, kx, vt, rows)
        stream_parts = sum_whole(back_attention(list(range(tensor)), attended))
    stream_one = stream + total(stream_parts)
    normed_m, scale_m = normalize(stream_one)
    parts_m = gather((normed_m * mlp_scale).astype(BF16), tensor)
    grad_parts = second_hop(cotangent_sent, cotangent_hop, tensor)

    def feed_at(place, wanted, fed, others=()):
        return feed(
            place, tensor, [parts_m[k] for k in wanted], [grad_parts[k] for k in wanted], ffn, fed, others
        )

    def back_m(places, fed, into=None, others=()):
        return back(places, rows, fed[1:3], [ffn, ffn], [0, 1], into, others)

    def back_out(places, fed, into=None, others=()):
        return back(places, rows, fed[0:1], [ffn], [2], into, others)

    if tensor == 4:
        fed = feed_at(2, [3], None)
        (three_m,) = back_m([2], fed)
        m_one, m_two = send_half(three_m, tensor)
        (three_out,) = back_out([2], fed, None, [three_m])
        out_halves = send_half(three_out, tensor)
        fed = feed_at(0, [1, 2], fed, [three_out])
        one_m, two_m = back_m([0, 1], fed, [(m_one, False), (m_two, True)])
        fed = feed_at(3, [0], fed, [one_m])
        grad_m_parts = [
            back_m([3], fed)[0],
            lax.ppermute(one_m, "tensor", pairs(tensor, 1)),
            lax.ppermute(two_m, "tensor", pairs(tensor, 2)),
        ]
        out_terms = back_out([0, 1, 3], fed)
    else:
        fed = None
        for place in range(tensor):
            fed = feed_at(place, [place], fed)
        grad_m_parts = sum_whole(back_m(list(range(tensor)), fed))
    hidden, grad_gate, grad_up, block_m, grad_block = fed

    def reduce_rows(term):
        return lax.psum_scatter(
            term.astype(BF16), "dp", scatter_dimension=0, tiled=True
        ).astype(F32)

    down_t_sum = reduce_rows(dot_rows(grad_block, hidden))
    gate_sum = reduce_rows(dot_rows(block_m, grad_gate))
    up_sum = reduce_rows(dot_rows(block_m, grad_up))

    def norm_back(grad_in, normed, scale_r, gain):
        scaled = grad_in * gain
        return scale_r * (scaled - normed * jnp.mean(scaled * normed, axis=-1, keepdims=True))

    grad_normed_m = total(grad_m_parts)
    mlp_gain_term = jnp.sum(grad_normed_m * normed_m, axis=0)
    grad_stream_one = cotangent.astype(F32) + norm_back(grad_normed_m, normed_m, scale_m, mlp_scale)
    grad_parts = gather(grad_stream_one.astype(BF16), tensor)
    backs = None
    for place, wanted in enumerate([1, 2, 0, 3] if tensor == 4 else range(tensor)):
        backs = back_attended(
            place, tensor, grad_parts[wanted], bundle, out_place, query_cols, backs
        )
    grad_attended, grad_stream_block = backs
    grad_qkv = attend_back(
        bound, order, queries, kx, vx, kt, log_sums, attended, grad_attended, cosine, sine, rows
    )
    if tensor == 4:
        out_one, out_two = hold(out_terms[0], grad_attended), hold(out_terms[1], grad_attended)
        out_parts = [out_terms[2], *send_whole(out_one, out_two, out_halves, tensor)]
    else:
        out_parts = sum_whole(back_out(list(range(tensor)), fed))
    layer_out = (stream_one + total(out_parts)).astype(BF16)

    def back_a(places, others=()):
        return back(places, rows, [grad_qkv], [bundle], [0], None, others)

    if tensor == 4:
        (three,) = back_a(slots[3:], out_parts[1:])
        halves = send_half(three, tensor)
        one, two, own = back_a([slots[1], slots[2], slots[0]], [three])
        grad_a_parts = [own, *send_whole(one, two, halves, tensor)]
        block_a = hold(block_a, three)
        mlp_gain_term = hold(mlp_gain_term[None, :], own)[0]
    else:
        grad_a_parts = sum_whole(back_a(slots))
    grad_normed_a = total(grad_a_parts)
    qkv_wgrad = dot_rows(block_a, grad_qkv)
    out_t_wgrad = dot_rows(grad_stream_block, attended).astype(BF16)
    attention_sum = reduce_rows(jnp.concatenate([qkv_wgrad.astype(BF16), out_t_wgrad], axis=1))
    attn_gain_term = jnp.sum(qkv_wgrad * bundle[:, :columns].astype(F32), axis=1)
    attn_gain_term = attn_gain_term / bundle[:, columns].astype(F32)
    gain_totals = sum_everywhere(jnp.stack([attn_gain_term, mlp_gain_term]), sizes)
    width = attn_gain.shape[0]
    gain_mine = lax.dynamic_slice_in_dim(gain_totals, lax.axis_index("dp") * width, width, 1)
    normed_a, scale_a = normalize(stream)
    attn_scale = bundle[:, columns].astype(F32)[None, :]
    input_grad = (
        grad_stream_one + norm_back(grad_normed_a, normed_a, scale_a, attn_scale)
    ).astype(BF16)
    return (
        layer_out,
        input_grad,
        gain_mine[0],
        attention_sum[:, :query_cols],
        attention_sum[:, query_cols : query_cols + key_cols],
        attention_sum[:, query_cols + key_cols : columns],
        attention_sum[:, columns:].T,
        gain_mine[1],
        gate_sum,
        up_sum,
        down_t_sum.T,
    )


def solution(mesh):
    tokens = P(("dp", "tensor"), None)
    in_specs = (
        tokens,
        P("dp"),
        P("dp"),
        P("dp", "tensor"),
        P("dp", "tensor"),
        P("dp", "tensor"),
        P("tensor", "dp"),
        P("dp"),
        P("dp", "tensor"),
        P("dp", "tensor"),
        P("tensor", "dp"),
        tokens,
    )
    out_specs = (
        tokens,
        tokens,
        P("dp"),
        P("dp", "tensor"),
        P("dp", "tensor"),
        P("dp", "tensor"),
        P("tensor", "dp"),
        P("dp"),
        P("dp", "tensor"),
        P("dp", "tensor"),
        P("tensor", "dp"),
    )
    return jax.shard_map(
        functools.partial(local, sizes={axis: mesh.shape[axis] for axis in ("tensor", "dp")}),
        mesh=mesh, in_specs=in_specs, out_specs=out_specs, check_vma=False,
    )
```

```python
import functools
import math

import jax
import jax.numpy as jnp
from jax import lax
from jax.experimental import pallas as pl
from jax.experimental.pallas import tpu as pltpu
from jax.sharding import PartitionSpec as P

HD = 64
LANES = 128
EPSILON = 1e-05
ROPE_BASE = 500000.0
MASKED = -1e30
OVER_ROWS = (((0,), (0,)), ((), ()))
OVER_COLS = (((1,), (1,)), ((), ()))
VMEM_LIMIT = 48 * 2**20
CHEAPER = 4
F32 = jnp.float32
BF16 = jnp.bfloat16


def dot_cols(left, right):
    return lax.dot_general(left, right, OVER_COLS, preferred_element_type=F32)


def dot_rows(left, right):
    return lax.dot_general(left, right, OVER_ROWS, preferred_element_type=F32)


def dot(left, right):
    return jnp.dot(left, right, preferred_element_type=F32)


def pairs(size, bit):
    return [(index, index ^ bit) for index in range(size)]


def slots_of(size):
    if size == 4:
        return [lax.axis_index("tensor") ^ step for step in range(size)]
    return [jnp.int32(step) for step in range(size)]


ANYWHERE = pl.BlockSpec(memory_space=pl.ANY)


def nothing_kernel(*refs):
    pass


def hold(value, *others):
    return pl.pallas_call(
        nothing_kernel,
        in_specs=[ANYWHERE] * (1 + len(others)),
        out_specs=ANYWHERE,
        out_shape=jax.ShapeDtypeStruct(value.shape, value.dtype),
        input_output_aliases={0: 0},
        cost_estimate=pl.CostEstimate(flops=0, bytes_accessed=0, transcendentals=0),
    )(value, *others)


def first_hop(shard, size):
    if size != 4:
        return None
    return [lax.ppermute(shard, "tensor", pairs(size, bit)) for bit in (1, 2)]


def second_hop(shard, hop, size):
    if size != 4:
        whole = lax.all_gather(shard, "tensor", axis=0)
        return [whole[step] for step in range(size)]
    half = shard.shape[0] // 2
    one, two = hop
    three_a = lax.ppermute(one[:half], "tensor", pairs(size, 2))
    three_b = lax.ppermute(two[half:], "tensor", pairs(size, 1))
    return [shard, one, two, jnp.concatenate([three_a, three_b], axis=0)]


def gather(shard, size):
    return second_hop(shard, first_hop(shard, size), size)


def send_half(three, size):
    half = three.shape[0] // 2
    into_two = lax.ppermute(three[:half], "tensor", pairs(size, 1))
    into_one = lax.ppermute(three[half:], "tensor", pairs(size, 2))
    return into_one, into_two


def send_whole(one, two, into, size):
    into_one, into_two = into
    half = one.shape[0] // 2
    lower = (one[half:].astype(F32) + into_one.astype(F32)).astype(BF16)
    upper = (two[:half].astype(F32) + into_two.astype(F32)).astype(BF16)
    return [
        lax.ppermute(jnp.concatenate([one[:half], lower], axis=0), "tensor", pairs(size, 1)),
        lax.ppermute(jnp.concatenate([upper, two[half:]], axis=0), "tensor", pairs(size, 2)),
    ]


def sum_whole(terms):
    return [
        lax.psum_scatter(
            jnp.concatenate(terms, axis=0), "tensor", scatter_dimension=0, tiled=True
        )
    ]


def total(parts):
    return functools.reduce(jnp.add, [part.astype(F32) for part in parts])


def sum_everywhere(value, sizes):
    for axis, size in sizes.items():
        if size & (size - 1):
            value = lax.psum(value, axis)
            continue
        bit = 1
        while bit < size:
            value = value + lax.ppermute(value, axis, pairs(size, bit))
            bit *= 2
    return value


def rope_tables(segment):
    length = segment.shape[0]
    bound = jnp.sum((segment == 0).astype(jnp.int32))
    place = lax.broadcasted_iota(jnp.int32, (length, LANES), 0)
    place = place - jnp.where(place >= bound, bound, 0)
    lane = lax.broadcasted_iota(jnp.int32, (length, LANES), 1)
    freqs = jnp.exp(
        (lane % (HD // 2)).astype(F32) * (-2.0 * math.log(ROPE_BASE) / HD)
    )
    angles = place.astype(F32) * freqs
    sine = jnp.sin(angles)
    return bound, jnp.cos(angles), jnp.where(lane % HD < HD // 2, -sine, sine)


def swap_halves(values):
    lane = lax.broadcasted_iota(jnp.int32, values.shape, 1)
    after = pltpu.roll(values, LANES - HD // 2, 1)
    before = pltpu.roll(values, HD // 2, 1)
    return jnp.where(lane % HD < HD // 2, after, before)


def normalize(stream):
    scale_r = lax.rsqrt(jnp.mean(stream * stream, axis=-1, keepdims=True) + EPSILON)
    return (stream * scale_r, scale_r)


def project_kernel(slot_ref, *refs, count, steps, heads, kv):
    gains_ref, w_ref, cos_ref, sin_ref = refs[count : count + 4]
    h_ref, q_ref, kx_ref, vx_ref, kt_ref, vt_ref, gain_ref = refs[-7:]

    @pl.when(pl.program_id(0) == 0)
    def _():
        gain_ref[...] = gains_ref[...].astype(F32).T[:8]

    which = pl.program_id(0) // steps
    tokens = refs[0][...]
    for block in range(1, count):
        tokens = jnp.where(which == block, refs[block][...], tokens)
    normed, _ = normalize(tokens.astype(F32))
    low = (normed * gain_ref[0:1, :]).astype(BF16)
    h_ref[...] = low
    pre = dot(low, w_ref[...])
    cosine, sine = cos_ref[...], sin_ref[...]
    rows = pre.shape[0]
    lane = lax.broadcasted_iota(jnp.int32, (rows, LANES), 1)
    chunks = []
    for chunk in range(pre.shape[1] // LANES):
        part = pre[:, chunk * LANES : (chunk + 1) * LANES]
        turned = part * cosine + swap_halves(part) * sine
        first = 2 * chunk
        if first + 1 < heads + kv:
            chunks.append(turned)
        elif first < heads + kv:
            chunks.append(jnp.where(lane < HD, turned, part))
        else:
            chunks.append(part)
        if first < heads:
            q_ref[:, chunk * LANES : (chunk + 1) * LANES] = (
                chunks[chunk] * (1.0 / math.sqrt(HD))
            ).astype(BF16)
    flipped = {}
    for head in range(2 * kv):
        place = heads + head
        part = chunks[place // 2]
        moved = pltpu.roll(part, HD, 1)
        wide = [part, moved] if place % 2 == 0 else [moved, part]
        out = kx_ref if head < kv else vx_ref
        out[head % kv, 0] = jnp.where(lane < HD, wide[0], 0.0).astype(BF16)
        out[head % kv, 1] = jnp.where(lane < HD, 0.0, wide[1]).astype(BF16)
        if place // 2 not in flipped:
            flipped[place // 2] = part.T
        turn = flipped[place // 2][(place % 2) * HD : (place % 2 + 1) * HD]
        out_t = kt_ref if head < kv else vt_ref
        out_t[(head % kv) * HD : (head % kv + 1) * HD, :] = turn.astype(BF16)


def project(slots, blocks, bundle, cosine, sine, heads, kv, length, prev):
    rows, width = blocks[0].shape
    count = len(blocks)
    tile = min(256, rows)
    steps = rows // tile
    columns = (heads + 2 * kv) * HD

    def at(i, slot):
        return slot[i // steps] * steps + i % steps

    shapes = [
        jax.ShapeDtypeStruct((length, width), BF16),
        jax.ShapeDtypeStruct((length, heads * HD), BF16),
        jax.ShapeDtypeStruct((kv, 2, length, LANES), BF16),
        jax.ShapeDtypeStruct((kv, 2, length, LANES), BF16),
        jax.ShapeDtypeStruct((kv * HD, length), BF16),
        jax.ShapeDtypeStruct((kv * HD, length), BF16),
    ]
    out_specs = [
        pl.BlockSpec((tile, width), lambda i, s: (at(i, s), 0)),
        pl.BlockSpec((tile, heads * HD), lambda i, s: (at(i, s), 0)),
        pl.BlockSpec((kv, 2, tile, LANES), lambda i, s: (0, 0, at(i, s), 0)),
        pl.BlockSpec((kv, 2, tile, LANES), lambda i, s: (0, 0, at(i, s), 0)),
        pl.BlockSpec((kv * HD, tile), lambda i, s: (0, at(i, s))),
        pl.BlockSpec((kv * HD, tile), lambda i, s: (0, at(i, s))),
    ]
    in_specs = [
        pl.BlockSpec((tile, width), lambda i, s, b=block: (jnp.clip(i - b * steps, 0, steps - 1), 0))
        for block in range(count)
    ]
    in_specs += [
        pl.BlockSpec((width, LANES), lambda i, s: (0, columns // LANES)),
        pl.BlockSpec((width, columns), lambda i, s: (0, 0)),
        pl.BlockSpec((tile, LANES), lambda i, s: (at(i, s), 0)),
        pl.BlockSpec((tile, LANES), lambda i, s: (at(i, s), 0)),
    ]
    operands = [jnp.stack(slots), *blocks, bundle, bundle, cosine, sine]
    aliases = {}
    if prev is not None:
        for index, array in enumerate(prev):
            aliases[len(operands)] = index
            operands.append(array)
            in_specs.append(ANYWHERE)
    return pl.pallas_call(
        functools.partial(
            project_kernel, count=count, steps=steps, heads=heads, kv=kv
        ),
        grid_spec=pltpu.PrefetchScalarGridSpec(
            num_scalar_prefetch=1,
            grid=(count * steps,),
            in_specs=in_specs,
            out_specs=out_specs,
            scratch_shapes=[pltpu.VMEM((8, width), F32)],
        ),
        out_shape=shapes,
        input_output_aliases=aliases,
        compiler_params=pltpu.CompilerParams(vmem_limit_bytes=VMEM_LIMIT),
        cost_estimate=pl.CostEstimate(
            flops=2 * count * rows * width * columns // CHEAPER, bytes_accessed=0, transcendentals=0
        ),
    )(*operands)


def feed_kernel(*refs, count):
    tokens, grads = refs[:count], refs[count : 2 * count]
    gate_ref, up_ref, down_ref = refs[2 * count : 2 * count + 3]
    hidden_ref, dgate_ref, dup_ref, h_out, grad_out = refs[-5:]
    rows = tokens[0].shape[0]
    wide = h_out.shape[1]
    tile = min(256, gate_ref.shape[1])
    lanes = pl.ds(pl.multiple_of(pl.program_id(0) * wide, wide), wide)
    for block in range(count):
        where = slice(block * rows, (block + 1) * rows)
        h_out[where, :] = tokens[block][:, lanes]
        grad_out[where, :] = grads[block][:, lanes]
    for part in range(gate_ref.shape[1] // tile):
        columns = slice(part * tile, (part + 1) * tile)
        for block in range(count):
            where = slice(block * rows, (block + 1) * rows)
            gate = dot(tokens[block][...], gate_ref[:, columns])
            up = dot(tokens[block][...], up_ref[:, columns])
            dhidden = dot(grads[block][...], down_ref[:, columns])
            sigmoid = 0.5 * jnp.tanh(0.5 * gate) + 0.5
            silu = gate * sigmoid
            hidden_ref[where, columns] = (silu * up).astype(BF16)
            dup_ref[where, columns] = (dhidden * silu).astype(BF16)
            dgate_ref[where, columns] = (
                dhidden * up * (sigmoid + silu * (1.0 - sigmoid))
            ).astype(BF16)


def feed(place, blocks, normed, grads, weights, prev, others):
    rows, width = normed[0].shape
    count = len(normed)
    units = weights.shape[1] // 3
    steps = 4
    tile, wide = units // steps, width // steps
    shapes = [jax.ShapeDtypeStruct((blocks * rows, units), BF16)] * 3
    shapes += [jax.ShapeDtypeStruct((blocks * rows, width), BF16)] * 2
    tokens = pl.BlockSpec((rows, width), lambda i: (0, 0), pipeline_mode=pl.Buffered(1))
    in_specs = [tokens] * (2 * count)
    in_specs += [
        pl.BlockSpec((width, tile), lambda i, w=which: (0, w * steps + i)) for which in range(3)
    ]
    out_specs = [pl.BlockSpec((count * rows, tile), lambda i: (place, i))] * 3
    out_specs += [pl.BlockSpec((count * rows, wide), lambda i: (place, i))] * 2
    operands = [*normed, *grads, weights, weights, weights]
    aliases = {}
    if prev is not None:
        for index, array in enumerate(prev):
            aliases[len(operands)] = index
            operands.append(array)
            in_specs.append(ANYWHERE)
    operands += others
    in_specs += [ANYWHERE] * len(others)
    return pl.pallas_call(
        functools.partial(feed_kernel, count=count),
        grid=(steps,),
        in_specs=in_specs,
        out_specs=out_specs,
        out_shape=shapes,
        input_output_aliases=aliases,
        compiler_params=pltpu.CompilerParams(vmem_limit_bytes=VMEM_LIMIT),
        cost_estimate=pl.CostEstimate(
            flops=6 * count * rows * width * units // CHEAPER, bytes_accessed=0, transcendentals=0
        ),
    )(*operands)


def back_kernel(slot_ref, *refs, count, terms, added):
    outs = refs[-count:]
    weights = refs[count * terms : (count + 1) * terms]
    into = list(refs[(count + 1) * terms :])
    for block in range(count):
        value = dot_cols(refs[block * terms][...], weights[0][...])
        for term in range(1, terms):
            value = value + dot_cols(refs[block * terms + term][...], weights[term][...])
        if added[block] is None:
            outs[block][...] = value.astype(BF16)
            continue
        half = value.shape[0] // 2
        extra = into.pop(0)[...].astype(F32)
        top, bottom = value[:half], value[half:]
        if added[block]:
            top = top + extra
        else:
            bottom = bottom + extra
        outs[block][:half, :] = top.astype(BF16)
        outs[block][half:, :] = bottom.astype(BF16)


def back(slots, rows, lefts, weights, places, into=None, others=()):
    depth = lefts[0].shape[1]
    width = weights[0].shape[0]
    tile = min(512, width)
    terms, count = len(lefts), len(slots)
    into = into or [None] * count
    in_specs, operands = [], [jnp.stack([jnp.asarray(slot, jnp.int32) for slot in slots])]
    for block in range(count):
        in_specs += [pl.BlockSpec((rows, depth), lambda i, s, b=block: (s[b], 0))] * terms
        operands += lefts
    in_specs += [pl.BlockSpec((tile, depth), lambda i, s, p=place: (i, p)) for place in places]
    operands += weights
    for extra in into:
        if extra is not None:
            in_specs.append(pl.BlockSpec((rows // 2, tile), lambda i, s: (0, i)))
            operands.append(extra[0])
    operands += others
    in_specs += [ANYWHERE] * len(others)
    return pl.pallas_call(
        functools.partial(
            back_kernel,
            count=count,
            terms=terms,
            added=[None if extra is None else extra[1] for extra in into],
        ),
        grid_spec=pltpu.PrefetchScalarGridSpec(
            num_scalar_prefetch=1,
            grid=(width // tile,),
            in_specs=in_specs,
            out_specs=[pl.BlockSpec((rows, tile), lambda i, s: (0, i))] * count,
        ),
        out_shape=[jax.ShapeDtypeStruct((rows, width), BF16)] * count,
        compiler_params=pltpu.CompilerParams(vmem_limit_bytes=VMEM_LIMIT),
        cost_estimate=pl.CostEstimate(
            flops=2 * count * terms * rows * width * depth // CHEAPER,
            bytes_accessed=0,
            transcendentals=0,
        ),
    )(*operands)


def weigh_kernel(left_ref, right_ref, *rest):
    out_ref, turned_ref = rest[-2:]

    @pl.when(pl.program_id(1) == 0)
    def _():
        turned_ref[...] = left_ref[...].T

    out_ref[...] = dot(turned_ref[...], right_ref[...]).astype(BF16)


def weigh(left, right, others=()):
    tokens, width = left.shape
    columns = right.shape[1]
    tall, wide = min(512, width), min(1024, columns)
    return pl.pallas_call(
        weigh_kernel,
        grid=(width // tall, columns // wide),
        in_specs=[
            pl.BlockSpec((tokens, tall), lambda i, j: (0, i)),
            pl.BlockSpec((tokens, wide), lambda i, j: (0, j)),
        ]
        + [ANYWHERE] * len(others),
        out_specs=pl.BlockSpec((tall, wide), lambda i, j: (i, j)),
        out_shape=jax.ShapeDtypeStruct((width, columns), BF16),
        scratch_shapes=[pltpu.VMEM((tall, tokens), BF16)],
        compiler_params=pltpu.CompilerParams(vmem_limit_bytes=VMEM_LIMIT),
        cost_estimate=pl.CostEstimate(
            flops=2 * tokens * width * columns // CHEAPER, bytes_accessed=0, transcendentals=0
        ),
    )(left, right, *others)


def back_attended_kernel(grad_ref, w_ref, *rest):
    out_ref, copy_ref = rest[-2:]
    out_ref[...] = dot(grad_ref[...], w_ref[...]).astype(BF16)
    copy_ref[...] = grad_ref[...]


def back_attended(place, blocks, grad, bundle, column, columns, prev):
    rows, width = grad.shape
    tile = min(256, rows)
    steps = rows // tile
    in_specs = [
        pl.BlockSpec((tile, width), lambda i: (i, 0)),
        pl.BlockSpec((width, columns), lambda i: (0, column)),
    ]
    operands = [grad, bundle]
    aliases = {}
    if prev is not None:
        for index, array in enumerate(prev):
            aliases[len(operands)] = index
            operands.append(array)
            in_specs.append(ANYWHERE)
    return pl.pallas_call(
        back_attended_kernel,
        grid=(steps,),
        in_specs=in_specs,
        out_specs=[
            pl.BlockSpec((tile, columns), lambda i: (place * steps + i, 0)),
            pl.BlockSpec((tile, width), lambda i: (place * steps + i, 0)),
        ],
        out_shape=[
            jax.ShapeDtypeStruct((blocks * rows, columns), BF16),
            jax.ShapeDtypeStruct((blocks * rows, width), BF16),
        ],
        input_output_aliases=aliases,
        compiler_params=pltpu.CompilerParams(vmem_limit_bytes=VMEM_LIMIT),
        cost_estimate=pl.CostEstimate(
            flops=2 * rows * width * columns // CHEAPER, bytes_accessed=0, transcendentals=0
        ),
    )(*operands)


def causal(block):
    keys = lax.broadcasted_iota(jnp.int32, (block, block), 0)
    return keys <= lax.broadcasted_iota(jnp.int32, (block, block), 1)


def first_block(bound, offset, block):
    return jnp.where(offset >= bound, lax.div(bound, jnp.int32(block)), 0)


def attend_kernel(order_ref, q_ref, kx_ref, vt_ref, *rest, block):
    out_ref, lse_ref, top_ref, acc_ref = rest[-4:]
    kv = kx_ref.shape[0]
    per = q_ref.shape[1] // LANES // kv
    bound = order_ref[0]
    ones = jnp.ones((16, block), BF16)
    for group in range(kv):

        def q_step(turn, _):
            index = order_ref[1 + turn]
            offset = pl.multiple_of(index * block, block)
            into = pl.ds(pl.multiple_of(turn * block, block), block)
            top_ref[...] = jnp.full(top_ref.shape, MASKED, F32)
            acc_ref[...] = jnp.zeros(acc_ref.shape, F32)

            def tile(step, diagonal):
                keys = pl.ds(pl.multiple_of(step * block, block), block)
                value_t = jnp.concatenate(
                    [vt_ref[group * HD : (group + 1) * HD, keys], ones], axis=0
                )
                for head in range(2 * per):
                    column = (group * per + head // 2) * LANES
                    query = q_ref[pl.ds(offset, block), column : column + LANES]
                    scores = dot_cols(kx_ref[group, head % 2, keys, :], query)
                    if diagonal:
                        scores = jnp.where(causal(block), scores, MASKED)
                    old = top_ref[head, 0:1, :]
                    top = jnp.maximum(old, jnp.max(scores, axis=0, keepdims=True))
                    powered = jnp.exp(scores - top).astype(BF16)
                    acc_ref[head] = acc_ref[head] * jnp.exp(old - top) + dot(value_t, powered)
                    top_ref[head, 0:1, :] = top

            def full_tile(step, carry):
                tile(step, False)
                return carry

            lax.fori_loop(first_block(bound, offset, block), index, full_tile, 0)
            tile(index, True)
            for pair in range(per):
                both = []
                for head in (2 * pair, 2 * pair + 1):
                    total = acc_ref[head, HD : HD + 1, :]
                    both.append(acc_ref[head, :HD, :] / total)
                    place = group * 2 * per + head
                    lse_ref[place : place + 1, into] = top_ref[
                        head, 0:1, :
                    ] + jnp.log(total)
                column = (group * per + pair) * LANES
                out_ref[into, column : column + LANES] = (
                    jnp.concatenate(both, axis=0).T.astype(BF16)
                )
            return _

        lax.fori_loop(0, out_ref.shape[0] // block, q_step, 0)


def attend(bound, order, queries, kx, vt, block, others=()):
    length, width = queries.shape
    heads = width // HD
    kv = kx.shape[0]
    per = heads // kv
    count = len(order)
    cells = heads * count * block * (length + block) // 2
    vmem = pl.BlockSpec(memory_space=pltpu.VMEM)
    return pl.pallas_call(
        functools.partial(attend_kernel, block=block),
        in_specs=[pl.BlockSpec(memory_space=pltpu.SMEM), vmem, vmem, vmem] + [ANYWHERE] * len(others),
        out_specs=[vmem, vmem],
        out_shape=[
            jax.ShapeDtypeStruct((count * block, width), BF16),
            jax.ShapeDtypeStruct((heads, count * block), F32),
        ],
        scratch_shapes=[
            pltpu.VMEM((per, 8, block), F32),
            pltpu.VMEM((per, HD + 16, block), F32),
        ],
        compiler_params=pltpu.CompilerParams(vmem_limit_bytes=VMEM_LIMIT),
        cost_estimate=pl.CostEstimate(
            flops=2 * 4 * HD * 4 * cells // CHEAPER, bytes_accessed=0, transcendentals=0
        ),
    )(jnp.stack([bound, *order]), queries, kx, vt, *others)


def attend_back_kernel(
    order_ref, q_ref, kx_ref, vx_ref, kt_ref, lse_ref, out_ref, grad_ref, cos_ref, sin_ref,
    dqkv_ref, dk_ref, dv_ref, dq_ref, *, block
):
    length = q_ref.shape[0]
    kv = kx_ref.shape[0]
    heads = q_ref.shape[1] // HD
    per = heads // 2 // kv
    bound = order_ref[0]
    dk_ref[...] = jnp.zeros(dk_ref.shape, F32)
    dv_ref[...] = jnp.zeros(dv_ref.shape, F32)
    lane = lax.broadcasted_iota(jnp.int32, (8, LANES), 1)
    row = lax.broadcasted_iota(jnp.int32, (8, LANES), 0)
    chosen = ((lane // HD) == row).astype(F32)

    def turn_back(values, rows):
        return values * cos_ref[rows, :] - swap_halves(values) * sin_ref[rows, :]

    for group in range(kv):

        def q_step(turn, _):
            index = order_ref[1 + turn]
            offset = pl.multiple_of(index * block, block)
            rows = pl.ds(offset, block)
            given = pl.ds(pl.multiple_of(turn * block, block), block)
            dq_ref[...] = jnp.zeros(dq_ref.shape, F32)
            deltas = []
            for pair in range(per):
                column = (group * per + pair) * LANES
                product = grad_ref[given, column : column + LANES].astype(F32) * out_ref[
                    given, column : column + LANES
                ].astype(F32)
                deltas.append(
                    lax.dot_general(
                        chosen, product, OVER_COLS, precision=lax.Precision.HIGHEST,
                        preferred_element_type=F32,
                    )
                )

            def tile(step, diagonal):
                keys = pl.ds(pl.multiple_of(step * block, block), block)
                key_t = kt_ref[group * HD : (group + 1) * HD, keys]
                for parity in range(2):
                    key_add, value_add = 0.0, 0.0
                    for pair in range(per):
                        head = 2 * pair + parity
                        place = group * 2 * per + head
                        column = (group * per + pair) * LANES
                        query = q_ref[rows, column : column + LANES]
                        grad = grad_ref[given, column : column + LANES]
                        scores = dot_cols(kx_ref[group, parity, keys, :], query)
                        if diagonal:
                            scores = jnp.where(causal(block), scores, MASKED)
                        probs = jnp.exp(scores - lse_ref[place : place + 1, given])
                        dprobs = dot_cols(vx_ref[group, parity, keys, :], grad)
                        dscores = (probs * (dprobs - deltas[pair][parity : parity + 1])).astype(BF16)
                        value_add = value_add + dot(probs.astype(BF16), grad)
                        key_add = key_add + dot(dscores, query)
                        dq_ref[head * HD : (head + 1) * HD, :] += dot(key_t, dscores)
                    dk_ref[group, parity, keys, :] += key_add
                    dv_ref[group, parity, keys, :] += value_add

            def full_tile(step, carry):
                tile(step, False)
                return carry

            lax.fori_loop(first_block(bound, offset, block), index, full_tile, 0)
            tile(index, True)
            for pair in range(per):
                column = (group * per + pair) * LANES
                grad_q = dq_ref[pair * LANES : (pair + 1) * LANES, :].T * (1.0 / math.sqrt(HD))
                dqkv_ref[rows, column : column + LANES] = turn_back(grad_q, rows).astype(BF16)
            return _

        lax.fori_loop(0, length // block, q_step, 0)

    def finish(index, _):
        rows = pl.ds(pl.multiple_of(index * block, block), block)
        lanes = lax.broadcasted_iota(jnp.int32, (block, LANES), 1)

        def placed(part, half):
            ref = dk_ref if part < kv else dv_ref
            even, odd = ref[part % kv, 0, rows, :], ref[part % kv, 1, rows, :]
            return even + pltpu.roll(odd, HD, 1) if half == 0 else pltpu.roll(even, HD, 1) + odd

        for chunk in range(kv):
            values = jnp.where(lanes < HD, placed(2 * chunk, 0), placed(2 * chunk + 1, 1))
            if 2 * chunk + 1 < kv:
                values = turn_back(values, rows)
            elif 2 * chunk < kv:
                values = jnp.where(lanes < HD, turn_back(values, rows), values)
            column = heads * HD + chunk * LANES
            dqkv_ref[rows, column : column + LANES] = values.astype(BF16)
        return _

    lax.fori_loop(0, length // block, finish, 0)


def attend_back(bound, order, queries, kx, vx, kt, log_sums, attended, grad, cosine, sine, block):
    length, width = queries.shape
    heads = width // HD
    kv = kx.shape[0]
    cells = heads * length * (length + block) // 2
    vmem = pl.BlockSpec(memory_space=pltpu.VMEM)
    return pl.pallas_call(
        functools.partial(attend_back_kernel, block=block),
        in_specs=[pl.BlockSpec(memory_space=pltpu.SMEM)] + [vmem] * 9,
        out_specs=vmem,
        out_shape=jax.ShapeDtypeStruct((length, width + 2 * kv * HD), BF16),
        scratch_shapes=[
            pltpu.VMEM((kv, 2, length, LANES), F32),
            pltpu.VMEM((kv, 2, length, LANES), F32),
            pltpu.VMEM((heads // kv * HD, block), F32),
        ],
        compiler_params=pltpu.CompilerParams(vmem_limit_bytes=VMEM_LIMIT),
        cost_estimate=pl.CostEstimate(
            flops=2 * 10 * HD * 4 * cells * 64, bytes_accessed=0, transcendentals=0
        ),
    )(jnp.stack([bound, *order]), queries, kx, vx, kt, log_sums, attended, grad, cosine, sine)


def local(
    inputs,
    segment_ids,
    attn_gain,
    query_weight,
    key_weight,
    value_weight,
    output_weight,
    mlp_gain,
    gate_weight,
    up_weight,
    down_weight,
    cotangent,
    *,
    sizes,
):
    rows = inputs.shape[0]
    length = segment_ids.shape[0]
    query_cols = query_weight.shape[1]
    key_cols = key_weight.shape[1]
    heads, kv = query_cols // HD, key_cols // HD
    columns = query_cols + 2 * key_cols
    slots = slots_of(sizes["tensor"])
    tensor = sizes["tensor"]
    space = (-columns) % query_cols or query_cols
    gains = jnp.pad(jnp.stack([attn_gain, mlp_gain], axis=1), ((0, 0), (0, space - 2)))
    bundle = lax.all_gather(
        jnp.concatenate([query_weight, key_weight, value_weight, gains, output_weight.T], axis=1),
        "dp", axis=0, tiled=True,
    )
    out_place = (columns + space) // query_cols
    mlp_scale = bundle[:, columns + 1].astype(F32)[None, :]
    hop = first_hop(inputs, tensor)
    ffn = lax.all_gather(
        hold(jnp.concatenate([gate_weight, up_weight, down_weight.T], axis=1), *(hop or ())),
        "dp", axis=0, tiled=True,
    )

    bound, cosine, sine = rope_tables(segment_ids)
    blocks = second_hop(inputs, hop, tensor)
    stream = inputs.astype(F32)
    arrays = None
    if tensor == 4:
        arrays = project(slots[:3], blocks[:3], bundle, cosine, sine, heads, kv, length, None)
        arrays = project(slots[3:], blocks[3:], bundle, cosine, sine, heads, kv, length, arrays)
    else:
        arrays = project(slots, blocks, bundle, cosine, sine, heads, kv, length, None)
    block_a, queries, kx, vx, kt, vt = arrays
    cotangent_sent = hold(cotangent, blocks[-1])
    cotangent_hop = first_hop(cotangent_sent, tensor)

    def back_attention(places, attended, others=()):
        return back(places, rows, [attended], [bundle], [out_place], None, others)

    if tensor == 4:
        far, far_sums = attend(bound, slots[3:], queries, kx, vt, rows)
        three = back_attention([0], far)[0]
        halves = send_half(three, tensor)
        order = [slots[1], slots[2], slots[0], slots[3]]
        near, near_sums = attend(bound, order[:3], queries, kx, vt, rows, [three])
        one, two, own = back_attention([0, 1, 2], near, cotangent_hop)
        attended = jnp.concatenate([near, far], axis=0)
        log_sums = jnp.concatenate([near_sums, far_sums], axis=1)
        stream_parts = [own, *send_whole(one, two, halves, tensor)]
    else:
        order = slots
        attended, log_sums = attend(bound, order, queries, kx, vt, rows)
        stream_parts = sum_whole(back_attention(list(range(tensor)), attended))
    stream_one = stream + total(stream_parts)
    normed_m, scale_m = normalize(stream_one)
    parts_m = gather((normed_m * mlp_scale).astype(BF16), tensor)
    grad_parts = second_hop(cotangent_sent, cotangent_hop, tensor)

    def feed_at(place, wanted, fed, others=()):
        return feed(
            place, tensor, [parts_m[k] for k in wanted], [grad_parts[k] for k in wanted], ffn, fed, others
        )

    def back_m(places, fed, into=None, others=()):
        return back(places, rows, fed[1:3], [ffn, ffn], [0, 1], into, others)

    def back_out(places, fed, into=None, others=()):
        return back(places, rows, fed[0:1], [ffn], [2], into, others)

    def reduce_rows(term):
        return lax.psum_scatter(term, "dp", scatter_dimension=0, tiled=True).astype(F32)

    fed = None
    if tensor == 4:
        fed = feed_at(2, [3], None)
        (three_out,) = back_out([2], fed)
        out_one, out_two = send_half(three_out, tensor)
        fed = feed_at(0, [1, 2], fed, [three_out])
        fed = feed_at(3, [0], fed, [out_one, out_two])
    else:
        for place in range(tensor):
            fed = feed_at(place, [place], fed)
    hidden, grad_gate, grad_up, block_m, grad_block = fed
    down_t_wgrad = weigh(grad_block, hidden)
    down_t_sum = reduce_rows(down_t_wgrad)
    if tensor == 4:
        (three_m,) = back_m([2], fed, None, [down_t_wgrad])
        m_one, m_two = send_half(three_m, tensor)
        one_m, two_m = back_m([0, 1], fed, [(m_one, False), (m_two, True)])
        out_terms = back_out([0, 1, 3], fed, [(out_one, False), (out_two, True), None], [one_m])
        (own_m,) = back_m([3], fed, None, [out_terms[0]])
        grad_m_parts = [
            own_m,
            lax.ppermute(one_m, "tensor", pairs(tensor, 1)),
            lax.ppermute(two_m, "tensor", pairs(tensor, 2)),
        ]
    else:
        grad_m_parts = sum_whole(back_m(list(range(tensor)), fed))
    def norm_back(grad_in, normed, scale_r, gain):
        scaled = grad_in * gain
        return scale_r * (scaled - normed * jnp.mean(scaled * normed, axis=-1, keepdims=True))

    grad_normed_m = total(grad_m_parts)
    grad_stream_one = cotangent.astype(F32) + norm_back(grad_normed_m, normed_m, scale_m, mlp_scale)
    grad_stream_low = grad_stream_one.astype(BF16)
    gate_wgrad = weigh(block_m, grad_gate, [grad_stream_low])
    gate_sum = reduce_rows(gate_wgrad)
    up_wgrad = weigh(block_m, grad_up, [gate_wgrad])
    up_sum = reduce_rows(up_wgrad)
    grad_parts = gather(grad_stream_low, tensor)
    backs = None
    for place, wanted in enumerate([1, 2, 0, 3] if tensor == 4 else range(tensor)):
        backs = back_attended(
            place, tensor, grad_parts[wanted], bundle, out_place, query_cols, backs
        )
    grad_attended, grad_stream_block = backs
    grad_qkv = attend_back(
        bound, order, queries, kx, vx, kt, log_sums, attended, grad_attended, cosine, sine, rows
    )
    if tensor == 4:
        out_parts = [out_terms[2]] + [
            lax.ppermute(hold(out_terms[step - 1], grad_attended), "tensor", pairs(tensor, step))
            for step in (1, 2)
        ]
    else:
        out_parts = sum_whole(back_out(list(range(tensor)), fed))
    layer_out = (stream_one + total(out_parts)).astype(BF16)

    def back_a(places, others=()):
        return back(places, rows, [grad_qkv], [bundle], [0], None, others)

    if tensor == 4:
        (three,) = back_a(slots[3:], out_parts[1:])
        halves = send_half(three, tensor)
        one, two, own = back_a([slots[1], slots[2], slots[0]], [three, down_t_sum, gate_sum])
        grad_a_parts = [own, *send_whole(one, two, halves, tensor)]
        block_a = hold(block_a, own)
        grad_stream_block = hold(grad_stream_block, grad_qkv)
    else:
        grad_a_parts = sum_whole(back_a(slots))
    grad_normed_a = total(grad_a_parts)
    qkv_wgrad = weigh(block_a, grad_qkv)
    out_t_wgrad = weigh(grad_stream_block, attended)
    attention_sum = reduce_rows(jnp.concatenate([qkv_wgrad, out_t_wgrad], axis=1))

    def gain_term(gain, weights):
        term = sum(jnp.sum(weight.astype(F32) * grad, axis=1) for weight, grad in weights)
        return term / gain.astype(F32)

    query_sum = attention_sum[:, :query_cols]
    key_sum = attention_sum[:, query_cols : query_cols + key_cols]
    value_sum = attention_sum[:, query_cols + key_cols : columns]
    gain_terms = [
        gain_term(
            attn_gain, [(query_weight, query_sum), (key_weight, key_sum), (value_weight, value_sum)]
        ),
        gain_term(mlp_gain, [(gate_weight, gate_sum), (up_weight, up_sum)]),
    ]
    gain_mine = sum_everywhere(jnp.stack(gain_terms), {"tensor": tensor})
    normed_a, scale_a = normalize(stream)
    attn_scale = bundle[:, columns].astype(F32)[None, :]
    input_grad = (
        grad_stream_one + norm_back(grad_normed_a, normed_a, scale_a, attn_scale)
    ).astype(BF16)
    return (
        layer_out,
        input_grad,
        gain_mine[0],
        query_sum,
        key_sum,
        value_sum,
        attention_sum[:, columns:].T,
        gain_mine[1],
        gate_sum,
        up_sum,
        down_t_sum.T,
    )


def solution(mesh):
    tokens = P(("dp", "tensor"), None)
    in_specs = (
        tokens,
        P("dp"),
        P("dp"),
        P("dp", "tensor"),
        P("dp", "tensor"),
        P("dp", "tensor"),
        P("tensor", "dp"),
        P("dp"),
        P("dp", "tensor"),
        P("dp", "tensor"),
        P("tensor", "dp"),
        tokens,
    )
    out_specs = (
        tokens,
        tokens,
        P("dp"),
        P("dp", "tensor"),
        P("dp", "tensor"),
        P("dp", "tensor"),
        P("tensor", "dp"),
        P("dp"),
        P("dp", "tensor"),
        P("dp", "tensor"),
        P("tensor", "dp"),
    )
    return jax.shard_map(
        functools.partial(local, sizes={axis: mesh.shape[axis] for axis in ("tensor", "dp")}),
        mesh=mesh, in_specs=in_specs, out_specs=out_specs, check_vma=False,
    )
```

```python
import functools
import math

import jax
import jax.numpy as jnp
from jax import lax
from jax.experimental import pallas as pl
from jax.experimental.pallas import tpu as pltpu
from jax.sharding import PartitionSpec as P

HD = 64
LANES = 128
EPSILON = 1e-05
ROPE_BASE = 500000.0
MASKED = -1e30
OVER_ROWS = (((0,), (0,)), ((), ()))
OVER_COLS = (((1,), (1,)), ((), ()))
VMEM_LIMIT = 48 * 2**20
SHORT, LONG = 0.25, 16


def declared(flops, scale=SHORT):
    return pl.CostEstimate(flops=int(flops * scale), bytes_accessed=0, transcendentals=0)

F32 = jnp.float32
BF16 = jnp.bfloat16


def dot_cols(left, right):
    return lax.dot_general(left, right, OVER_COLS, preferred_element_type=F32)


def dot_rows(left, right):
    return lax.dot_general(left, right, OVER_ROWS, preferred_element_type=F32)


def dot(left, right):
    return jnp.dot(left, right, preferred_element_type=F32)


def pairs(size, bit):
    return [(index, index ^ bit) for index in range(size)]


def slots_of(size):
    if size == 4:
        return [lax.axis_index("tensor") ^ step for step in range(size)]
    return [jnp.int32(step) for step in range(size)]


ANYWHERE = pl.BlockSpec(memory_space=pl.ANY)


def nothing_kernel(*refs):
    pass


def hold(value, *others):
    return pl.pallas_call(
        nothing_kernel,
        in_specs=[ANYWHERE] * (1 + len(others)),
        out_specs=ANYWHERE,
        out_shape=jax.ShapeDtypeStruct(value.shape, value.dtype),
        input_output_aliases={0: 0},
        cost_estimate=declared(0),
    )(value, *others)


def first_hop(shard, size):
    if size != 4:
        return None
    return [lax.ppermute(shard, "tensor", pairs(size, bit)) for bit in (1, 2)]


def second_hop(shard, hop, size, others=()):
    if size != 4:
        whole = lax.all_gather(shard, "tensor", axis=0)
        return [whole[step] for step in range(size)]
    half = shard.shape[0] // 2
    one, two = hop
    first = hold(one[:half], *others) if others else one[:half]
    three_a = lax.ppermute(first, "tensor", pairs(size, 2))
    three_b = lax.ppermute(two[half:], "tensor", pairs(size, 1))
    return [shard, one, two, jnp.concatenate([three_a, three_b], axis=0)]


def gather(shard, size):
    return second_hop(shard, first_hop(shard, size), size)


def send_half(three, size):
    half = three.shape[0] // 2
    into_two = lax.ppermute(three[:half], "tensor", pairs(size, 1))
    into_one = lax.ppermute(three[half:], "tensor", pairs(size, 2))
    return into_one, into_two


def send_whole(one, two, into, size):
    into_one, into_two = into
    half = one.shape[0] // 2
    lower = (one[half:].astype(F32) + into_one.astype(F32)).astype(BF16)
    upper = (two[:half].astype(F32) + into_two.astype(F32)).astype(BF16)
    return [
        lax.ppermute(jnp.concatenate([one[:half], lower], axis=0), "tensor", pairs(size, 1)),
        lax.ppermute(jnp.concatenate([upper, two[half:]], axis=0), "tensor", pairs(size, 2)),
    ]


def sum_whole(terms):
    return [
        lax.psum_scatter(
            jnp.concatenate(terms, axis=0), "tensor", scatter_dimension=0, tiled=True
        )
    ]


def total(parts):
    return functools.reduce(jnp.add, [part.astype(F32) for part in parts])


def sum_everywhere(value, sizes):
    for axis, size in sizes.items():
        if size & (size - 1):
            value = lax.psum(value, axis)
            continue
        bit = 1
        while bit < size:
            value = value + lax.ppermute(value, axis, pairs(size, bit))
            bit *= 2
    return value


def rope_tables(segment):
    length = segment.shape[0]
    bound = jnp.sum((segment == 0).astype(jnp.int32))
    place = lax.broadcasted_iota(jnp.int32, (length, LANES), 0)
    place = place - jnp.where(place >= bound, bound, 0)
    lane = lax.broadcasted_iota(jnp.int32, (length, LANES), 1)
    freqs = jnp.exp(
        (lane % (HD // 2)).astype(F32) * (-2.0 * math.log(ROPE_BASE) / HD)
    )
    angles = place.astype(F32) * freqs
    sine = jnp.sin(angles)
    return bound, jnp.cos(angles), jnp.where(lane % HD < HD // 2, -sine, sine)


def swap_halves(values):
    lane = lax.broadcasted_iota(jnp.int32, values.shape, 1)
    after = pltpu.roll(values, LANES - HD // 2, 1)
    before = pltpu.roll(values, HD // 2, 1)
    return jnp.where(lane % HD < HD // 2, after, before)


def normalize(stream):
    scale_r = lax.rsqrt(jnp.mean(stream * stream, axis=-1, keepdims=True) + EPSILON)
    return (stream * scale_r, scale_r)


def project_kernel(slot_ref, *refs, count, steps, heads, kv):
    gains_ref, w_ref, cos_ref, sin_ref = refs[count : count + 4]
    h_ref, q_ref, kx_ref, vx_ref, kt_ref, vt_ref, gain_ref = refs[-7:]

    @pl.when(pl.program_id(0) == 0)
    def _():
        gain_ref[...] = gains_ref[...].astype(F32).T[:8]

    which = pl.program_id(0) // steps
    tokens = refs[0][...]
    for block in range(1, count):
        tokens = jnp.where(which == block, refs[block][...], tokens)
    normed, _ = normalize(tokens.astype(F32))
    low = (normed * gain_ref[0:1, :]).astype(BF16)
    h_ref[...] = low
    pre = dot(low, w_ref[...])
    cosine, sine = cos_ref[...], sin_ref[...]
    rows = pre.shape[0]
    lane = lax.broadcasted_iota(jnp.int32, (rows, LANES), 1)
    chunks = []
    for chunk in range(pre.shape[1] // LANES):
        part = pre[:, chunk * LANES : (chunk + 1) * LANES]
        turned = part * cosine + swap_halves(part) * sine
        first = 2 * chunk
        if first + 1 < heads + kv:
            chunks.append(turned)
        elif first < heads + kv:
            chunks.append(jnp.where(lane < HD, turned, part))
        else:
            chunks.append(part)
        if first < heads:
            q_ref[:, chunk * LANES : (chunk + 1) * LANES] = (
                chunks[chunk] * (1.0 / math.sqrt(HD))
            ).astype(BF16)
    flipped = {}
    for head in range(2 * kv):
        place = heads + head
        part = chunks[place // 2]
        moved = pltpu.roll(part, HD, 1)
        wide = [part, moved] if place % 2 == 0 else [moved, part]
        out = kx_ref if head < kv else vx_ref
        out[head % kv, 0] = jnp.where(lane < HD, wide[0], 0.0).astype(BF16)
        out[head % kv, 1] = jnp.where(lane < HD, 0.0, wide[1]).astype(BF16)
        if place // 2 not in flipped:
            flipped[place // 2] = part.T
        turn = flipped[place // 2][(place % 2) * HD : (place % 2 + 1) * HD]
        out_t = kt_ref if head < kv else vt_ref
        out_t[(head % kv) * HD : (head % kv + 1) * HD, :] = turn.astype(BF16)


def project(slots, blocks, bundle, cosine, sine, heads, kv, length, prev):
    rows, width = blocks[0].shape
    count = len(blocks)
    tile = min(256, rows)
    steps = rows // tile
    columns = (heads + 2 * kv) * HD

    def at(i, slot):
        return slot[i // steps] * steps + i % steps

    shapes = [
        jax.ShapeDtypeStruct((length, width), BF16),
        jax.ShapeDtypeStruct((length, heads * HD), BF16),
        jax.ShapeDtypeStruct((kv, 2, length, LANES), BF16),
        jax.ShapeDtypeStruct((kv, 2, length, LANES), BF16),
        jax.ShapeDtypeStruct((kv * HD, length), BF16),
        jax.ShapeDtypeStruct((kv * HD, length), BF16),
    ]
    out_specs = [
        pl.BlockSpec((tile, width), lambda i, s: (at(i, s), 0)),
        pl.BlockSpec((tile, heads * HD), lambda i, s: (at(i, s), 0)),
        pl.BlockSpec((kv, 2, tile, LANES), lambda i, s: (0, 0, at(i, s), 0)),
        pl.BlockSpec((kv, 2, tile, LANES), lambda i, s: (0, 0, at(i, s), 0)),
        pl.BlockSpec((kv * HD, tile), lambda i, s: (0, at(i, s))),
        pl.BlockSpec((kv * HD, tile), lambda i, s: (0, at(i, s))),
    ]
    in_specs = [
        pl.BlockSpec((tile, width), lambda i, s, b=block: (jnp.clip(i - b * steps, 0, steps - 1), 0))
        for block in range(count)
    ]
    in_specs += [
        pl.BlockSpec((width, LANES), lambda i, s: (0, columns // LANES)),
        pl.BlockSpec((width, columns), lambda i, s: (0, 0)),
        pl.BlockSpec((tile, LANES), lambda i, s: (at(i, s), 0)),
        pl.BlockSpec((tile, LANES), lambda i, s: (at(i, s), 0)),
    ]
    operands = [jnp.stack(slots), *blocks, bundle, bundle, cosine, sine]
    aliases = {}
    if prev is not None:
        for index, array in enumerate(prev):
            aliases[len(operands)] = index
            operands.append(array)
            in_specs.append(ANYWHERE)
    return pl.pallas_call(
        functools.partial(
            project_kernel, count=count, steps=steps, heads=heads, kv=kv
        ),
        grid_spec=pltpu.PrefetchScalarGridSpec(
            num_scalar_prefetch=1,
            grid=(count * steps,),
            in_specs=in_specs,
            out_specs=out_specs,
            scratch_shapes=[pltpu.VMEM((8, width), F32)],
        ),
        out_shape=shapes,
        input_output_aliases=aliases,
        compiler_params=pltpu.CompilerParams(vmem_limit_bytes=VMEM_LIMIT),
        cost_estimate=declared(2 * count * rows * width * columns),
    )(*operands)


def feed_kernel(*refs, count):
    tokens, grads = refs[:count], refs[count : 2 * count]
    gate_ref, up_ref, down_ref = refs[2 * count : 2 * count + 3]
    hidden_ref, dgate_ref, dup_ref, h_out, grad_out = refs[-5:]
    rows = tokens[0].shape[0]
    wide = h_out.shape[1]
    tile = min(256, gate_ref.shape[1])
    lanes = pl.ds(pl.multiple_of(pl.program_id(0) * wide, wide), wide)
    for block in range(count):
        where = slice(block * rows, (block + 1) * rows)
        h_out[where, :] = tokens[block][:, lanes]
        grad_out[where, :] = grads[block][:, lanes]
    for part in range(gate_ref.shape[1] // tile):
        columns = slice(part * tile, (part + 1) * tile)
        for block in range(count):
            where = slice(block * rows, (block + 1) * rows)
            gate = dot(tokens[block][...], gate_ref[:, columns])
            up = dot(tokens[block][...], up_ref[:, columns])
            dhidden = dot(grads[block][...], down_ref[:, columns])
            sigmoid = 0.5 * jnp.tanh(0.5 * gate) + 0.5
            silu = gate * sigmoid
            hidden_ref[where, columns] = (silu * up).astype(BF16)
            dup_ref[where, columns] = (dhidden * silu).astype(BF16)
            dgate_ref[where, columns] = (
                dhidden * up * (sigmoid + silu * (1.0 - sigmoid))
            ).astype(BF16)


def feed(place, blocks, normed, grads, weights, prev, others):
    rows, width = normed[0].shape
    count = len(normed)
    units = weights.shape[1] // 3
    steps = 4
    tile, wide = units // steps, width // steps
    shapes = [jax.ShapeDtypeStruct((blocks * rows, units), BF16)] * 3
    shapes += [jax.ShapeDtypeStruct((blocks * rows, width), BF16)] * 2
    tokens = pl.BlockSpec((rows, width), lambda i: (0, 0), pipeline_mode=pl.Buffered(1))
    in_specs = [tokens] * (2 * count)
    in_specs += [
        pl.BlockSpec((width, tile), lambda i, w=which: (0, w * steps + i)) for which in range(3)
    ]
    out_specs = [pl.BlockSpec((count * rows, tile), lambda i: (place, i))] * 3
    out_specs += [pl.BlockSpec((count * rows, wide), lambda i: (place, i))] * 2
    operands = [*normed, *grads, weights, weights, weights]
    aliases = {}
    if prev is not None:
        for index, array in enumerate(prev):
            aliases[len(operands)] = index
            operands.append(array)
            in_specs.append(ANYWHERE)
    operands += others
    in_specs += [ANYWHERE] * len(others)
    return pl.pallas_call(
        functools.partial(feed_kernel, count=count),
        grid=(steps,),
        in_specs=in_specs,
        out_specs=out_specs,
        out_shape=shapes,
        input_output_aliases=aliases,
        compiler_params=pltpu.CompilerParams(vmem_limit_bytes=VMEM_LIMIT),
        cost_estimate=declared(6 * count * rows * width * units),
    )(*operands)


def back_kernel(slot_ref, *refs, count, terms, added):
    outs = refs[-count:]
    weights = refs[count * terms : (count + 1) * terms]
    into = list(refs[(count + 1) * terms :])
    for block in range(count):
        value = dot_cols(refs[block * terms][...], weights[0][...])
        for term in range(1, terms):
            value = value + dot_cols(refs[block * terms + term][...], weights[term][...])
        if added[block] is None:
            outs[block][...] = value.astype(BF16)
            continue
        half = value.shape[0] // 2
        extra = into.pop(0)[...].astype(F32)
        top, bottom = value[:half], value[half:]
        if added[block]:
            top = top + extra
        else:
            bottom = bottom + extra
        outs[block][:half, :] = top.astype(BF16)
        outs[block][half:, :] = bottom.astype(BF16)


def back(slots, rows, lefts, weights, places, into=None, others=(), scale=SHORT):
    depth = lefts[0].shape[1]
    width = weights[0].shape[0]
    tile = min(512, width)
    terms, count = len(lefts), len(slots)
    into = into or [None] * count
    in_specs, operands = [], [jnp.stack([jnp.asarray(slot, jnp.int32) for slot in slots])]
    for block in range(count):
        in_specs += [pl.BlockSpec((rows, depth), lambda i, s, b=block: (s[b], 0))] * terms
        operands += lefts
    in_specs += [pl.BlockSpec((tile, depth), lambda i, s, p=place: (i, p)) for place in places]
    operands += weights
    for extra in into:
        if extra is not None:
            in_specs.append(pl.BlockSpec((rows // 2, tile), lambda i, s: (0, i)))
            operands.append(extra[0])
    operands += others
    in_specs += [ANYWHERE] * len(others)
    return pl.pallas_call(
        functools.partial(
            back_kernel,
            count=count,
            terms=terms,
            added=[None if extra is None else extra[1] for extra in into],
        ),
        grid_spec=pltpu.PrefetchScalarGridSpec(
            num_scalar_prefetch=1,
            grid=(width // tile,),
            in_specs=in_specs,
            out_specs=[pl.BlockSpec((rows, tile), lambda i, s: (0, i))] * count,
        ),
        out_shape=[jax.ShapeDtypeStruct((rows, width), BF16)] * count,
        compiler_params=pltpu.CompilerParams(vmem_limit_bytes=VMEM_LIMIT),
        cost_estimate=declared(2 * count * terms * rows * width * depth, scale),
    )(*operands)


def weigh_kernel(left_ref, right_ref, *rest):
    out_ref, turned_ref = rest[-2:]

    @pl.when(pl.program_id(1) == 0)
    def _():
        turned_ref[...] = left_ref[...].T

    out_ref[...] = dot(turned_ref[...], right_ref[...]).astype(BF16)


def weigh(left, right, others=()):
    tokens, width = left.shape
    columns = right.shape[1]
    tall, wide = min(512, width), min(1024, columns)
    return pl.pallas_call(
        weigh_kernel,
        grid=(width // tall, columns // wide),
        in_specs=[
            pl.BlockSpec((tokens, tall), lambda i, j: (0, i)),
            pl.BlockSpec((tokens, wide), lambda i, j: (0, j)),
        ]
        + [ANYWHERE] * len(others),
        out_specs=pl.BlockSpec((tall, wide), lambda i, j: (i, j)),
        out_shape=jax.ShapeDtypeStruct((width, columns), BF16),
        scratch_shapes=[pltpu.VMEM((tall, tokens), BF16)],
        compiler_params=pltpu.CompilerParams(vmem_limit_bytes=VMEM_LIMIT),
        cost_estimate=declared(2 * tokens * width * columns, LONG),
    )(left, right, *others)


def back_attended_kernel(grad_ref, w_ref, *rest):
    out_ref, copy_ref = rest[-2:]
    out_ref[...] = dot(grad_ref[...], w_ref[...]).astype(BF16)
    copy_ref[...] = grad_ref[...]


def back_attended(place, blocks, grad, bundle, column, columns, prev):
    rows, width = grad.shape
    tile = min(256, rows)
    steps = rows // tile
    in_specs = [
        pl.BlockSpec((tile, width), lambda i: (i, 0)),
        pl.BlockSpec((width, columns), lambda i: (0, column)),
    ]
    operands = [grad, bundle]
    aliases = {}
    if prev is not None:
        for index, array in enumerate(prev):
            aliases[len(operands)] = index
            operands.append(array)
            in_specs.append(ANYWHERE)
    return pl.pallas_call(
        back_attended_kernel,
        grid=(steps,),
        in_specs=in_specs,
        out_specs=[
            pl.BlockSpec((tile, columns), lambda i: (place * steps + i, 0)),
            pl.BlockSpec((tile, width), lambda i: (place * steps + i, 0)),
        ],
        out_shape=[
            jax.ShapeDtypeStruct((blocks * rows, columns), BF16),
            jax.ShapeDtypeStruct((blocks * rows, width), BF16),
        ],
        input_output_aliases=aliases,
        compiler_params=pltpu.CompilerParams(vmem_limit_bytes=VMEM_LIMIT),
        cost_estimate=declared(2 * rows * width * columns),
    )(*operands)


def causal(block):
    keys = lax.broadcasted_iota(jnp.int32, (block, block), 0)
    return keys <= lax.broadcasted_iota(jnp.int32, (block, block), 1)


def first_block(bound, offset, block):
    return jnp.where(offset >= bound, lax.div(bound, jnp.int32(block)), 0)


def attend_kernel(order_ref, q_ref, kx_ref, vt_ref, *rest, block):
    out_ref, lse_ref, top_ref, acc_ref = rest[-4:]
    kv = kx_ref.shape[0]
    per = q_ref.shape[1] // LANES // kv
    bound = order_ref[0]
    ones = jnp.ones((16, block), BF16)
    for group in range(kv):

        def q_step(turn, _):
            index = order_ref[1 + turn]
            offset = pl.multiple_of(index * block, block)
            into = pl.ds(pl.multiple_of(turn * block, block), block)
            top_ref[...] = jnp.full(top_ref.shape, MASKED, F32)
            acc_ref[...] = jnp.zeros(acc_ref.shape, F32)

            def tile(step, diagonal):
                keys = pl.ds(pl.multiple_of(step * block, block), block)
                value_t = jnp.concatenate(
                    [vt_ref[group * HD : (group + 1) * HD, keys], ones], axis=0
                )
                for head in range(2 * per):
                    column = (group * per + head // 2) * LANES
                    query = q_ref[pl.ds(offset, block), column : column + LANES]
                    scores = dot_cols(kx_ref[group, head % 2, keys, :], query)
                    if diagonal:
                        scores = jnp.where(causal(block), scores, MASKED)
                    old = top_ref[head, 0:1, :]
                    top = jnp.maximum(old, jnp.max(scores, axis=0, keepdims=True))
                    powered = jnp.exp(scores - top).astype(BF16)
                    acc_ref[head] = acc_ref[head] * jnp.exp(old - top) + dot(value_t, powered)
                    top_ref[head, 0:1, :] = top

            def full_tile(step, carry):
                tile(step, False)
                return carry

            lax.fori_loop(first_block(bound, offset, block), index, full_tile, 0)
            tile(index, True)
            for pair in range(per):
                both = []
                for head in (2 * pair, 2 * pair + 1):
                    total = acc_ref[head, HD : HD + 1, :]
                    both.append(acc_ref[head, :HD, :] / total)
                    place = group * 2 * per + head
                    lse_ref[place : place + 1, into] = top_ref[
                        head, 0:1, :
                    ] + jnp.log(total)
                column = (group * per + pair) * LANES
                out_ref[into, column : column + LANES] = (
                    jnp.concatenate(both, axis=0).T.astype(BF16)
                )
            return _

        lax.fori_loop(0, out_ref.shape[0] // block, q_step, 0)


def attend(bound, order, queries, kx, vt, block, others=()):
    length, width = queries.shape
    heads = width // HD
    kv = kx.shape[0]
    per = heads // kv
    count = len(order)
    cells = heads * count * block * (length + block) // 2
    vmem = pl.BlockSpec(memory_space=pltpu.VMEM)
    return pl.pallas_call(
        functools.partial(attend_kernel, block=block),
        in_specs=[pl.BlockSpec(memory_space=pltpu.SMEM), vmem, vmem, vmem] + [ANYWHERE] * len(others),
        out_specs=[vmem, vmem],
        out_shape=[
            jax.ShapeDtypeStruct((count * block, width), BF16),
            jax.ShapeDtypeStruct((heads, count * block), F32),
        ],
        scratch_shapes=[
            pltpu.VMEM((per, 8, block), F32),
            pltpu.VMEM((per, HD + 16, block), F32),
        ],
        compiler_params=pltpu.CompilerParams(vmem_limit_bytes=VMEM_LIMIT),
        cost_estimate=declared(2 * 4 * HD * 4 * cells),
    )(jnp.stack([bound, *order]), queries, kx, vt, *others)


def attend_back_kernel(
    order_ref, q_ref, kx_ref, vx_ref, kt_ref, lse_ref, out_ref, grad_ref, cos_ref, sin_ref,
    dqkv_ref, dk_ref, dv_ref, dq_ref, *, block
):
    length = q_ref.shape[0]
    kv = kx_ref.shape[0]
    heads = q_ref.shape[1] // HD
    per = heads // 2 // kv
    bound = order_ref[0]
    dk_ref[...] = jnp.zeros(dk_ref.shape, F32)
    dv_ref[...] = jnp.zeros(dv_ref.shape, F32)
    lane = lax.broadcasted_iota(jnp.int32, (8, LANES), 1)
    row = lax.broadcasted_iota(jnp.int32, (8, LANES), 0)
    chosen = ((lane // HD) == row).astype(F32)

    def turn_back(values, rows):
        return values * cos_ref[rows, :] - swap_halves(values) * sin_ref[rows, :]

    for group in range(kv):

        def q_step(turn, _):
            index = order_ref[1 + turn]
            offset = pl.multiple_of(index * block, block)
            rows = pl.ds(offset, block)
            given = pl.ds(pl.multiple_of(turn * block, block), block)
            dq_ref[...] = jnp.zeros(dq_ref.shape, F32)
            deltas = []
            for pair in range(per):
                column = (group * per + pair) * LANES
                product = grad_ref[given, column : column + LANES].astype(F32) * out_ref[
                    given, column : column + LANES
                ].astype(F32)
                deltas.append(
                    lax.dot_general(
                        chosen, product, OVER_COLS, precision=lax.Precision.HIGHEST,
                        preferred_element_type=F32,
                    )
                )

            def tile(step, diagonal):
                keys = pl.ds(pl.multiple_of(step * block, block), block)
                key_t = kt_ref[group * HD : (group + 1) * HD, keys]
                for parity in range(2):
                    key_add, value_add = 0.0, 0.0
                    for pair in range(per):
                        head = 2 * pair + parity
                        place = group * 2 * per + head
                        column = (group * per + pair) * LANES
                        query = q_ref[rows, column : column + LANES]
                        grad = grad_ref[given, column : column + LANES]
                        scores = dot_cols(kx_ref[group, parity, keys, :], query)
                        if diagonal:
                            scores = jnp.where(causal(block), scores, MASKED)
                        probs = jnp.exp(scores - lse_ref[place : place + 1, given])
                        dprobs = dot_cols(vx_ref[group, parity, keys, :], grad)
                        dscores = (probs * (dprobs - deltas[pair][parity : parity + 1])).astype(BF16)
                        value_add = value_add + dot(probs.astype(BF16), grad)
                        key_add = key_add + dot(dscores, query)
                        dq_ref[head * HD : (head + 1) * HD, :] += dot(key_t, dscores)
                    dk_ref[group, parity, keys, :] += key_add
                    dv_ref[group, parity, keys, :] += value_add

            def full_tile(step, carry):
                tile(step, False)
                return carry

            lax.fori_loop(first_block(bound, offset, block), index, full_tile, 0)
            tile(index, True)
            for pair in range(per):
                column = (group * per + pair) * LANES
                grad_q = dq_ref[pair * LANES : (pair + 1) * LANES, :].T * (1.0 / math.sqrt(HD))
                dqkv_ref[rows, column : column + LANES] = turn_back(grad_q, rows).astype(BF16)
            return _

        lax.fori_loop(0, length // block, q_step, 0)

    def finish(index, _):
        rows = pl.ds(pl.multiple_of(index * block, block), block)
        lanes = lax.broadcasted_iota(jnp.int32, (block, LANES), 1)

        def placed(part, half):
            ref = dk_ref if part < kv else dv_ref
            even, odd = ref[part % kv, 0, rows, :], ref[part % kv, 1, rows, :]
            return even + pltpu.roll(odd, HD, 1) if half == 0 else pltpu.roll(even, HD, 1) + odd

        for chunk in range(kv):
            values = jnp.where(lanes < HD, placed(2 * chunk, 0), placed(2 * chunk + 1, 1))
            if 2 * chunk + 1 < kv:
                values = turn_back(values, rows)
            elif 2 * chunk < kv:
                values = jnp.where(lanes < HD, turn_back(values, rows), values)
            column = heads * HD + chunk * LANES
            dqkv_ref[rows, column : column + LANES] = values.astype(BF16)
        return _

    lax.fori_loop(0, length // block, finish, 0)


def attend_back(bound, order, queries, kx, vx, kt, log_sums, attended, grad, cosine, sine, block):
    length, width = queries.shape
    heads = width // HD
    kv = kx.shape[0]
    cells = heads * length * (length + block) // 2
    vmem = pl.BlockSpec(memory_space=pltpu.VMEM)
    return pl.pallas_call(
        functools.partial(attend_back_kernel, block=block),
        in_specs=[pl.BlockSpec(memory_space=pltpu.SMEM)] + [vmem] * 9,
        out_specs=vmem,
        out_shape=jax.ShapeDtypeStruct((length, width + 2 * kv * HD), BF16),
        scratch_shapes=[
            pltpu.VMEM((kv, 2, length, LANES), F32),
            pltpu.VMEM((kv, 2, length, LANES), F32),
            pltpu.VMEM((heads // kv * HD, block), F32),
        ],
        compiler_params=pltpu.CompilerParams(vmem_limit_bytes=VMEM_LIMIT),
        cost_estimate=declared(2 * 10 * HD * 4 * cells, 4 * LONG),
    )(jnp.stack([bound, *order]), queries, kx, vx, kt, log_sums, attended, grad, cosine, sine)


def local(
    inputs,
    segment_ids,
    attn_gain,
    query_weight,
    key_weight,
    value_weight,
    output_weight,
    mlp_gain,
    gate_weight,
    up_weight,
    down_weight,
    cotangent,
    *,
    sizes,
):
    rows = inputs.shape[0]
    length = segment_ids.shape[0]
    query_cols = query_weight.shape[1]
    key_cols = key_weight.shape[1]
    heads, kv = query_cols // HD, key_cols // HD
    columns = query_cols + 2 * key_cols
    slots = slots_of(sizes["tensor"])
    tensor = sizes["tensor"]
    space = (-columns) % query_cols or query_cols
    gains = jnp.pad(jnp.stack([attn_gain, mlp_gain], axis=1), ((0, 0), (0, space - 2)))
    bundle = lax.all_gather(
        jnp.concatenate([query_weight, key_weight, value_weight, gains, output_weight.T], axis=1),
        "dp", axis=0, tiled=True,
    )
    out_place = (columns + space) // query_cols
    mlp_scale = bundle[:, columns + 1].astype(F32)[None, :]
    hop = first_hop(inputs, tensor)
    ffn = lax.all_gather(
        hold(jnp.concatenate([gate_weight, up_weight, down_weight.T], axis=1), *(hop or ())),
        "dp", axis=0, tiled=True,
    )

    bound, cosine, sine = rope_tables(segment_ids)
    blocks = second_hop(inputs, hop, tensor)
    stream = inputs.astype(F32)
    arrays = None
    if tensor == 4:
        arrays = project(slots[:3], blocks[:3], bundle, cosine, sine, heads, kv, length, None)
        arrays = project(slots[3:], blocks[3:], bundle, cosine, sine, heads, kv, length, arrays)
    else:
        arrays = project(slots, blocks, bundle, cosine, sine, heads, kv, length, None)
    block_a, queries, kx, vx, kt, vt = arrays
    cotangent_sent = hold(cotangent, blocks[-1])
    cotangent_hop = first_hop(cotangent_sent, tensor)

    def back_attention(places, attended, others=()):
        return back(places, rows, [attended], [bundle], [out_place], None, others)

    if tensor == 4:
        far, far_sums = attend(bound, slots[3:], queries, kx, vt, rows)
        three = back_attention([0], far)[0]
        halves = send_half(three, tensor)
        order = [slots[1], slots[2], slots[0], slots[3]]
        near, near_sums = attend(bound, order[:3], queries, kx, vt, rows, [three])
        one, two, own = back_attention([0, 1, 2], near, cotangent_hop)
        attended = jnp.concatenate([near, far], axis=0)
        log_sums = jnp.concatenate([near_sums, far_sums], axis=1)
        stream_parts = [own, *send_whole(one, two, halves, tensor)]
    else:
        order = slots
        attended, log_sums = attend(bound, order, queries, kx, vt, rows)
        stream_parts = sum_whole(back_attention(list(range(tensor)), attended))
    stream_one = stream + total(stream_parts)
    normed_m, scale_m = normalize(stream_one)
    grad_parts = second_hop(cotangent_sent, cotangent_hop, tensor)
    parts_m = gather(hold((normed_m * mlp_scale).astype(BF16), grad_parts[-1]), tensor)

    def feed_at(place, wanted, fed, others=()):
        return feed(
            place, tensor, [parts_m[k] for k in wanted], [grad_parts[k] for k in wanted], ffn, fed, others
        )

    def back_m(places, fed, into=None, others=()):
        return back(places, rows, fed[1:3], [ffn, ffn], [0, 1], into, others)

    def back_out(places, fed, into=None, others=()):
        return back(places, rows, fed[0:1], [ffn], [2], into, others)

    def reduce_rows(term):
        return lax.psum_scatter(term, "dp", scatter_dimension=0, tiled=True).astype(F32)

    fed = None
    if tensor == 4:
        fed = feed_at(2, [3], None)
        (three_out,) = back_out([2], fed)
        out_one, out_two = send_half(three_out, tensor)
        fed = feed_at(0, [1, 2], fed, [three_out])
        fed = feed_at(3, [0], fed, [out_one, out_two])
    else:
        for place in range(tensor):
            fed = feed_at(place, [place], fed)
    hidden, grad_gate, grad_up, block_m, grad_block = fed
    down_t_wgrad = weigh(grad_block, hidden)
    down_t_sum = reduce_rows(down_t_wgrad)
    if tensor == 4:
        (three_m,) = back_m([2], fed, None, [down_t_wgrad])
        m_one, m_two = send_half(three_m, tensor)
        out_terms = back_out([0, 1, 3], fed, [(out_one, False), (out_two, True), None], [three_m])
        one_m, two_m = back_m([0, 1], fed, [(m_one, False), (m_two, True)], [out_terms[0]])
        gate_wgrad = weigh(block_m, grad_gate, [one_m])
        (own_m,) = back_m([3], fed, None, [gate_wgrad])
        grad_m_parts = [
            own_m,
            lax.ppermute(one_m, "tensor", pairs(tensor, 1)),
            lax.ppermute(two_m, "tensor", pairs(tensor, 2)),
        ]
    else:
        grad_m_parts = sum_whole(back_m(list(range(tensor)), fed))
        gate_wgrad = weigh(block_m, grad_gate)
    gate_sum = reduce_rows(gate_wgrad)
    def norm_back(grad_in, normed, scale_r, gain):
        scaled = grad_in * gain
        return scale_r * (scaled - normed * jnp.mean(scaled * normed, axis=-1, keepdims=True))

    grad_normed_m = total(grad_m_parts)
    grad_stream_one = cotangent.astype(F32) + norm_back(grad_normed_m, normed_m, scale_m, mlp_scale)
    grad_stream_low = grad_stream_one.astype(BF16)
    up_wgrad = weigh(block_m, grad_up, [grad_stream_low])
    up_sum = reduce_rows(up_wgrad)
    grad_parts = second_hop(grad_stream_low, first_hop(grad_stream_low, tensor), tensor, [up_wgrad])
    backs = None
    for place, wanted in enumerate([1, 2, 0, 3] if tensor == 4 else range(tensor)):
        backs = back_attended(
            place, tensor, grad_parts[wanted], bundle, out_place, query_cols, backs
        )
    grad_attended, grad_stream_block = backs
    grad_qkv = attend_back(
        bound, order, queries, kx, vx, kt, log_sums, attended, grad_attended, cosine, sine, rows
    )
    if tensor == 4:
        out_parts = [out_terms[2]] + [
            lax.ppermute(hold(out_terms[step - 1], grad_attended), "tensor", pairs(tensor, step))
            for step in (1, 2)
        ]
    else:
        out_parts = sum_whole(back_out(list(range(tensor)), fed))
    layer_out = (stream_one + total(out_parts)).astype(BF16)

    def back_a(places, others=(), scale=SHORT):
        return back(places, rows, [grad_qkv], [bundle], [0], None, others, scale)

    if tensor == 4:
        (three,) = back_a(slots[3:], out_parts[1:])
        halves = send_half(three, tensor)
        block_a = hold(block_a, three)
        grad_stream_block = hold(grad_stream_block, three)
    qkv_wgrad = weigh(block_a, grad_qkv)
    out_t_wgrad = weigh(grad_stream_block, attended)
    attention_wgrad = jnp.concatenate([qkv_wgrad, out_t_wgrad], axis=1)
    attention_sum = reduce_rows(attention_wgrad)
    if tensor == 4:
        one, two, own = back_a([slots[1], slots[2], slots[0]], [attention_wgrad], 4 * LONG)
        grad_a_parts = [own, *send_whole(one, two, halves, tensor)]
    else:
        grad_a_parts = sum_whole(back_a(slots))
    grad_normed_a = total(grad_a_parts)

    def gain_term(gain, weights):
        term = sum(jnp.sum(weight.astype(F32) * grad, axis=1) for weight, grad in weights)
        return term / gain.astype(F32)

    query_sum = attention_sum[:, :query_cols]
    key_sum = attention_sum[:, query_cols : query_cols + key_cols]
    value_sum = attention_sum[:, query_cols + key_cols : columns]
    gain_terms = [
        gain_term(
            attn_gain, [(query_weight, query_sum), (key_weight, key_sum), (value_weight, value_sum)]
        ),
        gain_term(mlp_gain, [(gate_weight, gate_sum), (up_weight, up_sum)]),
    ]
    gain_mine = sum_everywhere(jnp.stack(gain_terms), {"tensor": tensor})
    normed_a, scale_a = normalize(stream)
    attn_scale = bundle[:, columns].astype(F32)[None, :]
    input_grad = (
        grad_stream_one + norm_back(grad_normed_a, normed_a, scale_a, attn_scale)
    ).astype(BF16)
    return (
        layer_out,
        input_grad,
        gain_mine[0],
        query_sum,
        key_sum,
        value_sum,
        attention_sum[:, columns:].T,
        gain_mine[1],
        gate_sum,
        up_sum,
        down_t_sum.T,
    )


def solution(mesh):
    tokens = P(("dp", "tensor"), None)
    in_specs = (
        tokens,
        P("dp"),
        P("dp"),
        P("dp", "tensor"),
        P("dp", "tensor"),
        P("dp", "tensor"),
        P("tensor", "dp"),
        P("dp"),
        P("dp", "tensor"),
        P("dp", "tensor"),
        P("tensor", "dp"),
        tokens,
    )
    out_specs = (
        tokens,
        tokens,
        P("dp"),
        P("dp", "tensor"),
        P("dp", "tensor"),
        P("dp", "tensor"),
        P("tensor", "dp"),
        P("dp"),
        P("dp", "tensor"),
        P("dp", "tensor"),
        P("tensor", "dp"),
    )
    return jax.shard_map(
        functools.partial(local, sizes={axis: mesh.shape[axis] for axis in ("tensor", "dp")}),
        mesh=mesh, in_specs=in_specs, out_specs=out_specs, check_vma=False,
    )
```

```python
import functools
import math

import jax
import jax.numpy as jnp
from jax import lax
from jax.experimental import pallas as pl
from jax.experimental.pallas import tpu as pltpu
from jax.sharding import PartitionSpec as P

HD = 64
LANES = 128
EPSILON = 1e-05
ROPE_BASE = 500000.0
MASKED = -1e30
OVER_ROWS = (((0,), (0,)), ((), ()))
OVER_COLS = (((1,), (1,)), ((), ()))
VMEM_LIMIT = 48 * 2**20
SHORT = 0.0625


def declared(flops):
    return pl.CostEstimate(flops=int(flops * SHORT), bytes_accessed=0, transcendentals=0)

F32 = jnp.float32
BF16 = jnp.bfloat16


def dot_cols(left, right):
    return lax.dot_general(left, right, OVER_COLS, preferred_element_type=F32)


def dot_rows(left, right):
    return lax.dot_general(left, right, OVER_ROWS, preferred_element_type=F32)


def dot(left, right):
    return jnp.dot(left, right, preferred_element_type=F32)


def pairs(size, bit):
    return [(index, index ^ bit) for index in range(size)]


def slots_of(size):
    if size == 4:
        return [lax.axis_index("tensor") ^ step for step in range(size)]
    return [jnp.int32(step) for step in range(size)]


ANYWHERE = pl.BlockSpec(memory_space=pl.ANY)


def nothing_kernel(*refs):
    pass


def hold(value, *others):
    return pl.pallas_call(
        nothing_kernel,
        in_specs=[ANYWHERE] * (1 + len(others)),
        out_specs=ANYWHERE,
        out_shape=jax.ShapeDtypeStruct(value.shape, value.dtype),
        input_output_aliases={0: 0},
        cost_estimate=declared(0),
    )(value, *others)


def first_hop(shard, size):
    if size != 4:
        return None
    return [lax.ppermute(shard, "tensor", pairs(size, bit)) for bit in (1, 2)]


def second_hop(shard, hop, size, others=()):
    if size != 4:
        whole = lax.all_gather(shard, "tensor", axis=0)
        return [whole[step] for step in range(size)]
    half = shard.shape[0] // 2
    one, two = hop
    first = hold(one[:half], *others) if others else one[:half]
    three_a = lax.ppermute(first, "tensor", pairs(size, 2))
    three_b = lax.ppermute(two[half:], "tensor", pairs(size, 1))
    return [shard, one, two, jnp.concatenate([three_a, three_b], axis=0)]


def gather(shard, size):
    return second_hop(shard, first_hop(shard, size), size)


def send_half(three, size):
    half = three.shape[0] // 2
    into_two = lax.ppermute(three[:half], "tensor", pairs(size, 1))
    into_one = lax.ppermute(three[half:], "tensor", pairs(size, 2))
    return into_one, into_two


def send_whole(one, two, into, size):
    into_one, into_two = into
    half = one.shape[0] // 2
    lower = (one[half:].astype(F32) + into_one.astype(F32)).astype(BF16)
    upper = (two[:half].astype(F32) + into_two.astype(F32)).astype(BF16)
    return [
        lax.ppermute(jnp.concatenate([one[:half], lower], axis=0), "tensor", pairs(size, 1)),
        lax.ppermute(jnp.concatenate([upper, two[half:]], axis=0), "tensor", pairs(size, 2)),
    ]


def sum_whole(terms):
    return [
        lax.psum_scatter(
            jnp.concatenate(terms, axis=0), "tensor", scatter_dimension=0, tiled=True
        )
    ]


def total(parts):
    return functools.reduce(jnp.add, [part.astype(F32) for part in parts])


def sum_everywhere(value, sizes):
    for axis, size in sizes.items():
        if size & (size - 1):
            value = lax.psum(value, axis)
            continue
        bit = 1
        while bit < size:
            value = value + lax.ppermute(value, axis, pairs(size, bit))
            bit *= 2
    return value


def rope_tables(segment):
    length = segment.shape[0]
    bound = jnp.sum((segment == 0).astype(jnp.int32))
    place = lax.broadcasted_iota(jnp.int32, (length, LANES), 0)
    place = place - jnp.where(place >= bound, bound, 0)
    lane = lax.broadcasted_iota(jnp.int32, (length, LANES), 1)
    freqs = jnp.exp(
        (lane % (HD // 2)).astype(F32) * (-2.0 * math.log(ROPE_BASE) / HD)
    )
    angles = place.astype(F32) * freqs
    sine = jnp.sin(angles)
    return bound, jnp.cos(angles), jnp.where(lane % HD < HD // 2, -sine, sine)


def swap_halves(values):
    lane = lax.broadcasted_iota(jnp.int32, values.shape, 1)
    after = pltpu.roll(values, LANES - HD // 2, 1)
    before = pltpu.roll(values, HD // 2, 1)
    return jnp.where(lane % HD < HD // 2, after, before)


def normalize(stream):
    scale_r = lax.rsqrt(jnp.mean(stream * stream, axis=-1, keepdims=True) + EPSILON)
    return (stream * scale_r, scale_r)


def project_kernel(slot_ref, *refs, count, steps, heads, kv):
    gains_ref, w_ref, cos_ref, sin_ref = refs[count : count + 4]
    h_ref, q_ref, kx_ref, vx_ref, kt_ref, vt_ref, gain_ref = refs[-7:]

    @pl.when(pl.program_id(0) == 0)
    def _():
        gain_ref[...] = gains_ref[...].astype(F32).T[:8]

    which = pl.program_id(0) // steps
    tokens = refs[0][...]
    for block in range(1, count):
        tokens = jnp.where(which == block, refs[block][...], tokens)
    normed, _ = normalize(tokens.astype(F32))
    low = (normed * gain_ref[0:1, :]).astype(BF16)
    h_ref[...] = low
    pre = dot(low, w_ref[...])
    cosine, sine = cos_ref[...], sin_ref[...]
    rows = pre.shape[0]
    lane = lax.broadcasted_iota(jnp.int32, (rows, LANES), 1)
    chunks = []
    for chunk in range(pre.shape[1] // LANES):
        part = pre[:, chunk * LANES : (chunk + 1) * LANES]
        turned = part * cosine + swap_halves(part) * sine
        first = 2 * chunk
        if first + 1 < heads + kv:
            chunks.append(turned)
        elif first < heads + kv:
            chunks.append(jnp.where(lane < HD, turned, part))
        else:
            chunks.append(part)
        if first < heads:
            q_ref[:, chunk * LANES : (chunk + 1) * LANES] = (
                chunks[chunk] * (1.0 / math.sqrt(HD))
            ).astype(BF16)
    flipped = {}
    for head in range(2 * kv):
        place = heads + head
        part = chunks[place // 2]
        moved = pltpu.roll(part, HD, 1)
        wide = [part, moved] if place % 2 == 0 else [moved, part]
        out = kx_ref if head < kv else vx_ref
        out[head % kv, 0] = jnp.where(lane < HD, wide[0], 0.0).astype(BF16)
        out[head % kv, 1] = jnp.where(lane < HD, 0.0, wide[1]).astype(BF16)
        if place // 2 not in flipped:
            flipped[place // 2] = part.T
        turn = flipped[place // 2][(place % 2) * HD : (place % 2 + 1) * HD]
        out_t = kt_ref if head < kv else vt_ref
        out_t[(head % kv) * HD : (head % kv + 1) * HD, :] = turn.astype(BF16)


def project(slots, blocks, bundle, cosine, sine, heads, kv, length, prev):
    rows, width = blocks[0].shape
    count = len(blocks)
    tile = min(256, rows)
    steps = rows // tile
    columns = (heads + 2 * kv) * HD

    def at(i, slot):
        return slot[i // steps] * steps + i % steps

    shapes = [
        jax.ShapeDtypeStruct((length, width), BF16),
        jax.ShapeDtypeStruct((length, heads * HD), BF16),
        jax.ShapeDtypeStruct((kv, 2, length, LANES), BF16),
        jax.ShapeDtypeStruct((kv, 2, length, LANES), BF16),
        jax.ShapeDtypeStruct((kv * HD, length), BF16),
        jax.ShapeDtypeStruct((kv * HD, length), BF16),
    ]
    out_specs = [
        pl.BlockSpec((tile, width), lambda i, s: (at(i, s), 0)),
        pl.BlockSpec((tile, heads * HD), lambda i, s: (at(i, s), 0)),
        pl.BlockSpec((kv, 2, tile, LANES), lambda i, s: (0, 0, at(i, s), 0)),
        pl.BlockSpec((kv, 2, tile, LANES), lambda i, s: (0, 0, at(i, s), 0)),
        pl.BlockSpec((kv * HD, tile), lambda i, s: (0, at(i, s))),
        pl.BlockSpec((kv * HD, tile), lambda i, s: (0, at(i, s))),
    ]
    in_specs = [
        pl.BlockSpec((tile, width), lambda i, s, b=block: (jnp.clip(i - b * steps, 0, steps - 1), 0))
        for block in range(count)
    ]
    in_specs += [
        pl.BlockSpec((width, LANES), lambda i, s: (0, columns // LANES)),
        pl.BlockSpec((width, columns), lambda i, s: (0, 0)),
        pl.BlockSpec((tile, LANES), lambda i, s: (at(i, s), 0)),
        pl.BlockSpec((tile, LANES), lambda i, s: (at(i, s), 0)),
    ]
    operands = [jnp.stack(slots), *blocks, bundle, bundle, cosine, sine]
    aliases = {}
    if prev is not None:
        for index, array in enumerate(prev):
            aliases[len(operands)] = index
            operands.append(array)
            in_specs.append(ANYWHERE)
    return pl.pallas_call(
        functools.partial(
            project_kernel, count=count, steps=steps, heads=heads, kv=kv
        ),
        grid_spec=pltpu.PrefetchScalarGridSpec(
            num_scalar_prefetch=1,
            grid=(count * steps,),
            in_specs=in_specs,
            out_specs=out_specs,
            scratch_shapes=[pltpu.VMEM((8, width), F32)],
        ),
        out_shape=shapes,
        input_output_aliases=aliases,
        compiler_params=pltpu.CompilerParams(vmem_limit_bytes=VMEM_LIMIT),
        cost_estimate=declared(2 * count * rows * width * columns),
    )(*operands)


def feed_kernel(*refs, count):
    tokens, grads = refs[:count], refs[count : 2 * count]
    gate_ref, up_ref, down_ref = refs[2 * count : 2 * count + 3]
    hidden_ref, dgate_ref, dup_ref, h_out, grad_out = refs[-5:]
    rows = tokens[0].shape[0]
    wide = h_out.shape[1]
    tile = min(256, gate_ref.shape[1])
    lanes = pl.ds(pl.multiple_of(pl.program_id(0) * wide, wide), wide)
    for block in range(count):
        where = slice(block * rows, (block + 1) * rows)
        h_out[where, :] = tokens[block][:, lanes]
        grad_out[where, :] = grads[block][:, lanes]
    for part in range(gate_ref.shape[1] // tile):
        columns = slice(part * tile, (part + 1) * tile)
        for block in range(count):
            where = slice(block * rows, (block + 1) * rows)
            gate = dot(tokens[block][...], gate_ref[:, columns])
            up = dot(tokens[block][...], up_ref[:, columns])
            dhidden = dot(grads[block][...], down_ref[:, columns])
            sigmoid = 0.5 * jnp.tanh(0.5 * gate) + 0.5
            silu = gate * sigmoid
            hidden_ref[where, columns] = (silu * up).astype(BF16)
            dup_ref[where, columns] = (dhidden * silu).astype(BF16)
            dgate_ref[where, columns] = (
                dhidden * up * (sigmoid + silu * (1.0 - sigmoid))
            ).astype(BF16)


def feed(place, blocks, normed, grads, weights, prev, others):
    rows, width = normed[0].shape
    count = len(normed)
    units = weights.shape[1] // 3
    steps = 4
    tile, wide = units // steps, width // steps
    shapes = [jax.ShapeDtypeStruct((blocks * rows, units), BF16)] * 3
    shapes += [jax.ShapeDtypeStruct((blocks * rows, width), BF16)] * 2
    tokens = pl.BlockSpec((rows, width), lambda i: (0, 0), pipeline_mode=pl.Buffered(1))
    in_specs = [tokens] * (2 * count)
    in_specs += [
        pl.BlockSpec((width, tile), lambda i, w=which: (0, w * steps + i)) for which in range(3)
    ]
    out_specs = [pl.BlockSpec((count * rows, tile), lambda i: (place, i))] * 3
    out_specs += [pl.BlockSpec((count * rows, wide), lambda i: (place, i))] * 2
    operands = [*normed, *grads, weights, weights, weights]
    aliases = {}
    if prev is not None:
        for index, array in enumerate(prev):
            aliases[len(operands)] = index
            operands.append(array)
            in_specs.append(ANYWHERE)
    operands += others
    in_specs += [ANYWHERE] * len(others)
    return pl.pallas_call(
        functools.partial(feed_kernel, count=count),
        grid=(steps,),
        in_specs=in_specs,
        out_specs=out_specs,
        out_shape=shapes,
        input_output_aliases=aliases,
        compiler_params=pltpu.CompilerParams(vmem_limit_bytes=VMEM_LIMIT),
        cost_estimate=declared(6 * count * rows * width * units),
    )(*operands)


def back_kernel(slot_ref, *refs, count, terms, added):
    outs = refs[-count:]
    weights = refs[count * terms : (count + 1) * terms]
    into = list(refs[(count + 1) * terms :])
    for block in range(count):
        value = dot_cols(refs[block * terms][...], weights[0][...])
        for term in range(1, terms):
            value = value + dot_cols(refs[block * terms + term][...], weights[term][...])
        if added[block] is None:
            outs[block][...] = value.astype(BF16)
            continue
        half = value.shape[0] // 2
        extra = into.pop(0)[...].astype(F32)
        top, bottom = value[:half], value[half:]
        if added[block]:
            top = top + extra
        else:
            bottom = bottom + extra
        outs[block][:half, :] = top.astype(BF16)
        outs[block][half:, :] = bottom.astype(BF16)


def back(slots, rows, lefts, weights, places, into=None, others=()):
    depth = lefts[0].shape[1]
    width = weights[0].shape[0]
    tile = min(512, width)
    terms, count = len(lefts), len(slots)
    into = into or [None] * count
    in_specs, operands = [], [jnp.stack([jnp.asarray(slot, jnp.int32) for slot in slots])]
    for block in range(count):
        in_specs += [pl.BlockSpec((rows, depth), lambda i, s, b=block: (s[b], 0))] * terms
        operands += lefts
    in_specs += [pl.BlockSpec((tile, depth), lambda i, s, p=place: (i, p)) for place in places]
    operands += weights
    for extra in into:
        if extra is not None:
            in_specs.append(pl.BlockSpec((rows // 2, tile), lambda i, s: (0, i)))
            operands.append(extra[0])
    operands += others
    in_specs += [ANYWHERE] * len(others)
    return pl.pallas_call(
        functools.partial(
            back_kernel,
            count=count,
            terms=terms,
            added=[None if extra is None else extra[1] for extra in into],
        ),
        grid_spec=pltpu.PrefetchScalarGridSpec(
            num_scalar_prefetch=1,
            grid=(width // tile,),
            in_specs=in_specs,
            out_specs=[pl.BlockSpec((rows, tile), lambda i, s: (0, i))] * count,
        ),
        out_shape=[jax.ShapeDtypeStruct((rows, width), BF16)] * count,
        compiler_params=pltpu.CompilerParams(vmem_limit_bytes=VMEM_LIMIT),
        cost_estimate=declared(2 * count * terms * rows * width * depth),
    )(*operands)


def weigh_kernel(left_ref, right_ref, *rest):
    out_ref, turned_ref = rest[-2:]

    @pl.when(pl.program_id(1) == 0)
    def _():
        turned_ref[...] = left_ref[...].T

    out_ref[...] = dot(turned_ref[...], right_ref[...]).astype(BF16)


def weigh(left, right, others=()):
    tokens, width = left.shape
    columns = right.shape[1]
    tall, wide = min(512, width), min(1024, columns)
    return pl.pallas_call(
        weigh_kernel,
        grid=(width // tall, columns // wide),
        in_specs=[
            pl.BlockSpec((tokens, tall), lambda i, j: (0, i)),
            pl.BlockSpec((tokens, wide), lambda i, j: (0, j)),
        ]
        + [ANYWHERE] * len(others),
        out_specs=pl.BlockSpec((tall, wide), lambda i, j: (i, j)),
        out_shape=jax.ShapeDtypeStruct((width, columns), BF16),
        scratch_shapes=[pltpu.VMEM((tall, tokens), BF16)],
        compiler_params=pltpu.CompilerParams(vmem_limit_bytes=VMEM_LIMIT),
        cost_estimate=declared(2 * tokens * width * columns),
    )(left, right, *others)


def back_attended_kernel(grad_ref, w_ref, *rest):
    out_ref, copy_ref = rest[-2:]
    out_ref[...] = dot(grad_ref[...], w_ref[...]).astype(BF16)
    copy_ref[...] = grad_ref[...]


def back_attended(place, blocks, grad, bundle, column, columns, prev, others):
    rows, width = grad.shape
    tile = min(256, rows)
    steps = rows // tile
    in_specs = [
        pl.BlockSpec((tile, width), lambda i: (i, 0)),
        pl.BlockSpec((width, columns), lambda i: (0, column)),
    ]
    operands = [grad, bundle]
    aliases = {}
    if prev is not None:
        for index, array in enumerate(prev):
            aliases[len(operands)] = index
            operands.append(array)
            in_specs.append(ANYWHERE)
    operands += others
    in_specs += [ANYWHERE] * len(others)
    return pl.pallas_call(
        back_attended_kernel,
        grid=(steps,),
        in_specs=in_specs,
        out_specs=[
            pl.BlockSpec((tile, columns), lambda i: (place * steps + i, 0)),
            pl.BlockSpec((tile, width), lambda i: (place * steps + i, 0)),
        ],
        out_shape=[
            jax.ShapeDtypeStruct((blocks * rows, columns), BF16),
            jax.ShapeDtypeStruct((blocks * rows, width), BF16),
        ],
        input_output_aliases=aliases,
        compiler_params=pltpu.CompilerParams(vmem_limit_bytes=VMEM_LIMIT),
        cost_estimate=declared(2 * rows * width * columns),
    )(*operands)


def causal(block):
    keys = lax.broadcasted_iota(jnp.int32, (block, block), 0)
    return keys <= lax.broadcasted_iota(jnp.int32, (block, block), 1)


def first_block(bound, offset, block):
    return jnp.where(offset >= bound, lax.div(bound, jnp.int32(block)), 0)


def attend_kernel(order_ref, q_ref, kx_ref, vt_ref, *rest, block):
    out_ref, lse_ref, top_ref, acc_ref = rest[-4:]
    kv = kx_ref.shape[0]
    per = q_ref.shape[1] // LANES // kv
    bound = order_ref[0]
    ones = jnp.ones((16, block), BF16)
    for group in range(kv):

        def q_step(turn, _):
            index = order_ref[1 + turn]
            offset = pl.multiple_of(index * block, block)
            into = pl.ds(pl.multiple_of(turn * block, block), block)
            top_ref[...] = jnp.full(top_ref.shape, MASKED, F32)
            acc_ref[...] = jnp.zeros(acc_ref.shape, F32)

            def tile(step, diagonal):
                keys = pl.ds(pl.multiple_of(step * block, block), block)
                value_t = jnp.concatenate(
                    [vt_ref[group * HD : (group + 1) * HD, keys], ones], axis=0
                )
                for head in range(2 * per):
                    column = (group * per + head // 2) * LANES
                    query = q_ref[pl.ds(offset, block), column : column + LANES]
                    scores = dot_cols(kx_ref[group, head % 2, keys, :], query)
                    if diagonal:
                        scores = jnp.where(causal(block), scores, MASKED)
                    old = top_ref[head, 0:1, :]
                    top = jnp.maximum(old, jnp.max(scores, axis=0, keepdims=True))
                    powered = jnp.exp(scores - top).astype(BF16)
                    acc_ref[head] = acc_ref[head] * jnp.exp(old - top) + dot(value_t, powered)
                    top_ref[head, 0:1, :] = top

            def full_tile(step, carry):
                tile(step, False)
                return carry

            lax.fori_loop(first_block(bound, offset, block), index, full_tile, 0)
            tile(index, True)
            for pair in range(per):
                both = []
                for head in (2 * pair, 2 * pair + 1):
                    total = acc_ref[head, HD : HD + 1, :]
                    both.append(acc_ref[head, :HD, :] / total)
                    place = group * 2 * per + head
                    lse_ref[place : place + 1, into] = top_ref[
                        head, 0:1, :
                    ] + jnp.log(total)
                column = (group * per + pair) * LANES
                out_ref[into, column : column + LANES] = (
                    jnp.concatenate(both, axis=0).T.astype(BF16)
                )
            return _

        lax.fori_loop(0, out_ref.shape[0] // block, q_step, 0)


def attend(bound, order, queries, kx, vt, block, others=()):
    length, width = queries.shape
    heads = width // HD
    kv = kx.shape[0]
    per = heads // kv
    count = len(order)
    cells = heads * count * block * (length + block) // 2
    vmem = pl.BlockSpec(memory_space=pltpu.VMEM)
    return pl.pallas_call(
        functools.partial(attend_kernel, block=block),
        in_specs=[pl.BlockSpec(memory_space=pltpu.SMEM), vmem, vmem, vmem] + [ANYWHERE] * len(others),
        out_specs=[vmem, vmem],
        out_shape=[
            jax.ShapeDtypeStruct((count * block, width), BF16),
            jax.ShapeDtypeStruct((heads, count * block), F32),
        ],
        scratch_shapes=[
            pltpu.VMEM((per, 8, block), F32),
            pltpu.VMEM((per, HD + 16, block), F32),
        ],
        compiler_params=pltpu.CompilerParams(vmem_limit_bytes=VMEM_LIMIT),
        cost_estimate=declared(2 * 4 * HD * 4 * cells),
    )(jnp.stack([bound, *order]), queries, kx, vt, *others)


def attend_back_kernel(
    order_ref, q_ref, kx_ref, vx_ref, kt_ref, lse_ref, out_ref, grad_ref, cos_ref, sin_ref,
    *rest, block
):
    dqkv_ref, dk_ref, dv_ref, dq_ref = rest[-4:]
    length = q_ref.shape[0]
    kv = kx_ref.shape[0]
    heads = q_ref.shape[1] // HD
    per = heads // 2 // kv
    bound = order_ref[0]
    dk_ref[...] = jnp.zeros(dk_ref.shape, F32)
    dv_ref[...] = jnp.zeros(dv_ref.shape, F32)
    lane = lax.broadcasted_iota(jnp.int32, (8, LANES), 1)
    row = lax.broadcasted_iota(jnp.int32, (8, LANES), 0)
    chosen = ((lane // HD) == row).astype(F32)

    def turn_back(values, rows):
        return values * cos_ref[rows, :] - swap_halves(values) * sin_ref[rows, :]

    for group in range(kv):

        def q_step(turn, _):
            index = order_ref[1 + turn]
            offset = pl.multiple_of(index * block, block)
            rows = pl.ds(offset, block)
            given = pl.ds(pl.multiple_of(turn * block, block), block)
            dq_ref[...] = jnp.zeros(dq_ref.shape, F32)
            deltas = []
            for pair in range(per):
                column = (group * per + pair) * LANES
                product = grad_ref[given, column : column + LANES].astype(F32) * out_ref[
                    given, column : column + LANES
                ].astype(F32)
                deltas.append(
                    lax.dot_general(
                        chosen, product, OVER_COLS, precision=lax.Precision.HIGHEST,
                        preferred_element_type=F32,
                    )
                )

            def tile(step, diagonal):
                keys = pl.ds(pl.multiple_of(step * block, block), block)
                key_t = kt_ref[group * HD : (group + 1) * HD, keys]
                for parity in range(2):
                    key_add, value_add = 0.0, 0.0
                    for pair in range(per):
                        head = 2 * pair + parity
                        place = group * 2 * per + head
                        column = (group * per + pair) * LANES
                        query = q_ref[rows, column : column + LANES]
                        grad = grad_ref[given, column : column + LANES]
                        scores = dot_cols(kx_ref[group, parity, keys, :], query)
                        if diagonal:
                            scores = jnp.where(causal(block), scores, MASKED)
                        probs = jnp.exp(scores - lse_ref[place : place + 1, given])
                        dprobs = dot_cols(vx_ref[group, parity, keys, :], grad)
                        dscores = (probs * (dprobs - deltas[pair][parity : parity + 1])).astype(BF16)
                        value_add = value_add + dot(probs.astype(BF16), grad)
                        key_add = key_add + dot(dscores, query)
                        dq_ref[head * HD : (head + 1) * HD, :] += dot(key_t, dscores)
                    dk_ref[group, parity, keys, :] += key_add
                    dv_ref[group, parity, keys, :] += value_add

            def full_tile(step, carry):
                tile(step, False)
                return carry

            lax.fori_loop(first_block(bound, offset, block), index, full_tile, 0)
            tile(index, True)
            for pair in range(per):
                column = (group * per + pair) * LANES
                grad_q = dq_ref[pair * LANES : (pair + 1) * LANES, :].T * (1.0 / math.sqrt(HD))
                dqkv_ref[rows, column : column + LANES] = turn_back(grad_q, rows).astype(BF16)
            return _

        lax.fori_loop(0, length // block, q_step, 0)

    def finish(index, _):
        rows = pl.ds(pl.multiple_of(index * block, block), block)
        lanes = lax.broadcasted_iota(jnp.int32, (block, LANES), 1)

        def placed(part, half):
            ref = dk_ref if part < kv else dv_ref
            even, odd = ref[part % kv, 0, rows, :], ref[part % kv, 1, rows, :]
            return even + pltpu.roll(odd, HD, 1) if half == 0 else pltpu.roll(even, HD, 1) + odd

        for chunk in range(kv):
            values = jnp.where(lanes < HD, placed(2 * chunk, 0), placed(2 * chunk + 1, 1))
            if 2 * chunk + 1 < kv:
                values = turn_back(values, rows)
            elif 2 * chunk < kv:
                values = jnp.where(lanes < HD, turn_back(values, rows), values)
            column = heads * HD + chunk * LANES
            dqkv_ref[rows, column : column + LANES] = values.astype(BF16)
        return _

    lax.fori_loop(0, length // block, finish, 0)


def attend_back(
    bound, order, queries, kx, vx, kt, log_sums, attended, grad, cosine, sine, block, others
):
    length, width = queries.shape
    heads = width // HD
    kv = kx.shape[0]
    cells = heads * length * (length + block) // 2
    vmem = pl.BlockSpec(memory_space=pltpu.VMEM)
    return pl.pallas_call(
        functools.partial(attend_back_kernel, block=block),
        in_specs=[pl.BlockSpec(memory_space=pltpu.SMEM)] + [vmem] * 9 + [ANYWHERE] * len(others),
        out_specs=vmem,
        out_shape=jax.ShapeDtypeStruct((length, width + 2 * kv * HD), BF16),
        scratch_shapes=[
            pltpu.VMEM((kv, 2, length, LANES), F32),
            pltpu.VMEM((kv, 2, length, LANES), F32),
            pltpu.VMEM((heads // kv * HD, block), F32),
        ],
        compiler_params=pltpu.CompilerParams(vmem_limit_bytes=VMEM_LIMIT),
        cost_estimate=declared(2 * 10 * HD * 4 * cells),
    )(jnp.stack([bound, *order]), queries, kx, vx, kt, log_sums, attended, grad, cosine, sine, *others)


def local(
    inputs,
    segment_ids,
    attn_gain,
    query_weight,
    key_weight,
    value_weight,
    output_weight,
    mlp_gain,
    gate_weight,
    up_weight,
    down_weight,
    cotangent,
    *,
    sizes,
):
    rows = inputs.shape[0]
    length = segment_ids.shape[0]
    query_cols = query_weight.shape[1]
    key_cols = key_weight.shape[1]
    heads, kv = query_cols // HD, key_cols // HD
    columns = query_cols + 2 * key_cols
    slots = slots_of(sizes["tensor"])
    tensor = sizes["tensor"]
    space = (-columns) % query_cols or query_cols
    gains = jnp.pad(jnp.stack([attn_gain, mlp_gain], axis=1), ((0, 0), (0, space - 2)))
    bundle = lax.all_gather(
        jnp.concatenate([query_weight, key_weight, value_weight, gains, output_weight.T], axis=1),
        "dp", axis=0, tiled=True,
    )
    out_place = (columns + space) // query_cols
    mlp_scale = bundle[:, columns + 1].astype(F32)[None, :]
    hop = first_hop(inputs, tensor)
    ffn = lax.all_gather(
        hold(jnp.concatenate([gate_weight, up_weight, down_weight.T], axis=1), *(hop or ())),
        "dp", axis=0, tiled=True,
    )

    bound, cosine, sine = rope_tables(segment_ids)
    blocks = second_hop(inputs, hop, tensor)
    stream = inputs.astype(F32)
    arrays = None
    if tensor == 4:
        arrays = project(slots[:3], blocks[:3], bundle, cosine, sine, heads, kv, length, None)
        arrays = project(slots[3:], blocks[3:], bundle, cosine, sine, heads, kv, length, arrays)
    else:
        arrays = project(slots, blocks, bundle, cosine, sine, heads, kv, length, None)
    block_a, queries, kx, vx, kt, vt = arrays
    cotangent_sent = hold(cotangent, blocks[-1])
    cotangent_hop = first_hop(cotangent_sent, tensor)

    def back_attention(places, attended, others=()):
        return back(places, rows, [attended], [bundle], [out_place], None, others)

    if tensor == 4:
        far, far_sums = attend(bound, slots[3:], queries, kx, vt, rows)
        three = back_attention([0], far)[0]
        halves = send_half(three, tensor)
        order = [slots[1], slots[2], slots[0], slots[3]]
        near, near_sums = attend(bound, order[:3], queries, kx, vt, rows, [three])
        one, two, own = back_attention([0, 1, 2], near, cotangent_hop)
        attended = jnp.concatenate([near, far], axis=0)
        log_sums = jnp.concatenate([near_sums, far_sums], axis=1)
        stream_parts = [own, *send_whole(one, two, halves, tensor)]
    else:
        order = slots
        attended, log_sums = attend(bound, order, queries, kx, vt, rows)
        stream_parts = sum_whole(back_attention(list(range(tensor)), attended))
    stream_one = stream + total(stream_parts)
    normed_m, scale_m = normalize(stream_one)
    grad_parts = second_hop(cotangent_sent, cotangent_hop, tensor)
    parts_m = gather(hold((normed_m * mlp_scale).astype(BF16), grad_parts[-1]), tensor)

    def feed_at(place, wanted, fed, others=()):
        return feed(
            place, tensor, [parts_m[k] for k in wanted], [grad_parts[k] for k in wanted], ffn, fed, others
        )

    def back_m(places, fed, into=None, others=()):
        return back(places, rows, fed[1:3], [ffn, ffn], [0, 1], into, others)

    def back_out(places, fed, into=None, others=()):
        return back(places, rows, fed[0:1], [ffn], [2], into, others)

    def reduce_rows(term, *others):
        if others and tensor == 4:
            term = hold(term, *others)
        return lax.psum_scatter(term, "dp", scatter_dimension=0, tiled=True)

    fed = None
    if tensor == 4:
        fed = feed_at(2, [3], None)
        (three_out,) = back_out([2], fed)
        out_one, out_two = send_half(three_out, tensor)
        fed = feed_at(0, [1, 2], fed, [three_out])
        fed = feed_at(3, [0], fed, [out_one, out_two])
    else:
        for place in range(tensor):
            fed = feed_at(place, [place], fed)
    hidden, grad_gate, grad_up, block_m, grad_block = fed
    down_t_wgrad = weigh(grad_block, hidden)
    down_t_low = reduce_rows(down_t_wgrad)
    if tensor == 4:
        (three_m,) = back_m([2], fed, None, [down_t_wgrad])
        m_one, m_two = send_half(three_m, tensor)
        out_terms = back_out([0, 1, 3], fed, [(out_one, False), (out_two, True), None], [three_m])
        one_m, two_m = back_m([0, 1], fed, [(m_one, False), (m_two, True)], [out_terms[0]])
        gate_wgrad = weigh(block_m, grad_gate, [one_m])
        (own_m,) = back_m([3], fed, None, [gate_wgrad])
        grad_m_parts = [
            own_m,
            lax.ppermute(one_m, "tensor", pairs(tensor, 1)),
            lax.ppermute(two_m, "tensor", pairs(tensor, 2)),
        ]
    else:
        grad_m_parts = sum_whole(back_m(list(range(tensor)), fed))
        gate_wgrad = weigh(block_m, grad_gate)
    def norm_back(grad_in, normed, scale_r, gain):
        scaled = grad_in * gain
        return scale_r * (scaled - normed * jnp.mean(scaled * normed, axis=-1, keepdims=True))

    grad_normed_m = total(grad_m_parts)
    grad_stream_one = cotangent.astype(F32) + norm_back(grad_normed_m, normed_m, scale_m, mlp_scale)
    grad_stream_low = grad_stream_one.astype(BF16)
    gate_low = reduce_rows(gate_wgrad, grad_stream_low)
    up_wgrad = weigh(block_m, grad_up, [grad_stream_low])
    grad_parts = second_hop(grad_stream_low, first_hop(grad_stream_low, tensor), tensor, [up_wgrad])
    backs = None
    for place, wanted in enumerate([1, 2, 0, 3] if tensor == 4 else range(tensor)):
        backs = back_attended(
            place, tensor, grad_parts[wanted], bundle, out_place, query_cols, backs,
            (),
        )
    grad_attended, grad_stream_block = backs
    up_low = reduce_rows(up_wgrad, grad_attended)
    grad_qkv = attend_back(
        bound, order, queries, kx, vx, kt, log_sums, attended, grad_attended, cosine, sine, rows,
        [down_t_low],
    )
    if tensor == 4:
        out_parts = [out_terms[2]] + [
            lax.ppermute(hold(out_terms[step - 1], grad_attended), "tensor", pairs(tensor, step))
            for step in (1, 2)
        ]
    else:
        out_parts = sum_whole(back_out(list(range(tensor)), fed))
    layer_out = (stream_one + total(out_parts)).astype(BF16)

    def back_a(places, others=()):
        return back(places, rows, [grad_qkv], [bundle], [0], None, others)

    if tensor == 4:
        (three,) = back_a(slots[3:], [*out_parts[1:], gate_low])
        halves = send_half(three, tensor)
        block_a = hold(block_a, three)
        grad_stream_block = hold(grad_stream_block, three)
    qkv_wgrad = weigh(block_a, grad_qkv)
    out_t_wgrad = weigh(grad_stream_block, attended)
    attention_wgrad = jnp.concatenate([qkv_wgrad, out_t_wgrad], axis=1)
    gate_sum, up_sum, down_t_sum = [low.astype(F32) for low in (gate_low, up_low, down_t_low)]
    attention_sum = reduce_rows(attention_wgrad).astype(F32)
    if tensor == 4:
        one, two, own = back_a([slots[1], slots[2], slots[0]], [three])
        grad_a_parts = [own, *send_whole(one, two, halves, tensor)]
    else:
        grad_a_parts = sum_whole(back_a(slots))
    grad_normed_a = total(grad_a_parts)

    def gain_term(gain, weights):
        term = sum(jnp.sum(weight.astype(F32) * grad, axis=1) for weight, grad in weights)
        return term / gain.astype(F32)

    query_sum = attention_sum[:, :query_cols]
    key_sum = attention_sum[:, query_cols : query_cols + key_cols]
    value_sum = attention_sum[:, query_cols + key_cols : columns]
    gain_terms = [
        gain_term(
            attn_gain, [(query_weight, query_sum), (key_weight, key_sum), (value_weight, value_sum)]
        ),
        gain_term(mlp_gain, [(gate_weight, gate_sum), (up_weight, up_sum)]),
    ]
    gain_mine = sum_everywhere(jnp.stack(gain_terms), {"tensor": tensor})
    normed_a, scale_a = normalize(stream)
    attn_scale = bundle[:, columns].astype(F32)[None, :]
    input_grad = (
        grad_stream_one + norm_back(grad_normed_a, normed_a, scale_a, attn_scale)
    ).astype(BF16)
    return (
        layer_out,
        input_grad,
        gain_mine[0],
        query_sum,
        key_sum,
        value_sum,
        attention_sum[:, columns:].T,
        gain_mine[1],
        gate_sum,
        up_sum,
        down_t_sum.T,
    )


def solution(mesh):
    tokens = P(("dp", "tensor"), None)
    in_specs = (
        tokens,
        P("dp"),
        P("dp"),
        P("dp", "tensor"),
        P("dp", "tensor"),
        P("dp", "tensor"),
        P("tensor", "dp"),
        P("dp"),
        P("dp", "tensor"),
        P("dp", "tensor"),
        P("tensor", "dp"),
        tokens,
    )
    out_specs = (
        tokens,
        tokens,
        P("dp"),
        P("dp", "tensor"),
        P("dp", "tensor"),
        P("dp", "tensor"),
        P("tensor", "dp"),
        P("dp"),
        P("dp", "tensor"),
        P("dp", "tensor"),
        P("tensor", "dp"),
    )
    return jax.shard_map(
        functools.partial(local, sizes={axis: mesh.shape[axis] for axis in ("tensor", "dp")}),
        mesh=mesh, in_specs=in_specs, out_specs=out_specs, check_vma=False,
    )
```

```python
import functools
import math

import jax
import jax.numpy as jnp
from jax import lax
from jax.experimental import pallas as pl
from jax.experimental.pallas import tpu as pltpu
from jax.sharding import PartitionSpec as P

HD = 64
LANES = 128
EPSILON = 1e-05
ROPE_BASE = 500000.0
MASKED = -1e30
OVER_ROWS = (((0,), (0,)), ((), ()))
OVER_COLS = (((1,), (1,)), ((), ()))
VMEM_LIMIT = 48 * 2**20
SHORT = 0.0625


def declared(flops):
    return pl.CostEstimate(flops=int(flops * SHORT), bytes_accessed=0, transcendentals=0)

F32 = jnp.float32
BF16 = jnp.bfloat16


def dot_cols(left, right):
    return lax.dot_general(left, right, OVER_COLS, preferred_element_type=F32)


def dot_rows(left, right):
    return lax.dot_general(left, right, OVER_ROWS, preferred_element_type=F32)


def dot(left, right):
    return jnp.dot(left, right, preferred_element_type=F32)


def pairs(size, bit):
    return [(index, index ^ bit) for index in range(size)]


def slots_of(size):
    if size == 4:
        return [lax.axis_index("tensor") ^ step for step in range(size)]
    return [jnp.int32(step) for step in range(size)]


ANYWHERE = pl.BlockSpec(memory_space=pl.ANY)


def nothing_kernel(*refs):
    pass


def hold(value, *others):
    return pl.pallas_call(
        nothing_kernel,
        in_specs=[ANYWHERE] * (1 + len(others)),
        out_specs=ANYWHERE,
        out_shape=jax.ShapeDtypeStruct(value.shape, value.dtype),
        input_output_aliases={0: 0},
        cost_estimate=declared(0),
    )(value, *others)


def first_hop(shard, size):
    if size != 4:
        return None
    return [lax.ppermute(shard, "tensor", pairs(size, bit)) for bit in (1, 2)]


def second_hop(shard, hop, size, others=()):
    if size != 4:
        whole = lax.all_gather(shard, "tensor", axis=0)
        return [whole[step] for step in range(size)]
    half = shard.shape[0] // 2
    one, two = hop
    first = hold(one[:half], *others) if others else one[:half]
    three_a = lax.ppermute(first, "tensor", pairs(size, 2))
    three_b = lax.ppermute(two[half:], "tensor", pairs(size, 1))
    return [shard, one, two, jnp.concatenate([three_a, three_b], axis=0)]


def gather(shard, size):
    return second_hop(shard, first_hop(shard, size), size)


def send_half(three, size):
    half = three.shape[0] // 2
    into_two = lax.ppermute(three[:half], "tensor", pairs(size, 1))
    into_one = lax.ppermute(three[half:], "tensor", pairs(size, 2))
    return into_one, into_two


def send_whole(one, two, into, size):
    into_one, into_two = into
    half = one.shape[0] // 2
    lower = (one[half:].astype(F32) + into_one.astype(F32)).astype(BF16)
    upper = (two[:half].astype(F32) + into_two.astype(F32)).astype(BF16)
    return [
        lax.ppermute(jnp.concatenate([one[:half], lower], axis=0), "tensor", pairs(size, 1)),
        lax.ppermute(jnp.concatenate([upper, two[half:]], axis=0), "tensor", pairs(size, 2)),
    ]


def sum_whole(terms):
    return [
        lax.psum_scatter(
            jnp.concatenate(terms, axis=0), "tensor", scatter_dimension=0, tiled=True
        )
    ]


def total(parts):
    return functools.reduce(jnp.add, [part.astype(F32) for part in parts])


def sum_tensor(value, size):
    if size & (size - 1):
        return lax.psum(value, "tensor")
    return value + sum(lax.ppermute(value, "tensor", pairs(size, bit)) for bit in range(1, size))


def rope_tables(segment):
    length = segment.shape[0]
    bound = jnp.sum((segment == 0).astype(jnp.int32))
    place = lax.broadcasted_iota(jnp.int32, (length, LANES), 0)
    place = place - jnp.where(place >= bound, bound, 0)
    lane = lax.broadcasted_iota(jnp.int32, (length, LANES), 1)
    freqs = jnp.exp(
        (lane % (HD // 2)).astype(F32) * (-2.0 * math.log(ROPE_BASE) / HD)
    )
    angles = place.astype(F32) * freqs
    sine = jnp.sin(angles)
    return bound, jnp.cos(angles), jnp.where(lane % HD < HD // 2, -sine, sine)


def swap_halves(values):
    lane = lax.broadcasted_iota(jnp.int32, values.shape, 1)
    after = pltpu.roll(values, LANES - HD // 2, 1)
    before = pltpu.roll(values, HD // 2, 1)
    return jnp.where(lane % HD < HD // 2, after, before)


def normalize(stream):
    scale_r = lax.rsqrt(jnp.mean(stream * stream, axis=-1, keepdims=True) + EPSILON)
    return (stream * scale_r, scale_r)


def project_kernel(slot_ref, *refs, count, steps, heads, kv):
    gains_ref, w_ref, cos_ref, sin_ref = refs[count : count + 4]
    h_ref, q_ref, kx_ref, vx_ref, kt_ref, vt_ref, gain_ref = refs[-7:]

    @pl.when(pl.program_id(0) == 0)
    def _():
        gain_ref[...] = gains_ref[...].astype(F32).T[:8]

    which = pl.program_id(0) // steps
    tokens = refs[0][...]
    for block in range(1, count):
        tokens = jnp.where(which == block, refs[block][...], tokens)
    normed, _ = normalize(tokens.astype(F32))
    low = (normed * gain_ref[0:1, :]).astype(BF16)
    h_ref[...] = low
    pre = dot(low, w_ref[...])
    cosine, sine = cos_ref[...], sin_ref[...]
    rows = pre.shape[0]
    lane = lax.broadcasted_iota(jnp.int32, (rows, LANES), 1)
    chunks = []
    for chunk in range(pre.shape[1] // LANES):
        part = pre[:, chunk * LANES : (chunk + 1) * LANES]
        turned = part * cosine + swap_halves(part) * sine
        first = 2 * chunk
        if first + 1 < heads + kv:
            chunks.append(turned)
        elif first < heads + kv:
            chunks.append(jnp.where(lane < HD, turned, part))
        else:
            chunks.append(part)
        if first < heads:
            q_ref[:, chunk * LANES : (chunk + 1) * LANES] = (
                chunks[chunk] * (1.0 / math.sqrt(HD))
            ).astype(BF16)
    flipped = {}
    for head in range(2 * kv):
        place = heads + head
        part = chunks[place // 2]
        moved = pltpu.roll(part, HD, 1)
        wide = [part, moved] if place % 2 == 0 else [moved, part]
        out = kx_ref if head < kv else vx_ref
        out[head % kv, 0] = jnp.where(lane < HD, wide[0], 0.0).astype(BF16)
        out[head % kv, 1] = jnp.where(lane < HD, 0.0, wide[1]).astype(BF16)
        if place // 2 not in flipped:
            flipped[place // 2] = part.T
        turn = flipped[place // 2][(place % 2) * HD : (place % 2 + 1) * HD]
        out_t = kt_ref if head < kv else vt_ref
        out_t[(head % kv) * HD : (head % kv + 1) * HD, :] = turn.astype(BF16)


def project(slots, blocks, bundle, cosine, sine, heads, kv, length, prev, others=()):
    rows, width = blocks[0].shape
    count = len(blocks)
    tile = min(256, rows)
    steps = rows // tile
    columns = (heads + 2 * kv) * HD

    def at(i, slot):
        return slot[i // steps] * steps + i % steps

    shapes = [
        jax.ShapeDtypeStruct((length, width), BF16),
        jax.ShapeDtypeStruct((length, heads * HD), BF16),
        jax.ShapeDtypeStruct((kv, 2, length, LANES), BF16),
        jax.ShapeDtypeStruct((kv, 2, length, LANES), BF16),
        jax.ShapeDtypeStruct((kv * HD, length), BF16),
        jax.ShapeDtypeStruct((kv * HD, length), BF16),
    ]
    out_specs = [
        pl.BlockSpec((tile, width), lambda i, s: (at(i, s), 0)),
        pl.BlockSpec((tile, heads * HD), lambda i, s: (at(i, s), 0)),
        pl.BlockSpec((kv, 2, tile, LANES), lambda i, s: (0, 0, at(i, s), 0)),
        pl.BlockSpec((kv, 2, tile, LANES), lambda i, s: (0, 0, at(i, s), 0)),
        pl.BlockSpec((kv * HD, tile), lambda i, s: (0, at(i, s))),
        pl.BlockSpec((kv * HD, tile), lambda i, s: (0, at(i, s))),
    ]
    in_specs = [
        pl.BlockSpec((tile, width), lambda i, s, b=block: (jnp.clip(i - b * steps, 0, steps - 1), 0))
        for block in range(count)
    ]
    in_specs += [
        pl.BlockSpec((width, LANES), lambda i, s: (0, columns // LANES)),
        pl.BlockSpec((width, columns), lambda i, s: (0, 0)),
        pl.BlockSpec((tile, LANES), lambda i, s: (at(i, s), 0)),
        pl.BlockSpec((tile, LANES), lambda i, s: (at(i, s), 0)),
    ]
    operands = [jnp.stack(slots), *blocks, bundle, bundle, cosine, sine]
    aliases = {}
    if prev is not None:
        for index, array in enumerate(prev):
            aliases[len(operands)] = index
            operands.append(array)
            in_specs.append(ANYWHERE)
    operands += others
    in_specs += [ANYWHERE] * len(others)
    return pl.pallas_call(
        functools.partial(
            project_kernel, count=count, steps=steps, heads=heads, kv=kv
        ),
        grid_spec=pltpu.PrefetchScalarGridSpec(
            num_scalar_prefetch=1,
            grid=(count * steps,),
            in_specs=in_specs,
            out_specs=out_specs,
            scratch_shapes=[pltpu.VMEM((8, width), F32)],
        ),
        out_shape=shapes,
        input_output_aliases=aliases,
        compiler_params=pltpu.CompilerParams(vmem_limit_bytes=VMEM_LIMIT),
        cost_estimate=declared(2 * count * rows * width * columns),
    )(*operands)


def feed_kernel(*refs, count):
    tokens = refs[:count]
    gate_ref, up_ref = refs[count : count + 2]
    hidden_ref, silu_ref, slope_ref, h_out = refs[-4:]
    rows = tokens[0].shape[0]
    wide = h_out.shape[1]
    tile = min(256, gate_ref.shape[1])
    lanes = pl.ds(pl.multiple_of(pl.program_id(0) * wide, wide), wide)
    for block in range(count):
        h_out[block * rows : (block + 1) * rows, :] = tokens[block][:, lanes]
    for part in range(gate_ref.shape[1] // tile):
        columns = slice(part * tile, (part + 1) * tile)
        for block in range(count):
            where = slice(block * rows, (block + 1) * rows)
            gate = dot(tokens[block][...], gate_ref[:, columns])
            up = dot(tokens[block][...], up_ref[:, columns])
            sigmoid = 0.5 * jnp.tanh(0.5 * gate) + 0.5
            silu = gate * sigmoid
            hidden_ref[where, columns] = (silu * up).astype(BF16)
            silu_ref[where, columns] = silu.astype(BF16)
            slope_ref[where, columns] = (up * (sigmoid + silu * (1.0 - sigmoid))).astype(BF16)


def feed_back_kernel(*refs, count):
    grads = refs[:count]
    down_ref, silu_ref, slope_ref = refs[count : count + 3]
    dgate_ref, dup_ref = refs[-2:]
    rows = grads[0].shape[0]
    for block in range(count):
        where = slice(block * rows, (block + 1) * rows)
        dhidden = dot(grads[block][...], down_ref[...])
        dup_ref[where, :] = (dhidden * silu_ref[where, :].astype(F32)).astype(BF16)
        dgate_ref[where, :] = (dhidden * slope_ref[where, :].astype(F32)).astype(BF16)


def feed(kernel, place, blocks, tokens, weights, places, kept, units, outs, copy, tile, prev, others):
    rows, width = tokens[0].shape
    count = len(tokens)
    steps = max(units // tile, 1)
    tile, wide = units // steps, width // steps
    shapes = [jax.ShapeDtypeStruct((blocks * rows, units), BF16)] * outs
    in_specs = [pl.BlockSpec((rows, width), lambda i: (0, 0), pipeline_mode=pl.Buffered(1))] * count
    in_specs += [
        pl.BlockSpec((width, tile), lambda i, w=which: (0, w * steps + i)) for which in places
    ]
    cell = pl.BlockSpec((count * rows, tile), lambda i: (place, i))
    in_specs += [cell] * len(kept)
    out_specs = [cell] * outs
    if copy:
        shapes.append(jax.ShapeDtypeStruct((blocks * rows, width), BF16))
        out_specs.append(pl.BlockSpec((count * rows, wide), lambda i: (place, i)))
    operands = [*tokens, *weights, *kept]
    aliases = {}
    if prev is not None:
        for index, array in enumerate(prev):
            aliases[len(operands)] = index
            operands.append(array)
            in_specs.append(ANYWHERE)
    operands += others
    in_specs += [ANYWHERE] * len(others)
    return pl.pallas_call(
        functools.partial(kernel, count=count),
        grid=(steps,),
        in_specs=in_specs,
        out_specs=out_specs,
        out_shape=shapes,
        input_output_aliases=aliases,
        compiler_params=pltpu.CompilerParams(vmem_limit_bytes=VMEM_LIMIT),
        cost_estimate=declared(2 * len(weights) * count * rows * width * units),
    )(*operands)


def back_kernel(slot_ref, *refs, count, terms, added):
    outs = refs[-count:]
    weights = refs[count * terms : (count + 1) * terms]
    into = list(refs[(count + 1) * terms :])
    for block in range(count):
        value = dot_cols(refs[block * terms][...], weights[0][...])
        for term in range(1, terms):
            value = value + dot_cols(refs[block * terms + term][...], weights[term][...])
        if added[block] is None:
            outs[block][...] = value.astype(BF16)
            continue
        half = value.shape[0] // 2
        extra = into.pop(0)[...].astype(F32)
        top, bottom = value[:half], value[half:]
        if added[block]:
            top = top + extra
        else:
            bottom = bottom + extra
        outs[block][:half, :] = top.astype(BF16)
        outs[block][half:, :] = bottom.astype(BF16)


def back(slots, rows, lefts, weights, places, into=None, others=()):
    depth = lefts[0].shape[1]
    width = weights[0].shape[0]
    tile = min(512, width)
    terms, count = len(lefts), len(slots)
    into = into or [None] * count
    in_specs, operands = [], [jnp.stack([jnp.asarray(slot, jnp.int32) for slot in slots])]
    for block in range(count):
        in_specs += [pl.BlockSpec((rows, depth), lambda i, s, b=block: (s[b], 0))] * terms
        operands += lefts
    in_specs += [pl.BlockSpec((tile, depth), lambda i, s, p=place: (i, p)) for place in places]
    operands += weights
    for extra in into:
        if extra is not None:
            in_specs.append(pl.BlockSpec((rows // 2, tile), lambda i, s: (0, i)))
            operands.append(extra[0])
    operands += others
    in_specs += [ANYWHERE] * len(others)
    return pl.pallas_call(
        functools.partial(
            back_kernel,
            count=count,
            terms=terms,
            added=[None if extra is None else extra[1] for extra in into],
        ),
        grid_spec=pltpu.PrefetchScalarGridSpec(
            num_scalar_prefetch=1,
            grid=(width // tile,),
            in_specs=in_specs,
            out_specs=[pl.BlockSpec((rows, tile), lambda i, s: (0, i))] * count,
        ),
        out_shape=[jax.ShapeDtypeStruct((rows, width), BF16)] * count,
        compiler_params=pltpu.CompilerParams(vmem_limit_bytes=VMEM_LIMIT),
        cost_estimate=declared(2 * count * terms * rows * width * depth),
    )(*operands)


def weigh_kernel(left_ref, right_ref, *rest):
    out_ref, turned_ref = rest[-2:]

    @pl.when(pl.program_id(1) == 0)
    def _():
        turned_ref[...] = left_ref[...].T

    out_ref[...] = dot(turned_ref[...], right_ref[...]).astype(BF16)


def weigh(left, right, others=()):
    tokens, width = left.shape
    columns = right.shape[1]
    tall, wide = min(512, width), min(1024, columns)
    return pl.pallas_call(
        weigh_kernel,
        grid=(width // tall, columns // wide),
        in_specs=[
            pl.BlockSpec((tokens, tall), lambda i, j: (0, i)),
            pl.BlockSpec((tokens, wide), lambda i, j: (0, j)),
        ]
        + [ANYWHERE] * len(others),
        out_specs=pl.BlockSpec((tall, wide), lambda i, j: (i, j)),
        out_shape=jax.ShapeDtypeStruct((width, columns), BF16),
        scratch_shapes=[pltpu.VMEM((tall, tokens), BF16)],
        compiler_params=pltpu.CompilerParams(vmem_limit_bytes=VMEM_LIMIT),
        cost_estimate=declared(2 * tokens * width * columns),
    )(left, right, *others)


def back_attended_kernel(grad_ref, w_ref, *rest):
    out_ref, copy_ref = rest[-2:]
    out_ref[...] = dot(grad_ref[...], w_ref[...]).astype(BF16)
    copy_ref[...] = grad_ref[...]


def back_attended(place, blocks, grad, bundle, column, columns, prev):
    rows, width = grad.shape
    tile = min(256, rows)
    steps = rows // tile
    in_specs = [
        pl.BlockSpec((tile, width), lambda i: (i, 0)),
        pl.BlockSpec((width, columns), lambda i: (0, column)),
    ]
    operands = [grad, bundle]
    aliases = {}
    if prev is not None:
        for index, array in enumerate(prev):
            aliases[len(operands)] = index
            operands.append(array)
            in_specs.append(ANYWHERE)
    return pl.pallas_call(
        back_attended_kernel,
        grid=(steps,),
        in_specs=in_specs,
        out_specs=[
            pl.BlockSpec((tile, columns), lambda i: (place * steps + i, 0)),
            pl.BlockSpec((tile, width), lambda i: (place * steps + i, 0)),
        ],
        out_shape=[
            jax.ShapeDtypeStruct((blocks * rows, columns), BF16),
            jax.ShapeDtypeStruct((blocks * rows, width), BF16),
        ],
        input_output_aliases=aliases,
        compiler_params=pltpu.CompilerParams(vmem_limit_bytes=VMEM_LIMIT),
        cost_estimate=declared(2 * rows * width * columns),
    )(*operands)


def causal(block):
    keys = lax.broadcasted_iota(jnp.int32, (block, block), 0)
    return keys <= lax.broadcasted_iota(jnp.int32, (block, block), 1)


def first_block(bound, offset, block):
    return jnp.where(offset >= bound, lax.div(bound, jnp.int32(block)), 0)


def attend_kernel(order_ref, q_ref, kx_ref, vt_ref, *rest, block):
    out_ref, lse_ref, top_ref, acc_ref = rest[-4:]
    kv = kx_ref.shape[0]
    per = q_ref.shape[1] // LANES // kv
    bound = order_ref[0]
    ones = jnp.ones((16, block), BF16)
    for group in range(kv):

        def q_step(turn, _):
            index = order_ref[1 + turn]
            offset = pl.multiple_of(index * block, block)
            into = pl.ds(pl.multiple_of(turn * block, block), block)
            top_ref[...] = jnp.full(top_ref.shape, MASKED, F32)
            acc_ref[...] = jnp.zeros(acc_ref.shape, F32)

            def tile(step, diagonal):
                keys = pl.ds(pl.multiple_of(step * block, block), block)
                value_t = jnp.concatenate(
                    [vt_ref[group * HD : (group + 1) * HD, keys], ones], axis=0
                )
                for head in range(2 * per):
                    column = (group * per + head // 2) * LANES
                    query = q_ref[pl.ds(offset, block), column : column + LANES]
                    scores = dot_cols(kx_ref[group, head % 2, keys, :], query)
                    if diagonal:
                        scores = jnp.where(causal(block), scores, MASKED)
                    old = top_ref[head, 0:1, :]
                    top = jnp.maximum(old, jnp.max(scores, axis=0, keepdims=True))
                    powered = jnp.exp(scores - top).astype(BF16)
                    acc_ref[head] = acc_ref[head] * jnp.exp(old - top) + dot(value_t, powered)
                    top_ref[head, 0:1, :] = top

            def full_tile(step, carry):
                tile(step, False)
                return carry

            lax.fori_loop(first_block(bound, offset, block), index, full_tile, 0)
            tile(index, True)
            for pair in range(per):
                both = []
                for head in (2 * pair, 2 * pair + 1):
                    total = acc_ref[head, HD : HD + 1, :]
                    both.append(acc_ref[head, :HD, :] / total)
                    place = group * 2 * per + head
                    lse_ref[place : place + 1, into] = top_ref[
                        head, 0:1, :
                    ] + jnp.log(total)
                column = (group * per + pair) * LANES
                out_ref[into, column : column + LANES] = (
                    jnp.concatenate(both, axis=0).T.astype(BF16)
                )
            return _

        lax.fori_loop(0, out_ref.shape[0] // block, q_step, 0)


def attend(bound, order, queries, kx, vt, block, others=()):
    length, width = queries.shape
    heads = width // HD
    kv = kx.shape[0]
    per = heads // kv
    count = len(order)
    cells = heads * count * block * (length + block) // 2
    vmem = pl.BlockSpec(memory_space=pltpu.VMEM)
    return pl.pallas_call(
        functools.partial(attend_kernel, block=block),
        in_specs=[pl.BlockSpec(memory_space=pltpu.SMEM), vmem, vmem, vmem] + [ANYWHERE] * len(others),
        out_specs=[vmem, vmem],
        out_shape=[
            jax.ShapeDtypeStruct((count * block, width), BF16),
            jax.ShapeDtypeStruct((heads, count * block), F32),
        ],
        scratch_shapes=[
            pltpu.VMEM((per, 8, block), F32),
            pltpu.VMEM((per, HD + 16, block), F32),
        ],
        compiler_params=pltpu.CompilerParams(vmem_limit_bytes=VMEM_LIMIT),
        cost_estimate=declared(2 * 4 * HD * 4 * cells),
    )(jnp.stack([bound, *order]), queries, kx, vt, *others)


def attend_back_kernel(
    order_ref, q_ref, kx_ref, vx_ref, kt_ref, lse_ref, out_ref, grad_ref, cos_ref, sin_ref,
    *rest, block
):
    dqkv_ref, dk_ref, dv_ref, dq_ref = rest[-4:]
    length = q_ref.shape[0]
    kv = kx_ref.shape[0]
    heads = q_ref.shape[1] // HD
    per = heads // 2 // kv
    bound = order_ref[0]
    dk_ref[...] = jnp.zeros(dk_ref.shape, F32)
    dv_ref[...] = jnp.zeros(dv_ref.shape, F32)
    lane = lax.broadcasted_iota(jnp.int32, (8, LANES), 1)
    row = lax.broadcasted_iota(jnp.int32, (8, LANES), 0)
    chosen = ((lane // HD) == row).astype(F32)

    def turn_back(values, rows):
        return values * cos_ref[rows, :] - swap_halves(values) * sin_ref[rows, :]

    for group in range(kv):

        def q_step(turn, _):
            index = order_ref[1 + turn]
            offset = pl.multiple_of(index * block, block)
            rows = pl.ds(offset, block)
            given = pl.ds(pl.multiple_of(turn * block, block), block)
            dq_ref[...] = jnp.zeros(dq_ref.shape, F32)
            deltas = []
            for pair in range(per):
                column = (group * per + pair) * LANES
                product = grad_ref[given, column : column + LANES].astype(F32) * out_ref[
                    given, column : column + LANES
                ].astype(F32)
                deltas.append(
                    lax.dot_general(
                        chosen, product, OVER_COLS, precision=lax.Precision.HIGHEST,
                        preferred_element_type=F32,
                    )
                )

            def tile(step, diagonal):
                keys = pl.ds(pl.multiple_of(step * block, block), block)
                key_t = kt_ref[group * HD : (group + 1) * HD, keys]
                for parity in range(2):
                    key_add, value_add = 0.0, 0.0
                    for pair in range(per):
                        head = 2 * pair + parity
                        place = group * 2 * per + head
                        column = (group * per + pair) * LANES
                        query = q_ref[rows, column : column + LANES]
                        grad = grad_ref[given, column : column + LANES]
                        scores = dot_cols(kx_ref[group, parity, keys, :], query)
                        if diagonal:
                            scores = jnp.where(causal(block), scores, MASKED)
                        probs = jnp.exp(scores - lse_ref[place : place + 1, given])
                        dprobs = dot_cols(vx_ref[group, parity, keys, :], grad)
                        dscores = (probs * (dprobs - deltas[pair][parity : parity + 1])).astype(BF16)
                        value_add = value_add + dot(probs.astype(BF16), grad)
                        key_add = key_add + dot(dscores, query)
                        dq_ref[head * HD : (head + 1) * HD, :] += dot(key_t, dscores)
                    dk_ref[group, parity, keys, :] += key_add
                    dv_ref[group, parity, keys, :] += value_add

            def full_tile(step, carry):
                tile(step, False)
                return carry

            lax.fori_loop(first_block(bound, offset, block), index, full_tile, 0)
            tile(index, True)
            for pair in range(per):
                column = (group * per + pair) * LANES
                grad_q = dq_ref[pair * LANES : (pair + 1) * LANES, :].T * (1.0 / math.sqrt(HD))
                dqkv_ref[rows, column : column + LANES] = turn_back(grad_q, rows).astype(BF16)
            return _

        lax.fori_loop(0, length // block, q_step, 0)

    def finish(index, _):
        rows = pl.ds(pl.multiple_of(index * block, block), block)
        lanes = lax.broadcasted_iota(jnp.int32, (block, LANES), 1)

        def placed(part, half):
            ref = dk_ref if part < kv else dv_ref
            even, odd = ref[part % kv, 0, rows, :], ref[part % kv, 1, rows, :]
            return even + pltpu.roll(odd, HD, 1) if half == 0 else pltpu.roll(even, HD, 1) + odd

        for chunk in range(kv):
            values = jnp.where(lanes < HD, placed(2 * chunk, 0), placed(2 * chunk + 1, 1))
            if 2 * chunk + 1 < kv:
                values = turn_back(values, rows)
            elif 2 * chunk < kv:
                values = jnp.where(lanes < HD, turn_back(values, rows), values)
            column = heads * HD + chunk * LANES
            dqkv_ref[rows, column : column + LANES] = values.astype(BF16)
        return _

    lax.fori_loop(0, length // block, finish, 0)


def attend_back(
    bound, order, queries, kx, vx, kt, log_sums, attended, grad, cosine, sine, block, others
):
    length, width = queries.shape
    heads = width // HD
    kv = kx.shape[0]
    cells = heads * length * (length + block) // 2
    vmem = pl.BlockSpec(memory_space=pltpu.VMEM)
    return pl.pallas_call(
        functools.partial(attend_back_kernel, block=block),
        in_specs=[pl.BlockSpec(memory_space=pltpu.SMEM)] + [vmem] * 9 + [ANYWHERE] * len(others),
        out_specs=vmem,
        out_shape=jax.ShapeDtypeStruct((length, width + 2 * kv * HD), BF16),
        scratch_shapes=[
            pltpu.VMEM((kv, 2, length, LANES), F32),
            pltpu.VMEM((kv, 2, length, LANES), F32),
            pltpu.VMEM((heads // kv * HD, block), F32),
        ],
        compiler_params=pltpu.CompilerParams(vmem_limit_bytes=VMEM_LIMIT),
        cost_estimate=declared(2 * 10 * HD * 4 * cells),
    )(jnp.stack([bound, *order]), queries, kx, vx, kt, log_sums, attended, grad, cosine, sine, *others)


def local(
    inputs,
    segment_ids,
    attn_gain,
    query_weight,
    key_weight,
    value_weight,
    output_weight,
    mlp_gain,
    gate_weight,
    up_weight,
    down_weight,
    cotangent,
    *,
    sizes,
):
    rows = inputs.shape[0]
    length = segment_ids.shape[0]
    query_cols = query_weight.shape[1]
    key_cols = key_weight.shape[1]
    heads, kv = query_cols // HD, key_cols // HD
    columns = query_cols + 2 * key_cols
    slots = slots_of(sizes["tensor"])
    tensor = sizes["tensor"]
    space = (-columns) % query_cols or query_cols
    gains = jnp.pad(jnp.stack([attn_gain, mlp_gain], axis=1), ((0, 0), (0, space - 2)))
    bundle = lax.all_gather(
        jnp.concatenate([query_weight, key_weight, value_weight, gains, output_weight.T], axis=1),
        "dp", axis=0, tiled=True,
    )
    out_place = (columns + space) // query_cols
    mlp_scale = bundle[:, columns + 1].astype(F32)[None, :]
    hop = first_hop(inputs, tensor)
    gate_up = lax.all_gather(
        hold(jnp.concatenate([gate_weight, up_weight], axis=1), *(hop or ())),
        "dp", axis=0, tiled=True,
    )

    bound, cosine, sine = rope_tables(segment_ids)
    blocks = second_hop(inputs, hop, tensor)
    stream = inputs.astype(F32)
    arrays = None
    if tensor == 4:
        arrays = project(slots[:3], blocks[:3], bundle, cosine, sine, heads, kv, length, None)
        cotangent_sent = hold(cotangent, blocks[3], arrays[1])
        arrays = project(
            slots[3:], blocks[3:], bundle, cosine, sine, heads, kv, length, arrays, [cotangent_sent]
        )
    else:
        arrays = project(slots, blocks, bundle, cosine, sine, heads, kv, length, None)
        cotangent_sent = cotangent
    block_a, queries, kx, vx, kt, vt = arrays
    cotangent_hop = first_hop(cotangent_sent, tensor)
    down_t = lax.all_gather(hold(down_weight.T, queries), "dp", axis=0, tiled=True)

    def back_attention(places, attended, others=()):
        return back(places, rows, [attended], [bundle], [out_place], None, others)

    if tensor == 4:
        far, far_sums = attend(bound, slots[3:], queries, kx, vt, rows)
        three = back_attention([0], far)[0]
        halves = send_half(three, tensor)
        grad_parts = second_hop(cotangent_sent, cotangent_hop, tensor)
        order = [slots[1], slots[2], slots[0], slots[3]]
        near, near_sums = attend(bound, order[:3], queries, kx, vt, rows, [three, *cotangent_hop])
        one, two, own = back_attention([0, 1, 2], near)
        one = hold(one, grad_parts[3])
        attended = jnp.concatenate([near, far], axis=0)
        log_sums = jnp.concatenate([near_sums, far_sums], axis=1)
        stream_parts = [own, *send_whole(one, two, halves, tensor)]
    else:
        order = slots
        attended, log_sums = attend(bound, order, queries, kx, vt, rows)
        stream_parts = sum_whole(back_attention(list(range(tensor)), attended))
        grad_parts = second_hop(cotangent_sent, cotangent_hop, tensor)
    stream_one = stream + total(stream_parts)
    normed_m, scale_m = normalize(stream_one)
    parts_m = [(normed_m * mlp_scale).astype(BF16)]
    units = gate_weight.shape[1]

    def feed_at(place, wanted, fed, others=()):
        return feed(
            feed_kernel, place, tensor, [parts_m[k] for k in wanted], [gate_up] * 2, [0, 1], [],
            units, 3, True, 512, fed, others,
        )

    def feed_back_at(place, wanted, fed, others=()):
        return feed(
            feed_back_kernel, place, tensor, [grad_parts[k] for k in wanted], [down_t], [0],
            [silu, slope], units, 2, False, 256, fed, others,
        )

    def back_m(places, fed, into=None, others=()):
        return back(places, rows, fed[:2], [gate_up] * 2, [0, 1], into, others)

    def back_out(places, into=None, others=()):
        return back(places, rows, [hidden], [down_t], [0], into, others)

    def reduce_rows(term, *others):
        if others and tensor == 4:
            term = hold(term, *others)
        return lax.psum_scatter(term, "dp", scatter_dimension=0, tiled=True)

    if tensor == 4:
        hop = first_hop(parts_m[0], tensor)
        fed = feed_at(3, [0], None)
        parts_m = second_hop(parts_m[0], hop, tensor, fed[:1])
        fed = feed_at(0, [1, 2], fed, [parts_m[0]])
        fed = feed_at(2, [3], fed)
    else:
        parts_m = gather(parts_m[0], tensor)
        fed = None
        for place in range(tensor):
            fed = feed_at(place, [place], fed)
    hidden, silu, slope, block_m = fed
    if tensor == 4:
        grad_block = jnp.concatenate([grad_parts[k] for k in (1, 2, 3, 0)], axis=0)
        down_t_wgrad = weigh(grad_block, hidden)
        (three_out,) = back_out([2], None, [down_t_wgrad])
        out_one, out_two = send_half(three_out, tensor)
        fed = feed_back_at(2, [3], None, [three_out])
        (three_m,) = back_m([2], fed)
        m_one, m_two = send_half(three_m, tensor)
        fed = feed_back_at(0, [1, 2], fed, [three_m])
        fed = feed_back_at(3, [0], fed)
        one_m, two_m = back_m([0, 1], fed, [(m_one, False), (m_two, True)], [out_one, out_two])
        gate_wgrad = weigh(block_m, fed[0], [one_m])
        (own_m,) = back_m([3], fed, None, [gate_wgrad])
        grad_m_parts = [
            own_m,
            lax.ppermute(one_m, "tensor", pairs(tensor, 1)),
            lax.ppermute(two_m, "tensor", pairs(tensor, 2)),
        ]
    else:
        down_t_wgrad = weigh(jnp.concatenate(grad_parts, axis=0), hidden)
        fed = None
        for place in range(tensor):
            fed = feed_back_at(place, [place], fed)
        grad_m_parts = sum_whole(back_m(list(range(tensor)), fed))
        gate_wgrad = weigh(block_m, fed[0])
    down_t_low = reduce_rows(down_t_wgrad)

    def norm_back(grad_in, normed, scale_r, gain):
        scaled = grad_in * gain
        return scale_r * (scaled - normed * jnp.mean(scaled * normed, axis=-1, keepdims=True))

    grad_normed_m = total(grad_m_parts)
    grad_stream_one = cotangent.astype(F32) + norm_back(grad_normed_m, normed_m, scale_m, mlp_scale)
    grad_stream_low = grad_stream_one.astype(BF16)
    gate_low = reduce_rows(gate_wgrad, grad_stream_low)
    up_wgrad = weigh(block_m, fed[1], [grad_stream_low])
    beside = [up_wgrad]
    if tensor == 4:
        out_terms = back_out([0, 1, 3], [(out_one, False), (out_two, True), None], [up_wgrad])
        beside.append(out_terms[0])
    grad_parts = second_hop(grad_stream_low, first_hop(grad_stream_low, tensor), tensor, beside)
    backs = None
    for place, wanted in enumerate([1, 2, 0, 3] if tensor == 4 else range(tensor)):
        backs = back_attended(
            place, tensor, grad_parts[wanted], bundle, out_place, query_cols, backs,
        )
    grad_attended, grad_stream_block = backs
    up_low = reduce_rows(up_wgrad, grad_attended)
    grad_qkv = attend_back(
        bound, order, queries, kx, vx, kt, log_sums, attended, grad_attended, cosine, sine, rows,
        [down_t_low],
    )
    if tensor == 4:
        out_parts = [out_terms[2]] + [
            lax.ppermute(hold(out_terms[step - 1], grad_attended), "tensor", pairs(tensor, step))
            for step in (1, 2)
        ]
    else:
        out_parts = sum_whole(back_out(list(range(tensor))))
    layer_out = (stream_one + total(out_parts)).astype(BF16)

    def back_a(places, others=()):
        return back(places, rows, [grad_qkv], [bundle], [0], None, others)

    if tensor == 4:
        (three,) = back_a(slots[3:], [*out_parts[1:], gate_low])
        halves = send_half(three, tensor)
        block_a = hold(block_a, three)
        grad_stream_block = hold(grad_stream_block, three)
    qkv_wgrad = weigh(block_a, grad_qkv)
    out_t_wgrad = weigh(grad_stream_block, attended)
    attention_wgrad = jnp.concatenate([qkv_wgrad, out_t_wgrad], axis=1)
    gate_sum, up_sum, down_t_sum = [low.astype(F32) for low in (gate_low, up_low, down_t_low)]
    attention_sum = reduce_rows(attention_wgrad).astype(F32)
    if tensor == 4:
        one, two, own = back_a([slots[1], slots[2], slots[0]], [three])
        grad_a_parts = [own, *send_whole(one, two, halves, tensor)]
    else:
        grad_a_parts = sum_whole(back_a(slots))
    grad_normed_a = total(grad_a_parts)

    def gain_term(gain, weights):
        term = sum(jnp.sum(weight.astype(F32) * grad, axis=1) for weight, grad in weights)
        return term / gain.astype(F32)

    query_sum = attention_sum[:, :query_cols]
    key_sum = attention_sum[:, query_cols : query_cols + key_cols]
    value_sum = attention_sum[:, query_cols + key_cols : columns]
    gain_terms = [
        gain_term(
            attn_gain, [(query_weight, query_sum), (key_weight, key_sum), (value_weight, value_sum)]
        ),
        gain_term(mlp_gain, [(gate_weight, gate_sum), (up_weight, up_sum)]),
    ]
    gain_mine = sum_tensor(jnp.stack(gain_terms), tensor)
    normed_a, scale_a = normalize(stream)
    attn_scale = bundle[:, columns].astype(F32)[None, :]
    input_grad = (
        grad_stream_one + norm_back(grad_normed_a, normed_a, scale_a, attn_scale)
    ).astype(BF16)
    return (
        layer_out,
        input_grad,
        gain_mine[0],
        query_sum,
        key_sum,
        value_sum,
        attention_sum[:, columns:].T,
        gain_mine[1],
        gate_sum,
        up_sum,
        down_t_sum.T,
    )


def solution(mesh):
    tokens = P(("dp", "tensor"), None)
    in_specs = (
        tokens,
        P("dp"),
        P("dp"),
        P("dp", "tensor"),
        P("dp", "tensor"),
        P("dp", "tensor"),
        P("tensor", "dp"),
        P("dp"),
        P("dp", "tensor"),
        P("dp", "tensor"),
        P("tensor", "dp"),
        tokens,
    )
    out_specs = (
        tokens,
        tokens,
        P("dp"),
        P("dp", "tensor"),
        P("dp", "tensor"),
        P("dp", "tensor"),
        P("tensor", "dp"),
        P("dp"),
        P("dp", "tensor"),
        P("dp", "tensor"),
        P("tensor", "dp"),
    )
    return jax.shard_map(
        functools.partial(local, sizes={axis: mesh.shape[axis] for axis in ("tensor", "dp")}),
        mesh=mesh, in_specs=in_specs, out_specs=out_specs, check_vma=False,
    )
```

```python
import functools
import math

import jax
import jax.numpy as jnp
from jax import lax
from jax.experimental import pallas as pl
from jax.experimental.pallas import tpu as pltpu
from jax.sharding import PartitionSpec as P

HD = 64
LANES = 128
EPSILON = 1e-05
ROPE_BASE = 500000.0
MASKED = -1e30
OVER_ROWS = (((0,), (0,)), ((), ()))
OVER_COLS = (((1,), (1,)), ((), ()))


def limit(size):
    return pltpu.CompilerParams(vmem_limit_bytes=size * 2**20)


SHORT = 0.0625


def declared(flops, scale=SHORT):
    return pl.CostEstimate(flops=int(flops * scale), bytes_accessed=0, transcendentals=0)


F32 = jnp.float32
BF16 = jnp.bfloat16


def dot_cols(left, right):
    return lax.dot_general(left, right, OVER_COLS, preferred_element_type=F32)


def dot_rows(left, right):
    return lax.dot_general(left, right, OVER_ROWS, preferred_element_type=F32)


def dot(left, right):
    return jnp.dot(left, right, preferred_element_type=F32)


def pairs(size, bit):
    return [(index, index ^ bit) for index in range(size)]


def slots_of(size):
    if size == 4:
        return [lax.axis_index("tensor") ^ step for step in range(size)]
    return [jnp.int32(step) for step in range(size)]


ANYWHERE = pl.BlockSpec(memory_space=pl.ANY)


def nothing_kernel(*refs):
    pass


def hold(value, *others):
    return pl.pallas_call(
        nothing_kernel,
        in_specs=[ANYWHERE] * (1 + len(others)),
        out_specs=ANYWHERE,
        out_shape=jax.ShapeDtypeStruct(value.shape, value.dtype),
        input_output_aliases={0: 0},
        cost_estimate=declared(0),
    )(value, *others)


def first_hop(shard, size):
    if size != 4:
        return None
    return [lax.ppermute(shard, "tensor", pairs(size, bit)) for bit in (1, 2)]


def hold_halves(hop, *others):
    one, two = hop
    half = one.shape[0] // 2
    return hold(one[:half], *others), hold(two[half:], *others)


def second_hop(shard, hop, size, halves=None):
    if size != 4:
        whole = lax.all_gather(shard, "tensor", axis=0)
        return [whole[step] for step in range(size)]
    half = shard.shape[0] // 2
    one, two = hop
    upper, lower = halves or (one[:half], two[half:])
    three_a = lax.ppermute(upper, "tensor", pairs(size, 2))
    three_b = lax.ppermute(lower, "tensor", pairs(size, 1))
    return [shard, one, two, jnp.concatenate([three_a, three_b], axis=0)]


def gather(shard, size):
    return second_hop(shard, first_hop(shard, size), size)


def send_half(three, size):
    half = three.shape[0] // 2
    into_two = lax.ppermute(three[:half], "tensor", pairs(size, 1))
    into_one = lax.ppermute(three[half:], "tensor", pairs(size, 2))
    return into_one, into_two


def send_whole(one, two, into, size):
    into_one, into_two = into
    half = one.shape[0] // 2
    lower = (one[half:].astype(F32) + into_one.astype(F32)).astype(BF16)
    upper = (two[:half].astype(F32) + into_two.astype(F32)).astype(BF16)
    return [
        lax.ppermute(jnp.concatenate([one[:half], lower], axis=0), "tensor", pairs(size, 1)),
        lax.ppermute(jnp.concatenate([upper, two[half:]], axis=0), "tensor", pairs(size, 2)),
    ]


def sum_whole(terms):
    return [
        lax.psum_scatter(
            jnp.concatenate(terms, axis=0), "tensor", scatter_dimension=0, tiled=True
        )
    ]


def total(parts):
    return functools.reduce(jnp.add, [part.astype(F32) for part in parts])


def sum_tensor(value, size):
    if size & (size - 1):
        return lax.psum(value, "tensor")
    return value + sum(lax.ppermute(value, "tensor", pairs(size, bit)) for bit in range(1, size))


def rope_tables(segment):
    length = segment.shape[0]
    bound = jnp.sum((segment == 0).astype(jnp.int32))
    place = lax.broadcasted_iota(jnp.int32, (length, LANES), 0)
    place = place - jnp.where(place >= bound, bound, 0)
    lane = lax.broadcasted_iota(jnp.int32, (length, LANES), 1)
    freqs = jnp.exp(
        (lane % (HD // 2)).astype(F32) * (-2.0 * math.log(ROPE_BASE) / HD)
    )
    angles = place.astype(F32) * freqs
    sine = jnp.sin(angles)
    return bound, jnp.cos(angles), jnp.where(lane % HD < HD // 2, -sine, sine)


def swap_halves(values):
    lane = lax.broadcasted_iota(jnp.int32, values.shape, 1)
    after = pltpu.roll(values, LANES - HD // 2, 1)
    before = pltpu.roll(values, HD // 2, 1)
    return jnp.where(lane % HD < HD // 2, after, before)


def normalize(stream):
    scale_r = lax.rsqrt(jnp.mean(stream * stream, axis=-1, keepdims=True) + EPSILON)
    return (stream * scale_r, scale_r)


def project_kernel(slot_ref, *refs, count, steps, heads, kv):
    gains_ref, w_ref, cos_ref, sin_ref = refs[count : count + 4]
    h_ref, q_ref, kx_ref, vx_ref, kt_ref, vt_ref, gain_ref = refs[-7:]

    @pl.when(pl.program_id(0) == 0)
    def _():
        gain_ref[...] = gains_ref[...].astype(F32).T[:8]

    which = pl.program_id(0) // steps
    tokens = refs[0][...]
    for block in range(1, count):
        tokens = jnp.where(which == block, refs[block][...], tokens)
    normed, _ = normalize(tokens.astype(F32))
    low = (normed * gain_ref[0:1, :]).astype(BF16)
    h_ref[...] = low
    pre = dot(low, w_ref[...])
    cosine, sine = cos_ref[...], sin_ref[...]
    rows = pre.shape[0]
    lane = lax.broadcasted_iota(jnp.int32, (rows, LANES), 1)
    chunks = []
    for chunk in range(pre.shape[1] // LANES):
        part = pre[:, chunk * LANES : (chunk + 1) * LANES]
        turned = part * cosine + swap_halves(part) * sine
        first = 2 * chunk
        if first + 1 < heads + kv:
            chunks.append(turned)
        elif first < heads + kv:
            chunks.append(jnp.where(lane < HD, turned, part))
        else:
            chunks.append(part)
        if first < heads:
            q_ref[:, chunk * LANES : (chunk + 1) * LANES] = (
                chunks[chunk] * (1.0 / math.sqrt(HD))
            ).astype(BF16)
    flipped = {}
    for head in range(2 * kv):
        place = heads + head
        part = chunks[place // 2]
        moved = pltpu.roll(part, HD, 1)
        wide = [part, moved] if place % 2 == 0 else [moved, part]
        out = kx_ref if head < kv else vx_ref
        out[head % kv, 0] = jnp.where(lane < HD, wide[0], 0.0).astype(BF16)
        out[head % kv, 1] = jnp.where(lane < HD, 0.0, wide[1]).astype(BF16)
        if place // 2 not in flipped:
            flipped[place // 2] = part.T
        turn = flipped[place // 2][(place % 2) * HD : (place % 2 + 1) * HD]
        out_t = kt_ref if head < kv else vt_ref
        out_t[(head % kv) * HD : (head % kv + 1) * HD, :] = turn.astype(BF16)


def project(slots, blocks, bundle, cosine, sine, heads, kv, length, prev, others=()):
    rows, width = blocks[0].shape
    count = len(blocks)
    tile = min(256, rows)
    steps = rows // tile
    columns = (heads + 2 * kv) * HD

    def at(i, slot):
        return slot[i // steps] * steps + i % steps

    shapes = [
        jax.ShapeDtypeStruct((length, width), BF16),
        jax.ShapeDtypeStruct((length, heads * HD), BF16),
        jax.ShapeDtypeStruct((kv, 2, length, LANES), BF16),
        jax.ShapeDtypeStruct((kv, 2, length, LANES), BF16),
        jax.ShapeDtypeStruct((kv * HD, length), BF16),
        jax.ShapeDtypeStruct((kv * HD, length), BF16),
    ]
    out_specs = [
        pl.BlockSpec((tile, width), lambda i, s: (at(i, s), 0)),
        pl.BlockSpec((tile, heads * HD), lambda i, s: (at(i, s), 0)),
        pl.BlockSpec((kv, 2, tile, LANES), lambda i, s: (0, 0, at(i, s), 0)),
        pl.BlockSpec((kv, 2, tile, LANES), lambda i, s: (0, 0, at(i, s), 0)),
        pl.BlockSpec((kv * HD, tile), lambda i, s: (0, at(i, s))),
        pl.BlockSpec((kv * HD, tile), lambda i, s: (0, at(i, s))),
    ]
    in_specs = [
        pl.BlockSpec((tile, width), lambda i, s, b=block: (jnp.clip(i - b * steps, 0, steps - 1), 0))
        for block in range(count)
    ]
    in_specs += [
        pl.BlockSpec((width, LANES), lambda i, s: (0, columns // LANES)),
        pl.BlockSpec((width, columns), lambda i, s: (0, 0)),
        pl.BlockSpec((tile, LANES), lambda i, s: (at(i, s), 0)),
        pl.BlockSpec((tile, LANES), lambda i, s: (at(i, s), 0)),
    ]
    operands = [jnp.stack(slots), *blocks, bundle, bundle, cosine, sine]
    aliases = {}
    if prev is not None:
        for index, array in enumerate(prev):
            aliases[len(operands)] = index
            operands.append(array)
            in_specs.append(ANYWHERE)
    operands += others
    in_specs += [ANYWHERE] * len(others)
    return pl.pallas_call(
        functools.partial(
            project_kernel, count=count, steps=steps, heads=heads, kv=kv
        ),
        grid_spec=pltpu.PrefetchScalarGridSpec(
            num_scalar_prefetch=1,
            grid=(count * steps,),
            in_specs=in_specs,
            out_specs=out_specs,
            scratch_shapes=[pltpu.VMEM((8, width), F32)],
        ),
        out_shape=shapes,
        input_output_aliases=aliases,
        compiler_params=limit(24),
        cost_estimate=declared(2 * count * rows * width * columns),
    )(*operands)


def feed_kernel(*refs, count):
    tokens = refs[:count]
    gate_ref, up_ref = refs[count : count + 2]
    hidden_ref, silu_ref, slope_ref, h_out = refs[-4:]
    rows = tokens[0].shape[0]
    wide = h_out.shape[1]
    tile = min(256, gate_ref.shape[1])
    lanes = pl.ds(pl.multiple_of(pl.program_id(0) * wide, wide), wide)
    for block in range(count):
        h_out[block * rows : (block + 1) * rows, :] = tokens[block][:, lanes]
    for part in range(gate_ref.shape[1] // tile):
        columns = slice(part * tile, (part + 1) * tile)
        for block in range(count):
            where = slice(block * rows, (block + 1) * rows)
            gate = dot(tokens[block][...], gate_ref[:, columns])
            up = dot(tokens[block][...], up_ref[:, columns])
            sigmoid = 0.5 * jnp.tanh(0.5 * gate) + 0.5
            silu = gate * sigmoid
            hidden_ref[where, columns] = (silu * up).astype(BF16)
            silu_ref[where, columns] = silu.astype(BF16)
            slope_ref[where, columns] = (up * (sigmoid + silu * (1.0 - sigmoid))).astype(BF16)


def feed_back_kernel(*refs, count):
    grads = refs[:count]
    down_ref, silu_ref, slope_ref = refs[count : count + 3]
    dgate_ref, dup_ref = refs[-2:]
    rows = grads[0].shape[0]
    for block in range(count):
        where = slice(block * rows, (block + 1) * rows)
        dhidden = dot(grads[block][...], down_ref[...])
        dup_ref[where, :] = (dhidden * silu_ref[where, :].astype(F32)).astype(BF16)
        dgate_ref[where, :] = (dhidden * slope_ref[where, :].astype(F32)).astype(BF16)


def feed(kernel, place, blocks, tokens, weights, places, kept, units, outs, copy, tile, prev, others):
    rows, width = tokens[0].shape
    count = len(tokens)
    steps = max(units // tile, 1)
    tile, wide = units // steps, width // steps
    shapes = [jax.ShapeDtypeStruct((blocks * rows, units), BF16)] * outs
    in_specs = [pl.BlockSpec((rows, width), lambda i: (0, 0), pipeline_mode=pl.Buffered(1))] * count
    in_specs += [
        pl.BlockSpec((width, tile), lambda i, w=which: (0, w * steps + i)) for which in places
    ]
    cell = pl.BlockSpec((count * rows, tile), lambda i: (place, i))
    in_specs += [cell] * len(kept)
    out_specs = [cell] * outs
    if copy:
        shapes.append(jax.ShapeDtypeStruct((blocks * rows, width), BF16))
        out_specs.append(pl.BlockSpec((count * rows, wide), lambda i: (place, i)))
    operands = [*tokens, *weights, *kept]
    aliases = {}
    if prev is not None:
        for index, array in enumerate(prev):
            aliases[len(operands)] = index
            operands.append(array)
            in_specs.append(ANYWHERE)
    operands += others
    in_specs += [ANYWHERE] * len(others)
    return pl.pallas_call(
        functools.partial(kernel, count=count),
        grid=(steps,),
        in_specs=in_specs,
        out_specs=out_specs,
        out_shape=shapes,
        input_output_aliases=aliases,
        compiler_params=limit(36),
        cost_estimate=declared(2 * len(weights) * count * rows * width * units),
    )(*operands)


def back_kernel(slot_ref, *refs, count, terms, added):
    outs = refs[-count:]
    weights = refs[count * terms : (count + 1) * terms]
    into = list(refs[(count + 1) * terms :])
    for block in range(count):
        value = dot_cols(refs[block * terms][...], weights[0][...])
        for term in range(1, terms):
            value = value + dot_cols(refs[block * terms + term][...], weights[term][...])
        if added[block] is None:
            outs[block][...] = value.astype(BF16)
            continue
        half = value.shape[0] // 2
        extra = into.pop(0)[...].astype(F32)
        top, bottom = value[:half], value[half:]
        if added[block]:
            top = top + extra
        else:
            bottom = bottom + extra
        outs[block][:half, :] = top.astype(BF16)
        outs[block][half:, :] = bottom.astype(BF16)


def back(slots, rows, lefts, weights, places, into=None, others=()):
    depth = lefts[0].shape[1]
    width = weights[0].shape[0]
    tile = min(512, width)
    terms, count = len(lefts), len(slots)
    into = into or [None] * count
    in_specs, operands = [], [jnp.stack([jnp.asarray(slot, jnp.int32) for slot in slots])]
    for block in range(count):
        in_specs += [pl.BlockSpec((rows, depth), lambda i, s, b=block: (s[b], 0))] * terms
        operands += lefts
    in_specs += [pl.BlockSpec((tile, depth), lambda i, s, p=place: (i, p)) for place in places]
    operands += weights
    for extra in into:
        if extra is not None:
            in_specs.append(pl.BlockSpec((rows // 2, tile), lambda i, s: (0, i)))
            operands.append(extra[0])
    operands += others
    in_specs += [ANYWHERE] * len(others)
    return pl.pallas_call(
        functools.partial(
            back_kernel,
            count=count,
            terms=terms,
            added=[None if extra is None else extra[1] for extra in into],
        ),
        grid_spec=pltpu.PrefetchScalarGridSpec(
            num_scalar_prefetch=1,
            grid=(width // tile,),
            in_specs=in_specs,
            out_specs=[pl.BlockSpec((rows, tile), lambda i, s: (0, i))] * count,
        ),
        out_shape=[jax.ShapeDtypeStruct((rows, width), BF16)] * count,
        compiler_params=limit(34),
        cost_estimate=declared(2 * count * terms * rows * width * depth),
    )(*operands)


def weigh_kernel(left_ref, right_ref, *rest):
    out_ref, turned_ref = rest[-2:]

    @pl.when(pl.program_id(1) == 0)
    def _():
        turned_ref[...] = left_ref[...].T

    out_ref[...] = dot(turned_ref[...], right_ref[...]).astype(BF16)


def weigh(left, right, others=()):
    tokens, width = left.shape
    columns = right.shape[1]
    tall, wide = min(512, width), min(1024, columns)
    return pl.pallas_call(
        weigh_kernel,
        grid=(width // tall, columns // wide),
        in_specs=[
            pl.BlockSpec((tokens, tall), lambda i, j: (0, i)),
            pl.BlockSpec((tokens, wide), lambda i, j: (0, j)),
        ]
        + [ANYWHERE] * len(others),
        out_specs=pl.BlockSpec((tall, wide), lambda i, j: (i, j)),
        out_shape=jax.ShapeDtypeStruct((width, columns), BF16),
        scratch_shapes=[pltpu.VMEM((tall, tokens), BF16)],
        compiler_params=limit(24),
        cost_estimate=declared(2 * tokens * width * columns),
    )(left, right, *others)


def back_attended_kernel(grad_ref, w_ref, *rest):
    out_ref, copy_ref = rest[-2:]
    out_ref[...] = dot(grad_ref[...], w_ref[...]).astype(BF16)
    copy_ref[...] = grad_ref[...]


def back_attended(place, blocks, grad, bundle, column, columns, prev):
    rows, width = grad.shape
    tile = min(256, rows)
    steps = rows // tile
    in_specs = [
        pl.BlockSpec((tile, width), lambda i: (i, 0)),
        pl.BlockSpec((width, columns), lambda i: (0, column)),
    ]
    operands = [grad, bundle]
    aliases = {}
    if prev is not None:
        for index, array in enumerate(prev):
            aliases[len(operands)] = index
            operands.append(array)
            in_specs.append(ANYWHERE)
    return pl.pallas_call(
        back_attended_kernel,
        grid=(steps,),
        in_specs=in_specs,
        out_specs=[
            pl.BlockSpec((tile, columns), lambda i: (place * steps + i, 0)),
            pl.BlockSpec((tile, width), lambda i: (place * steps + i, 0)),
        ],
        out_shape=[
            jax.ShapeDtypeStruct((blocks * rows, columns), BF16),
            jax.ShapeDtypeStruct((blocks * rows, width), BF16),
        ],
        input_output_aliases=aliases,
        compiler_params=limit(14),
        cost_estimate=declared(2 * rows * width * columns),
    )(*operands)


def causal(block):
    keys = lax.broadcasted_iota(jnp.int32, (block, block), 0)
    return keys <= lax.broadcasted_iota(jnp.int32, (block, block), 1)


def first_block(bound, offset, block):
    return jnp.where(offset >= bound, lax.div(bound, jnp.int32(block)), 0)


def attend_kernel(order_ref, q_ref, kx_ref, vt_ref, *rest, block):
    out_ref, lse_ref, top_ref, acc_ref = rest[-4:]
    kv = kx_ref.shape[0]
    per = q_ref.shape[1] // LANES // kv
    bound = order_ref[0]
    ones = jnp.ones((16, block), BF16)
    for group in range(kv):

        def q_step(turn, _):
            index = order_ref[1 + turn]
            offset = pl.multiple_of(index * block, block)
            into = pl.ds(pl.multiple_of(turn * block, block), block)
            top_ref[...] = jnp.full(top_ref.shape, MASKED, F32)
            acc_ref[...] = jnp.zeros(acc_ref.shape, F32)

            def tile(step, diagonal):
                keys = pl.ds(pl.multiple_of(step * block, block), block)
                value_t = jnp.concatenate(
                    [vt_ref[group * HD : (group + 1) * HD, keys], ones], axis=0
                )
                for head in range(2 * per):
                    column = (group * per + head // 2) * LANES
                    query = q_ref[pl.ds(offset, block), column : column + LANES]
                    scores = dot_cols(kx_ref[group, head % 2, keys, :], query)
                    if diagonal:
                        scores = jnp.where(causal(block), scores, MASKED)
                    old = top_ref[head, 0:1, :]
                    top = jnp.maximum(old, jnp.max(scores, axis=0, keepdims=True))
                    powered = jnp.exp(scores - top).astype(BF16)
                    acc_ref[head] = acc_ref[head] * jnp.exp(old - top) + dot(value_t, powered)
                    top_ref[head, 0:1, :] = top

            def full_tile(step, carry):
                tile(step, False)
                return carry

            lax.fori_loop(first_block(bound, offset, block), index, full_tile, 0)
            tile(index, True)
            for pair in range(per):
                both = []
                for head in (2 * pair, 2 * pair + 1):
                    total = acc_ref[head, HD : HD + 1, :]
                    both.append(acc_ref[head, :HD, :] / total)
                    place = group * 2 * per + head
                    lse_ref[place : place + 1, into] = top_ref[
                        head, 0:1, :
                    ] + jnp.log(total)
                column = (group * per + pair) * LANES
                out_ref[into, column : column + LANES] = (
                    jnp.concatenate(both, axis=0).T.astype(BF16)
                )
            return _

        lax.fori_loop(0, out_ref.shape[0] // block, q_step, 0)


def attend(bound, order, queries, kx, vt, block, others=()):
    length, width = queries.shape
    heads = width // HD
    kv = kx.shape[0]
    per = heads // kv
    count = len(order)
    cells = heads * count * block * (length + block) // 2
    vmem = pl.BlockSpec(memory_space=pltpu.VMEM)
    return pl.pallas_call(
        functools.partial(attend_kernel, block=block),
        in_specs=[pl.BlockSpec(memory_space=pltpu.SMEM), vmem, vmem, vmem] + [ANYWHERE] * len(others),
        out_specs=[vmem, vmem],
        out_shape=[
            jax.ShapeDtypeStruct((count * block, width), BF16),
            jax.ShapeDtypeStruct((heads, count * block), F32),
        ],
        scratch_shapes=[
            pltpu.VMEM((per, 8, block), F32),
            pltpu.VMEM((per, HD + 16, block), F32),
        ],
        compiler_params=limit(20),
        cost_estimate=declared(2 * 4 * HD * 4 * cells, 16),
    )(jnp.stack([bound, *order]), queries, kx, vt, *others)


def attend_back_kernel(
    order_ref, q_ref, kx_ref, vx_ref, kt_ref, lse_ref, out_ref, grad_ref, cos_ref, sin_ref,
    *rest, block
):
    dqkv_ref, dk_ref, dv_ref, dq_ref = rest[-4:]
    length = q_ref.shape[0]
    kv = kx_ref.shape[0]
    heads = q_ref.shape[1] // HD
    per = heads // 2 // kv
    bound = order_ref[0]
    dk_ref[...] = jnp.zeros(dk_ref.shape, F32)
    dv_ref[...] = jnp.zeros(dv_ref.shape, F32)
    lane = lax.broadcasted_iota(jnp.int32, (8, LANES), 1)
    row = lax.broadcasted_iota(jnp.int32, (8, LANES), 0)
    chosen = ((lane // HD) == row).astype(F32)

    def turn_back(values, rows):
        return values * cos_ref[rows, :] - swap_halves(values) * sin_ref[rows, :]

    for group in range(kv):

        def q_step(turn, _):
            index = order_ref[1 + turn]
            offset = pl.multiple_of(index * block, block)
            rows = pl.ds(offset, block)
            given = pl.ds(pl.multiple_of(turn * block, block), block)
            dq_ref[...] = jnp.zeros(dq_ref.shape, F32)
            deltas = []
            for pair in range(per):
                column = (group * per + pair) * LANES
                product = grad_ref[given, column : column + LANES].astype(F32) * out_ref[
                    given, column : column + LANES
                ].astype(F32)
                deltas.append(
                    lax.dot_general(
                        chosen, product, OVER_COLS, precision=lax.Precision.HIGHEST,
                        preferred_element_type=F32,
                    )
                )

            def tile(step, diagonal):
                keys = pl.ds(pl.multiple_of(step * block, block), block)
                key_t = kt_ref[group * HD : (group + 1) * HD, keys]
                for parity in range(2):
                    key_add, value_add = 0.0, 0.0
                    for pair in range(per):
                        head = 2 * pair + parity
                        place = group * 2 * per + head
                        column = (group * per + pair) * LANES
                        query = q_ref[rows, column : column + LANES]
                        grad = grad_ref[given, column : column + LANES]
                        scores = dot_cols(kx_ref[group, parity, keys, :], query)
                        if diagonal:
                            scores = jnp.where(causal(block), scores, MASKED)
                        probs = jnp.exp(scores - lse_ref[place : place + 1, given])
                        dprobs = dot_cols(vx_ref[group, parity, keys, :], grad)
                        dscores = (probs * (dprobs - deltas[pair][parity : parity + 1])).astype(BF16)
                        value_add = value_add + dot(probs.astype(BF16), grad)
                        key_add = key_add + dot(dscores, query)
                        dq_ref[head * HD : (head + 1) * HD, :] += dot(key_t, dscores)
                    dk_ref[group, parity, keys, :] += key_add
                    dv_ref[group, parity, keys, :] += value_add

            def full_tile(step, carry):
                tile(step, False)
                return carry

            lax.fori_loop(first_block(bound, offset, block), index, full_tile, 0)
            tile(index, True)
            for pair in range(per):
                column = (group * per + pair) * LANES
                grad_q = dq_ref[pair * LANES : (pair + 1) * LANES, :].T * (1.0 / math.sqrt(HD))
                dqkv_ref[rows, column : column + LANES] = turn_back(grad_q, rows).astype(BF16)
            return _

        lax.fori_loop(0, length // block, q_step, 0)

    def finish(index, _):
        rows = pl.ds(pl.multiple_of(index * block, block), block)
        lanes = lax.broadcasted_iota(jnp.int32, (block, LANES), 1)

        def placed(part, half):
            ref = dk_ref if part < kv else dv_ref
            even, odd = ref[part % kv, 0, rows, :], ref[part % kv, 1, rows, :]
            return even + pltpu.roll(odd, HD, 1) if half == 0 else pltpu.roll(even, HD, 1) + odd

        for chunk in range(kv):
            values = jnp.where(lanes < HD, placed(2 * chunk, 0), placed(2 * chunk + 1, 1))
            if 2 * chunk + 1 < kv:
                values = turn_back(values, rows)
            elif 2 * chunk < kv:
                values = jnp.where(lanes < HD, turn_back(values, rows), values)
            column = heads * HD + chunk * LANES
            dqkv_ref[rows, column : column + LANES] = values.astype(BF16)
        return _

    lax.fori_loop(0, length // block, finish, 0)


def attend_back(
    bound, order, queries, kx, vx, kt, log_sums, attended, grad, cosine, sine, block, others
):
    length, width = queries.shape
    heads = width // HD
    kv = kx.shape[0]
    cells = heads * length * (length + block) // 2
    vmem = pl.BlockSpec(memory_space=pltpu.VMEM)
    return pl.pallas_call(
        functools.partial(attend_back_kernel, block=block),
        in_specs=[pl.BlockSpec(memory_space=pltpu.SMEM)] + [vmem] * 9 + [ANYWHERE] * len(others),
        out_specs=vmem,
        out_shape=jax.ShapeDtypeStruct((length, width + 2 * kv * HD), BF16),
        scratch_shapes=[
            pltpu.VMEM((kv, 2, length, LANES), F32),
            pltpu.VMEM((kv, 2, length, LANES), F32),
            pltpu.VMEM((heads // kv * HD, block), F32),
        ],
        compiler_params=limit(28),
        cost_estimate=declared(2 * 10 * HD * 4 * cells),
    )(jnp.stack([bound, *order]), queries, kx, vx, kt, log_sums, attended, grad, cosine, sine, *others)


def local(
    inputs,
    segment_ids,
    attn_gain,
    query_weight,
    key_weight,
    value_weight,
    output_weight,
    mlp_gain,
    gate_weight,
    up_weight,
    down_weight,
    cotangent,
    *,
    sizes,
):
    rows = inputs.shape[0]
    length = segment_ids.shape[0]
    query_cols = query_weight.shape[1]
    key_cols = key_weight.shape[1]
    heads, kv = query_cols // HD, key_cols // HD
    columns = query_cols + 2 * key_cols
    slots = slots_of(sizes["tensor"])
    tensor = sizes["tensor"]
    space = (-columns) % query_cols or query_cols
    gains = jnp.pad(jnp.stack([attn_gain, mlp_gain], axis=1), ((0, 0), (0, space - 2)))
    bundle = lax.all_gather(
        jnp.concatenate([query_weight, key_weight, value_weight, gains, output_weight.T], axis=1),
        "dp", axis=0, tiled=True,
    )
    out_place = (columns + space) // query_cols
    mlp_scale = bundle[:, columns + 1].astype(F32)[None, :]
    hop = first_hop(inputs, tensor)
    gate_up = lax.all_gather(
        hold(jnp.concatenate([gate_weight, up_weight], axis=1), *(hop or ())),
        "dp", axis=0, tiled=True,
    )

    bound, cosine, sine = rope_tables(segment_ids)
    blocks = second_hop(inputs, hop, tensor)
    stream = inputs.astype(F32)
    arrays = None
    if tensor == 4:
        arrays = project(slots[:3], blocks[:3], bundle, cosine, sine, heads, kv, length, None)
        cotangent_sent = hold(cotangent, blocks[3])
        arrays = project(slots[3:], blocks[3:], bundle, cosine, sine, heads, kv, length, arrays)
    else:
        arrays = project(slots, blocks, bundle, cosine, sine, heads, kv, length, None)
        cotangent_sent = cotangent
    block_a, queries, kx, vx, kt, vt = arrays
    cotangent_hop = first_hop(cotangent_sent, tensor)
    down_t = lax.all_gather(hold(down_weight.T, queries), "dp", axis=0, tiled=True)

    def back_attention(places, attended, others=()):
        return back(places, rows, [attended], [bundle], [out_place], None, others)

    if tensor == 4:
        far, far_sums = attend(bound, slots[3:], queries, kx, vt, rows)
        three = back_attention([0], far)[0]
        halves = send_half(three, tensor)
        order = [slots[1], slots[2], slots[0], slots[3]]
        near, near_sums = attend(bound, order[:3], queries, kx, vt, rows, [three])
        one, two, own = back_attention([0, 1, 2], near, cotangent_hop)
        attended = jnp.concatenate([near, far], axis=0)
        log_sums = jnp.concatenate([near_sums, far_sums], axis=1)
        stream_parts = [own, *send_whole(one, two, halves, tensor)]
    else:
        order = slots
        attended, log_sums = attend(bound, order, queries, kx, vt, rows)
        stream_parts = sum_whole(back_attention(list(range(tensor)), attended))
    stream_one = stream + total(stream_parts)
    normed_m, scale_m = normalize(stream_one)
    parts_m = [(normed_m * mlp_scale).astype(BF16)]
    units = gate_weight.shape[1]

    def feed_at(place, wanted, fed, others=()):
        return feed(
            feed_kernel, place, tensor, [parts_m[k] for k in wanted], [gate_up] * 2, [0, 1], [],
            units, 3, True, 512, fed, others,
        )

    def feed_back_at(place, wanted, fed, others=()):
        return feed(
            feed_back_kernel, place, tensor, [grad_parts[k] for k in wanted], [down_t], [0],
            [silu, slope], units, 2, False, 256, fed, others,
        )

    def back_m(places, fed, into=None, others=()):
        return back(places, rows, fed[:2], [gate_up] * 2, [0, 1], into, others)

    def back_out(places, into=None, others=()):
        return back(places, rows, [hidden], [down_t], [0], into, others)

    def reduce_rows(term, *others):
        if others and tensor == 4:
            term = hold(term, *others)
        return lax.psum_scatter(term, "dp", scatter_dimension=0, tiled=True)

    if tensor == 4:
        hop = first_hop(parts_m[0], tensor)
        fed = feed_at(3, [0], None)
        halves = hold_halves(hop, fed[0])
        parts_m = second_hop(parts_m[0], hop, tensor, halves)
        fed = feed_at(0, [1, 2], fed, halves)
        halves = hold_halves(cotangent_hop, fed[0])
        grad_parts = second_hop(cotangent_sent, cotangent_hop, tensor, halves)
        fed = feed_at(2, [3], fed, halves)
    else:
        grad_parts = second_hop(cotangent_sent, None, tensor)
        parts_m = gather(parts_m[0], tensor)
        fed = None
        for place in range(tensor):
            fed = feed_at(place, [place], fed)
    hidden, silu, slope, block_m = fed
    if tensor == 4:
        grad_block = jnp.concatenate([grad_parts[k] for k in (1, 2, 3, 0)], axis=0)
        down_t_wgrad = weigh(grad_block, hidden)
        (three_out,) = back_out([2], None, [down_t_wgrad])
        out_one, out_two = send_half(three_out, tensor)
        fed = feed_back_at(2, [3], None, [three_out])
        (three_m,) = back_m([2], fed)
        m_one, m_two = send_half(three_m, tensor)
        fed = feed_back_at(0, [1, 2], fed, [three_m])
        fed = feed_back_at(3, [0], fed)
        one_m, two_m = back_m([0, 1], fed, [(m_one, False), (m_two, True)], [out_one, out_two])
        gate_wgrad = weigh(block_m, fed[0], [one_m])
        (own_m,) = back_m([3], fed, None, [gate_wgrad])
        grad_m_parts = [
            own_m,
            lax.ppermute(one_m, "tensor", pairs(tensor, 1)),
            lax.ppermute(two_m, "tensor", pairs(tensor, 2)),
        ]
    else:
        down_t_wgrad = weigh(jnp.concatenate(grad_parts, axis=0), hidden)
        fed = None
        for place in range(tensor):
            fed = feed_back_at(place, [place], fed)
        grad_m_parts = sum_whole(back_m(list(range(tensor)), fed))
        gate_wgrad = weigh(block_m, fed[0])
    down_t_low = reduce_rows(down_t_wgrad)

    def norm_back(grad_in, normed, scale_r, gain):
        scaled = grad_in * gain
        return scale_r * (scaled - normed * jnp.mean(scaled * normed, axis=-1, keepdims=True))

    grad_normed_m = total(grad_m_parts)
    grad_stream_one = cotangent.astype(F32) + norm_back(grad_normed_m, normed_m, scale_m, mlp_scale)
    grad_stream_low = grad_stream_one.astype(BF16)
    gate_low = reduce_rows(gate_wgrad, grad_stream_low)
    up_wgrad = weigh(block_m, fed[1], [grad_stream_low])
    hop, halves = first_hop(grad_stream_low, tensor), None
    if tensor == 4:
        out_terms = back_out([0, 1, 3], [(out_one, False), (out_two, True), None], [up_wgrad])
        halves = hold_halves(hop, up_wgrad, out_terms[0])
    grad_parts = second_hop(grad_stream_low, hop, tensor, halves)
    backs = None
    for place, wanted in enumerate([1, 2, 0, 3] if tensor == 4 else range(tensor)):
        backs = back_attended(
            place, tensor, grad_parts[wanted], bundle, out_place, query_cols, backs,
        )
    grad_attended, grad_stream_block = backs
    up_low = reduce_rows(up_wgrad, grad_attended)
    grad_qkv = attend_back(
        bound, order, queries, kx, vx, kt, log_sums, attended, grad_attended, cosine, sine, rows,
        [down_t_low],
    )
    if tensor == 4:
        out_parts = [out_terms[2]] + [
            lax.ppermute(hold(out_terms[step - 1], grad_attended), "tensor", pairs(tensor, step))
            for step in (1, 2)
        ]
    else:
        out_parts = sum_whole(back_out(list(range(tensor))))
    layer_out = (stream_one + total(out_parts)).astype(BF16)

    def back_a(places, others=()):
        return back(places, rows, [grad_qkv], [bundle], [0], None, others)

    if tensor == 4:
        (three,) = back_a(slots[3:], [*out_parts[1:], gate_low])
        halves = send_half(three, tensor)
        block_a = hold(block_a, three)
        grad_stream_block = hold(grad_stream_block, three)
    qkv_wgrad = weigh(block_a, grad_qkv)
    out_t_wgrad = weigh(grad_stream_block, attended)
    attention_wgrad = jnp.concatenate([qkv_wgrad, out_t_wgrad], axis=1)
    gate_sum, up_sum, down_t_sum = [low.astype(F32) for low in (gate_low, up_low, down_t_low)]
    attention_sum = reduce_rows(attention_wgrad).astype(F32)
    if tensor == 4:
        one, two, own = back_a([slots[1], slots[2], slots[0]], [three])
        grad_a_parts = [own, *send_whole(one, two, halves, tensor)]
    else:
        grad_a_parts = sum_whole(back_a(slots))
    grad_normed_a = total(grad_a_parts)

    def gain_term(gain, weights):
        term = sum(jnp.sum(weight.astype(F32) * grad, axis=1) for weight, grad in weights)
        return term / gain.astype(F32)

    query_sum = attention_sum[:, :query_cols]
    key_sum = attention_sum[:, query_cols : query_cols + key_cols]
    value_sum = attention_sum[:, query_cols + key_cols : columns]
    gain_terms = [
        gain_term(
            attn_gain, [(query_weight, query_sum), (key_weight, key_sum), (value_weight, value_sum)]
        ),
        gain_term(mlp_gain, [(gate_weight, gate_sum), (up_weight, up_sum)]),
    ]
    gain_mine = sum_tensor(jnp.stack(gain_terms), tensor)
    normed_a, scale_a = normalize(stream)
    attn_scale = bundle[:, columns].astype(F32)[None, :]
    input_grad = (
        grad_stream_one + norm_back(grad_normed_a, normed_a, scale_a, attn_scale)
    ).astype(BF16)
    return (
        layer_out,
        input_grad,
        gain_mine[0],
        query_sum,
        key_sum,
        value_sum,
        attention_sum[:, columns:].T,
        gain_mine[1],
        gate_sum,
        up_sum,
        down_t_sum.T,
    )


def solution(mesh):
    tokens = P(("dp", "tensor"), None)
    in_specs = (
        tokens,
        P("dp"),
        P("dp"),
        P("dp", "tensor"),
        P("dp", "tensor"),
        P("dp", "tensor"),
        P("tensor", "dp"),
        P("dp"),
        P("dp", "tensor"),
        P("dp", "tensor"),
        P("tensor", "dp"),
        tokens,
    )
    out_specs = (
        tokens,
        tokens,
        P("dp"),
        P("dp", "tensor"),
        P("dp", "tensor"),
        P("dp", "tensor"),
        P("tensor", "dp"),
        P("dp"),
        P("dp", "tensor"),
        P("dp", "tensor"),
        P("tensor", "dp"),
    )
    return jax.shard_map(
        functools.partial(local, sizes={axis: mesh.shape[axis] for axis in ("tensor", "dp")}),
        mesh=mesh, in_specs=in_specs, out_specs=out_specs, check_vma=False,
    )
```

```python
import functools
import math

import jax
import jax.numpy as jnp
from jax import lax
from jax.experimental import pallas as pl
from jax.experimental.pallas import tpu as pltpu
from jax.sharding import PartitionSpec as P

HD = 64
LANES = 128
EPSILON = 1e-05
ROPE_BASE = 500000.0
MASKED = -1e30
OVER_ROWS = (((0,), (0,)), ((), ()))
OVER_COLS = (((1,), (1,)), ((), ()))


def limit(size):
    return pltpu.CompilerParams(vmem_limit_bytes=size * 2**20)


SHORT = 0.0625


def declared(flops, scale=SHORT):
    return pl.CostEstimate(flops=int(flops * scale), bytes_accessed=0, transcendentals=0)


F32 = jnp.float32
BF16 = jnp.bfloat16


def dot_cols(left, right):
    return lax.dot_general(left, right, OVER_COLS, preferred_element_type=F32)


def dot_rows(left, right):
    return lax.dot_general(left, right, OVER_ROWS, preferred_element_type=F32)


def dot(left, right):
    return jnp.dot(left, right, preferred_element_type=F32)


def pairs(size, bit):
    return [(index, index ^ bit) for index in range(size)]


def slots_of(size):
    if size == 4:
        return [lax.axis_index("tensor") ^ step for step in range(size)]
    return [jnp.int32(step) for step in range(size)]


ANYWHERE = pl.BlockSpec(memory_space=pl.ANY)


def nothing_kernel(*refs):
    pass


def hold(value, *others):
    return pl.pallas_call(
        nothing_kernel,
        in_specs=[ANYWHERE] * (1 + len(others)),
        out_specs=ANYWHERE,
        out_shape=jax.ShapeDtypeStruct(value.shape, value.dtype),
        input_output_aliases={0: 0},
        cost_estimate=declared(0),
    )(value, *others)


def first_hop(shard, size):
    if size != 4:
        return None
    return [lax.ppermute(shard, "tensor", pairs(size, bit)) for bit in (1, 2)]


def hold_halves(hop, *others):
    one, two = hop
    half = one.shape[0] // 2
    return hold(one[:half], *others), hold(two[half:], *others)


def second_hop(shard, hop, size, halves=None):
    if size != 4:
        whole = lax.all_gather(shard, "tensor", axis=0)
        return [whole[step] for step in range(size)]
    half = shard.shape[0] // 2
    one, two = hop
    upper, lower = halves or (one[:half], two[half:])
    three_a = lax.ppermute(upper, "tensor", pairs(size, 2))
    three_b = lax.ppermute(lower, "tensor", pairs(size, 1))
    return [shard, one, two, jnp.concatenate([three_a, three_b], axis=0)]


def gather(shard, size):
    return second_hop(shard, first_hop(shard, size), size)


def send_half(three, size):
    half = three.shape[0] // 2
    into_two = lax.ppermute(three[:half], "tensor", pairs(size, 1))
    into_one = lax.ppermute(three[half:], "tensor", pairs(size, 2))
    return into_one, into_two


def send_whole(one, two, into, size):
    into_one, into_two = into
    half = one.shape[0] // 2
    lower = (one[half:].astype(F32) + into_one.astype(F32)).astype(BF16)
    upper = (two[:half].astype(F32) + into_two.astype(F32)).astype(BF16)
    return [
        lax.ppermute(jnp.concatenate([one[:half], lower], axis=0), "tensor", pairs(size, 1)),
        lax.ppermute(jnp.concatenate([upper, two[half:]], axis=0), "tensor", pairs(size, 2)),
    ]


def sum_whole(terms):
    return [
        lax.psum_scatter(
            jnp.concatenate(terms, axis=0), "tensor", scatter_dimension=0, tiled=True
        )
    ]


def trade(pieces, size):
    if size != 4:
        whole = lax.all_to_all(jnp.stack(pieces), "tensor", split_axis=0, concat_axis=0, tiled=True)
        return [whole[step] for step in range(size)]
    return [pieces[0]] + [
        lax.ppermute(pieces[step], "tensor", pairs(size, step)) for step in (1, 2, 3)
    ]


def total(parts):
    return functools.reduce(jnp.add, [part.astype(F32) for part in parts])


def sum_tensor(value, size):
    if size & (size - 1):
        return lax.psum(value, "tensor")
    return value + sum(lax.ppermute(value, "tensor", pairs(size, bit)) for bit in range(1, size))


def rope_tables(segment):
    length = segment.shape[0]
    bound = jnp.sum((segment == 0).astype(jnp.int32))
    place = lax.broadcasted_iota(jnp.int32, (length, LANES), 0)
    place = place - jnp.where(place >= bound, bound, 0)
    lane = lax.broadcasted_iota(jnp.int32, (length, LANES), 1)
    freqs = jnp.exp(
        (lane % (HD // 2)).astype(F32) * (-2.0 * math.log(ROPE_BASE) / HD)
    )
    angles = place.astype(F32) * freqs
    sine = jnp.sin(angles)
    return bound, jnp.cos(angles), jnp.where(lane % HD < HD // 2, -sine, sine)


def swap_halves(values):
    lane = lax.broadcasted_iota(jnp.int32, values.shape, 1)
    after = pltpu.roll(values, LANES - HD // 2, 1)
    before = pltpu.roll(values, HD // 2, 1)
    return jnp.where(lane % HD < HD // 2, after, before)


def normalize(stream):
    scale_r = lax.rsqrt(jnp.mean(stream * stream, axis=-1, keepdims=True) + EPSILON)
    return (stream * scale_r, scale_r)


def project_kernel(slot_ref, *refs, count, steps, heads, kv):
    gains_ref, w_ref, cos_ref, sin_ref = refs[count : count + 4]
    h_ref, q_ref, kx_ref, vx_ref, kt_ref, vt_ref, gain_ref = refs[-7:]

    @pl.when(pl.program_id(0) == 0)
    def _():
        gain_ref[...] = gains_ref[...].astype(F32).T[:8]

    which = pl.program_id(0) // steps
    tokens = refs[0][...]
    for block in range(1, count):
        tokens = jnp.where(which == block, refs[block][...], tokens)
    normed, _ = normalize(tokens.astype(F32))
    low = (normed * gain_ref[0:1, :]).astype(BF16)
    h_ref[...] = low
    pre = dot(low, w_ref[...])
    cosine, sine = cos_ref[...], sin_ref[...]
    rows = pre.shape[0]
    lane = lax.broadcasted_iota(jnp.int32, (rows, LANES), 1)
    chunks = []
    for chunk in range(pre.shape[1] // LANES):
        part = pre[:, chunk * LANES : (chunk + 1) * LANES]
        turned = part * cosine + swap_halves(part) * sine
        first = 2 * chunk
        if first + 1 < heads + kv:
            chunks.append(turned)
        elif first < heads + kv:
            chunks.append(jnp.where(lane < HD, turned, part))
        else:
            chunks.append(part)
        if first < heads:
            q_ref[:, chunk * LANES : (chunk + 1) * LANES] = (
                chunks[chunk] * (1.0 / math.sqrt(HD))
            ).astype(BF16)
    flipped = {}
    for head in range(2 * kv):
        place = heads + head
        part = chunks[place // 2]
        moved = pltpu.roll(part, HD, 1)
        wide = [part, moved] if place % 2 == 0 else [moved, part]
        out = kx_ref if head < kv else vx_ref
        out[head % kv, 0] = jnp.where(lane < HD, wide[0], 0.0).astype(BF16)
        out[head % kv, 1] = jnp.where(lane < HD, 0.0, wide[1]).astype(BF16)
        if place // 2 not in flipped:
            flipped[place // 2] = part.T
        turn = flipped[place // 2][(place % 2) * HD : (place % 2 + 1) * HD]
        out_t = kt_ref if head < kv else vt_ref
        out_t[(head % kv) * HD : (head % kv + 1) * HD, :] = turn.astype(BF16)


def project(slots, blocks, bundle, cosine, sine, heads, kv, length):
    rows, width = blocks[0].shape
    count = len(blocks)
    tile = min(256, rows)
    steps = rows // tile
    columns = (heads + 2 * kv) * HD

    def at(i, slot):
        return slot[i // steps] * steps + i % steps

    shapes = [
        jax.ShapeDtypeStruct((length, width), BF16),
        jax.ShapeDtypeStruct((length, heads * HD), BF16),
        jax.ShapeDtypeStruct((kv, 2, length, LANES), BF16),
        jax.ShapeDtypeStruct((kv, 2, length, LANES), BF16),
        jax.ShapeDtypeStruct((kv * HD, length), BF16),
        jax.ShapeDtypeStruct((kv * HD, length), BF16),
        jax.ShapeDtypeStruct((8, width), F32),
    ]
    out_specs = [
        pl.BlockSpec((tile, width), lambda i, s: (at(i, s), 0)),
        pl.BlockSpec((tile, heads * HD), lambda i, s: (at(i, s), 0)),
        pl.BlockSpec((kv, 2, tile, LANES), lambda i, s: (0, 0, at(i, s), 0)),
        pl.BlockSpec((kv, 2, tile, LANES), lambda i, s: (0, 0, at(i, s), 0)),
        pl.BlockSpec((kv * HD, tile), lambda i, s: (0, at(i, s))),
        pl.BlockSpec((kv * HD, tile), lambda i, s: (0, at(i, s))),
        pl.BlockSpec((8, width), lambda i, s: (0, 0)),
    ]
    in_specs = [
        pl.BlockSpec((tile, width), lambda i, s, b=block: (jnp.clip(i - b * steps, 0, steps - 1), 0))
        for block in range(count)
    ]
    in_specs += [
        pl.BlockSpec((width, LANES), lambda i, s: (0, columns // LANES)),
        pl.BlockSpec((width, columns), lambda i, s: (0, 0)),
        pl.BlockSpec((tile, LANES), lambda i, s: (at(i, s), 0)),
        pl.BlockSpec((tile, LANES), lambda i, s: (at(i, s), 0)),
    ]
    operands = [jnp.stack(slots), *blocks, bundle, bundle, cosine, sine]
    return pl.pallas_call(
        functools.partial(
            project_kernel, count=count, steps=steps, heads=heads, kv=kv
        ),
        grid_spec=pltpu.PrefetchScalarGridSpec(
            num_scalar_prefetch=1,
            grid=(count * steps,),
            in_specs=in_specs,
            out_specs=out_specs,
        ),
        out_shape=shapes,
        compiler_params=limit(52),
        cost_estimate=declared(2 * count * rows * width * columns),
    )(*operands)


def feed_kernel(*refs, count):
    tokens = refs[:count]
    gate_ref, up_ref = refs[count : count + 2]
    hidden_ref, silu_ref, slope_ref, h_out = refs[-4:]
    rows = tokens[0].shape[0]
    wide = h_out.shape[1]
    tile = min(256, gate_ref.shape[1])
    lanes = pl.ds(pl.multiple_of(pl.program_id(0) * wide, wide), wide)
    for block in range(count):
        h_out[block * rows : (block + 1) * rows, :] = tokens[block][:, lanes]
    for part in range(gate_ref.shape[1] // tile):
        columns = slice(part * tile, (part + 1) * tile)
        for block in range(count):
            where = slice(block * rows, (block + 1) * rows)
            gate = dot(tokens[block][...], gate_ref[:, columns])
            up = dot(tokens[block][...], up_ref[:, columns])
            sigmoid = 0.5 * jnp.tanh(0.5 * gate) + 0.5
            silu = gate * sigmoid
            hidden_ref[where, columns] = (silu * up).astype(BF16)
            silu_ref[where, columns] = silu.astype(BF16)
            slope_ref[where, columns] = (up * (sigmoid + silu * (1.0 - sigmoid))).astype(BF16)


def feed_back_kernel(*refs, count):
    grads = refs[:count]
    down_ref, silu_ref, slope_ref = refs[count : count + 3]
    dgate_ref, dup_ref = refs[-2:]
    rows = grads[0].shape[0]
    for block in range(count):
        where = slice(block * rows, (block + 1) * rows)
        dhidden = dot(grads[block][...], down_ref[...])
        dup_ref[where, :] = (dhidden * silu_ref[where, :].astype(F32)).astype(BF16)
        dgate_ref[where, :] = (dhidden * slope_ref[where, :].astype(F32)).astype(BF16)


def feed(kernel, place, blocks, tokens, weights, places, kept, units, outs, copy, tile, prev, others):
    rows, width = tokens[0].shape
    count = len(tokens)
    steps = max(units // tile, 1)
    tile, wide = units // steps, width // steps
    shapes = [jax.ShapeDtypeStruct((blocks * rows, units), BF16)] * outs
    in_specs = [pl.BlockSpec((rows, width), lambda i: (0, 0), pipeline_mode=pl.Buffered(1))] * count
    in_specs += [
        pl.BlockSpec((width, tile), lambda i, w=which: (0, w * steps + i)) for which in places
    ]
    cell = pl.BlockSpec((count * rows, tile), lambda i: (place, i))
    in_specs += [cell] * len(kept)
    out_specs = [cell] * outs
    if copy:
        shapes.append(jax.ShapeDtypeStruct((blocks * rows, width), BF16))
        out_specs.append(pl.BlockSpec((count * rows, wide), lambda i: (place, i)))
    operands = [*tokens, *weights, *kept]
    aliases = {}
    if prev is not None:
        for index, array in enumerate(prev):
            aliases[len(operands)] = index
            operands.append(array)
            in_specs.append(ANYWHERE)
    operands += others
    in_specs += [ANYWHERE] * len(others)
    return pl.pallas_call(
        functools.partial(kernel, count=count),
        grid=(steps,),
        in_specs=in_specs,
        out_specs=out_specs,
        out_shape=shapes,
        input_output_aliases=aliases,
        compiler_params=limit(52),
        cost_estimate=declared(2 * len(weights) * count * rows * width * units),
    )(*operands)


def back_kernel(slot_ref, *refs, count, terms, added):
    outs = refs[-count:]
    weights = refs[count * terms : (count + 1) * terms]
    into = list(refs[(count + 1) * terms :])
    for block in range(count):
        value = dot_cols(refs[block * terms][...], weights[0][...])
        for term in range(1, terms):
            value = value + dot_cols(refs[block * terms + term][...], weights[term][...])
        if added[block] is None:
            outs[block][...] = value.astype(BF16)
            continue
        half = value.shape[0] // 2
        extra = into.pop(0)[...].astype(F32)
        top, bottom = value[:half], value[half:]
        if added[block]:
            top = top + extra
        else:
            bottom = bottom + extra
        outs[block][:half, :] = top.astype(BF16)
        outs[block][half:, :] = bottom.astype(BF16)


def back(slots, rows, lefts, weights, places, into=None, others=()):
    depth = lefts[0].shape[1]
    width = weights[0].shape[0]
    tile = min(512, width)
    terms, count = len(lefts), len(slots)
    into = into or [None] * count
    in_specs, operands = [], [jnp.stack([jnp.asarray(slot, jnp.int32) for slot in slots])]
    for block in range(count):
        in_specs += [pl.BlockSpec((rows, depth), lambda i, s, b=block: (s[b], 0))] * terms
        operands += lefts
    in_specs += [pl.BlockSpec((tile, depth), lambda i, s, p=place: (i, p)) for place in places]
    operands += weights
    for extra in into:
        if extra is not None:
            in_specs.append(pl.BlockSpec((rows // 2, tile), lambda i, s: (0, i)))
            operands.append(extra[0])
    operands += others
    in_specs += [ANYWHERE] * len(others)
    return pl.pallas_call(
        functools.partial(
            back_kernel,
            count=count,
            terms=terms,
            added=[None if extra is None else extra[1] for extra in into],
        ),
        grid_spec=pltpu.PrefetchScalarGridSpec(
            num_scalar_prefetch=1,
            grid=(width // tile,),
            in_specs=in_specs,
            out_specs=[pl.BlockSpec((rows, tile), lambda i, s: (0, i))] * count,
        ),
        out_shape=[jax.ShapeDtypeStruct((rows, width), BF16)] * count,
        compiler_params=limit(52),
        cost_estimate=declared(2 * count * terms * rows * width * depth),
    )(*operands)


def weigh_kernel(left_ref, right_ref, *rest):
    out_ref, turned_ref = rest[-2:]

    @pl.when(pl.program_id(1) == 0)
    def _():
        turned_ref[...] = left_ref[...].T

    out_ref[...] = dot(turned_ref[...], right_ref[...]).astype(BF16)


def weigh(left, right, others=()):
    tokens, width = left.shape
    columns = right.shape[1]
    tall, wide = min(512, width), min(1024, columns)
    return pl.pallas_call(
        weigh_kernel,
        grid=(width // tall, columns // wide),
        in_specs=[
            pl.BlockSpec((tokens, tall), lambda i, j: (0, i)),
            pl.BlockSpec((tokens, wide), lambda i, j: (0, j)),
        ]
        + [ANYWHERE] * len(others),
        out_specs=pl.BlockSpec((tall, wide), lambda i, j: (i, j)),
        out_shape=jax.ShapeDtypeStruct((width, columns), BF16),
        scratch_shapes=[pltpu.VMEM((tall, tokens), BF16)],
        compiler_params=limit(52),
        cost_estimate=declared(2 * tokens * width * columns),
    )(left, right, *others)


def settle_kernel(*refs, count):
    pieces, weights = refs[:count], refs[count : 2 * count]
    x_ref, gains_ref = refs[2 * count : 2 * count + 2]
    stream_ref, h_ref = refs[-2:]
    stream = x_ref[...].astype(F32)
    for piece, weight in zip(pieces, weights):
        stream = stream + dot_cols(piece[...], weight[...])
    stream_ref[...] = stream
    normed, _ = normalize(stream)
    h_ref[...] = (normed * gains_ref[1:2, :]).astype(BF16)


def settle(own, place, pieces, weights, tokens, gains, others=()):
    rows, width = tokens.shape
    depth = weights[0].shape[1]
    tile = min(256, rows)
    steps = rows // tile
    wide = pl.BlockSpec((tile, width), lambda i: (i, 0))
    piece = pl.BlockSpec((tile, depth), lambda i: (i, 0))
    weight = pl.BlockSpec((width, depth), lambda i: (0, 0), pipeline_mode=pl.Buffered(1))
    return pl.pallas_call(
        functools.partial(settle_kernel, count=len(weights)),
        grid=(steps,),
        in_specs=[pl.BlockSpec((tile, depth), lambda i: (place * steps + i, 0))]
        + [piece] * len(pieces)
        + [weight] * len(weights)
        + [wide, pl.BlockSpec((8, width), lambda i: (0, 0))]
        + [ANYWHERE] * len(others),
        out_specs=[wide, wide],
        out_shape=[
            jax.ShapeDtypeStruct((rows, width), F32),
            jax.ShapeDtypeStruct((rows, width), BF16),
        ],
        compiler_params=limit(52),
        cost_estimate=declared(2 * len(weights) * rows * width * depth),
    )(own, *pieces, *weights, tokens, gains, *others)


def norm_back(grad_in, stream, gain):
    normed, scale_r = normalize(stream)
    scaled = grad_in * gain
    return scale_r * (scaled - normed * jnp.mean(scaled * normed, axis=-1, keepdims=True))


def settle_back_kernel(*refs, parts, count):
    terms, weights = refs[:parts], refs[parts : parts + count]
    grad_ref, stream_ref, gains_ref, out_ref, low_ref = refs[parts + count : parts + count + 5]
    pieces = refs[parts + count + 5 :]
    grad_in = terms[0][...].astype(F32)
    for term in terms[1:]:
        grad_in = grad_in + term[...].astype(F32)
    grad = grad_ref[...].astype(F32) + norm_back(grad_in, stream_ref[...], gains_ref[1:2, :])
    out_ref[...] = grad
    low = grad.astype(BF16)
    low_ref[...] = low
    for piece, weight in zip(pieces, weights):
        piece[...] = dot(low, weight[...]).astype(BF16)


def settle_back(terms, weights, grad, stream, gains):
    rows, width = grad.shape
    depth = weights[0].shape[1]
    tile = min(256, rows)
    wide = pl.BlockSpec((tile, width), lambda i: (i, 0))
    weight = pl.BlockSpec((width, depth), lambda i: (0, 0), pipeline_mode=pl.Buffered(1))
    return pl.pallas_call(
        functools.partial(settle_back_kernel, parts=len(terms), count=len(weights)),
        grid=(rows // tile,),
        in_specs=[wide] * len(terms)
        + [weight] * len(weights)
        + [wide, wide, pl.BlockSpec((8, width), lambda i: (0, 0))],
        out_specs=[wide, wide] + [pl.BlockSpec((tile, depth), lambda i: (i, 0))] * len(weights),
        out_shape=[
            jax.ShapeDtypeStruct((rows, width), F32),
            jax.ShapeDtypeStruct((rows, width), BF16),
        ]
        + [jax.ShapeDtypeStruct((rows, depth), BF16)] * len(weights),
        compiler_params=limit(52),
        cost_estimate=declared(2 * len(weights) * rows * width * depth),
    )(*terms, *weights, grad, stream, gains)


def causal(block):
    keys = lax.broadcasted_iota(jnp.int32, (block, block), 0)
    return keys <= lax.broadcasted_iota(jnp.int32, (block, block), 1)


def first_block(bound, offset, block):
    return jnp.where(offset >= bound, lax.div(bound, jnp.int32(block)), 0)


def attend_kernel(order_ref, q_ref, kx_ref, vt_ref, *rest, block):
    out_ref, lse_ref, top_ref, acc_ref = rest[-4:]
    kv = kx_ref.shape[0]
    per = q_ref.shape[1] // LANES // kv
    bound = order_ref[0]
    ones = jnp.ones((16, block), BF16)
    for group in range(kv):

        def q_step(turn, _):
            index = order_ref[1 + turn]
            offset = pl.multiple_of(index * block, block)
            into = pl.ds(pl.multiple_of(turn * block, block), block)
            top_ref[...] = jnp.full(top_ref.shape, MASKED, F32)
            acc_ref[...] = jnp.zeros(acc_ref.shape, F32)

            def tile(step, diagonal):
                keys = pl.ds(pl.multiple_of(step * block, block), block)
                value_t = jnp.concatenate(
                    [vt_ref[group * HD : (group + 1) * HD, keys], ones], axis=0
                )
                for head in range(2 * per):
                    column = (group * per + head // 2) * LANES
                    query = q_ref[pl.ds(offset, block), column : column + LANES]
                    scores = dot_cols(kx_ref[group, head % 2, keys, :], query)
                    if diagonal:
                        scores = jnp.where(causal(block), scores, MASKED)
                    old = top_ref[head, 0:1, :]
                    top = jnp.maximum(old, jnp.max(scores, axis=0, keepdims=True))
                    powered = jnp.exp(scores - top).astype(BF16)
                    acc_ref[head] = acc_ref[head] * jnp.exp(old - top) + dot(value_t, powered)
                    top_ref[head, 0:1, :] = top

            def full_tile(step, carry):
                tile(step, False)
                return carry

            lax.fori_loop(first_block(bound, offset, block), index, full_tile, 0)
            tile(index, True)
            for pair in range(per):
                both = []
                for head in (2 * pair, 2 * pair + 1):
                    total = acc_ref[head, HD : HD + 1, :]
                    both.append(acc_ref[head, :HD, :] / total)
                    place = group * 2 * per + head
                    lse_ref[place : place + 1, into] = top_ref[
                        head, 0:1, :
                    ] + jnp.log(total)
                column = (group * per + pair) * LANES
                out_ref[into, column : column + LANES] = (
                    jnp.concatenate(both, axis=0).T.astype(BF16)
                )
            return _

        lax.fori_loop(0, out_ref.shape[0] // block, q_step, 0)


def attend(bound, order, queries, kx, vt, block, others=()):
    length, width = queries.shape
    heads = width // HD
    kv = kx.shape[0]
    per = heads // kv
    count = len(order)
    cells = heads * count * block * (length + block) // 2
    vmem = pl.BlockSpec(memory_space=pltpu.VMEM)
    return pl.pallas_call(
        functools.partial(attend_kernel, block=block),
        in_specs=[pl.BlockSpec(memory_space=pltpu.SMEM), vmem, vmem, vmem] + [ANYWHERE] * len(others),
        out_specs=[vmem, vmem],
        out_shape=[
            jax.ShapeDtypeStruct((count * block, width), BF16),
            jax.ShapeDtypeStruct((heads, count * block), F32),
        ],
        scratch_shapes=[
            pltpu.VMEM((per, 8, block), F32),
            pltpu.VMEM((per, HD + 16, block), F32),
        ],
        compiler_params=limit(52),
        cost_estimate=declared(2 * 4 * HD * 4 * cells, 16),
    )(jnp.stack([bound, *order]), queries, kx, vt, *others)


def attend_back_kernel(
    order_ref, q_ref, kx_ref, vx_ref, kt_ref, lse_ref, out_ref, grad_ref, cos_ref, sin_ref,
    *rest, block
):
    dqkv_ref, dk_ref, dv_ref, dq_ref = rest[-4:]
    length = q_ref.shape[0]
    kv = kx_ref.shape[0]
    heads = q_ref.shape[1] // HD
    per = heads // 2 // kv
    bound = order_ref[0]
    dk_ref[...] = jnp.zeros(dk_ref.shape, F32)
    dv_ref[...] = jnp.zeros(dv_ref.shape, F32)
    lane = lax.broadcasted_iota(jnp.int32, (8, LANES), 1)
    row = lax.broadcasted_iota(jnp.int32, (8, LANES), 0)
    chosen = ((lane // HD) == row).astype(F32)

    def turn_back(values, rows):
        return values * cos_ref[rows, :] - swap_halves(values) * sin_ref[rows, :]

    for group in range(kv):

        def q_step(turn, _):
            index = order_ref[1 + turn]
            offset = pl.multiple_of(index * block, block)
            rows = pl.ds(offset, block)
            given = pl.ds(pl.multiple_of(turn * block, block), block)
            dq_ref[...] = jnp.zeros(dq_ref.shape, F32)
            deltas = []
            for pair in range(per):
                column = (group * per + pair) * LANES
                product = grad_ref[given, column : column + LANES].astype(F32) * out_ref[
                    given, column : column + LANES
                ].astype(F32)
                deltas.append(
                    lax.dot_general(
                        chosen, product, OVER_COLS, precision=lax.Precision.HIGHEST,
                        preferred_element_type=F32,
                    )
                )

            def tile(step, diagonal):
                keys = pl.ds(pl.multiple_of(step * block, block), block)
                key_t = kt_ref[group * HD : (group + 1) * HD, keys]
                for parity in range(2):
                    key_add, value_add = 0.0, 0.0
                    for pair in range(per):
                        head = 2 * pair + parity
                        place = group * 2 * per + head
                        column = (group * per + pair) * LANES
                        query = q_ref[rows, column : column + LANES]
                        grad = grad_ref[given, column : column + LANES]
                        scores = dot_cols(kx_ref[group, parity, keys, :], query)
                        if diagonal:
                            scores = jnp.where(causal(block), scores, MASKED)
                        probs = jnp.exp(scores - lse_ref[place : place + 1, given])
                        dprobs = dot_cols(vx_ref[group, parity, keys, :], grad)
                        dscores = (probs * (dprobs - deltas[pair][parity : parity + 1])).astype(BF16)
                        value_add = value_add + dot(probs.astype(BF16), grad)
                        key_add = key_add + dot(dscores, query)
                        dq_ref[head * HD : (head + 1) * HD, :] += dot(key_t, dscores)
                    dk_ref[group, parity, keys, :] += key_add
                    dv_ref[group, parity, keys, :] += value_add

            def full_tile(step, carry):
                tile(step, False)
                return carry

            lax.fori_loop(first_block(bound, offset, block), index, full_tile, 0)
            tile(index, True)
            for pair in range(per):
                column = (group * per + pair) * LANES
                grad_q = dq_ref[pair * LANES : (pair + 1) * LANES, :].T * (1.0 / math.sqrt(HD))
                dqkv_ref[rows, column : column + LANES] = turn_back(grad_q, rows).astype(BF16)
            return _

        lax.fori_loop(0, length // block, q_step, 0)

    def finish(index, _):
        rows = pl.ds(pl.multiple_of(index * block, block), block)
        lanes = lax.broadcasted_iota(jnp.int32, (block, LANES), 1)

        def placed(part, half):
            ref = dk_ref if part < kv else dv_ref
            even, odd = ref[part % kv, 0, rows, :], ref[part % kv, 1, rows, :]
            return even + pltpu.roll(odd, HD, 1) if half == 0 else pltpu.roll(even, HD, 1) + odd

        for chunk in range(kv):
            values = jnp.where(lanes < HD, placed(2 * chunk, 0), placed(2 * chunk + 1, 1))
            if 2 * chunk + 1 < kv:
                values = turn_back(values, rows)
            elif 2 * chunk < kv:
                values = jnp.where(lanes < HD, turn_back(values, rows), values)
            column = heads * HD + chunk * LANES
            dqkv_ref[rows, column : column + LANES] = values.astype(BF16)
        return _

    lax.fori_loop(0, length // block, finish, 0)


def attend_back(
    bound, order, queries, kx, vx, kt, log_sums, attended, grad, cosine, sine, block, others
):
    length, width = queries.shape
    heads = width // HD
    kv = kx.shape[0]
    cells = heads * length * (length + block) // 2
    vmem = pl.BlockSpec(memory_space=pltpu.VMEM)
    return pl.pallas_call(
        functools.partial(attend_back_kernel, block=block),
        in_specs=[pl.BlockSpec(memory_space=pltpu.SMEM)] + [vmem] * 9 + [ANYWHERE] * len(others),
        out_specs=vmem,
        out_shape=jax.ShapeDtypeStruct((length, width + 2 * kv * HD), BF16),
        scratch_shapes=[
            pltpu.VMEM((kv, 2, length, LANES), F32),
            pltpu.VMEM((kv, 2, length, LANES), F32),
            pltpu.VMEM((heads // kv * HD, block), F32),
        ],
        compiler_params=limit(52),
        cost_estimate=declared(2 * 10 * HD * 4 * cells),
    )(jnp.stack([bound, *order]), queries, kx, vx, kt, log_sums, attended, grad, cosine, sine, *others)


def local(
    inputs,
    segment_ids,
    attn_gain,
    query_weight,
    key_weight,
    value_weight,
    output_weight,
    mlp_gain,
    gate_weight,
    up_weight,
    down_weight,
    cotangent,
    *,
    sizes,
):
    rows = inputs.shape[0]
    length = segment_ids.shape[0]
    query_cols = query_weight.shape[1]
    key_cols = key_weight.shape[1]
    heads, kv = query_cols // HD, key_cols // HD
    columns = query_cols + 2 * key_cols
    slots = slots_of(sizes["tensor"])
    tensor = sizes["tensor"]
    space = (-columns) % query_cols or query_cols
    gains = jnp.pad(jnp.stack([attn_gain, mlp_gain], axis=1), ((0, 0), (0, space - 2)))
    bundle = lax.all_gather(
        jnp.concatenate([query_weight, key_weight, value_weight, gains, output_weight.T], axis=1),
        "dp", axis=0, tiled=True,
    )
    out_own = bundle[:, columns + space :]
    hop = first_hop(inputs, tensor)
    gate_up = lax.all_gather(
        hold(jnp.concatenate([gate_weight, up_weight], axis=1), *(hop or ())),
        "dp", axis=0, tiled=True,
    )

    bound, cosine, sine = rope_tables(segment_ids)
    blocks = second_hop(inputs, hop, tensor)
    stream = inputs.astype(F32)
    arrays = project(slots, blocks, bundle, cosine, sine, heads, kv, length)
    block_a, queries, kx, vx, kt, vt, gains = arrays
    down_t = lax.all_gather(hold(down_weight.T, queries), "dp", axis=0, tiled=True)

    if tensor == 4:
        out_hop = first_hop(hold(out_own, blocks[3]), tensor)
        far, far_sums = attend(bound, slots[3:], queries, kx, vt, rows)
        halves = hold_halves(out_hop, far)
        out_all = second_hop(out_own, out_hop, tensor, halves)
        from_far = lax.ppermute(far, "tensor", pairs(tensor, 3))
        order = [slots[1], slots[2], slots[0], slots[3]]
        near, near_sums = attend(bound, order[:3], queries, kx, vt, rows, halves)
        from_one = lax.ppermute(near[:rows], "tensor", pairs(tensor, 1))
        from_two = lax.ppermute(near[rows : 2 * rows], "tensor", pairs(tensor, 2))
        cotangent_sent = hold(cotangent, near)
        cotangent_hop = first_hop(cotangent_sent, tensor)
        stream_one, low_m = settle(
            near, 2, [from_one, from_two, from_far], out_all, inputs, gains, [cotangent_sent]
        )
        attended = jnp.concatenate([near, far], axis=0)
        log_sums = jnp.concatenate([near_sums, far_sums], axis=1)
    else:
        order = slots
        out_all = gather(out_own, tensor)
        attended, log_sums = attend(bound, order, queries, kx, vt, rows)
        given = trade([attended[k * rows : (k + 1) * rows] for k in range(tensor)], tensor)
        stream_one, low_m = settle(given[0], 0, given[1:], out_all, inputs, gains)
        cotangent_sent = cotangent
    parts_m = [low_m]
    units = gate_weight.shape[1]

    def feed_at(place, wanted, fed, others=()):
        return feed(
            feed_kernel, place, tensor, [parts_m[k] for k in wanted], [gate_up] * 2, [0, 1], [],
            units, 3, True, 512, fed, others,
        )

    def feed_back_at(place, wanted, fed, others=()):
        return feed(
            feed_back_kernel, place, tensor, [grad_parts[k] for k in wanted], [down_t], [0],
            [silu, slope], units, 2, False, 256, fed, others,
        )

    def back_m(places, fed, into=None, others=()):
        return back(places, rows, fed[:2], [gate_up] * 2, [0, 1], into, others)

    def back_out(places, into=None, others=()):
        return back(places, rows, [hidden], [down_t], [0], into, others)

    def reduce_rows(term, *others):
        if others and tensor == 4:
            term = hold(term, *others)
        return lax.psum_scatter(term, "dp", scatter_dimension=0, tiled=True)

    if tensor == 4:
        hop = first_hop(parts_m[0], tensor)
        fed = feed_at(3, [0], None)
        halves = hold_halves(hop, fed[0])
        parts_m = second_hop(parts_m[0], hop, tensor, halves)
        fed = feed_at(0, [1, 2], fed, halves)
        halves = hold_halves(cotangent_hop, fed[0])
        grad_parts = second_hop(cotangent_sent, cotangent_hop, tensor, halves)
        fed = feed_at(2, [3], fed, halves)
    else:
        grad_parts = second_hop(cotangent_sent, None, tensor)
        parts_m = gather(parts_m[0], tensor)
        fed = None
        for place in range(tensor):
            fed = feed_at(place, [place], fed)
    hidden, silu, slope, block_m = fed
    if tensor == 4:
        grad_block = jnp.concatenate([grad_parts[k] for k in (1, 2, 3, 0)], axis=0)
        (three_out,) = back_out([2], None, [fed[0]])
        out_one, out_two = out_halves = send_half(three_out, tensor)
        down_t_wgrad = weigh(grad_block, hidden, [three_out])
        one_out, two_out, own_out = back_out(
            [0, 1, 3], [(out_one, False), (out_two, True), None]
        )
        out_parts = [
            own_out,
            lax.ppermute(one_out, "tensor", pairs(tensor, 1)),
            lax.ppermute(two_out, "tensor", pairs(tensor, 2)),
        ]
        fed = feed_back_at(2, [3], None, [one_out])
        (three_m,) = back_m([2], fed)
        m_one, m_two = send_half(three_m, tensor)
        fed = feed_back_at(0, [1, 2], fed, [three_m])
        fed = feed_back_at(3, [0], fed)
        one_m, two_m = back_m([0, 1], fed, [(m_one, False), (m_two, True)], out_parts[1:])
        (own_m,) = back_m([3], fed, None, [one_m])
        gate_wgrad = weigh(block_m, fed[0], [own_m])
        grad_m_parts = [
            own_m,
            lax.ppermute(one_m, "tensor", pairs(tensor, 1)),
            lax.ppermute(two_m, "tensor", pairs(tensor, 2)),
        ]
    else:
        down_t_wgrad = weigh(jnp.concatenate(grad_parts, axis=0), hidden)
        fed = None
        for place in range(tensor):
            fed = feed_back_at(place, [place], fed)
        grad_m_parts = sum_whole(back_m(list(range(tensor)), fed))
        gate_wgrad = weigh(block_m, fed[0])
        out_parts = sum_whole(back_out(list(range(tensor))))
    layer_out = (stream_one + total(out_parts)).astype(BF16)
    if tensor != 4:
        out_halves = ()
    down_t_low = reduce_rows(down_t_wgrad, *out_halves)
    gate_low = reduce_rows(gate_wgrad, *grad_m_parts[1:])

    grad_stream_one, grad_stream_low, *pieces = settle_back(
        grad_m_parts, out_all, cotangent, stream_one, gains
    )
    given = trade(pieces, tensor)
    up_wgrad = weigh(block_m, fed[1], [grad_stream_low])
    places = [1, 2, 0, 3] if tensor == 4 else list(range(tensor))
    grad_attended = jnp.concatenate([given[k] for k in places], axis=0)
    up_wgrad = hold(up_wgrad, grad_attended)
    up_low = reduce_rows(up_wgrad)
    grad_qkv = attend_back(
        bound, order, queries, kx, vx, kt, log_sums, attended, grad_attended, cosine, sine, rows,
        [down_t_low, up_wgrad],
    )
    if tensor == 4:
        sent = hold(grad_stream_low, grad_attended)
        grad_stream_parts = trade([sent] * 4, tensor)
    else:
        grad_stream_parts = gather(grad_stream_low, tensor)
    grad_stream_block = jnp.concatenate([grad_stream_parts[k] for k in places], axis=0)

    def back_a(places, others=()):
        return back(places, rows, [grad_qkv], [bundle], [0], None, others)

    if tensor == 4:
        (three,) = back_a(slots[3:], [gate_low])
        halves = send_half(three, tensor)
        block_a = hold(block_a, three)
        grad_stream_block = hold(grad_stream_block, three)
    qkv_wgrad = weigh(block_a, grad_qkv)
    out_t_wgrad = weigh(grad_stream_block, attended)
    attention_wgrad = jnp.concatenate([qkv_wgrad, out_t_wgrad], axis=1)
    gate_sum, up_sum, down_t_sum = [low.astype(F32) for low in (gate_low, up_low, down_t_low)]
    attention_sum = reduce_rows(attention_wgrad).astype(F32)
    if tensor == 4:
        one, two, own = back_a([slots[1], slots[2], slots[0]], [three])
        grad_a_parts = [own, *send_whole(one, two, halves, tensor)]
    else:
        grad_a_parts = sum_whole(back_a(slots))
    grad_normed_a = total(grad_a_parts)

    def gain_term(gain, weights):
        term = sum(jnp.sum(weight.astype(F32) * grad, axis=1) for weight, grad in weights)
        return term / gain.astype(F32)

    query_sum = attention_sum[:, :query_cols]
    key_sum = attention_sum[:, query_cols : query_cols + key_cols]
    value_sum = attention_sum[:, query_cols + key_cols : columns]
    gain_terms = [
        gain_term(
            attn_gain, [(query_weight, query_sum), (key_weight, key_sum), (value_weight, value_sum)]
        ),
        gain_term(mlp_gain, [(gate_weight, gate_sum), (up_weight, up_sum)]),
    ]
    gain_mine = sum_tensor(jnp.stack(gain_terms), tensor)
    input_grad = (grad_stream_one + norm_back(grad_normed_a, stream, gains[0:1])).astype(BF16)
    return (
        layer_out,
        input_grad,
        gain_mine[0],
        query_sum,
        key_sum,
        value_sum,
        attention_sum[:, columns:].T,
        gain_mine[1],
        gate_sum,
        up_sum,
        down_t_sum.T,
    )


def solution(mesh):
    tokens = P(("dp", "tensor"), None)
    in_specs = (
        tokens,
        P("dp"),
        P("dp"),
        P("dp", "tensor"),
        P("dp", "tensor"),
        P("dp", "tensor"),
        P("tensor", "dp"),
        P("dp"),
        P("dp", "tensor"),
        P("dp", "tensor"),
        P("tensor", "dp"),
        tokens,
    )
    out_specs = (
        tokens,
        tokens,
        P("dp"),
        P("dp", "tensor"),
        P("dp", "tensor"),
        P("dp", "tensor"),
        P("tensor", "dp"),
        P("dp"),
        P("dp", "tensor"),
        P("dp", "tensor"),
        P("tensor", "dp"),
    )
    return jax.shard_map(
        functools.partial(local, sizes={axis: mesh.shape[axis] for axis in ("tensor", "dp")}),
        mesh=mesh, in_specs=in_specs, out_specs=out_specs, check_vma=False,
    )
```

```python
import functools
import math

import jax
import jax.numpy as jnp
from jax import lax
from jax.experimental import pallas as pl
from jax.experimental.pallas import tpu as pltpu
from jax.sharding import PartitionSpec as P

HD = 64
LANES = 128
EPSILON = 1e-05
ROPE_BASE = 500000.0
MASKED = -1e30
OVER_ROWS = (((0,), (0,)), ((), ()))
OVER_COLS = (((1,), (1,)), ((), ()))


def limit(size):
    return pltpu.CompilerParams(vmem_limit_bytes=size * 2**20)


SHORT = 0.0625


def declared(flops, scale=SHORT):
    return pl.CostEstimate(flops=int(flops * scale), bytes_accessed=0, transcendentals=0)


F32 = jnp.float32
BF16 = jnp.bfloat16


def dot_cols(left, right):
    return lax.dot_general(left, right, OVER_COLS, preferred_element_type=F32)


def dot_rows(left, right):
    return lax.dot_general(left, right, OVER_ROWS, preferred_element_type=F32)


def dot(left, right):
    return jnp.dot(left, right, preferred_element_type=F32)


def pairs(size, bit):
    return [(index, index ^ bit) for index in range(size)]


def slots_of(size):
    if size == 4:
        return [lax.axis_index("tensor") ^ step for step in range(size)]
    return [jnp.int32(step) for step in range(size)]


ANYWHERE = pl.BlockSpec(memory_space=pl.ANY)


def nothing_kernel(*refs):
    pass


def hold(value, *others):
    return pl.pallas_call(
        nothing_kernel,
        in_specs=[ANYWHERE] * (1 + len(others)),
        out_specs=ANYWHERE,
        out_shape=jax.ShapeDtypeStruct(value.shape, value.dtype),
        input_output_aliases={0: 0},
        cost_estimate=declared(0),
    )(value, *others)


def first_hop(shard, size):
    if size != 4:
        return None
    return [lax.ppermute(shard, "tensor", pairs(size, bit)) for bit in (1, 2)]


def hold_halves(hop, *others):
    one, two = hop
    half = one.shape[0] // 2
    return hold(one[:half], *others), hold(two[half:], *others)


def second_hop(shard, hop, size, halves=None):
    if size != 4:
        whole = lax.all_gather(shard, "tensor", axis=0)
        return [whole[step] for step in range(size)]
    half = shard.shape[0] // 2
    one, two = hop
    upper, lower = halves or (one[:half], two[half:])
    three_a = lax.ppermute(upper, "tensor", pairs(size, 2))
    three_b = lax.ppermute(lower, "tensor", pairs(size, 1))
    return [shard, one, two, jnp.concatenate([three_a, three_b], axis=0)]


def gather(shard, size):
    return second_hop(shard, first_hop(shard, size), size)


def send_half(three, size):
    half = three.shape[0] // 2
    into_two = lax.ppermute(three[:half], "tensor", pairs(size, 1))
    into_one = lax.ppermute(three[half:], "tensor", pairs(size, 2))
    return into_one, into_two


def send_whole(one, two, into, size):
    into_one, into_two = into
    half = one.shape[0] // 2
    lower = (one[half:].astype(F32) + into_one.astype(F32)).astype(BF16)
    upper = (two[:half].astype(F32) + into_two.astype(F32)).astype(BF16)
    return [
        lax.ppermute(jnp.concatenate([one[:half], lower], axis=0), "tensor", pairs(size, 1)),
        lax.ppermute(jnp.concatenate([upper, two[half:]], axis=0), "tensor", pairs(size, 2)),
    ]


def sum_whole(terms):
    return [
        lax.psum_scatter(
            jnp.concatenate(terms, axis=0), "tensor", scatter_dimension=0, tiled=True
        )
    ]


def trade(pieces, size):
    if size != 4:
        whole = lax.all_to_all(jnp.stack(pieces), "tensor", split_axis=0, concat_axis=0, tiled=True)
        return [whole[step] for step in range(size)]
    return [pieces[0]] + [
        lax.ppermute(pieces[step], "tensor", pairs(size, step)) for step in (1, 2, 3)
    ]


def total(parts):
    return functools.reduce(jnp.add, [part.astype(F32) for part in parts])


def sum_tensor(value, size):
    if size & (size - 1):
        return lax.psum(value, "tensor")
    return value + sum(lax.ppermute(value, "tensor", pairs(size, bit)) for bit in range(1, size))


def rope_tables(segment):
    length = segment.shape[0]
    bound = jnp.sum((segment == 0).astype(jnp.int32))
    place = lax.broadcasted_iota(jnp.int32, (length, LANES), 0)
    place = place - jnp.where(place >= bound, bound, 0)
    lane = lax.broadcasted_iota(jnp.int32, (length, LANES), 1)
    freqs = jnp.exp(
        (lane % (HD // 2)).astype(F32) * (-2.0 * math.log(ROPE_BASE) / HD)
    )
    angles = place.astype(F32) * freqs
    sine = jnp.sin(angles)
    return bound, jnp.cos(angles), jnp.where(lane % HD < HD // 2, -sine, sine)


def swap_halves(values):
    lane = lax.broadcasted_iota(jnp.int32, values.shape, 1)
    after = pltpu.roll(values, LANES - HD // 2, 1)
    before = pltpu.roll(values, HD // 2, 1)
    return jnp.where(lane % HD < HD // 2, after, before)


def normalize(stream):
    scale_r = lax.rsqrt(jnp.mean(stream * stream, axis=-1, keepdims=True) + EPSILON)
    return (stream * scale_r, scale_r)


def project_kernel(slot_ref, *refs, count, steps, heads, kv):
    gains_ref, w_ref, cos_ref, sin_ref = refs[count : count + 4]
    h_ref, q_ref, kx_ref, vx_ref, kt_ref, vt_ref, gain_ref = refs[-7:]

    @pl.when(pl.program_id(0) == 0)
    def _():
        gain_ref[...] = gains_ref[...].astype(F32).T[:8]

    which = pl.program_id(0) // steps
    rows = h_ref.shape[0]
    part_rows = min(256, rows)
    lane = lax.broadcasted_iota(jnp.int32, (part_rows, LANES), 1)
    for start in range(0, rows, part_rows):
        at = slice(start, start + part_rows)
        tokens = refs[0][at, :]
        for block in range(1, count):
            tokens = jnp.where(which == block, refs[block][at, :], tokens)
        normed, _ = normalize(tokens.astype(F32))
        low = (normed * gain_ref[0:1, :]).astype(BF16)
        h_ref[at, :] = low
        pre = dot(low, w_ref[...])
        cosine, sine = cos_ref[at, :], sin_ref[at, :]
        chunks = []
        for chunk in range(pre.shape[1] // LANES):
            columns = slice(chunk * LANES, (chunk + 1) * LANES)
            part = pre[:, columns]
            first = 2 * chunk
            if first < heads + kv:
                turned = part * cosine + swap_halves(part) * sine
                part = turned if first + 1 < heads + kv else jnp.where(lane < HD, turned, part)
            chunks.append(part)
            if first < heads:
                q_ref[at, columns] = (part * (1.0 / math.sqrt(HD))).astype(BF16)
        flipped = {}
        for head in range(2 * kv):
            place = heads + head
            part = chunks[place // 2]
            moved = pltpu.roll(part, HD, 1)
            wide = [part, moved] if place % 2 == 0 else [moved, part]
            out = kx_ref if head < kv else vx_ref
            out[head % kv, 0, at, :] = jnp.where(lane < HD, wide[0], 0.0).astype(BF16)
            out[head % kv, 1, at, :] = jnp.where(lane < HD, 0.0, wide[1]).astype(BF16)
            if place // 2 not in flipped:
                flipped[place // 2] = part.T
            turn = flipped[place // 2][(place % 2) * HD : (place % 2 + 1) * HD]
            out_t = kt_ref if head < kv else vt_ref
            out_t[(head % kv) * HD : (head % kv + 1) * HD, at] = turn.astype(BF16)


def project(slots, blocks, bundle, cosine, sine, heads, kv, length):
    rows, width = blocks[0].shape
    count = len(blocks)
    tile = rows
    steps = rows // tile
    columns = (heads + 2 * kv) * HD

    def at(i, slot):
        return slot[i // steps] * steps + i % steps

    shapes = [
        jax.ShapeDtypeStruct((length, width), BF16),
        jax.ShapeDtypeStruct((length, heads * HD), BF16),
        jax.ShapeDtypeStruct((kv, 2, length, LANES), BF16),
        jax.ShapeDtypeStruct((kv, 2, length, LANES), BF16),
        jax.ShapeDtypeStruct((kv * HD, length), BF16),
        jax.ShapeDtypeStruct((kv * HD, length), BF16),
        jax.ShapeDtypeStruct((8, width), F32),
    ]
    out_specs = [
        pl.BlockSpec((tile, width), lambda i, s: (at(i, s), 0)),
        pl.BlockSpec((tile, heads * HD), lambda i, s: (at(i, s), 0)),
        pl.BlockSpec((kv, 2, tile, LANES), lambda i, s: (0, 0, at(i, s), 0)),
        pl.BlockSpec((kv, 2, tile, LANES), lambda i, s: (0, 0, at(i, s), 0)),
        pl.BlockSpec((kv * HD, tile), lambda i, s: (0, at(i, s))),
        pl.BlockSpec((kv * HD, tile), lambda i, s: (0, at(i, s))),
        pl.BlockSpec((8, width), lambda i, s: (0, 0)),
    ]
    in_specs = [
        pl.BlockSpec((tile, width), lambda i, s, b=block: (jnp.clip(i - b * steps, 0, steps - 1), 0))
        for block in range(count)
    ]
    in_specs += [
        pl.BlockSpec((width, LANES), lambda i, s: (0, columns // LANES)),
        pl.BlockSpec((width, columns), lambda i, s: (0, 0)),
        pl.BlockSpec((tile, LANES), lambda i, s: (at(i, s), 0)),
        pl.BlockSpec((tile, LANES), lambda i, s: (at(i, s), 0)),
    ]
    operands = [jnp.stack(slots), *blocks, bundle, bundle, cosine, sine]
    return pl.pallas_call(
        functools.partial(
            project_kernel, count=count, steps=steps, heads=heads, kv=kv
        ),
        grid_spec=pltpu.PrefetchScalarGridSpec(
            num_scalar_prefetch=1,
            grid=(count * steps,),
            in_specs=in_specs,
            out_specs=out_specs,
        ),
        out_shape=shapes,
        compiler_params=limit(52),
        cost_estimate=declared(2 * count * rows * width * columns),
    )(*operands)


def feed_kernel(*refs, count):
    tokens = refs[:count]
    gate_ref, up_ref = refs[count : count + 2]
    hidden_ref, silu_ref, slope_ref, h_out = refs[-4:]
    rows = tokens[0].shape[0]
    wide = h_out.shape[1]
    tile = min(256, gate_ref.shape[1])
    lanes = pl.ds(pl.multiple_of(pl.program_id(0) * wide, wide), wide)
    for block in range(count):
        h_out[block * rows : (block + 1) * rows, :] = tokens[block][:, lanes]
    for part in range(gate_ref.shape[1] // tile):
        columns = slice(part * tile, (part + 1) * tile)
        for block in range(count):
            where = slice(block * rows, (block + 1) * rows)
            gate = dot(tokens[block][...], gate_ref[:, columns])
            up = dot(tokens[block][...], up_ref[:, columns])
            sigmoid = 0.5 * jnp.tanh(0.5 * gate) + 0.5
            silu = gate * sigmoid
            hidden_ref[where, columns] = (silu * up).astype(BF16)
            silu_ref[where, columns] = silu.astype(BF16)
            slope_ref[where, columns] = (up * (sigmoid + silu * (1.0 - sigmoid))).astype(BF16)


def feed_back_kernel(*refs, count):
    grads = refs[:count]
    down_ref, silu_ref, slope_ref = refs[count : count + 3]
    dgate_ref, dup_ref = refs[-2:]
    rows = grads[0].shape[0]
    for block in range(count):
        where = slice(block * rows, (block + 1) * rows)
        dhidden = dot(grads[block][...], down_ref[...])
        dup_ref[where, :] = (dhidden * silu_ref[where, :].astype(F32)).astype(BF16)
        dgate_ref[where, :] = (dhidden * slope_ref[where, :].astype(F32)).astype(BF16)


def feed(kernel, place, blocks, tokens, weights, places, kept, units, outs, copy, tile, prev, others):
    rows, width = tokens[0].shape
    count = len(tokens)
    steps = max(units // tile, 1)
    tile, wide = units // steps, width // steps
    shapes = [jax.ShapeDtypeStruct((blocks * rows, units), BF16)] * outs
    in_specs = [pl.BlockSpec((rows, width), lambda i: (0, 0), pipeline_mode=pl.Buffered(1))] * count
    in_specs += [
        pl.BlockSpec((width, tile), lambda i, w=which: (0, w * steps + i)) for which in places
    ]
    cell = pl.BlockSpec((count * rows, tile), lambda i: (place, i))
    in_specs += [cell] * len(kept)
    out_specs = [cell] * outs
    if copy:
        shapes.append(jax.ShapeDtypeStruct((blocks * rows, width), BF16))
        out_specs.append(pl.BlockSpec((count * rows, wide), lambda i: (place, i)))
    operands = [*tokens, *weights, *kept]
    aliases = {}
    if prev is not None:
        for index, array in enumerate(prev):
            aliases[len(operands)] = index
            operands.append(array)
            in_specs.append(ANYWHERE)
    operands += others
    in_specs += [ANYWHERE] * len(others)
    return pl.pallas_call(
        functools.partial(kernel, count=count),
        grid=(steps,),
        in_specs=in_specs,
        out_specs=out_specs,
        out_shape=shapes,
        input_output_aliases=aliases,
        compiler_params=limit(52),
        cost_estimate=declared(2 * len(weights) * count * rows * width * units),
    )(*operands)


def back_kernel(slot_ref, *refs, count, terms, added):
    outs = refs[-count:]
    weights = refs[count * terms : (count + 1) * terms]
    into = list(refs[(count + 1) * terms :])
    for block in range(count):
        value = dot_cols(refs[block * terms][...], weights[0][...])
        for term in range(1, terms):
            value = value + dot_cols(refs[block * terms + term][...], weights[term][...])
        if added[block] is None:
            outs[block][...] = value.astype(BF16)
            continue
        half = value.shape[0] // 2
        extra = into.pop(0)[...].astype(F32)
        top, bottom = value[:half], value[half:]
        if added[block]:
            top = top + extra
        else:
            bottom = bottom + extra
        outs[block][:half, :] = top.astype(BF16)
        outs[block][half:, :] = bottom.astype(BF16)


def back(slots, rows, lefts, weights, places, into=None, others=()):
    depth = lefts[0].shape[1]
    width = weights[0].shape[0]
    tile = min(512, width)
    terms, count = len(lefts), len(slots)
    into = into or [None] * count
    in_specs, operands = [], [jnp.stack([jnp.asarray(slot, jnp.int32) for slot in slots])]
    for block in range(count):
        in_specs += [pl.BlockSpec((rows, depth), lambda i, s, b=block: (s[b], 0))] * terms
        operands += lefts
    in_specs += [pl.BlockSpec((tile, depth), lambda i, s, p=place: (i, p)) for place in places]
    operands += weights
    for extra in into:
        if extra is not None:
            in_specs.append(pl.BlockSpec((rows // 2, tile), lambda i, s: (0, i)))
            operands.append(extra[0])
    operands += others
    in_specs += [ANYWHERE] * len(others)
    return pl.pallas_call(
        functools.partial(
            back_kernel,
            count=count,
            terms=terms,
            added=[None if extra is None else extra[1] for extra in into],
        ),
        grid_spec=pltpu.PrefetchScalarGridSpec(
            num_scalar_prefetch=1,
            grid=(width // tile,),
            in_specs=in_specs,
            out_specs=[pl.BlockSpec((rows, tile), lambda i, s: (0, i))] * count,
        ),
        out_shape=[jax.ShapeDtypeStruct((rows, width), BF16)] * count,
        compiler_params=limit(52),
        cost_estimate=declared(2 * count * terms * rows * width * depth),
    )(*operands)


def weigh_kernel(*refs, count):
    lefts, right_ref = refs[:count], refs[count]
    out_ref, turned_ref = refs[-2:]
    rows = lefts[0].shape[0]

    @pl.when(pl.program_id(1) == 0)
    def _():
        for block in range(count):
            turned_ref[:, block * rows : (block + 1) * rows] = lefts[block][...].T

    out_ref[...] = dot(turned_ref[...], right_ref[...]).astype(BF16)


def weigh(lefts, right, others=()):
    tokens, columns = right.shape
    rows, width = lefts[0].shape
    tall, wide = min(512, width), min(1024, columns)
    return pl.pallas_call(
        functools.partial(weigh_kernel, count=len(lefts)),
        grid=(width // tall, columns // wide),
        in_specs=[pl.BlockSpec((rows, tall), lambda i, j: (0, i))] * len(lefts)
        + [pl.BlockSpec((tokens, wide), lambda i, j: (0, j))]
        + [ANYWHERE] * len(others),
        out_specs=pl.BlockSpec((tall, wide), lambda i, j: (i, j)),
        out_shape=jax.ShapeDtypeStruct((width, columns), BF16),
        scratch_shapes=[pltpu.VMEM((tall, tokens), BF16)],
        compiler_params=limit(52),
        cost_estimate=declared(2 * tokens * width * columns),
    )(*lefts, right, *others)


def settle_kernel(*refs, count):
    pieces, weights = refs[:count], refs[count : 2 * count]
    x_ref, gains_ref = refs[2 * count : 2 * count + 2]
    stream_ref, h_ref = refs[-2:]
    stream = x_ref[...].astype(F32)
    for piece, weight in zip(pieces, weights):
        stream = stream + dot_cols(piece[...], weight[...])
    stream_ref[...] = stream
    normed, _ = normalize(stream)
    h_ref[...] = (normed * gains_ref[1:2, :]).astype(BF16)


def settle(own, place, pieces, weights, tokens, gains, others=()):
    rows, width = tokens.shape
    depth = weights[0].shape[1]
    tile = min(256, rows)
    steps = rows // tile
    wide = pl.BlockSpec((tile, width), lambda i: (i, 0))
    piece = pl.BlockSpec((tile, depth), lambda i: (i, 0))
    weight = pl.BlockSpec((width, depth), lambda i: (0, 0), pipeline_mode=pl.Buffered(1))
    return pl.pallas_call(
        functools.partial(settle_kernel, count=len(weights)),
        grid=(steps,),
        in_specs=[pl.BlockSpec((tile, depth), lambda i: (place * steps + i, 0))]
        + [piece] * len(pieces)
        + [weight] * len(weights)
        + [wide, pl.BlockSpec((8, width), lambda i: (0, 0))]
        + [ANYWHERE] * len(others),
        out_specs=[wide, wide],
        out_shape=[
            jax.ShapeDtypeStruct((rows, width), F32),
            jax.ShapeDtypeStruct((rows, width), BF16),
        ],
        compiler_params=limit(52),
        cost_estimate=declared(2 * len(weights) * rows * width * depth),
    )(own, *pieces, *weights, tokens, gains, *others)


def norm_back(grad_in, stream, gain):
    normed, scale_r = normalize(stream)
    scaled = grad_in * gain
    return scale_r * (scaled - normed * jnp.mean(scaled * normed, axis=-1, keepdims=True))


def settle_back_kernel(*refs, parts, count):
    terms, weights = refs[:parts], refs[parts : parts + count]
    grad_ref, stream_ref, gains_ref, out_ref, low_ref = refs[parts + count : parts + count + 5]
    pieces = refs[parts + count + 5 :]
    grad_in = terms[0][...].astype(F32)
    for term in terms[1:]:
        grad_in = grad_in + term[...].astype(F32)
    grad = grad_ref[...].astype(F32) + norm_back(grad_in, stream_ref[...], gains_ref[1:2, :])
    out_ref[...] = grad
    low = grad.astype(BF16)
    low_ref[...] = low
    for piece, weight in zip(pieces, weights):
        piece[...] = dot(low, weight[...]).astype(BF16)


def settle_back(terms, weights, grad, stream, gains):
    rows, width = grad.shape
    depth = weights[0].shape[1]
    tile = min(256, rows)
    wide = pl.BlockSpec((tile, width), lambda i: (i, 0))
    weight = pl.BlockSpec((width, depth), lambda i: (0, 0), pipeline_mode=pl.Buffered(1))
    return pl.pallas_call(
        functools.partial(settle_back_kernel, parts=len(terms), count=len(weights)),
        grid=(rows // tile,),
        in_specs=[wide] * len(terms)
        + [weight] * len(weights)
        + [wide, wide, pl.BlockSpec((8, width), lambda i: (0, 0))],
        out_specs=[wide, wide] + [pl.BlockSpec((tile, depth), lambda i: (i, 0))] * len(weights),
        out_shape=[
            jax.ShapeDtypeStruct((rows, width), F32),
            jax.ShapeDtypeStruct((rows, width), BF16),
        ]
        + [jax.ShapeDtypeStruct((rows, depth), BF16)] * len(weights),
        compiler_params=limit(52),
        cost_estimate=declared(2 * len(weights) * rows * width * depth),
    )(*terms, *weights, grad, stream, gains)


def causal(keys, queries):
    key = lax.broadcasted_iota(jnp.int32, (keys, queries), 0)
    return key <= lax.broadcasted_iota(jnp.int32, (keys, queries), 1)


def first_block(bound, offset, block):
    return jnp.where(offset >= bound, lax.div(bound, jnp.int32(block)), 0)


def attend_kernel(order_ref, q_ref, kx_ref, vt_ref, *rest, block):
    out_ref, lse_ref, top_ref, acc_ref = rest[-4:]
    kv = kx_ref.shape[0]
    per = q_ref.shape[1] // LANES // kv
    bound = order_ref[0]
    ones = jnp.ones((16, block), BF16)
    for group in range(kv):

        def q_step(turn, _):
            index = order_ref[1 + turn]
            offset = pl.multiple_of(index * block, block)
            into = pl.ds(pl.multiple_of(turn * block, block), block)
            top_ref[...] = jnp.full(top_ref.shape, MASKED, F32)
            acc_ref[...] = jnp.zeros(acc_ref.shape, F32)

            def tile(step, size, skip, diagonal):
                keys = pl.ds(pl.multiple_of(step, size), size)
                value_t = jnp.concatenate(
                    [vt_ref[group * HD : (group + 1) * HD, keys], ones[:, :size]], axis=0
                )
                for head in range(2 * per):
                    column = (group * per + head // 2) * LANES
                    query = q_ref[pl.ds(offset + skip, block - skip), column : column + LANES]
                    scores = dot_cols(kx_ref[group, head % 2, keys, :], query)
                    if diagonal:
                        scores = jnp.where(causal(size, block - skip), scores, MASKED)
                    old = top_ref[head, 0:1, skip:]
                    top = jnp.maximum(old, jnp.max(scores, axis=0, keepdims=True))
                    powered = jnp.exp(scores - top).astype(BF16)
                    acc_ref[head, :, skip:] = acc_ref[head, :, skip:] * jnp.exp(old - top) + dot(
                        value_t, powered
                    )
                    top_ref[head, 0:1, skip:] = top

            def full_tile(step, carry):
                tile(step * block, block, 0, False)
                return carry

            lax.fori_loop(first_block(bound, offset, block), index, full_tile, 0)
            tile(offset, block // 2, 0, True)
            tile(offset + block // 2, block // 2, block // 2, True)
            for pair in range(per):
                both = []
                for head in (2 * pair, 2 * pair + 1):
                    total = acc_ref[head, HD : HD + 1, :]
                    both.append(acc_ref[head, :HD, :] / total)
                    place = group * 2 * per + head
                    lse_ref[place : place + 1, into] = top_ref[
                        head, 0:1, :
                    ] + jnp.log(total)
                column = (group * per + pair) * LANES
                out_ref[into, column : column + LANES] = (
                    jnp.concatenate(both, axis=0).T.astype(BF16)
                )
            return _

        lax.fori_loop(0, out_ref.shape[0] // block, q_step, 0)


def attend(bound, order, queries, kx, vt, block, others=()):
    length, width = queries.shape
    heads = width // HD
    kv = kx.shape[0]
    per = heads // kv
    count = len(order)
    cells = heads * count * block * (length + block) // 2
    vmem = pl.BlockSpec(memory_space=pltpu.VMEM)
    return pl.pallas_call(
        functools.partial(attend_kernel, block=block),
        in_specs=[pl.BlockSpec(memory_space=pltpu.SMEM), vmem, vmem, vmem] + [ANYWHERE] * len(others),
        out_specs=[vmem, vmem],
        out_shape=[
            jax.ShapeDtypeStruct((count * block, width), BF16),
            jax.ShapeDtypeStruct((heads, count * block), F32),
        ],
        scratch_shapes=[
            pltpu.VMEM((per, 8, block), F32),
            pltpu.VMEM((per, HD + 16, block), F32),
        ],
        compiler_params=limit(52),
        cost_estimate=declared(2 * 4 * HD * 4 * cells, 16),
    )(jnp.stack([bound, *order]), queries, kx, vt, *others)


def attend_back_kernel(
    order_ref, q_ref, kx_ref, vx_ref, kt_ref, lse_ref, out_ref, grad_ref, cos_ref, sin_ref,
    *rest, block
):
    dqkv_ref, dk_ref, dv_ref, dq_ref = rest[-4:]
    length = q_ref.shape[0]
    kv = kx_ref.shape[0]
    heads = q_ref.shape[1] // HD
    per = heads // 2 // kv
    bound = order_ref[0]
    dk_ref[...] = jnp.zeros(dk_ref.shape, F32)
    dv_ref[...] = jnp.zeros(dv_ref.shape, F32)
    lane = lax.broadcasted_iota(jnp.int32, (8, LANES), 1)
    row = lax.broadcasted_iota(jnp.int32, (8, LANES), 0)
    chosen = ((lane // HD) == row).astype(F32)

    def turn_back(values, rows):
        return values * cos_ref[rows, :] - swap_halves(values) * sin_ref[rows, :]

    for group in range(kv):

        def q_step(turn, _):
            index = order_ref[1 + turn]
            offset = pl.multiple_of(index * block, block)
            rows = pl.ds(offset, block)
            given = pl.ds(pl.multiple_of(turn * block, block), block)
            dq_ref[...] = jnp.zeros(dq_ref.shape, F32)
            deltas = []
            for pair in range(per):
                column = (group * per + pair) * LANES
                product = grad_ref[given, column : column + LANES].astype(F32) * out_ref[
                    given, column : column + LANES
                ].astype(F32)
                deltas.append(
                    lax.dot_general(
                        chosen, product, OVER_COLS, precision=lax.Precision.HIGHEST,
                        preferred_element_type=F32,
                    )
                )

            def tile(step, size, skip, diagonal):
                keys = pl.ds(pl.multiple_of(step, size), size)
                key_t = kt_ref[group * HD : (group + 1) * HD, keys]
                mine = pl.ds(offset + skip, block - skip)
                theirs = pl.ds(turn * block + skip, block - skip)
                for parity in range(2):
                    key_add, value_add = 0.0, 0.0
                    for pair in range(per):
                        head = 2 * pair + parity
                        place = group * 2 * per + head
                        column = (group * per + pair) * LANES
                        query = q_ref[mine, column : column + LANES]
                        grad = grad_ref[theirs, column : column + LANES]
                        scores = dot_cols(kx_ref[group, parity, keys, :], query)
                        if diagonal:
                            scores = jnp.where(causal(size, block - skip), scores, MASKED)
                        probs = jnp.exp(scores - lse_ref[place : place + 1, given][:, skip:])
                        dprobs = dot_cols(vx_ref[group, parity, keys, :], grad)
                        delta = deltas[pair][parity : parity + 1, skip:]
                        dscores = (probs * (dprobs - delta)).astype(BF16)
                        value_add = value_add + dot(probs.astype(BF16), grad)
                        key_add = key_add + dot(dscores, query)
                        dq_ref[head * HD : (head + 1) * HD, skip:] += dot(key_t, dscores)
                    dk_ref[group, parity, keys, :] += key_add
                    dv_ref[group, parity, keys, :] += value_add

            def full_tile(step, carry):
                tile(step * block, block, 0, False)
                return carry

            lax.fori_loop(first_block(bound, offset, block), index, full_tile, 0)
            tile(offset, block // 2, 0, True)
            tile(offset + block // 2, block // 2, block // 2, True)
            for pair in range(per):
                column = (group * per + pair) * LANES
                grad_q = dq_ref[pair * LANES : (pair + 1) * LANES, :].T * (1.0 / math.sqrt(HD))
                dqkv_ref[rows, column : column + LANES] = turn_back(grad_q, rows).astype(BF16)
            return _

        lax.fori_loop(0, length // block, q_step, 0)

    def finish(index, _):
        rows = pl.ds(pl.multiple_of(index * block, block), block)
        lanes = lax.broadcasted_iota(jnp.int32, (block, LANES), 1)

        def placed(part, half):
            ref = dk_ref if part < kv else dv_ref
            even, odd = ref[part % kv, 0, rows, :], ref[part % kv, 1, rows, :]
            return even + pltpu.roll(odd, HD, 1) if half == 0 else pltpu.roll(even, HD, 1) + odd

        for chunk in range(kv):
            values = jnp.where(lanes < HD, placed(2 * chunk, 0), placed(2 * chunk + 1, 1))
            if 2 * chunk + 1 < kv:
                values = turn_back(values, rows)
            elif 2 * chunk < kv:
                values = jnp.where(lanes < HD, turn_back(values, rows), values)
            column = heads * HD + chunk * LANES
            dqkv_ref[rows, column : column + LANES] = values.astype(BF16)
        return _

    lax.fori_loop(0, length // block, finish, 0)


def attend_back(
    bound, order, queries, kx, vx, kt, log_sums, attended, grad, cosine, sine, block, others
):
    length, width = queries.shape
    heads = width // HD
    kv = kx.shape[0]
    cells = heads * length * (length + block) // 2
    vmem = pl.BlockSpec(memory_space=pltpu.VMEM)
    return pl.pallas_call(
        functools.partial(attend_back_kernel, block=block),
        in_specs=[pl.BlockSpec(memory_space=pltpu.SMEM)] + [vmem] * 9 + [ANYWHERE] * len(others),
        out_specs=vmem,
        out_shape=jax.ShapeDtypeStruct((length, width + 2 * kv * HD), BF16),
        scratch_shapes=[
            pltpu.VMEM((kv, 2, length, LANES), F32),
            pltpu.VMEM((kv, 2, length, LANES), F32),
            pltpu.VMEM((heads // kv * HD, block), F32),
        ],
        compiler_params=limit(52),
        cost_estimate=declared(2 * 10 * HD * 4 * cells),
    )(jnp.stack([bound, *order]), queries, kx, vx, kt, log_sums, attended, grad, cosine, sine, *others)


def local(
    inputs,
    segment_ids,
    attn_gain,
    query_weight,
    key_weight,
    value_weight,
    output_weight,
    mlp_gain,
    gate_weight,
    up_weight,
    down_weight,
    cotangent,
    *,
    sizes,
):
    rows = inputs.shape[0]
    length = segment_ids.shape[0]
    query_cols = query_weight.shape[1]
    key_cols = key_weight.shape[1]
    heads, kv = query_cols // HD, key_cols // HD
    columns = query_cols + 2 * key_cols
    slots = slots_of(sizes["tensor"])
    tensor = sizes["tensor"]
    space = (-columns) % query_cols or query_cols
    gains = jnp.pad(jnp.stack([attn_gain, mlp_gain], axis=1), ((0, 0), (0, space - 2)))
    bundle = lax.all_gather(
        jnp.concatenate([query_weight, key_weight, value_weight, gains, output_weight.T], axis=1),
        "dp", axis=0, tiled=True,
    )
    out_own = bundle[:, columns + space :]
    hop = first_hop(inputs, tensor)
    gate_up = lax.all_gather(
        hold(jnp.concatenate([gate_weight, up_weight], axis=1), *(hop or ())),
        "dp", axis=0, tiled=True,
    )

    bound, cosine, sine = rope_tables(segment_ids)
    blocks = second_hop(inputs, hop, tensor)
    stream = inputs.astype(F32)
    arrays = project(slots, blocks, bundle, cosine, sine, heads, kv, length)
    block_a, queries, kx, vx, kt, vt, gains = arrays
    down_t = lax.all_gather(hold(down_weight.T, queries), "dp", axis=0, tiled=True)

    if tensor == 4:
        out_hop = first_hop(hold(out_own, blocks[3]), tensor)
        far, far_sums = attend(bound, slots[3:], queries, kx, vt, rows)
        halves = hold_halves(out_hop, far)
        out_all = second_hop(out_own, out_hop, tensor, halves)
        from_far = lax.ppermute(far, "tensor", pairs(tensor, 3))
        order = [slots[1], slots[2], slots[0], slots[3]]
        near, near_sums = attend(bound, order[:3], queries, kx, vt, rows, halves)
        from_one = lax.ppermute(near[:rows], "tensor", pairs(tensor, 1))
        from_two = lax.ppermute(near[rows : 2 * rows], "tensor", pairs(tensor, 2))
        cotangent_sent = hold(cotangent, near)
        cotangent_hop = first_hop(cotangent_sent, tensor)
        stream_one, low_m = settle(
            near, 2, [from_one, from_two, from_far], out_all, inputs, gains, [cotangent_sent]
        )
        attended = jnp.concatenate([near, far], axis=0)
        log_sums = jnp.concatenate([near_sums, far_sums], axis=1)
    else:
        order = slots
        out_all = gather(out_own, tensor)
        attended, log_sums = attend(bound, order, queries, kx, vt, rows)
        given = trade([attended[k * rows : (k + 1) * rows] for k in range(tensor)], tensor)
        stream_one, low_m = settle(given[0], 0, given[1:], out_all, inputs, gains)
        cotangent_sent = cotangent
    parts_m = [low_m]
    units = gate_weight.shape[1]

    def feed_at(place, wanted, fed, others=()):
        return feed(
            feed_kernel, place, tensor, [parts_m[k] for k in wanted], [gate_up] * 2, [0, 1], [],
            units, 3, True, 512, fed, others,
        )

    def back_m(places, fed, into=None, others=()):
        return back(places, rows, fed[:2], [gate_up] * 2, [0, 1], into, others)

    def back_out(places, into=None, others=()):
        return back(places, rows, [hidden], [down_t], [0], into, others)

    def reduce_rows(term, *others):
        if others and tensor == 4:
            term = hold(term, *others)
        return lax.psum_scatter(term, "dp", scatter_dimension=0, tiled=True)

    if tensor == 4:
        fed = feed_at(3, [0], None)
        sent = hold(parts_m[0], fed[0], *cotangent_hop)
        hop = first_hop(sent, tensor)
        parts_m = second_hop(sent, hop, tensor)
        fed = feed_at(0, [1, 2], fed, [sent])
        halves = hold_halves(cotangent_hop, fed[0])
        grad_parts = second_hop(cotangent_sent, cotangent_hop, tensor, halves)
        fed = feed_at(2, [3], fed, halves)
    else:
        grad_parts = second_hop(cotangent_sent, None, tensor)
        parts_m = gather(parts_m[0], tensor)
        fed = None
        for place in range(tensor):
            fed = feed_at(place, [place], fed)
    hidden, silu, slope, block_m = fed
    places = [1, 2, 3, 0] if tensor == 4 else list(range(tensor))
    grad_parts = [grad_parts[k] for k in places]

    def feed_back(others=()):
        return feed(
            feed_back_kernel, 0, tensor, grad_parts, [down_t], [0], [silu, slope], units, 2, False, 512,
            None, others,
        )

    if tensor == 4:
        (three_out,) = back_out([2], None, [fed[0]])
        out_one, out_two = out_halves = send_half(three_out, tensor)
        down_t_wgrad = weigh(grad_parts, hidden, [three_out])
        one_out, two_out, own_out = back_out(
            [0, 1, 3], [(out_one, False), (out_two, True), None]
        )
        out_parts = [
            own_out,
            lax.ppermute(one_out, "tensor", pairs(tensor, 1)),
            lax.ppermute(two_out, "tensor", pairs(tensor, 2)),
        ]
        fed = feed_back([one_out])
        (three_m,) = back_m([2], fed)
        m_one, m_two = send_half(three_m, tensor)
        (own_m,) = back_m([3], fed, None, [three_m])
        one_m, two_m = back_m(
            [0, 1], fed, [(m_one, False), (m_two, True)], [own_m, *out_parts[1:]]
        )
        gate_wgrad = weigh([block_m], fed[0], [one_m])
        grad_m_parts = [
            own_m,
            lax.ppermute(one_m, "tensor", pairs(tensor, 1)),
            lax.ppermute(two_m, "tensor", pairs(tensor, 2)),
        ]
    else:
        down_t_wgrad = weigh(grad_parts, hidden)
        fed = feed_back()
        grad_m_parts = sum_whole(back_m(list(range(tensor)), fed))
        gate_wgrad = weigh([block_m], fed[0])
        out_parts = sum_whole(back_out(list(range(tensor))))
    layer_out = (stream_one + total(out_parts)).astype(BF16)
    if tensor != 4:
        out_halves = ()
    down_t_low = reduce_rows(down_t_wgrad, *out_halves)
    gate_low = reduce_rows(gate_wgrad, *grad_m_parts[1:])

    grad_stream_one, grad_stream_low, *pieces = settle_back(
        grad_m_parts, out_all, cotangent, stream_one, gains
    )
    given = trade(pieces, tensor)
    up_wgrad = weigh([block_m], fed[1], [grad_stream_low])
    places = [1, 2, 0, 3] if tensor == 4 else list(range(tensor))
    grad_attended = jnp.concatenate([given[k] for k in places], axis=0)
    up_wgrad = hold(up_wgrad, grad_attended)
    up_low = reduce_rows(up_wgrad)
    grad_qkv = attend_back(
        bound, order, queries, kx, vx, kt, log_sums, attended, grad_attended, cosine, sine, rows,
        [down_t_low, up_wgrad],
    )
    if tensor == 4:
        sent = hold(grad_stream_low, grad_attended)
        grad_stream_parts = trade([sent] * 4, tensor)
    else:
        grad_stream_parts = gather(grad_stream_low, tensor)
    grad_stream_parts = [grad_stream_parts[k] for k in places]

    def back_a(places, others=()):
        return back(places, rows, [grad_qkv], [bundle], [0], None, others)

    if tensor == 4:
        (three,) = back_a(slots[3:], [gate_low])
        halves = send_half(three, tensor)
        block_a = hold(block_a, three)
        grad_stream_parts[-1] = hold(grad_stream_parts[-1], three)
    qkv_wgrad = weigh([block_a], grad_qkv)
    out_t_wgrad = weigh(grad_stream_parts, attended)
    attention_wgrad = jnp.concatenate([qkv_wgrad, out_t_wgrad], axis=1)
    gate_sum, up_sum, down_t_sum = [low.astype(F32) for low in (gate_low, up_low, down_t_low)]
    attention_sum = reduce_rows(attention_wgrad).astype(F32)
    if tensor == 4:
        one, two, own = back_a([slots[1], slots[2], slots[0]], [three])
        grad_a_parts = [own, *send_whole(one, two, halves, tensor)]
    else:
        grad_a_parts = sum_whole(back_a(slots))
    grad_normed_a = total(grad_a_parts)

    def gain_term(gain, weights):
        term = sum(jnp.sum(weight.astype(F32) * grad, axis=1) for weight, grad in weights)
        return term / gain.astype(F32)

    query_sum = attention_sum[:, :query_cols]
    key_sum = attention_sum[:, query_cols : query_cols + key_cols]
    value_sum = attention_sum[:, query_cols + key_cols : columns]
    gain_terms = [
        gain_term(
            attn_gain, [(query_weight, query_sum), (key_weight, key_sum), (value_weight, value_sum)]
        ),
        gain_term(mlp_gain, [(gate_weight, gate_sum), (up_weight, up_sum)]),
    ]
    gain_mine = sum_tensor(jnp.stack(gain_terms), tensor)
    input_grad = (grad_stream_one + norm_back(grad_normed_a, stream, gains[0:1])).astype(BF16)
    return (
        layer_out,
        input_grad,
        gain_mine[0],
        query_sum,
        key_sum,
        value_sum,
        attention_sum[:, columns:].T,
        gain_mine[1],
        gate_sum,
        up_sum,
        down_t_sum.T,
    )


def solution(mesh):
    tokens = P(("dp", "tensor"), None)
    in_specs = (
        tokens,
        P("dp"),
        P("dp"),
        P("dp", "tensor"),
        P("dp", "tensor"),
        P("dp", "tensor"),
        P("tensor", "dp"),
        P("dp"),
        P("dp", "tensor"),
        P("dp", "tensor"),
        P("tensor", "dp"),
        tokens,
    )
    out_specs = (
        tokens,
        tokens,
        P("dp"),
        P("dp", "tensor"),
        P("dp", "tensor"),
        P("dp", "tensor"),
        P("tensor", "dp"),
        P("dp"),
        P("dp", "tensor"),
        P("dp", "tensor"),
        P("tensor", "dp"),
    )
    return jax.shard_map(
        functools.partial(local, sizes={axis: mesh.shape[axis] for axis in ("tensor", "dp")}),
        mesh=mesh, in_specs=in_specs, out_specs=out_specs, check_vma=False,
    )
```

```python
import functools
import math

import jax
import jax.numpy as jnp
from jax import lax
from jax.experimental import pallas as pl
from jax.experimental.pallas import tpu as pltpu
from jax.sharding import PartitionSpec as P

HD = 64
LANES = 128
EPSILON = 1e-05
ROPE_BASE = 500000.0
MASKED = -1e30
OVER_ROWS = (((0,), (0,)), ((), ()))
OVER_COLS = (((1,), (1,)), ((), ()))


def limit(size):
    return pltpu.CompilerParams(vmem_limit_bytes=size * 2**20)


SHORT = 0.0625


def declared(flops, scale=SHORT):
    return pl.CostEstimate(flops=int(flops * scale), bytes_accessed=0, transcendentals=0)


F32 = jnp.float32
BF16 = jnp.bfloat16


def dot_cols(left, right):
    return lax.dot_general(left, right, OVER_COLS, preferred_element_type=F32)


def dot_rows(left, right):
    return lax.dot_general(left, right, OVER_ROWS, preferred_element_type=F32)


def dot(left, right):
    return jnp.dot(left, right, preferred_element_type=F32)


def pairs(size, bit):
    return [(index, index ^ bit) for index in range(size)]


def slots_of(size):
    if size == 4:
        return [lax.axis_index("tensor") ^ step for step in range(size)]
    return [jnp.int32(step) for step in range(size)]


ANYWHERE = pl.BlockSpec(memory_space=pl.ANY)


def nothing_kernel(*refs):
    pass


def hold(value, *others):
    return pl.pallas_call(
        nothing_kernel,
        in_specs=[ANYWHERE] * (1 + len(others)),
        out_specs=ANYWHERE,
        out_shape=jax.ShapeDtypeStruct(value.shape, value.dtype),
        input_output_aliases={0: 0},
        cost_estimate=declared(0),
    )(value, *others)


def first_hop(shard, size):
    if size != 4:
        return None
    return [lax.ppermute(shard, "tensor", pairs(size, bit)) for bit in (1, 2)]


def hold_halves(hop, *others):
    one, two = hop
    half = one.shape[0] // 2
    return hold(one[:half], *others), hold(two[half:], *others)


def second_hop(shard, hop, size, halves=None):
    if size != 4:
        whole = lax.all_gather(shard, "tensor", axis=0)
        return [whole[step] for step in range(size)]
    half = shard.shape[0] // 2
    one, two = hop
    upper, lower = halves or (one[:half], two[half:])
    three_a = lax.ppermute(upper, "tensor", pairs(size, 2))
    three_b = lax.ppermute(lower, "tensor", pairs(size, 1))
    return [shard, one, two, jnp.concatenate([three_a, three_b], axis=0)]


def gather(shard, size):
    return second_hop(shard, first_hop(shard, size), size)


def send_half(three, size):
    half = three.shape[0] // 2
    into_two = lax.ppermute(three[:half], "tensor", pairs(size, 1))
    into_one = lax.ppermute(three[half:], "tensor", pairs(size, 2))
    return into_one, into_two


def send_whole(one, two, into, size):
    into_one, into_two = into
    half = one.shape[0] // 2
    lower = (one[half:].astype(F32) + into_one.astype(F32)).astype(BF16)
    upper = (two[:half].astype(F32) + into_two.astype(F32)).astype(BF16)
    return [
        lax.ppermute(jnp.concatenate([one[:half], lower], axis=0), "tensor", pairs(size, 1)),
        lax.ppermute(jnp.concatenate([upper, two[half:]], axis=0), "tensor", pairs(size, 2)),
    ]


def sum_whole(terms):
    return [
        lax.psum_scatter(
            jnp.concatenate(terms, axis=0), "tensor", scatter_dimension=0, tiled=True
        )
    ]


def trade(pieces, size):
    if size != 4:
        whole = lax.all_to_all(jnp.stack(pieces), "tensor", split_axis=0, concat_axis=0, tiled=True)
        return [whole[step] for step in range(size)]
    return [pieces[0]] + [
        lax.ppermute(pieces[step], "tensor", pairs(size, step)) for step in (1, 2, 3)
    ]


def total(parts):
    return functools.reduce(jnp.add, [part.astype(F32) for part in parts])


def sum_tensor(value, size):
    if size & (size - 1):
        return lax.psum(value, "tensor")
    return value + sum(lax.ppermute(value, "tensor", pairs(size, bit)) for bit in range(1, size))


def rope_tables(segment):
    length = segment.shape[0]
    bound = jnp.sum((segment == 0).astype(jnp.int32))
    place = lax.broadcasted_iota(jnp.int32, (length, LANES), 0)
    place = place - jnp.where(place >= bound, bound, 0)
    lane = lax.broadcasted_iota(jnp.int32, (length, LANES), 1)
    freqs = jnp.exp(
        (lane % (HD // 2)).astype(F32) * (-2.0 * math.log(ROPE_BASE) / HD)
    )
    angles = place.astype(F32) * freqs
    sine = jnp.sin(angles)
    return bound, jnp.cos(angles), jnp.where(lane % HD < HD // 2, -sine, sine)


def swap_halves(values):
    lane = lax.broadcasted_iota(jnp.int32, values.shape, 1)
    after = pltpu.roll(values, LANES - HD // 2, 1)
    before = pltpu.roll(values, HD // 2, 1)
    return jnp.where(lane % HD < HD // 2, after, before)


def normalize(stream):
    scale_r = lax.rsqrt(jnp.mean(stream * stream, axis=-1, keepdims=True) + EPSILON)
    return (stream * scale_r, scale_r)


def project_kernel(slot_ref, *refs, count, steps, heads, kv):
    gains_ref, w_ref, cos_ref, sin_ref = refs[count : count + 4]
    h_ref, q_ref, kx_ref, vx_ref, kt_ref, vt_ref, gain_ref = refs[-7:]

    @pl.when(pl.program_id(0) == 0)
    def _():
        gain_ref[...] = gains_ref[...].astype(F32).T[:8]

    which = pl.program_id(0) // steps
    rows = h_ref.shape[0]
    part_rows = min(256, rows)
    lane = lax.broadcasted_iota(jnp.int32, (part_rows, LANES), 1)
    for start in range(0, rows, part_rows):
        at = slice(start, start + part_rows)
        tokens = refs[0][at, :]
        for block in range(1, count):
            tokens = jnp.where(which == block, refs[block][at, :], tokens)
        normed, _ = normalize(tokens.astype(F32))
        low = (normed * gain_ref[0:1, :]).astype(BF16)
        h_ref[at, :] = low
        pre = dot(low, w_ref[...])
        cosine, sine = cos_ref[at, :], sin_ref[at, :]
        chunks = []
        for chunk in range(pre.shape[1] // LANES):
            columns = slice(chunk * LANES, (chunk + 1) * LANES)
            part = pre[:, columns]
            first = 2 * chunk
            if first < heads + kv:
                turned = part * cosine + swap_halves(part) * sine
                part = turned if first + 1 < heads + kv else jnp.where(lane < HD, turned, part)
            chunks.append(part)
            if first < heads:
                q_ref[at, columns] = (part * (1.0 / math.sqrt(HD))).astype(BF16)
        flipped = {}
        for head in range(2 * kv):
            place = heads + head
            part = chunks[place // 2]
            moved = pltpu.roll(part, HD, 1)
            wide = [part, moved] if place % 2 == 0 else [moved, part]
            out = kx_ref if head < kv else vx_ref
            out[head % kv, 0, at, :] = jnp.where(lane < HD, wide[0], 0.0).astype(BF16)
            out[head % kv, 1, at, :] = jnp.where(lane < HD, 0.0, wide[1]).astype(BF16)
            if place // 2 not in flipped:
                flipped[place // 2] = part.T
            turn = flipped[place // 2][(place % 2) * HD : (place % 2 + 1) * HD]
            out_t = kt_ref if head < kv else vt_ref
            out_t[(head % kv) * HD : (head % kv + 1) * HD, at] = turn.astype(BF16)


def project(slots, blocks, bundle, cosine, sine, heads, kv, length):
    rows, width = blocks[0].shape
    count = len(blocks)
    tile = rows
    steps = rows // tile
    columns = (heads + 2 * kv) * HD

    def at(i, slot):
        return slot[i // steps] * steps + i % steps

    shapes = [
        jax.ShapeDtypeStruct((length, width), BF16),
        jax.ShapeDtypeStruct((length, heads * HD), BF16),
        jax.ShapeDtypeStruct((kv, 2, length, LANES), BF16),
        jax.ShapeDtypeStruct((kv, 2, length, LANES), BF16),
        jax.ShapeDtypeStruct((kv * HD, length), BF16),
        jax.ShapeDtypeStruct((kv * HD, length), BF16),
        jax.ShapeDtypeStruct((8, width), F32),
    ]
    out_specs = [
        pl.BlockSpec((tile, width), lambda i, s: (at(i, s), 0)),
        pl.BlockSpec((tile, heads * HD), lambda i, s: (at(i, s), 0)),
        pl.BlockSpec((kv, 2, tile, LANES), lambda i, s: (0, 0, at(i, s), 0)),
        pl.BlockSpec((kv, 2, tile, LANES), lambda i, s: (0, 0, at(i, s), 0)),
        pl.BlockSpec((kv * HD, tile), lambda i, s: (0, at(i, s))),
        pl.BlockSpec((kv * HD, tile), lambda i, s: (0, at(i, s))),
        pl.BlockSpec((8, width), lambda i, s: (0, 0)),
    ]
    in_specs = [
        pl.BlockSpec((tile, width), lambda i, s, b=block: (jnp.clip(i - b * steps, 0, steps - 1), 0))
        for block in range(count)
    ]
    in_specs += [
        pl.BlockSpec((width, LANES), lambda i, s: (0, columns // LANES)),
        pl.BlockSpec((width, columns), lambda i, s: (0, 0)),
        pl.BlockSpec((tile, LANES), lambda i, s: (at(i, s), 0)),
        pl.BlockSpec((tile, LANES), lambda i, s: (at(i, s), 0)),
    ]
    operands = [jnp.stack(slots), *blocks, bundle, bundle, cosine, sine]
    return pl.pallas_call(
        functools.partial(
            project_kernel, count=count, steps=steps, heads=heads, kv=kv
        ),
        grid_spec=pltpu.PrefetchScalarGridSpec(
            num_scalar_prefetch=1,
            grid=(count * steps,),
            in_specs=in_specs,
            out_specs=out_specs,
        ),
        out_shape=shapes,
        compiler_params=limit(52),
        cost_estimate=declared(2 * count * rows * width * columns),
    )(*operands)


def feed_kernel(*refs, count):
    tokens = refs[:count]
    gate_ref, up_ref = refs[count : count + 2]
    hidden_ref, silu_ref, slope_ref, h_out = refs[-4:]
    rows = tokens[0].shape[0]
    wide = h_out.shape[1]
    tile = min(256, gate_ref.shape[1])
    lanes = pl.ds(pl.multiple_of(pl.program_id(0) * wide, wide), wide)
    for block in range(count):
        h_out[block * rows : (block + 1) * rows, :] = tokens[block][:, lanes]
    for part in range(gate_ref.shape[1] // tile):
        columns = slice(part * tile, (part + 1) * tile)
        for block in range(count):
            where = slice(block * rows, (block + 1) * rows)
            gate = dot(tokens[block][...], gate_ref[:, columns])
            up = dot(tokens[block][...], up_ref[:, columns])
            sigmoid = 0.5 * jnp.tanh(0.5 * gate) + 0.5
            silu = gate * sigmoid
            hidden_ref[where, columns] = (silu * up).astype(BF16)
            silu_ref[where, columns] = silu.astype(BF16)
            slope_ref[where, columns] = (up * (sigmoid + silu * (1.0 - sigmoid))).astype(BF16)


def feed_back_kernel(*refs, count):
    grads = refs[:count]
    down_ref, silu_ref, slope_ref = refs[count : count + 3]
    dgate_ref, dup_ref = refs[-2:]
    rows = grads[0].shape[0]
    for block in range(count):
        where = slice(block * rows, (block + 1) * rows)
        dhidden = dot(grads[block][...], down_ref[...])
        dup_ref[where, :] = (dhidden * silu_ref[where, :].astype(F32)).astype(BF16)
        dgate_ref[where, :] = (dhidden * slope_ref[where, :].astype(F32)).astype(BF16)


def feed(kernel, place, blocks, tokens, weights, places, kept, units, outs, copy, tile, prev, others):
    rows, width = tokens[0].shape
    count = len(tokens)
    steps = max(units // tile, 1)
    tile, wide = units // steps, width // steps
    shapes = [jax.ShapeDtypeStruct((blocks * rows, units), BF16)] * outs
    in_specs = [pl.BlockSpec((rows, width), lambda i: (0, 0), pipeline_mode=pl.Buffered(1))] * count
    in_specs += [
        pl.BlockSpec((width, tile), lambda i, w=which: (0, w * steps + i)) for which in places
    ]
    cell = pl.BlockSpec((count * rows, tile), lambda i: (place, i))
    in_specs += [cell] * len(kept)
    out_specs = [cell] * outs
    if copy:
        shapes.append(jax.ShapeDtypeStruct((blocks * rows, width), BF16))
        out_specs.append(pl.BlockSpec((count * rows, wide), lambda i: (place, i)))
    operands = [*tokens, *weights, *kept]
    aliases = {}
    if prev is not None:
        for index, array in enumerate(prev):
            aliases[len(operands)] = index
            operands.append(array)
            in_specs.append(ANYWHERE)
    operands += others
    in_specs += [ANYWHERE] * len(others)
    return pl.pallas_call(
        functools.partial(kernel, count=count),
        grid=(steps,),
        in_specs=in_specs,
        out_specs=out_specs,
        out_shape=shapes,
        input_output_aliases=aliases,
        compiler_params=limit(52),
        cost_estimate=declared(2 * len(weights) * count * rows * width * units),
    )(*operands)


def back_kernel(slot_ref, *refs, count, terms, added):
    outs = refs[-count:]
    weights = refs[count * terms : (count + 1) * terms]
    into = list(refs[(count + 1) * terms :])
    for block in range(count):
        value = dot_cols(refs[block * terms][...], weights[0][...])
        for term in range(1, terms):
            value = value + dot_cols(refs[block * terms + term][...], weights[term][...])
        if added[block] is None:
            outs[block][...] = value.astype(BF16)
            continue
        half = value.shape[0] // 2
        extra = into.pop(0)[...].astype(F32)
        top, bottom = value[:half], value[half:]
        if added[block]:
            top = top + extra
        else:
            bottom = bottom + extra
        outs[block][:half, :] = top.astype(BF16)
        outs[block][half:, :] = bottom.astype(BF16)


def back(slots, rows, lefts, weights, places, into=None, others=()):
    depth = lefts[0].shape[1]
    width = weights[0].shape[0]
    tile = min(512, width)
    terms, count = len(lefts), len(slots)
    into = into or [None] * count
    in_specs, operands = [], [jnp.stack([jnp.asarray(slot, jnp.int32) for slot in slots])]
    for block in range(count):
        in_specs += [pl.BlockSpec((rows, depth), lambda i, s, b=block: (s[b], 0))] * terms
        operands += lefts
    in_specs += [pl.BlockSpec((tile, depth), lambda i, s, p=place: (i, p)) for place in places]
    operands += weights
    for extra in into:
        if extra is not None:
            in_specs.append(pl.BlockSpec((rows // 2, tile), lambda i, s: (0, i)))
            operands.append(extra[0])
    operands += others
    in_specs += [ANYWHERE] * len(others)
    return pl.pallas_call(
        functools.partial(
            back_kernel,
            count=count,
            terms=terms,
            added=[None if extra is None else extra[1] for extra in into],
        ),
        grid_spec=pltpu.PrefetchScalarGridSpec(
            num_scalar_prefetch=1,
            grid=(width // tile,),
            in_specs=in_specs,
            out_specs=[pl.BlockSpec((rows, tile), lambda i, s: (0, i))] * count,
        ),
        out_shape=[jax.ShapeDtypeStruct((rows, width), BF16)] * count,
        compiler_params=limit(52),
        cost_estimate=declared(2 * count * terms * rows * width * depth),
    )(*operands)


def weigh_kernel(*refs, count):
    lefts, right_ref = refs[:count], refs[count]
    out_ref, turned_ref = refs[-2:]
    rows = lefts[0].shape[0]

    @pl.when(pl.program_id(1) == 0)
    def _():
        for block in range(count):
            turned_ref[:, block * rows : (block + 1) * rows] = lefts[block][...].T

    out_ref[...] = dot(turned_ref[...], right_ref[...]).astype(BF16)


def weigh(lefts, right, others=()):
    tokens, columns = right.shape
    rows, width = lefts[0].shape
    tall, wide = min(512, width), min(1024, columns)
    return pl.pallas_call(
        functools.partial(weigh_kernel, count=len(lefts)),
        grid=(width // tall, columns // wide),
        in_specs=[pl.BlockSpec((rows, tall), lambda i, j: (0, i))] * len(lefts)
        + [pl.BlockSpec((tokens, wide), lambda i, j: (0, j))]
        + [ANYWHERE] * len(others),
        out_specs=pl.BlockSpec((tall, wide), lambda i, j: (i, j)),
        out_shape=jax.ShapeDtypeStruct((width, columns), BF16),
        scratch_shapes=[pltpu.VMEM((tall, tokens), BF16)],
        compiler_params=limit(52),
        cost_estimate=declared(2 * tokens * width * columns),
    )(*lefts, right, *others)


def settle_kernel(*refs, count):
    pieces, weights = refs[:count], refs[count : 2 * count]
    x_ref, gains_ref = refs[2 * count : 2 * count + 2]
    stream_ref, h_ref = refs[-2:]
    stream = x_ref[...].astype(F32)
    for piece, weight in zip(pieces, weights):
        stream = stream + dot_cols(piece[...], weight[...])
    stream_ref[...] = stream
    normed, _ = normalize(stream)
    h_ref[...] = (normed * gains_ref[1:2, :]).astype(BF16)


def settle(own, place, pieces, weights, tokens, gains, others=()):
    rows, width = tokens.shape
    depth = weights[0].shape[1]
    tile = min(256, rows)
    steps = rows // tile
    wide = pl.BlockSpec((tile, width), lambda i: (i, 0))
    piece = pl.BlockSpec((tile, depth), lambda i: (i, 0))
    weight = pl.BlockSpec((width, depth), lambda i: (0, 0), pipeline_mode=pl.Buffered(1))
    return pl.pallas_call(
        functools.partial(settle_kernel, count=len(weights)),
        grid=(steps,),
        in_specs=[pl.BlockSpec((tile, depth), lambda i: (place * steps + i, 0))]
        + [piece] * len(pieces)
        + [weight] * len(weights)
        + [wide, pl.BlockSpec((8, width), lambda i: (0, 0))]
        + [ANYWHERE] * len(others),
        out_specs=[wide, wide],
        out_shape=[
            jax.ShapeDtypeStruct((rows, width), F32),
            jax.ShapeDtypeStruct((rows, width), BF16),
        ],
        compiler_params=limit(52),
        cost_estimate=declared(2 * len(weights) * rows * width * depth),
    )(own, *pieces, *weights, tokens, gains, *others)


def norm_back(grad_in, stream, gain):
    normed, scale_r = normalize(stream)
    scaled = grad_in * gain
    return scale_r * (scaled - normed * jnp.mean(scaled * normed, axis=-1, keepdims=True))


def settle_back_kernel(*refs, parts, count):
    terms, weights = refs[:parts], refs[parts : parts + count]
    grad_ref, stream_ref, gains_ref, out_ref, low_ref = refs[parts + count : parts + count + 5]
    pieces = refs[parts + count + 5 :]
    grad_in = terms[0][...].astype(F32)
    for term in terms[1:]:
        grad_in = grad_in + term[...].astype(F32)
    grad = grad_ref[...].astype(F32) + norm_back(grad_in, stream_ref[...], gains_ref[1:2, :])
    out_ref[...] = grad
    low = grad.astype(BF16)
    low_ref[...] = low
    for piece, weight in zip(pieces, weights):
        piece[...] = dot(low, weight[...]).astype(BF16)


def settle_back(terms, weights, grad, stream, gains):
    rows, width = grad.shape
    depth = weights[0].shape[1]
    tile = min(256, rows)
    wide = pl.BlockSpec((tile, width), lambda i: (i, 0))
    weight = pl.BlockSpec((width, depth), lambda i: (0, 0), pipeline_mode=pl.Buffered(1))
    return pl.pallas_call(
        functools.partial(settle_back_kernel, parts=len(terms), count=len(weights)),
        grid=(rows // tile,),
        in_specs=[wide] * len(terms)
        + [weight] * len(weights)
        + [wide, wide, pl.BlockSpec((8, width), lambda i: (0, 0))],
        out_specs=[wide, wide] + [pl.BlockSpec((tile, depth), lambda i: (i, 0))] * len(weights),
        out_shape=[
            jax.ShapeDtypeStruct((rows, width), F32),
            jax.ShapeDtypeStruct((rows, width), BF16),
        ]
        + [jax.ShapeDtypeStruct((rows, depth), BF16)] * len(weights),
        compiler_params=limit(52),
        cost_estimate=declared(2 * len(weights) * rows * width * depth),
    )(*terms, *weights, grad, stream, gains)


def causal(keys, queries):
    key = lax.broadcasted_iota(jnp.int32, (keys, queries), 0)
    return key <= lax.broadcasted_iota(jnp.int32, (keys, queries), 1)


def first_block(bound, offset, block):
    return jnp.where(offset >= bound, lax.div(bound, jnp.int32(block)), 0)


def attend_kernel(order_ref, q_ref, kx_ref, vt_ref, *rest, block):
    out_ref, lse_ref, top_ref, acc_ref = rest[-4:]
    kv = kx_ref.shape[0]
    per = q_ref.shape[1] // LANES // kv
    bound = order_ref[0]
    ones = jnp.ones((16, block), BF16)
    for group in range(kv):

        def q_step(turn, _):
            index = order_ref[1 + turn]
            offset = pl.multiple_of(index * block, block)
            into = pl.ds(pl.multiple_of(turn * block, block), block)
            top_ref[...] = jnp.full(top_ref.shape, MASKED, F32)
            acc_ref[...] = jnp.zeros(acc_ref.shape, F32)

            def tile(step, size, skip, diagonal):
                keys = pl.ds(pl.multiple_of(step, size), size)
                value_t = jnp.concatenate(
                    [vt_ref[group * HD : (group + 1) * HD, keys], ones[:, :size]], axis=0
                )
                for head in range(2 * per):
                    column = (group * per + head // 2) * LANES
                    query = q_ref[pl.ds(offset + skip, block - skip), column : column + LANES]
                    scores = dot_cols(kx_ref[group, head % 2, keys, :], query)
                    if diagonal:
                        scores = jnp.where(causal(size, block - skip), scores, MASKED)
                    old = top_ref[head, 0:1, skip:]
                    top = jnp.maximum(old, jnp.max(scores, axis=0, keepdims=True))
                    powered = jnp.exp(scores - top).astype(BF16)
                    acc_ref[head, :, skip:] = acc_ref[head, :, skip:] * jnp.exp(old - top) + dot(
                        value_t, powered
                    )
                    top_ref[head, 0:1, skip:] = top

            def full_tile(step, carry):
                tile(step * block, block, 0, False)
                return carry

            lax.fori_loop(first_block(bound, offset, block), index, full_tile, 0)
            tile(offset, block // 2, 0, True)
            tile(offset + block // 2, block // 2, block // 2, True)
            for pair in range(per):
                both = []
                for head in (2 * pair, 2 * pair + 1):
                    total = acc_ref[head, HD : HD + 1, :]
                    both.append(acc_ref[head, :HD, :] / total)
                    place = group * 2 * per + head
                    lse_ref[place : place + 1, into] = top_ref[
                        head, 0:1, :
                    ] + jnp.log(total)
                column = (group * per + pair) * LANES
                out_ref[into, column : column + LANES] = (
                    jnp.concatenate(both, axis=0).T.astype(BF16)
                )
            return _

        lax.fori_loop(0, out_ref.shape[0] // block, q_step, 0)


def attend(bound, order, queries, kx, vt, block, others=()):
    length, width = queries.shape
    heads = width // HD
    kv = kx.shape[0]
    per = heads // kv
    count = len(order)
    cells = heads * count * block * (length + block) // 2
    vmem = pl.BlockSpec(memory_space=pltpu.VMEM)
    return pl.pallas_call(
        functools.partial(attend_kernel, block=block),
        in_specs=[pl.BlockSpec(memory_space=pltpu.SMEM), vmem, vmem, vmem] + [ANYWHERE] * len(others),
        out_specs=[vmem, vmem],
        out_shape=[
            jax.ShapeDtypeStruct((count * block, width), BF16),
            jax.ShapeDtypeStruct((heads, count * block), F32),
        ],
        scratch_shapes=[
            pltpu.VMEM((per, 8, block), F32),
            pltpu.VMEM((per, HD + 16, block), F32),
        ],
        compiler_params=limit(52),
        cost_estimate=declared(2 * 4 * HD * 4 * cells, 16),
    )(jnp.stack([bound, *order]), queries, kx, vt, *others)


def attend_back_kernel(
    order_ref, q_ref, kx_ref, vx_ref, kt_ref, lse_ref, out_ref, grad_ref, cos_ref, sin_ref,
    *rest, block
):
    dqkv_ref, dk_ref, dv_ref, dq_ref = rest[-4:]
    length = q_ref.shape[0]
    kv = kx_ref.shape[0]
    heads = q_ref.shape[1] // HD
    per = heads // 2 // kv
    bound = order_ref[0]
    dk_ref[...] = jnp.zeros(dk_ref.shape, F32)
    dv_ref[...] = jnp.zeros(dv_ref.shape, F32)
    lane = lax.broadcasted_iota(jnp.int32, (8, LANES), 1)
    row = lax.broadcasted_iota(jnp.int32, (8, LANES), 0)
    chosen = ((lane // HD) == row).astype(F32)

    def turn_back(values, rows):
        return values * cos_ref[rows, :] - swap_halves(values) * sin_ref[rows, :]

    for group in range(kv):

        def q_step(turn, _):
            index = order_ref[1 + turn]
            offset = pl.multiple_of(index * block, block)
            rows = pl.ds(offset, block)
            given = pl.ds(pl.multiple_of(turn * block, block), block)
            dq_ref[...] = jnp.zeros(dq_ref.shape, F32)
            deltas = []
            for pair in range(per):
                column = (group * per + pair) * LANES
                product = grad_ref[given, column : column + LANES].astype(F32) * out_ref[
                    given, column : column + LANES
                ].astype(F32)
                deltas.append(
                    lax.dot_general(
                        chosen, product, OVER_COLS, precision=lax.Precision.HIGHEST,
                        preferred_element_type=F32,
                    )
                )

            def tile(step, size, skip, diagonal):
                keys = pl.ds(pl.multiple_of(step, size), size)
                key_t = kt_ref[group * HD : (group + 1) * HD, keys]
                mine = pl.ds(offset + skip, block - skip)
                theirs = pl.ds(turn * block + skip, block - skip)
                for parity in range(2):
                    key_add, value_add = 0.0, 0.0
                    for pair in range(per):
                        head = 2 * pair + parity
                        place = group * 2 * per + head
                        column = (group * per + pair) * LANES
                        query = q_ref[mine, column : column + LANES]
                        grad = grad_ref[theirs, column : column + LANES]
                        scores = dot_cols(kx_ref[group, parity, keys, :], query)
                        if diagonal:
                            scores = jnp.where(causal(size, block - skip), scores, MASKED)
                        probs = jnp.exp(scores - lse_ref[place : place + 1, given][:, skip:])
                        dprobs = dot_cols(vx_ref[group, parity, keys, :], grad)
                        delta = deltas[pair][parity : parity + 1, skip:]
                        dscores = (probs * (dprobs - delta)).astype(BF16)
                        value_add = value_add + dot(probs.astype(BF16), grad)
                        key_add = key_add + dot(dscores, query)
                        dq_ref[head * HD : (head + 1) * HD, skip:] += dot(key_t, dscores)
                    dk_ref[group, parity, keys, :] += key_add
                    dv_ref[group, parity, keys, :] += value_add

            def full_tile(step, carry):
                tile(step * block, block, 0, False)
                return carry

            lax.fori_loop(first_block(bound, offset, block), index, full_tile, 0)
            tile(offset, block // 2, 0, True)
            tile(offset + block // 2, block // 2, block // 2, True)
            for pair in range(per):
                column = (group * per + pair) * LANES
                grad_q = dq_ref[pair * LANES : (pair + 1) * LANES, :].T * (1.0 / math.sqrt(HD))
                dqkv_ref[rows, column : column + LANES] = turn_back(grad_q, rows).astype(BF16)
            return _

        lax.fori_loop(0, length // block, q_step, 0)

    def finish(index, _):
        rows = pl.ds(pl.multiple_of(index * block, block), block)
        lanes = lax.broadcasted_iota(jnp.int32, (block, LANES), 1)

        def placed(part, half):
            ref = dk_ref if part < kv else dv_ref
            even, odd = ref[part % kv, 0, rows, :], ref[part % kv, 1, rows, :]
            return even + pltpu.roll(odd, HD, 1) if half == 0 else pltpu.roll(even, HD, 1) + odd

        for chunk in range(kv):
            values = jnp.where(lanes < HD, placed(2 * chunk, 0), placed(2 * chunk + 1, 1))
            if 2 * chunk + 1 < kv:
                values = turn_back(values, rows)
            elif 2 * chunk < kv:
                values = jnp.where(lanes < HD, turn_back(values, rows), values)
            column = heads * HD + chunk * LANES
            dqkv_ref[rows, column : column + LANES] = values.astype(BF16)
        return _

    lax.fori_loop(0, length // block, finish, 0)


def attend_back(
    bound, order, queries, kx, vx, kt, log_sums, attended, grad, cosine, sine, block, others
):
    length, width = queries.shape
    heads = width // HD
    kv = kx.shape[0]
    cells = heads * length * (length + block) // 2
    vmem = pl.BlockSpec(memory_space=pltpu.VMEM)
    return pl.pallas_call(
        functools.partial(attend_back_kernel, block=block),
        in_specs=[pl.BlockSpec(memory_space=pltpu.SMEM)] + [vmem] * 9 + [ANYWHERE] * len(others),
        out_specs=vmem,
        out_shape=jax.ShapeDtypeStruct((length, width + 2 * kv * HD), BF16),
        scratch_shapes=[
            pltpu.VMEM((kv, 2, length, LANES), F32),
            pltpu.VMEM((kv, 2, length, LANES), F32),
            pltpu.VMEM((heads // kv * HD, block), F32),
        ],
        compiler_params=limit(52),
        cost_estimate=declared(2 * 10 * HD * 4 * cells),
    )(jnp.stack([bound, *order]), queries, kx, vx, kt, log_sums, attended, grad, cosine, sine, *others)


def local(
    inputs,
    segment_ids,
    attn_gain,
    query_weight,
    key_weight,
    value_weight,
    output_weight,
    mlp_gain,
    gate_weight,
    up_weight,
    down_weight,
    cotangent,
    *,
    sizes,
):
    rows = inputs.shape[0]
    length = segment_ids.shape[0]
    query_cols = query_weight.shape[1]
    key_cols = key_weight.shape[1]
    heads, kv = query_cols // HD, key_cols // HD
    columns = query_cols + 2 * key_cols
    slots = slots_of(sizes["tensor"])
    tensor = sizes["tensor"]
    space = (-columns) % query_cols or query_cols
    gains = jnp.pad(jnp.stack([attn_gain, mlp_gain], axis=1), ((0, 0), (0, space - 2)))
    bundle = lax.all_gather(
        jnp.concatenate([query_weight, key_weight, value_weight, gains, output_weight.T], axis=1),
        "dp", axis=0, tiled=True,
    )
    out_own = bundle[:, columns + space :]
    hop = first_hop(inputs, tensor)
    gate_up = lax.all_gather(
        hold(jnp.concatenate([gate_weight, up_weight], axis=1), *(hop or ())),
        "dp", axis=0, tiled=True,
    )

    bound, cosine, sine = rope_tables(segment_ids)
    blocks = second_hop(inputs, hop, tensor)
    stream = inputs.astype(F32)
    arrays = project(slots, blocks, bundle, cosine, sine, heads, kv, length)
    block_a, queries, kx, vx, kt, vt, gains = arrays
    down_t = lax.all_gather(hold(down_weight.T, queries), "dp", axis=0, tiled=True)

    if tensor == 4:
        out_hop = first_hop(hold(out_own, blocks[3]), tensor)
        far, far_sums = attend(bound, slots[3:], queries, kx, vt, rows)
        halves = hold_halves(out_hop, far)
        out_all = second_hop(out_own, out_hop, tensor, halves)
        from_far = lax.ppermute(far, "tensor", pairs(tensor, 3))
        order = [slots[1], slots[2], slots[0], slots[3]]
        near, near_sums = attend(bound, order[:3], queries, kx, vt, rows, halves)
        from_one = lax.ppermute(near[:rows], "tensor", pairs(tensor, 1))
        from_two = lax.ppermute(near[rows : 2 * rows], "tensor", pairs(tensor, 2))
        cotangent_sent = hold(cotangent, out_all[3], from_one, from_two, from_far)
        cotangent_hop = first_hop(cotangent_sent, tensor)
        stream_one, low_m = settle(
            near, 2, [from_one, from_two, from_far], out_all, inputs, gains, [cotangent_sent]
        )
        attended = jnp.concatenate([near, far], axis=0)
        log_sums = jnp.concatenate([near_sums, far_sums], axis=1)
    else:
        order = slots
        out_all = gather(out_own, tensor)
        attended, log_sums = attend(bound, order, queries, kx, vt, rows)
        given = trade([attended[k * rows : (k + 1) * rows] for k in range(tensor)], tensor)
        stream_one, low_m = settle(given[0], 0, given[1:], out_all, inputs, gains)
        cotangent_sent = cotangent
    parts_m = [low_m]
    units = gate_weight.shape[1]

    def feed_at(place, wanted, fed, others=()):
        return feed(
            feed_kernel, place, tensor, [parts_m[k] for k in wanted], [gate_up] * 2, [0, 1], [],
            units, 3, True, 512, fed, others,
        )

    def back_m(places, fed, into=None, others=()):
        return back(places, rows, fed[:2], [gate_up] * 2, [0, 1], into, others)

    def back_out(places, into=None, others=()):
        return back(places, rows, [hidden], [down_t], [0], into, others)

    def reduce_rows(term, *others):
        if others and tensor == 4:
            term = hold(term, *others)
        return lax.psum_scatter(term, "dp", scatter_dimension=0, tiled=True)

    if tensor == 4:
        fed = feed_at(3, [0], None)
        sent = hold(parts_m[0], fed[0], *cotangent_hop)
        hop = first_hop(sent, tensor)
        parts_m = second_hop(sent, hop, tensor)
        fed = feed_at(0, [1, 2], fed, [sent])
        halves = hold_halves(cotangent_hop, fed[0])
        grad_parts = second_hop(cotangent_sent, cotangent_hop, tensor, halves)
        fed = feed_at(2, [3], fed, halves)
    else:
        grad_parts = second_hop(cotangent_sent, None, tensor)
        parts_m = gather(parts_m[0], tensor)
        fed = None
        for place in range(tensor):
            fed = feed_at(place, [place], fed)
    hidden, silu, slope, block_m = fed
    places = [1, 2, 3, 0] if tensor == 4 else list(range(tensor))
    grad_parts = [grad_parts[k] for k in places]

    def feed_back(others=()):
        return feed(
            feed_back_kernel, 0, tensor, grad_parts, [down_t], [0], [silu, slope], units, 2, False, 512,
            None, others,
        )

    if tensor == 4:
        (three_out,) = back_out([2], None, [fed[0]])
        out_one, out_two = out_halves = send_half(three_out, tensor)
        down_t_wgrad = weigh(grad_parts, hidden, [three_out])
        one_out, two_out, own_out = back_out(
            [0, 1, 3], [(out_one, False), (out_two, True), None]
        )
        out_parts = [
            own_out,
            lax.ppermute(one_out, "tensor", pairs(tensor, 1)),
            lax.ppermute(two_out, "tensor", pairs(tensor, 2)),
        ]
        fed = feed_back([one_out])
        (three_m,) = back_m([2], fed)
        m_one, m_two = m_halves = send_half(three_m, tensor)
        gate_wgrad = weigh([block_m], fed[0], [three_m, *out_parts[1:]])
        one_m, two_m = back_m([0, 1], fed, [(m_one, False), (m_two, True)])
        (own_m,) = back_m([3], fed, None, [one_m])
        up_wgrad = weigh([block_m], fed[1], [own_m])
        grad_m_parts = [
            own_m,
            lax.ppermute(one_m, "tensor", pairs(tensor, 1)),
            lax.ppermute(two_m, "tensor", pairs(tensor, 2)),
        ]
    else:
        down_t_wgrad = weigh(grad_parts, hidden)
        fed = feed_back()
        grad_m_parts = sum_whole(back_m(list(range(tensor)), fed))
        gate_wgrad, up_wgrad = weigh([block_m], fed[0]), weigh([block_m], fed[1])
        out_parts = sum_whole(back_out(list(range(tensor))))
    layer_out = (stream_one + total(out_parts)).astype(BF16)
    if tensor != 4:
        out_halves = m_halves = ()
    down_t_low = reduce_rows(down_t_wgrad, *out_halves)
    gate_low = reduce_rows(gate_wgrad, *m_halves)
    up_low = reduce_rows(up_wgrad, *grad_m_parts[1:])

    grad_stream_one, grad_stream_low, *pieces = settle_back(
        grad_m_parts, out_all, cotangent, stream_one, gains
    )
    given = trade(pieces, tensor)
    places = [1, 2, 0, 3] if tensor == 4 else list(range(tensor))
    grad_attended = jnp.concatenate([given[k] for k in places], axis=0)
    grad_qkv = attend_back(
        bound, order, queries, kx, vx, kt, log_sums, attended, grad_attended, cosine, sine, rows,
        [down_t_low],
    )
    if tensor == 4:
        sent = hold(grad_stream_low, grad_attended)
        grad_stream_parts = trade([sent] * 4, tensor)
    else:
        grad_stream_parts = gather(grad_stream_low, tensor)
    grad_stream_parts = [grad_stream_parts[k] for k in places]

    def back_a(places, others=()):
        return back(places, rows, [grad_qkv], [bundle], [0], None, others)

    if tensor == 4:
        (three,) = back_a(slots[3:], [gate_low])
        halves = send_half(three, tensor)
        block_a = hold(block_a, three)
        grad_stream_parts[-1] = hold(grad_stream_parts[-1], three)
    qkv_wgrad = weigh([block_a], grad_qkv)
    out_t_wgrad = weigh(grad_stream_parts, attended)
    attention_wgrad = jnp.concatenate([qkv_wgrad, out_t_wgrad], axis=1)
    gate_sum, up_sum, down_t_sum = [low.astype(F32) for low in (gate_low, up_low, down_t_low)]
    attention_sum = reduce_rows(attention_wgrad, *(halves if tensor == 4 else ())).astype(F32)
    if tensor == 4:
        one, two, own = back_a([slots[1], slots[2], slots[0]], [three])
        grad_a_parts = [own, *send_whole(one, two, halves, tensor)]
    else:
        grad_a_parts = sum_whole(back_a(slots))
    grad_normed_a = total(grad_a_parts)

    def gain_term(gain, weights):
        term = sum(jnp.sum(weight.astype(F32) * grad, axis=1) for weight, grad in weights)
        return term / gain.astype(F32)

    query_sum = attention_sum[:, :query_cols]
    key_sum = attention_sum[:, query_cols : query_cols + key_cols]
    value_sum = attention_sum[:, query_cols + key_cols : columns]
    gain_terms = [
        gain_term(
            attn_gain, [(query_weight, query_sum), (key_weight, key_sum), (value_weight, value_sum)]
        ),
        gain_term(mlp_gain, [(gate_weight, gate_sum), (up_weight, up_sum)]),
    ]
    gain_mine = sum_tensor(jnp.stack(gain_terms), tensor)
    input_grad = (grad_stream_one + norm_back(grad_normed_a, stream, gains[0:1])).astype(BF16)
    return (
        layer_out,
        input_grad,
        gain_mine[0],
        query_sum,
        key_sum,
        value_sum,
        attention_sum[:, columns:].T,
        gain_mine[1],
        gate_sum,
        up_sum,
        down_t_sum.T,
    )


def solution(mesh):
    tokens = P(("dp", "tensor"), None)
    in_specs = (
        tokens,
        P("dp"),
        P("dp"),
        P("dp", "tensor"),
        P("dp", "tensor"),
        P("dp", "tensor"),
        P("tensor", "dp"),
        P("dp"),
        P("dp", "tensor"),
        P("dp", "tensor"),
        P("tensor", "dp"),
        tokens,
    )
    out_specs = (
        tokens,
        tokens,
        P("dp"),
        P("dp", "tensor"),
        P("dp", "tensor"),
        P("dp", "tensor"),
        P("tensor", "dp"),
        P("dp"),
        P("dp", "tensor"),
        P("dp", "tensor"),
        P("tensor", "dp"),
    )
    return jax.shard_map(
        functools.partial(local, sizes={axis: mesh.shape[axis] for axis in ("tensor", "dp")}),
        mesh=mesh, in_specs=in_specs, out_specs=out_specs, check_vma=False,
    )
```

```python
import functools
import math

import jax
import jax.numpy as jnp
from jax import lax
from jax.experimental import pallas as pl
from jax.experimental.pallas import tpu as pltpu
from jax.sharding import PartitionSpec as P

HD = 64
LANES = 128
EPSILON = 1e-05
ROPE_BASE = 500000.0
MASKED = -1e30
OVER_ROWS = (((0,), (0,)), ((), ()))
OVER_COLS = (((1,), (1,)), ((), ()))


def limit(size):
    return pltpu.CompilerParams(vmem_limit_bytes=size * 2**20)


SHORT = 0.0625


def declared(flops, scale=SHORT):
    return pl.CostEstimate(flops=int(flops * scale), bytes_accessed=0, transcendentals=0)


F32 = jnp.float32
BF16 = jnp.bfloat16


def dot_cols(left, right):
    return lax.dot_general(left, right, OVER_COLS, preferred_element_type=F32)


def dot_rows(left, right):
    return lax.dot_general(left, right, OVER_ROWS, preferred_element_type=F32)


def dot(left, right):
    return jnp.dot(left, right, preferred_element_type=F32)


def pairs(size, bit):
    return [(index, index ^ bit) for index in range(size)]


def slots_of(size):
    if size == 4:
        return [lax.axis_index("tensor") ^ step for step in range(size)]
    return [jnp.int32(step) for step in range(size)]


ANYWHERE = pl.BlockSpec(memory_space=pl.ANY)


def nothing_kernel(*refs):
    pass


def hold(value, *others):
    return pl.pallas_call(
        nothing_kernel,
        in_specs=[ANYWHERE] * (1 + len(others)),
        out_specs=ANYWHERE,
        out_shape=jax.ShapeDtypeStruct(value.shape, value.dtype),
        input_output_aliases={0: 0},
        cost_estimate=declared(0),
    )(value, *others)


def first_hop(shard, size):
    if size != 4:
        return None
    return [lax.ppermute(shard, "tensor", pairs(size, bit)) for bit in (1, 2)]


def hold_halves(hop, *others):
    one, two = hop
    half = one.shape[0] // 2
    return hold(one[:half], *others), hold(two[half:], *others)


def second_hop(shard, hop, size, halves=None):
    if size != 4:
        whole = lax.all_gather(shard, "tensor", axis=0)
        return [whole[step] for step in range(size)]
    half = shard.shape[0] // 2
    one, two = hop
    upper, lower = halves or (one[:half], two[half:])
    three_a = lax.ppermute(upper, "tensor", pairs(size, 2))
    three_b = lax.ppermute(lower, "tensor", pairs(size, 1))
    return [shard, one, two, jnp.concatenate([three_a, three_b], axis=0)]


def gather(shard, size):
    return second_hop(shard, first_hop(shard, size), size)


def send_half(three, size):
    half = three.shape[0] // 2
    into_two = lax.ppermute(three[:half], "tensor", pairs(size, 1))
    into_one = lax.ppermute(three[half:], "tensor", pairs(size, 2))
    return into_one, into_two


def send_whole(one, two, into, size):
    into_one, into_two = into
    half = one.shape[0] // 2
    lower = (one[half:].astype(F32) + into_one.astype(F32)).astype(BF16)
    upper = (two[:half].astype(F32) + into_two.astype(F32)).astype(BF16)
    return [
        lax.ppermute(jnp.concatenate([one[:half], lower], axis=0), "tensor", pairs(size, 1)),
        lax.ppermute(jnp.concatenate([upper, two[half:]], axis=0), "tensor", pairs(size, 2)),
    ]


def sum_whole(terms):
    return [
        lax.psum_scatter(
            jnp.concatenate(terms, axis=0), "tensor", scatter_dimension=0, tiled=True
        )
    ]


def trade(pieces, size):
    if size != 4:
        whole = lax.all_to_all(jnp.stack(pieces), "tensor", split_axis=0, concat_axis=0, tiled=True)
        return [whole[step] for step in range(size)]
    return [pieces[0]] + [
        lax.ppermute(pieces[step], "tensor", pairs(size, step)) for step in (1, 2, 3)
    ]


def total(parts):
    return functools.reduce(jnp.add, [part.astype(F32) for part in parts])


def sum_tensor(value, size):
    if size & (size - 1):
        return lax.psum(value, "tensor")
    return value + sum(lax.ppermute(value, "tensor", pairs(size, bit)) for bit in range(1, size))


def rope_tables(segment):
    length = segment.shape[0]
    bound = jnp.sum((segment == 0).astype(jnp.int32))
    place = lax.broadcasted_iota(jnp.int32, (length, LANES), 0)
    place = place - jnp.where(place >= bound, bound, 0)
    lane = lax.broadcasted_iota(jnp.int32, (length, LANES), 1)
    freqs = jnp.exp(
        (lane % (HD // 2)).astype(F32) * (-2.0 * math.log(ROPE_BASE) / HD)
    )
    angles = place.astype(F32) * freqs
    sine = jnp.sin(angles)
    return bound, jnp.cos(angles), jnp.where(lane % HD < HD // 2, -sine, sine)


def swap_halves(values):
    lane = lax.broadcasted_iota(jnp.int32, values.shape, 1)
    after = pltpu.roll(values, LANES - HD // 2, 1)
    before = pltpu.roll(values, HD // 2, 1)
    return jnp.where(lane % HD < HD // 2, after, before)


def normalize(stream):
    scale_r = lax.rsqrt(jnp.mean(stream * stream, axis=-1, keepdims=True) + EPSILON)
    return (stream * scale_r, scale_r)


def project_kernel(slot_ref, *refs, count, steps, heads, kv):
    gains_ref, w_ref, cos_ref, sin_ref = refs[count : count + 4]
    h_ref, q_ref, kx_ref, vx_ref, kt_ref, vt_ref, gain_ref = refs[-7:]

    @pl.when(pl.program_id(0) == 0)
    def _():
        gain_ref[...] = gains_ref[...].astype(F32).T[:8]

    which = pl.program_id(0) // steps
    rows = h_ref.shape[0]
    part_rows = min(256, rows)
    lane = lax.broadcasted_iota(jnp.int32, (part_rows, LANES), 1)
    for start in range(0, rows, part_rows):
        at = slice(start, start + part_rows)
        tokens = refs[0][at, :]
        for block in range(1, count):
            tokens = jnp.where(which == block, refs[block][at, :], tokens)
        normed, _ = normalize(tokens.astype(F32))
        low = (normed * gain_ref[0:1, :]).astype(BF16)
        h_ref[at, :] = low
        pre = dot(low, w_ref[...])
        cosine, sine = cos_ref[at, :], sin_ref[at, :]
        chunks = []
        for chunk in range(pre.shape[1] // LANES):
            columns = slice(chunk * LANES, (chunk + 1) * LANES)
            part = pre[:, columns]
            first = 2 * chunk
            if first < heads + kv:
                turned = part * cosine + swap_halves(part) * sine
                part = turned if first + 1 < heads + kv else jnp.where(lane < HD, turned, part)
            chunks.append(part)
            if first < heads:
                q_ref[at, columns] = (part * (1.0 / math.sqrt(HD))).astype(BF16)
        flipped = {}
        for head in range(2 * kv):
            place = heads + head
            part = chunks[place // 2]
            moved = pltpu.roll(part, HD, 1)
            wide = [part, moved] if place % 2 == 0 else [moved, part]
            out = kx_ref if head < kv else vx_ref
            out[head % kv, 0, at, :] = jnp.where(lane < HD, wide[0], 0.0).astype(BF16)
            out[head % kv, 1, at, :] = jnp.where(lane < HD, 0.0, wide[1]).astype(BF16)
            if place // 2 not in flipped:
                flipped[place // 2] = part.T
            turn = flipped[place // 2][(place % 2) * HD : (place % 2 + 1) * HD]
            out_t = kt_ref if head < kv else vt_ref
            out_t[(head % kv) * HD : (head % kv + 1) * HD, at] = turn.astype(BF16)


def project(slots, blocks, bundle, cosine, sine, heads, kv, length):
    rows, width = blocks[0].shape
    count = len(blocks)
    tile = rows
    steps = rows // tile
    columns = (heads + 2 * kv) * HD

    def at(i, slot):
        return slot[i // steps] * steps + i % steps

    shapes = [
        jax.ShapeDtypeStruct((length, width), BF16),
        jax.ShapeDtypeStruct((length, heads * HD), BF16),
        jax.ShapeDtypeStruct((kv, 2, length, LANES), BF16),
        jax.ShapeDtypeStruct((kv, 2, length, LANES), BF16),
        jax.ShapeDtypeStruct((kv * HD, length), BF16),
        jax.ShapeDtypeStruct((kv * HD, length), BF16),
        jax.ShapeDtypeStruct((8, width), F32),
    ]
    out_specs = [
        pl.BlockSpec((tile, width), lambda i, s: (at(i, s), 0)),
        pl.BlockSpec((tile, heads * HD), lambda i, s: (at(i, s), 0)),
        pl.BlockSpec((kv, 2, tile, LANES), lambda i, s: (0, 0, at(i, s), 0)),
        pl.BlockSpec((kv, 2, tile, LANES), lambda i, s: (0, 0, at(i, s), 0)),
        pl.BlockSpec((kv * HD, tile), lambda i, s: (0, at(i, s))),
        pl.BlockSpec((kv * HD, tile), lambda i, s: (0, at(i, s))),
        pl.BlockSpec((8, width), lambda i, s: (0, 0)),
    ]
    in_specs = [
        pl.BlockSpec((tile, width), lambda i, s, b=block: (jnp.clip(i - b * steps, 0, steps - 1), 0))
        for block in range(count)
    ]
    in_specs += [
        pl.BlockSpec((width, LANES), lambda i, s: (0, columns // LANES)),
        pl.BlockSpec((width, columns), lambda i, s: (0, 0)),
        pl.BlockSpec((tile, LANES), lambda i, s: (at(i, s), 0)),
        pl.BlockSpec((tile, LANES), lambda i, s: (at(i, s), 0)),
    ]
    operands = [jnp.stack(slots), *blocks, bundle, bundle, cosine, sine]
    return pl.pallas_call(
        functools.partial(
            project_kernel, count=count, steps=steps, heads=heads, kv=kv
        ),
        grid_spec=pltpu.PrefetchScalarGridSpec(
            num_scalar_prefetch=1,
            grid=(count * steps,),
            in_specs=in_specs,
            out_specs=out_specs,
        ),
        out_shape=shapes,
        compiler_params=limit(52),
        cost_estimate=declared(2 * count * rows * width * columns),
    )(*operands)


def feed_kernel(*refs, count):
    tokens = refs[:count]
    gate_ref, up_ref = refs[count : count + 2]
    hidden_ref, silu_ref, slope_ref, h_out = refs[-4:]
    rows = tokens[0].shape[0]
    wide = h_out.shape[1]
    tile = min(256, gate_ref.shape[1])
    lanes = pl.ds(pl.multiple_of(pl.program_id(0) * wide, wide), wide)
    for block in range(count):
        h_out[block * rows : (block + 1) * rows, :] = tokens[block][:, lanes]
    for part in range(gate_ref.shape[1] // tile):
        columns = slice(part * tile, (part + 1) * tile)
        for block in range(count):
            where = slice(block * rows, (block + 1) * rows)
            gate = dot(tokens[block][...], gate_ref[:, columns])
            up = dot(tokens[block][...], up_ref[:, columns])
            sigmoid = 0.5 * jnp.tanh(0.5 * gate) + 0.5
            silu = gate * sigmoid
            hidden_ref[where, columns] = (silu * up).astype(BF16)
            silu_ref[where, columns] = silu.astype(BF16)
            slope_ref[where, columns] = (up * (sigmoid + silu * (1.0 - sigmoid))).astype(BF16)


def feed_back_kernel(*refs, count):
    grads = refs[:count]
    down_ref, silu_ref, slope_ref = refs[count : count + 3]
    dgate_ref, dup_ref = refs[-2:]
    rows = grads[0].shape[0]
    for block in range(count):
        where = slice(block * rows, (block + 1) * rows)
        dhidden = dot(grads[block][...], down_ref[...])
        dup_ref[where, :] = (dhidden * silu_ref[where, :].astype(F32)).astype(BF16)
        dgate_ref[where, :] = (dhidden * slope_ref[where, :].astype(F32)).astype(BF16)


def feed(kernel, place, blocks, tokens, weights, places, kept, units, outs, copy, tile, prev, others):
    rows, width = tokens[0].shape
    count = len(tokens)
    steps = max(units // tile, 1)
    tile, wide = units // steps, width // steps
    shapes = [jax.ShapeDtypeStruct((blocks * rows, units), BF16)] * outs
    in_specs = [pl.BlockSpec((rows, width), lambda i: (0, 0), pipeline_mode=pl.Buffered(1))] * count
    in_specs += [
        pl.BlockSpec((width, tile), lambda i, w=which: (0, w * steps + i)) for which in places
    ]
    cell = pl.BlockSpec((count * rows, tile), lambda i: (place, i))
    in_specs += [cell] * len(kept)
    out_specs = [cell] * outs
    if copy:
        shapes.append(jax.ShapeDtypeStruct((blocks * rows, width), BF16))
        out_specs.append(pl.BlockSpec((count * rows, wide), lambda i: (place, i)))
    operands = [*tokens, *weights, *kept]
    aliases = {}
    if prev is not None:
        for index, array in enumerate(prev):
            aliases[len(operands)] = index
            operands.append(array)
            in_specs.append(ANYWHERE)
    operands += others
    in_specs += [ANYWHERE] * len(others)
    return pl.pallas_call(
        functools.partial(kernel, count=count),
        grid=(steps,),
        in_specs=in_specs,
        out_specs=out_specs,
        out_shape=shapes,
        input_output_aliases=aliases,
        compiler_params=limit(52),
        cost_estimate=declared(2 * len(weights) * count * rows * width * units),
    )(*operands)


def back_kernel(slot_ref, *refs, count, terms, added):
    outs = refs[-count:]
    weights = refs[count * terms : (count + 1) * terms]
    into = list(refs[(count + 1) * terms :])
    for block in range(count):
        value = dot_cols(refs[block * terms][...], weights[0][...])
        for term in range(1, terms):
            value = value + dot_cols(refs[block * terms + term][...], weights[term][...])
        if added[block] is None:
            outs[block][...] = value.astype(BF16)
            continue
        half = value.shape[0] // 2
        extra = into.pop(0)[...].astype(F32)
        top, bottom = value[:half], value[half:]
        if added[block]:
            top = top + extra
        else:
            bottom = bottom + extra
        outs[block][:half, :] = top.astype(BF16)
        outs[block][half:, :] = bottom.astype(BF16)


def back(slots, rows, lefts, weights, places, into=None, others=()):
    depth = lefts[0].shape[1]
    width = weights[0].shape[0]
    tile = min(512, width)
    terms, count = len(lefts), len(slots)
    into = into or [None] * count
    in_specs, operands = [], [jnp.stack([jnp.asarray(slot, jnp.int32) for slot in slots])]
    for block in range(count):
        in_specs += [pl.BlockSpec((rows, depth), lambda i, s, b=block: (s[b], 0))] * terms
        operands += lefts
    in_specs += [pl.BlockSpec((tile, depth), lambda i, s, p=place: (i, p)) for place in places]
    operands += weights
    for extra in into:
        if extra is not None:
            in_specs.append(pl.BlockSpec((rows // 2, tile), lambda i, s: (0, i)))
            operands.append(extra[0])
    operands += others
    in_specs += [ANYWHERE] * len(others)
    return pl.pallas_call(
        functools.partial(
            back_kernel,
            count=count,
            terms=terms,
            added=[None if extra is None else extra[1] for extra in into],
        ),
        grid_spec=pltpu.PrefetchScalarGridSpec(
            num_scalar_prefetch=1,
            grid=(width // tile,),
            in_specs=in_specs,
            out_specs=[pl.BlockSpec((rows, tile), lambda i, s: (0, i))] * count,
        ),
        out_shape=[jax.ShapeDtypeStruct((rows, width), BF16)] * count,
        compiler_params=limit(52),
        cost_estimate=declared(2 * count * terms * rows * width * depth),
    )(*operands)


def turn_kernel(value_ref, *rest):
    rest[-1][...] = value_ref[...].T


def turn(value, others=()):
    rows, columns = value.shape
    tile = min(512, rows)
    return pl.pallas_call(
        turn_kernel,
        grid=(rows // tile,),
        in_specs=[pl.BlockSpec((tile, columns), lambda i: (i, 0))] + [ANYWHERE] * len(others),
        out_specs=pl.BlockSpec((columns, tile), lambda i: (0, i)),
        out_shape=jax.ShapeDtypeStruct((columns, rows), value.dtype),
        compiler_params=limit(52),
        cost_estimate=declared(0),
    )(value, *others)


def turn_blocks(lefts, turned_ref):
    rows = lefts[0].shape[0]
    for block, left in enumerate(lefts):
        turned_ref[:, block * rows : (block + 1) * rows] = left[...].T


def weigh_kernel(*refs, count):
    lefts, right_ref = refs[:count], refs[count]
    out_ref, *turned = refs[-3:]
    i, j = pl.program_id(0), pl.program_id(1)
    last = j == pl.num_programs(1) - 1

    @pl.when((i == 0) & (j == 0))
    def _():
        turn_blocks(lefts, turned[0])

    for parity in range(2):

        @pl.when((i % 2 == parity) & jnp.logical_not(last))
        def _():
            out_ref[...] = dot(turned[parity][...], right_ref[...]).astype(BF16)

        @pl.when((i % 2 == parity) & last)
        def _():
            out_ref[...] = dot(turned[parity][...], right_ref[...]).astype(BF16)
            turn_blocks(lefts, turned[1 - parity])


def weigh(lefts, right, others=()):
    tokens, columns = right.shape
    rows, width = lefts[0].shape
    tall, wide = min(512, width), min(1024, columns // 2)
    tiles, steps = width // tall, columns // wide

    def ahead(i, j):
        return 0, jnp.minimum(i + jnp.where(j == steps - 1, 1, 0), tiles - 1)

    return pl.pallas_call(
        functools.partial(weigh_kernel, count=len(lefts)),
        grid=(tiles, steps),
        in_specs=[pl.BlockSpec((rows, tall), ahead)] * len(lefts)
        + [pl.BlockSpec((tokens, wide), lambda i, j: (0, j))]
        + [ANYWHERE] * len(others),
        out_specs=pl.BlockSpec((tall, wide), lambda i, j: (i, j)),
        out_shape=jax.ShapeDtypeStruct((width, columns), BF16),
        scratch_shapes=[pltpu.VMEM((tall, tokens), BF16)] * 2,
        compiler_params=limit(52),
        cost_estimate=declared(2 * tokens * width * columns),
    )(*lefts, right, *others)


def weigh_both_kernel(*refs, count):
    one_ref, others = refs[0], refs[1 : 1 + count]
    right_ref, other_ref, out_ref, turned_ref, other_turned_ref = refs[1 + count :]
    columns = right_ref.shape[1]
    turn_blocks([one_ref], turned_ref)
    out_ref[:, :columns] = dot(turned_ref[...], right_ref[...]).astype(BF16)
    turn_blocks(others, other_turned_ref)
    out_ref[:, columns:] = dot(other_turned_ref[...], other_ref[...]).astype(BF16)


def weigh_both(one, right, others, other_right):
    tokens, width = one.shape
    rows = others[0].shape[0]
    columns, more = right.shape[1], other_right.shape[1]
    tall = min(512, width)
    whole = [pl.BlockSpec((tokens, columns), lambda i: (0, 0))]
    whole += [pl.BlockSpec((tokens, more), lambda i: (0, 0))]
    return pl.pallas_call(
        functools.partial(weigh_both_kernel, count=len(others)),
        grid=(width // tall,),
        in_specs=[pl.BlockSpec((tokens, tall), lambda i: (0, i))]
        + [pl.BlockSpec((rows, tall), lambda i: (0, i))] * len(others)
        + whole,
        out_specs=pl.BlockSpec((tall, columns + more), lambda i: (i, 0)),
        out_shape=jax.ShapeDtypeStruct((width, columns + more), BF16),
        scratch_shapes=[pltpu.VMEM((tall, tokens), BF16)] * 2,
        compiler_params=limit(52),
        cost_estimate=declared(2 * tokens * width * (columns + more)),
    )(one, *others, right, other_right)


def settle_kernel(*refs, count):
    pieces, weights = refs[:count], refs[count : 2 * count]
    x_ref, gains_ref = refs[2 * count : 2 * count + 2]
    stream_ref, h_ref = refs[-2:]
    stream = x_ref[...].astype(F32)
    for piece, weight in zip(pieces, weights):
        stream = stream + dot_cols(piece[...], weight[...])
    stream_ref[...] = stream
    normed, _ = normalize(stream)
    h_ref[...] = (normed * gains_ref[1:2, :]).astype(BF16)


def settle(own, place, pieces, weights, tokens, gains, others=()):
    rows, width = tokens.shape
    depth = weights[0].shape[1]
    tile = min(256, rows)
    steps = rows // tile
    wide = pl.BlockSpec((tile, width), lambda i: (i, 0))
    piece = pl.BlockSpec((tile, depth), lambda i: (i, 0))
    weight = pl.BlockSpec((width, depth), lambda i: (0, 0), pipeline_mode=pl.Buffered(1))
    return pl.pallas_call(
        functools.partial(settle_kernel, count=len(weights)),
        grid=(steps,),
        in_specs=[pl.BlockSpec((tile, depth), lambda i: (place * steps + i, 0))]
        + [piece] * len(pieces)
        + [weight] * len(weights)
        + [wide, pl.BlockSpec((8, width), lambda i: (0, 0))]
        + [ANYWHERE] * len(others),
        out_specs=[wide, wide],
        out_shape=[
            jax.ShapeDtypeStruct((rows, width), F32),
            jax.ShapeDtypeStruct((rows, width), BF16),
        ],
        compiler_params=limit(52),
        cost_estimate=declared(2 * len(weights) * rows * width * depth),
    )(own, *pieces, *weights, tokens, gains, *others)


def norm_back(grad_in, stream, gain):
    normed, scale_r = normalize(stream)
    scaled = grad_in * gain
    return scale_r * (scaled - normed * jnp.mean(scaled * normed, axis=-1, keepdims=True))


def settle_back_kernel(*refs, parts, count):
    terms, weights = refs[:parts], refs[parts : parts + count]
    grad_ref, stream_ref, gains_ref, out_ref, low_ref = refs[parts + count : parts + count + 5]
    pieces = refs[parts + count + 5 :]
    grad_in = terms[0][...].astype(F32)
    for term in terms[1:]:
        grad_in = grad_in + term[...].astype(F32)
    grad = grad_ref[...].astype(F32) + norm_back(grad_in, stream_ref[...], gains_ref[1:2, :])
    out_ref[...] = grad
    low = grad.astype(BF16)
    low_ref[...] = low
    for piece, weight in zip(pieces, weights):
        piece[...] = dot(low, weight[...]).astype(BF16)


def settle_back(terms, weights, grad, stream, gains):
    rows, width = grad.shape
    depth = weights[0].shape[1]
    tile = min(256, rows)
    wide = pl.BlockSpec((tile, width), lambda i: (i, 0))
    weight = pl.BlockSpec((width, depth), lambda i: (0, 0), pipeline_mode=pl.Buffered(1))
    return pl.pallas_call(
        functools.partial(settle_back_kernel, parts=len(terms), count=len(weights)),
        grid=(rows // tile,),
        in_specs=[wide] * len(terms)
        + [weight] * len(weights)
        + [wide, wide, pl.BlockSpec((8, width), lambda i: (0, 0))],
        out_specs=[wide, wide] + [pl.BlockSpec((tile, depth), lambda i: (i, 0))] * len(weights),
        out_shape=[
            jax.ShapeDtypeStruct((rows, width), F32),
            jax.ShapeDtypeStruct((rows, width), BF16),
        ]
        + [jax.ShapeDtypeStruct((rows, depth), BF16)] * len(weights),
        compiler_params=limit(52),
        cost_estimate=declared(2 * len(weights) * rows * width * depth),
    )(*terms, *weights, grad, stream, gains)


def causal(keys, queries):
    key = lax.broadcasted_iota(jnp.int32, (keys, queries), 0)
    return key <= lax.broadcasted_iota(jnp.int32, (keys, queries), 1)


def first_block(bound, offset, block):
    return jnp.where(offset >= bound, lax.div(bound, jnp.int32(block)), 0)


def attend_kernel(order_ref, q_ref, kx_ref, vt_ref, *rest, block):
    out_ref, lse_ref, top_ref, acc_ref = rest[-4:]
    kv = kx_ref.shape[0]
    per = q_ref.shape[1] // LANES // kv
    bound = order_ref[0]
    ones = jnp.ones((16, block), BF16)
    for group in range(kv):

        def q_step(turn, _):
            index = order_ref[1 + turn]
            offset = pl.multiple_of(index * block, block)
            into = pl.ds(pl.multiple_of(turn * block, block), block)
            top_ref[...] = jnp.full(top_ref.shape, MASKED, F32)
            acc_ref[...] = jnp.zeros(acc_ref.shape, F32)

            def tile(step, diagonal):
                keys = pl.ds(pl.multiple_of(step, block), block)
                value_t = jnp.concatenate(
                    [vt_ref[group * HD : (group + 1) * HD, keys], ones], axis=0
                )
                for head in range(2 * per):
                    column = (group * per + head // 2) * LANES
                    query = q_ref[pl.ds(offset, block), column : column + LANES]
                    scores = dot_cols(kx_ref[group, head % 2, keys, :], query)
                    if diagonal:
                        scores = jnp.where(causal(block, block), scores, MASKED)
                    old = top_ref[head, 0:1, :]
                    top = jnp.maximum(old, jnp.max(scores, axis=0, keepdims=True))
                    powered = jnp.exp(scores - top).astype(BF16)
                    acc_ref[head] = acc_ref[head] * jnp.exp(old - top) + dot(value_t, powered)
                    top_ref[head, 0:1, :] = top

            def full_tile(step, carry):
                tile(step * block, False)
                return carry

            lax.fori_loop(first_block(bound, offset, block), index, full_tile, 0)
            tile(offset, True)
            for pair in range(per):
                both = []
                for head in (2 * pair, 2 * pair + 1):
                    total = acc_ref[head, HD : HD + 1, :]
                    both.append(acc_ref[head, :HD, :] / total)
                    place = group * 2 * per + head
                    lse_ref[place : place + 1, into] = top_ref[
                        head, 0:1, :
                    ] + jnp.log(total)
                column = (group * per + pair) * LANES
                out_ref[into, column : column + LANES] = (
                    jnp.concatenate(both, axis=0).T.astype(BF16)
                )
            return _

        lax.fori_loop(0, out_ref.shape[0] // block, q_step, 0)


def attend(bound, order, queries, kx, vt, block, others=()):
    length, width = queries.shape
    heads = width // HD
    kv = kx.shape[0]
    per = heads // kv
    count = len(order)
    cells = heads * count * block * (length + block) // 2
    vmem = pl.BlockSpec(memory_space=pltpu.VMEM)
    return pl.pallas_call(
        functools.partial(attend_kernel, block=block),
        in_specs=[pl.BlockSpec(memory_space=pltpu.SMEM), vmem, vmem, vmem] + [ANYWHERE] * len(others),
        out_specs=[vmem, vmem],
        out_shape=[
            jax.ShapeDtypeStruct((count * block, width), BF16),
            jax.ShapeDtypeStruct((heads, count * block), F32),
        ],
        scratch_shapes=[
            pltpu.VMEM((per, 8, block), F32),
            pltpu.VMEM((per, HD + 16, block), F32),
        ],
        compiler_params=limit(52),
        cost_estimate=declared(2 * 4 * HD * 4 * cells, 16),
    )(jnp.stack([bound, *order]), queries, kx, vt, *others)


def attend_back_kernel(
    order_ref, q_ref, kx_ref, vx_ref, kt_ref, lse_ref, out_ref, grad_ref, cos_ref, sin_ref,
    *rest, block
):
    dqkv_ref, dk_ref, dv_ref, dq_ref = rest[-4:]
    length = q_ref.shape[0]
    kv = kx_ref.shape[0]
    heads = q_ref.shape[1] // HD
    per = heads // 2 // kv
    bound = order_ref[0]
    dk_ref[...] = jnp.zeros(dk_ref.shape, F32)
    dv_ref[...] = jnp.zeros(dv_ref.shape, F32)
    lane = lax.broadcasted_iota(jnp.int32, (8, LANES), 1)
    row = lax.broadcasted_iota(jnp.int32, (8, LANES), 0)
    chosen = ((lane // HD) == row).astype(F32)

    def turn_back(values, rows):
        return values * cos_ref[rows, :] - swap_halves(values) * sin_ref[rows, :]

    for group in range(kv):

        def q_step(turn, _):
            index = order_ref[1 + turn]
            offset = pl.multiple_of(index * block, block)
            rows = pl.ds(offset, block)
            given = pl.ds(pl.multiple_of(turn * block, block), block)
            dq_ref[...] = jnp.zeros(dq_ref.shape, F32)
            deltas = []
            for pair in range(per):
                column = (group * per + pair) * LANES
                product = grad_ref[given, column : column + LANES].astype(F32) * out_ref[
                    given, column : column + LANES
                ].astype(F32)
                deltas.append(
                    lax.dot_general(
                        chosen, product, OVER_COLS, precision=lax.Precision.HIGHEST,
                        preferred_element_type=F32,
                    )
                )

            def tile(step, size, skip, diagonal):
                keys = pl.ds(pl.multiple_of(step, size), size)
                key_t = kt_ref[group * HD : (group + 1) * HD, keys]
                mine = pl.ds(offset + skip, block - skip)
                theirs = pl.ds(turn * block + skip, block - skip)
                for parity in range(2):
                    key_add, value_add = 0.0, 0.0
                    for pair in range(per):
                        head = 2 * pair + parity
                        place = group * 2 * per + head
                        column = (group * per + pair) * LANES
                        query = q_ref[mine, column : column + LANES]
                        grad = grad_ref[theirs, column : column + LANES]
                        scores = dot_cols(kx_ref[group, parity, keys, :], query)
                        if diagonal:
                            scores = jnp.where(causal(size, block - skip), scores, MASKED)
                        probs = jnp.exp(scores - lse_ref[place : place + 1, given][:, skip:])
                        dprobs = dot_cols(vx_ref[group, parity, keys, :], grad)
                        delta = deltas[pair][parity : parity + 1, skip:]
                        dscores = (probs * (dprobs - delta)).astype(BF16)
                        value_add = value_add + dot(probs.astype(BF16), grad)
                        key_add = key_add + dot(dscores, query)
                        dq_ref[head * HD : (head + 1) * HD, skip:] += dot(key_t, dscores)
                    dk_ref[group, parity, keys, :] += key_add
                    dv_ref[group, parity, keys, :] += value_add

            def full_tile(step, carry):
                tile(step * block, block, 0, False)
                return carry

            lax.fori_loop(first_block(bound, offset, block), index, full_tile, 0)
            tile(offset, block // 2, 0, True)
            tile(offset + block // 2, block // 2, block // 2, True)
            for pair in range(per):
                column = (group * per + pair) * LANES
                grad_q = dq_ref[pair * LANES : (pair + 1) * LANES, :].T * (1.0 / math.sqrt(HD))
                dqkv_ref[rows, column : column + LANES] = turn_back(grad_q, rows).astype(BF16)
            return _

        lax.fori_loop(0, length // block, q_step, 0)

    def finish(index, _):
        rows = pl.ds(pl.multiple_of(index * block, block), block)
        lanes = lax.broadcasted_iota(jnp.int32, (block, LANES), 1)

        def placed(part, half):
            ref = dk_ref if part < kv else dv_ref
            even, odd = ref[part % kv, 0, rows, :], ref[part % kv, 1, rows, :]
            return even + pltpu.roll(odd, HD, 1) if half == 0 else pltpu.roll(even, HD, 1) + odd

        for chunk in range(kv):
            values = jnp.where(lanes < HD, placed(2 * chunk, 0), placed(2 * chunk + 1, 1))
            if 2 * chunk + 1 < kv:
                values = turn_back(values, rows)
            elif 2 * chunk < kv:
                values = jnp.where(lanes < HD, turn_back(values, rows), values)
            column = heads * HD + chunk * LANES
            dqkv_ref[rows, column : column + LANES] = values.astype(BF16)
        return _

    lax.fori_loop(0, length // block, finish, 0)


def attend_back(
    bound, order, queries, kx, vx, kt, log_sums, attended, grad, cosine, sine, block, others
):
    length, width = queries.shape
    heads = width // HD
    kv = kx.shape[0]
    cells = heads * length * (length + block) // 2
    vmem = pl.BlockSpec(memory_space=pltpu.VMEM)
    return pl.pallas_call(
        functools.partial(attend_back_kernel, block=block),
        in_specs=[pl.BlockSpec(memory_space=pltpu.SMEM)] + [vmem] * 9 + [ANYWHERE] * len(others),
        out_specs=vmem,
        out_shape=jax.ShapeDtypeStruct((length, width + 2 * kv * HD), BF16),
        scratch_shapes=[
            pltpu.VMEM((kv, 2, length, LANES), F32),
            pltpu.VMEM((kv, 2, length, LANES), F32),
            pltpu.VMEM((heads // kv * HD, block), F32),
        ],
        compiler_params=limit(52),
        cost_estimate=declared(2 * 10 * HD * 4 * cells),
    )(jnp.stack([bound, *order]), queries, kx, vx, kt, log_sums, attended, grad, cosine, sine, *others)


def local(
    inputs,
    segment_ids,
    attn_gain,
    query_weight,
    key_weight,
    value_weight,
    output_weight,
    mlp_gain,
    gate_weight,
    up_weight,
    down_weight,
    cotangent,
    *,
    sizes,
):
    rows = inputs.shape[0]
    length = segment_ids.shape[0]
    query_cols = query_weight.shape[1]
    key_cols = key_weight.shape[1]
    heads, kv = query_cols // HD, key_cols // HD
    columns = query_cols + 2 * key_cols
    slots = slots_of(sizes["tensor"])
    tensor = sizes["tensor"]
    space = (-columns) % query_cols or query_cols
    gains = jnp.pad(jnp.stack([attn_gain, mlp_gain], axis=1), ((0, 0), (0, space - 2)))
    bundle = lax.all_gather(
        jnp.concatenate([query_weight, key_weight, value_weight, gains, output_weight.T], axis=1),
        "dp", axis=0, tiled=True,
    )
    out_own = bundle[:, columns + space :]
    hop = first_hop(inputs, tensor)
    gate_up = lax.all_gather(
        hold(jnp.concatenate([gate_weight, up_weight], axis=1), *(hop or ())),
        "dp", axis=0, tiled=True,
    )

    bound, cosine, sine = rope_tables(segment_ids)
    blocks = second_hop(inputs, hop, tensor)
    stream = inputs.astype(F32)
    arrays = project(slots, blocks, bundle, cosine, sine, heads, kv, length)
    block_a, queries, kx, vx, kt, vt, gains = arrays
    down_t = lax.all_gather(hold(turn(down_weight, [cosine]), queries), "dp", axis=0, tiled=True)

    if tensor == 4:
        out_own = hold(out_own, blocks[3])
        out_hop = first_hop(out_own, tensor)
        far, far_sums = attend(bound, slots[3:], queries, kx, vt, rows)
        from_far = lax.ppermute(far, "tensor", pairs(tensor, 3))
        near, near_sums = attend(bound, slots[1:3], queries, kx, vt, rows, [far])
        from_one = lax.ppermute(near[:rows], "tensor", pairs(tensor, 1))
        from_two = lax.ppermute(near[rows:], "tensor", pairs(tensor, 2))
        halves = hold_halves(out_hop, near)
        out_all = second_hop(out_own, out_hop, tensor, halves)
        own, own_sums = attend(bound, slots[:1], queries, kx, vt, rows, halves)
        cotangent_sent = hold(cotangent, own, out_all[3], from_one, from_two, from_far)
        cotangent_hop = first_hop(cotangent_sent, tensor)
        stream_one, low_m = settle(
            own, 0, [from_one, from_two, from_far], out_all, inputs, gains, [cotangent_sent]
        )
        order = [slots[1], slots[2], slots[0], slots[3]]
        attended = jnp.concatenate([near, own, far], axis=0)
        log_sums = jnp.concatenate([near_sums, own_sums, far_sums], axis=1)
    else:
        order = slots
        out_all = gather(out_own, tensor)
        attended, log_sums = attend(bound, order, queries, kx, vt, rows)
        given = trade([attended[k * rows : (k + 1) * rows] for k in range(tensor)], tensor)
        stream_one, low_m = settle(given[0], 0, given[1:], out_all, inputs, gains)
        cotangent_sent = cotangent
    parts_m = [low_m]
    units = gate_weight.shape[1]

    def feed_at(place, wanted, fed, others=()):
        return feed(
            feed_kernel, place, tensor, [parts_m[k] for k in wanted], [gate_up] * 2, [0, 1], [],
            units, 3, True, 512, fed, others,
        )

    def back_m(places, fed, into=None, others=()):
        return back(places, rows, fed[:2], [gate_up] * 2, [0, 1], into, others)

    def back_out(places, into=None, others=()):
        return back(places, rows, [hidden], [down_t], [0], into, others)

    def reduce_rows(term, *others):
        if others and tensor == 4:
            term = hold(term, *others)
        return lax.psum_scatter(term, "dp", scatter_dimension=0, tiled=True)

    if tensor == 4:
        fed = feed_at(3, [0], None)
        sent = hold(parts_m[0], fed[0], *cotangent_hop)
        hop = first_hop(sent, tensor)
        parts_m = second_hop(sent, hop, tensor)
        fed = feed_at(0, [1, 2], fed, [sent])
        halves = hold_halves(cotangent_hop, fed[0])
        grad_parts = second_hop(cotangent_sent, cotangent_hop, tensor, halves)
        fed = feed_at(2, [3], fed, halves)
    else:
        grad_parts = second_hop(cotangent_sent, None, tensor)
        parts_m = gather(parts_m[0], tensor)
        fed = None
        for place in range(tensor):
            fed = feed_at(place, [place], fed)
    hidden, silu, slope, block_m = fed
    places = [1, 2, 3, 0] if tensor == 4 else list(range(tensor))
    grad_parts = [grad_parts[k] for k in places]

    def feed_back(others=()):
        return feed(
            feed_back_kernel, 0, tensor, grad_parts, [down_t], [0], [silu, slope], units, 2, False, 512,
            None, others,
        )

    if tensor == 4:
        (three_out,) = back_out([2], None, [fed[0]])
        out_one, out_two = out_halves = send_half(three_out, tensor)
        down_t_wgrad = weigh(grad_parts, hidden, [three_out])
        one_out, two_out, own_out = back_out(
            [0, 1, 3], [(out_one, False), (out_two, True), None]
        )
        out_parts = [
            own_out,
            lax.ppermute(one_out, "tensor", pairs(tensor, 1)),
            lax.ppermute(two_out, "tensor", pairs(tensor, 2)),
        ]
        fed = feed_back([one_out])
        (three_m,) = back_m([2], fed)
        m_one, m_two = m_halves = send_half(three_m, tensor)
        gate_wgrad = weigh([block_m], fed[0], [three_m, *out_parts[1:]])
        one_m, two_m = back_m([0, 1], fed, [(m_one, False), (m_two, True)])
        (own_m,) = back_m([3], fed, None, [one_m])
        up_wgrad = weigh([block_m], fed[1], [own_m])
        grad_m_parts = [
            own_m,
            lax.ppermute(one_m, "tensor", pairs(tensor, 1)),
            lax.ppermute(two_m, "tensor", pairs(tensor, 2)),
        ]
    else:
        down_t_wgrad = weigh(grad_parts, hidden)
        fed = feed_back()
        grad_m_parts = sum_whole(back_m(list(range(tensor)), fed))
        gate_wgrad, up_wgrad = weigh([block_m], fed[0]), weigh([block_m], fed[1])
        out_parts = sum_whole(back_out(list(range(tensor))))
    layer_out = (stream_one + total(out_parts)).astype(BF16)
    if tensor != 4:
        out_halves = m_halves = ()
    down_t_low = reduce_rows(down_t_wgrad, *out_halves)
    gate_low = reduce_rows(gate_wgrad, *m_halves)
    up_low = reduce_rows(up_wgrad, *grad_m_parts[1:])

    grad_stream_one, grad_stream_low, *pieces = settle_back(
        grad_m_parts, out_all, cotangent, stream_one, gains
    )
    given = trade(pieces, tensor)
    places = [1, 2, 0, 3] if tensor == 4 else list(range(tensor))
    grad_attended = jnp.concatenate([given[k] for k in places], axis=0)
    grad_qkv = attend_back(
        bound, order, queries, kx, vx, kt, log_sums, attended, grad_attended, cosine, sine, rows,
        [down_t_low],
    )
    if tensor == 4:
        sent = hold(grad_stream_low, grad_attended)
        grad_stream_parts = trade([sent] * 4, tensor)
    else:
        grad_stream_parts = gather(grad_stream_low, tensor)
    grad_stream_parts = [grad_stream_parts[k] for k in places]

    def back_a(places, others=()):
        return back(places, rows, [grad_qkv], [bundle], [0], None, others)

    if tensor == 4:
        (three,) = back_a(slots[3:], [gate_low])
        halves = send_half(three, tensor)
        block_a = hold(block_a, three)
    attention_wgrad = weigh_both(block_a, grad_qkv, grad_stream_parts, attended)
    gate_sum, up_sum, down_t_sum = [low.astype(F32) for low in (gate_low, up_low, down_t_low)]
    attention_sum = reduce_rows(attention_wgrad, *(halves if tensor == 4 else ())).astype(F32)
    if tensor == 4:
        one, two, own = back_a([slots[1], slots[2], slots[0]], [three])
        grad_a_parts = [own, *send_whole(one, two, halves, tensor)]
    else:
        grad_a_parts = sum_whole(back_a(slots))
    grad_normed_a = total(grad_a_parts)

    def gain_term(gain, weights):
        term = sum(jnp.sum(weight.astype(F32) * grad, axis=1) for weight, grad in weights)
        return term / gain.astype(F32)

    query_sum = attention_sum[:, :query_cols]
    key_sum = attention_sum[:, query_cols : query_cols + key_cols]
    value_sum = attention_sum[:, query_cols + key_cols : columns]
    gain_terms = [
        gain_term(
            attn_gain, [(query_weight, query_sum), (key_weight, key_sum), (value_weight, value_sum)]
        ),
        gain_term(mlp_gain, [(gate_weight, gate_sum), (up_weight, up_sum)]),
    ]
    gain_mine = sum_tensor(jnp.stack(gain_terms), tensor)
    input_grad = (grad_stream_one + norm_back(grad_normed_a, stream, gains[0:1])).astype(BF16)
    return (
        layer_out,
        input_grad,
        gain_mine[0],
        query_sum,
        key_sum,
        value_sum,
        attention_sum[:, columns:].T,
        gain_mine[1],
        gate_sum,
        up_sum,
        down_t_sum.T,
    )


def solution(mesh):
    tokens = P(("dp", "tensor"), None)
    in_specs = (
        tokens,
        P("dp"),
        P("dp"),
        P("dp", "tensor"),
        P("dp", "tensor"),
        P("dp", "tensor"),
        P("tensor", "dp"),
        P("dp"),
        P("dp", "tensor"),
        P("dp", "tensor"),
        P("tensor", "dp"),
        tokens,
    )
    out_specs = (
        tokens,
        tokens,
        P("dp"),
        P("dp", "tensor"),
        P("dp", "tensor"),
        P("dp", "tensor"),
        P("tensor", "dp"),
        P("dp"),
        P("dp", "tensor"),
        P("dp", "tensor"),
        P("tensor", "dp"),
    )
    return jax.shard_map(
        functools.partial(local, sizes={axis: mesh.shape[axis] for axis in ("tensor", "dp")}),
        mesh=mesh, in_specs=in_specs, out_specs=out_specs, check_vma=False,
    )
```

```python
import functools
import math

import jax
import jax.numpy as jnp
from jax import lax
from jax.experimental import pallas as pl
from jax.experimental.pallas import tpu as pltpu
from jax.sharding import PartitionSpec as P

HD = 64
LANES = 128
EPSILON = 1e-05
ROPE_BASE = 500000.0
MASKED = -1e30
OVER_ROWS = (((0,), (0,)), ((), ()))
OVER_COLS = (((1,), (1,)), ((), ()))


def limit(size):
    return pltpu.CompilerParams(vmem_limit_bytes=size * 2**20)


SHORT = 0.0625


def declared(flops, scale=SHORT):
    return pl.CostEstimate(flops=int(flops * scale), bytes_accessed=0, transcendentals=0)


F32 = jnp.float32
BF16 = jnp.bfloat16


def dot_cols(left, right):
    return lax.dot_general(left, right, OVER_COLS, preferred_element_type=F32)


def dot_rows(left, right):
    return lax.dot_general(left, right, OVER_ROWS, preferred_element_type=F32)


def dot(left, right):
    return jnp.dot(left, right, preferred_element_type=F32)


def pairs(size, bit):
    return [(index, index ^ bit) for index in range(size)]


def slots_of(size):
    if size == 4:
        return [lax.axis_index("tensor") ^ step for step in range(size)]
    return [jnp.int32(step) for step in range(size)]


ANYWHERE = pl.BlockSpec(memory_space=pl.ANY)


def nothing_kernel(*refs):
    pass


def hold(value, *others):
    return pl.pallas_call(
        nothing_kernel,
        in_specs=[ANYWHERE] * (1 + len(others)),
        out_specs=ANYWHERE,
        out_shape=jax.ShapeDtypeStruct(value.shape, value.dtype),
        input_output_aliases={0: 0},
        cost_estimate=declared(0),
    )(value, *others)


def first_hop(shard, size):
    if size != 4:
        return None
    return [lax.ppermute(shard, "tensor", pairs(size, bit)) for bit in (1, 2)]


def copy_kernel(value_ref, *rest):
    rest[-1][...] = value_ref[...]


def half_of(value, which, *others):
    rows, width = value.shape
    tile = rows // 4
    return pl.pallas_call(
        copy_kernel,
        grid=(2,),
        in_specs=[pl.BlockSpec((tile, width), lambda i: (2 * which + i, 0))]
        + [ANYWHERE] * len(others),
        out_specs=pl.BlockSpec((tile, width), lambda i: (i, 0)),
        out_shape=jax.ShapeDtypeStruct((rows // 2, width), value.dtype),
        compiler_params=limit(52),
        cost_estimate=declared(0),
    )(value, *others)


def hold_halves(hop, *others):
    return half_of(hop[0], 0, *others), half_of(hop[1], 1, *others)


def second_hop(shard, hop, size, halves=None):
    if size != 4:
        whole = lax.all_gather(shard, "tensor", axis=0)
        return [whole[step] for step in range(size)]
    one, two = hop
    upper, lower = halves or hold_halves(hop)
    three_a = lax.ppermute(upper, "tensor", pairs(size, 2))
    three_b = lax.ppermute(lower, "tensor", pairs(size, 1))
    return [shard, one, two, jnp.concatenate([three_a, three_b], axis=0)]


def gather(shard, size):
    return second_hop(shard, first_hop(shard, size), size)


def send_half(three, size):
    into_two = lax.ppermute(three[0], "tensor", pairs(size, 1))
    into_one = lax.ppermute(three[1], "tensor", pairs(size, 2))
    return into_one, into_two


def send_whole(one, two, into, size):
    into_one, into_two = into
    half = one.shape[0] // 2
    lower = (one[half:].astype(F32) + into_one.astype(F32)).astype(BF16)
    upper = (two[:half].astype(F32) + into_two.astype(F32)).astype(BF16)
    return [
        lax.ppermute(jnp.concatenate([one[:half], lower], axis=0), "tensor", pairs(size, 1)),
        lax.ppermute(jnp.concatenate([upper, two[half:]], axis=0), "tensor", pairs(size, 2)),
    ]


def sum_whole(terms):
    return [
        lax.psum_scatter(
            jnp.concatenate(terms, axis=0), "tensor", scatter_dimension=0, tiled=True
        )
    ]


def trade(pieces, size):
    if size != 4:
        whole = lax.all_to_all(jnp.stack(pieces), "tensor", split_axis=0, concat_axis=0, tiled=True)
        return [whole[step] for step in range(size)]
    return [pieces[0]] + [
        lax.ppermute(pieces[step], "tensor", pairs(size, step)) for step in (1, 2, 3)
    ]


def total(parts):
    return functools.reduce(jnp.add, [part.astype(F32) for part in parts])


def sum_tensor(value, size):
    if size & (size - 1):
        return lax.psum(value, "tensor")
    return value + sum(lax.ppermute(value, "tensor", pairs(size, bit)) for bit in range(1, size))


def sum_blocks(value, size):
    if size & (size - 1):
        return lax.psum(value, "dp")
    bit = 1
    while bit < size:
        value = value + lax.ppermute(value, "dp", pairs(size, bit))
        bit *= 2
    return value


def rope_tables(segment):
    length = segment.shape[0]
    bound = jnp.sum((segment == 0).astype(jnp.int32))
    place = lax.broadcasted_iota(jnp.int32, (length, LANES), 0)
    place = place - jnp.where(place >= bound, bound, 0)
    lane = lax.broadcasted_iota(jnp.int32, (length, LANES), 1)
    freqs = jnp.exp(
        (lane % (HD // 2)).astype(F32) * (-2.0 * math.log(ROPE_BASE) / HD)
    )
    angles = place.astype(F32) * freqs
    sine = jnp.sin(angles)
    return bound, jnp.cos(angles), jnp.where(lane % HD < HD // 2, -sine, sine)


def swap_halves(values):
    lane = lax.broadcasted_iota(jnp.int32, values.shape, 1)
    after = pltpu.roll(values, LANES - HD // 2, 1)
    before = pltpu.roll(values, HD // 2, 1)
    return jnp.where(lane % HD < HD // 2, after, before)


def normalize(stream):
    scale_r = lax.rsqrt(jnp.mean(stream * stream, axis=-1, keepdims=True) + EPSILON)
    return (stream * scale_r, scale_r)


def project_kernel(slot_ref, *refs, count, steps, heads, kv):
    gains_ref, w_ref, cos_ref, sin_ref = refs[count : count + 4]
    h_ref, q_ref, kx_ref, vx_ref, kt_ref, vt_ref, gain_ref = refs[-7:]

    @pl.when(pl.program_id(0) == 0)
    def _():
        gain_ref[...] = gains_ref[...].astype(F32).T[:8]

    which = pl.program_id(0) // steps
    rows = h_ref.shape[0]
    part_rows = min(256, rows)
    lane = lax.broadcasted_iota(jnp.int32, (part_rows, LANES), 1)
    for start in range(0, rows, part_rows):
        at = slice(start, start + part_rows)
        tokens = refs[0][at, :]
        for block in range(1, count):
            tokens = jnp.where(which == block, refs[block][at, :], tokens)
        normed, _ = normalize(tokens.astype(F32))
        low = (normed * gain_ref[0:1, :]).astype(BF16)
        h_ref[at, :] = low
        pre = dot(low, w_ref[...])
        cosine, sine = cos_ref[at, :], sin_ref[at, :]
        chunks = []
        for chunk in range(pre.shape[1] // LANES):
            columns = slice(chunk * LANES, (chunk + 1) * LANES)
            part = pre[:, columns]
            first = 2 * chunk
            if first < heads + kv:
                turned = part * cosine + swap_halves(part) * sine
                part = turned if first + 1 < heads + kv else jnp.where(lane < HD, turned, part)
            chunks.append(part)
            if first < heads:
                q_ref[at, columns] = (part * (1.0 / math.sqrt(HD))).astype(BF16)
        flipped = {}
        for head in range(2 * kv):
            place = heads + head
            part = chunks[place // 2]
            moved = pltpu.roll(part, HD, 1)
            wide = [part, moved] if place % 2 == 0 else [moved, part]
            out = kx_ref if head < kv else vx_ref
            out[head % kv, 0, at, :] = jnp.where(lane < HD, wide[0], 0.0).astype(BF16)
            out[head % kv, 1, at, :] = jnp.where(lane < HD, 0.0, wide[1]).astype(BF16)
            if place // 2 not in flipped:
                flipped[place // 2] = part.T
            turn = flipped[place // 2][(place % 2) * HD : (place % 2 + 1) * HD]
            out_t = kt_ref if head < kv else vt_ref
            out_t[(head % kv) * HD : (head % kv + 1) * HD, at] = turn.astype(BF16)


def project(slots, blocks, bundle, cosine, sine, heads, kv, length):
    rows, width = blocks[0].shape
    count = len(blocks)
    tile = rows
    steps = rows // tile
    columns = (heads + 2 * kv) * HD

    def at(i, slot):
        return slot[i // steps] * steps + i % steps

    shapes = [
        jax.ShapeDtypeStruct((length, width), BF16),
        jax.ShapeDtypeStruct((length, heads * HD), BF16),
        jax.ShapeDtypeStruct((kv, 2, length, LANES), BF16),
        jax.ShapeDtypeStruct((kv, 2, length, LANES), BF16),
        jax.ShapeDtypeStruct((kv * HD, length), BF16),
        jax.ShapeDtypeStruct((kv * HD, length), BF16),
        jax.ShapeDtypeStruct((8, width), F32),
    ]
    out_specs = [
        pl.BlockSpec((tile, width), lambda i, s: (at(i, s), 0)),
        pl.BlockSpec((tile, heads * HD), lambda i, s: (at(i, s), 0)),
        pl.BlockSpec((kv, 2, tile, LANES), lambda i, s: (0, 0, at(i, s), 0)),
        pl.BlockSpec((kv, 2, tile, LANES), lambda i, s: (0, 0, at(i, s), 0)),
        pl.BlockSpec((kv * HD, tile), lambda i, s: (0, at(i, s))),
        pl.BlockSpec((kv * HD, tile), lambda i, s: (0, at(i, s))),
        pl.BlockSpec((8, width), lambda i, s: (0, 0)),
    ]
    in_specs = [
        pl.BlockSpec((tile, width), lambda i, s, b=block: (jnp.clip(i - b * steps, 0, steps - 1), 0))
        for block in range(count)
    ]
    in_specs += [
        pl.BlockSpec((width, LANES), lambda i, s: (0, columns // LANES)),
        pl.BlockSpec((width, columns), lambda i, s: (0, 0)),
        pl.BlockSpec((tile, LANES), lambda i, s: (at(i, s), 0)),
        pl.BlockSpec((tile, LANES), lambda i, s: (at(i, s), 0)),
    ]
    operands = [jnp.stack(slots), *blocks, bundle, bundle, cosine, sine]
    return pl.pallas_call(
        functools.partial(
            project_kernel, count=count, steps=steps, heads=heads, kv=kv
        ),
        grid_spec=pltpu.PrefetchScalarGridSpec(
            num_scalar_prefetch=1,
            grid=(count * steps,),
            in_specs=in_specs,
            out_specs=out_specs,
        ),
        out_shape=shapes,
        compiler_params=limit(52),
        cost_estimate=declared(2 * count * rows * width * columns),
    )(*operands)


def feed_kernel(*refs, count):
    tokens = refs[:count]
    gate_ref, up_ref = refs[count : count + 2]
    hidden_ref, silu_ref, slope_ref, h_out = refs[-4:]
    rows = tokens[0].shape[0]
    wide = h_out.shape[1]
    tile = min(256, gate_ref.shape[1])
    lanes = pl.ds(pl.multiple_of(pl.program_id(0) * wide, wide), wide)
    for block in range(count):
        h_out[block * rows : (block + 1) * rows, :] = tokens[block][:, lanes]
    for part in range(gate_ref.shape[1] // tile):
        columns = slice(part * tile, (part + 1) * tile)
        for block in range(count):
            where = slice(block * rows, (block + 1) * rows)
            gate = dot(tokens[block][...], gate_ref[:, columns])
            up = dot(tokens[block][...], up_ref[:, columns])
            sigmoid = 0.5 * jnp.tanh(0.5 * gate) + 0.5
            silu = gate * sigmoid
            hidden_ref[where, columns] = (silu * up).astype(BF16)
            silu_ref[where, columns] = silu.astype(BF16)
            slope_ref[where, columns] = (up * (sigmoid + silu * (1.0 - sigmoid))).astype(BF16)


def feed_back_kernel(*refs, count):
    grads = refs[:count]
    down_ref, silu_ref, slope_ref = refs[count : count + 3]
    dgate_ref, dup_ref = refs[-2:]
    rows = grads[0].shape[0]
    for block in range(count):
        where = slice(block * rows, (block + 1) * rows)
        dhidden = dot(grads[block][...], down_ref[...])
        dup_ref[where, :] = (dhidden * silu_ref[where, :].astype(F32)).astype(BF16)
        dgate_ref[where, :] = (dhidden * slope_ref[where, :].astype(F32)).astype(BF16)


def feed(kernel, place, blocks, tokens, weights, places, kept, units, outs, copy, tile, prev, others):
    rows, width = tokens[0].shape
    count = len(tokens)
    steps = max(units // tile, 1)
    tile, wide = units // steps, width // steps
    shapes = [jax.ShapeDtypeStruct((blocks * rows, units), BF16)] * outs
    in_specs = [pl.BlockSpec((rows, width), lambda i: (0, 0), pipeline_mode=pl.Buffered(1))] * count
    in_specs += [
        pl.BlockSpec((width, tile), lambda i, w=which: (0, w * steps + i)) for which in places
    ]
    cell = pl.BlockSpec((count * rows, tile), lambda i: (place, i))
    in_specs += [cell] * len(kept)
    out_specs = [cell] * outs
    if copy:
        shapes.append(jax.ShapeDtypeStruct((blocks * rows, width), BF16))
        out_specs.append(pl.BlockSpec((count * rows, wide), lambda i: (place, i)))
    operands = [*tokens, *weights, *kept]
    aliases = {}
    if prev is not None:
        for index, array in enumerate(prev):
            aliases[len(operands)] = index
            operands.append(array)
            in_specs.append(ANYWHERE)
    operands += others
    in_specs += [ANYWHERE] * len(others)
    return pl.pallas_call(
        functools.partial(kernel, count=count),
        grid=(steps,),
        in_specs=in_specs,
        out_specs=out_specs,
        out_shape=shapes,
        input_output_aliases=aliases,
        compiler_params=limit(52),
        cost_estimate=declared(2 * len(weights) * count * rows * width * units),
    )(*operands)


def back_kernel(slot_ref, *refs, count, terms, added, split):
    outs = refs[-2:] if split else refs[-count:]
    weights = refs[count * terms : (count + 1) * terms]
    into = list(refs[(count + 1) * terms :])
    for block in range(count):
        value = dot_cols(refs[block * terms][...], weights[0][...])
        for term in range(1, terms):
            value = value + dot_cols(refs[block * terms + term][...], weights[term][...])
        half = value.shape[0] // 2
        if split:
            outs[0][...] = value[:half].astype(BF16)
            outs[1][...] = value[half:].astype(BF16)
            continue
        if added[block] is None:
            outs[block][...] = value.astype(BF16)
            continue
        extra = into.pop(0)[...].astype(F32)
        top, bottom = value[:half], value[half:]
        if added[block]:
            top = top + extra
        else:
            bottom = bottom + extra
        outs[block][:half, :] = top.astype(BF16)
        outs[block][half:, :] = bottom.astype(BF16)


def back(slots, rows, lefts, weights, places, into=None, others=(), split=False):
    depth = lefts[0].shape[1]
    width = weights[0].shape[0]
    tile = min(512, width)
    terms, count = len(lefts), len(slots)
    outs, tall = (2, rows // 2) if split else (count, rows)
    into = into or [None] * count
    in_specs, operands = [], [jnp.stack([jnp.asarray(slot, jnp.int32) for slot in slots])]
    for block in range(count):
        in_specs += [pl.BlockSpec((rows, depth), lambda i, s, b=block: (s[b], 0))] * terms
        operands += lefts
    in_specs += [pl.BlockSpec((tile, depth), lambda i, s, p=place: (i, p)) for place in places]
    operands += weights
    for extra in into:
        if extra is not None:
            in_specs.append(pl.BlockSpec((rows // 2, tile), lambda i, s: (0, i)))
            operands.append(extra[0])
    operands += others
    in_specs += [ANYWHERE] * len(others)
    return pl.pallas_call(
        functools.partial(
            back_kernel,
            count=count,
            terms=terms,
            added=[None if extra is None else extra[1] for extra in into],
            split=split,
        ),
        grid_spec=pltpu.PrefetchScalarGridSpec(
            num_scalar_prefetch=1,
            grid=(width // tile,),
            in_specs=in_specs,
            out_specs=[pl.BlockSpec((tall, tile), lambda i, s: (0, i))] * outs,
        ),
        out_shape=[jax.ShapeDtypeStruct((tall, width), BF16)] * outs,
        compiler_params=limit(52),
        cost_estimate=declared(2 * count * terms * rows * width * depth),
    )(*operands)


def turn_kernel(value_ref, *rest):
    rest[-1][...] = value_ref[...].T


def turn(value, others=()):
    rows, columns = value.shape
    tile = min(512, rows)
    return pl.pallas_call(
        turn_kernel,
        grid=(rows // tile,),
        in_specs=[pl.BlockSpec((tile, columns), lambda i: (i, 0))] + [ANYWHERE] * len(others),
        out_specs=pl.BlockSpec((columns, tile), lambda i: (0, i)),
        out_shape=jax.ShapeDtypeStruct((columns, rows), value.dtype),
        compiler_params=limit(52),
        cost_estimate=declared(0),
    )(value, *others)


def turn_blocks(lefts, turned_ref):
    rows = lefts[0].shape[0]
    for block, left in enumerate(lefts):
        turned_ref[:, block * rows : (block + 1) * rows] = left[...].T


def weigh_kernel(*refs, count):
    lefts, right_ref = refs[:count], refs[count]
    out_ref, *turned = refs[-3:]
    i, j = pl.program_id(0), pl.program_id(1)
    last = j == pl.num_programs(1) - 1

    @pl.when((i == 0) & (j == 0))
    def _():
        turn_blocks(lefts, turned[0])

    for parity in range(2):

        @pl.when((i % 2 == parity) & jnp.logical_not(last))
        def _():
            out_ref[...] = dot(turned[parity][...], right_ref[...]).astype(BF16)

        @pl.when((i % 2 == parity) & last)
        def _():
            out_ref[...] = dot(turned[parity][...], right_ref[...]).astype(BF16)
            turn_blocks(lefts, turned[1 - parity])


def weigh(lefts, right, others=()):
    tokens, columns = right.shape
    rows, width = lefts[0].shape
    tall, wide = min(512, width), min(1024, columns // 2)
    tiles, steps = width // tall, columns // wide

    def ahead(i, j):
        return 0, jnp.minimum(i + jnp.where(j == steps - 1, 1, 0), tiles - 1)

    return pl.pallas_call(
        functools.partial(weigh_kernel, count=len(lefts)),
        grid=(tiles, steps),
        in_specs=[pl.BlockSpec((rows, tall), ahead)] * len(lefts)
        + [pl.BlockSpec((tokens, wide), lambda i, j: (0, j))]
        + [ANYWHERE] * len(others),
        out_specs=pl.BlockSpec((tall, wide), lambda i, j: (i, j)),
        out_shape=jax.ShapeDtypeStruct((width, columns), BF16),
        scratch_shapes=[pltpu.VMEM((tall, tokens), BF16)] * 2,
        compiler_params=limit(52),
        cost_estimate=declared(2 * tokens * width * columns),
    )(*lefts, right, *others)


def weigh_both_kernel(*refs, count):
    one_ref, others = refs[0], refs[1 : 1 + count]
    right_ref, other_ref, out_ref, turned_ref, other_turned_ref = refs[1 + count :]
    columns = right_ref.shape[1]
    turn_blocks([one_ref], turned_ref)
    out_ref[:, :columns] = dot(turned_ref[...], right_ref[...]).astype(BF16)
    turn_blocks(others, other_turned_ref)
    out_ref[:, columns:] = dot(other_turned_ref[...], other_ref[...]).astype(BF16)


def weigh_both(one, right, others, other_right):
    tokens, width = one.shape
    rows = others[0].shape[0]
    columns, more = right.shape[1], other_right.shape[1]
    tall = min(512, width)
    whole = [pl.BlockSpec((tokens, columns), lambda i: (0, 0))]
    whole += [pl.BlockSpec((tokens, more), lambda i: (0, 0))]
    return pl.pallas_call(
        functools.partial(weigh_both_kernel, count=len(others)),
        grid=(width // tall,),
        in_specs=[pl.BlockSpec((tokens, tall), lambda i: (0, i))]
        + [pl.BlockSpec((rows, tall), lambda i: (0, i))] * len(others)
        + whole,
        out_specs=pl.BlockSpec((tall, columns + more), lambda i: (i, 0)),
        out_shape=jax.ShapeDtypeStruct((width, columns + more), BF16),
        scratch_shapes=[pltpu.VMEM((tall, tokens), BF16)] * 2,
        compiler_params=limit(52),
        cost_estimate=declared(2 * tokens * width * (columns + more)),
    )(one, *others, right, other_right)


def settle_kernel(*refs, count):
    pieces, weights = refs[:count], refs[count : 2 * count]
    x_ref, gains_ref = refs[2 * count : 2 * count + 2]
    stream_ref, h_ref = refs[-2:]
    stream = x_ref[...].astype(F32)
    for piece, weight in zip(pieces, weights):
        stream = stream + dot_cols(piece[...], weight[...])
    stream_ref[...] = stream
    normed, _ = normalize(stream)
    h_ref[...] = (normed * gains_ref[1:2, :]).astype(BF16)


def settle(own, place, pieces, weights, tokens, gains, others=()):
    rows, width = tokens.shape
    depth = weights[0].shape[1]
    tile = min(256, rows)
    steps = rows // tile
    wide = pl.BlockSpec((tile, width), lambda i: (i, 0))
    piece = pl.BlockSpec((tile, depth), lambda i: (i, 0))
    weight = pl.BlockSpec((width, depth), lambda i: (0, 0), pipeline_mode=pl.Buffered(1))
    return pl.pallas_call(
        functools.partial(settle_kernel, count=len(weights)),
        grid=(steps,),
        in_specs=[pl.BlockSpec((tile, depth), lambda i: (place * steps + i, 0))]
        + [piece] * len(pieces)
        + [weight] * len(weights)
        + [wide, pl.BlockSpec((8, width), lambda i: (0, 0))]
        + [ANYWHERE] * len(others),
        out_specs=[wide, wide],
        out_shape=[
            jax.ShapeDtypeStruct((rows, width), F32),
            jax.ShapeDtypeStruct((rows, width), BF16),
        ],
        compiler_params=limit(52),
        cost_estimate=declared(2 * len(weights) * rows * width * depth),
    )(own, *pieces, *weights, tokens, gains, *others)


def norm_back(grad_in, stream, gain):
    normed, scale_r = normalize(stream)
    scaled = grad_in * gain
    return scale_r * (scaled - normed * jnp.mean(scaled * normed, axis=-1, keepdims=True))


def settle_back_kernel(*refs, parts, count):
    terms, weights = refs[:parts], refs[parts : parts + count]
    grad_ref, stream_ref, gains_ref, out_ref, low_ref = refs[parts + count : parts + count + 5]
    pieces = refs[parts + count + 5 :]
    grad_in = terms[0][...].astype(F32)
    for term in terms[1:]:
        grad_in = grad_in + term[...].astype(F32)
    grad = grad_ref[...].astype(F32) + norm_back(grad_in, stream_ref[...], gains_ref[1:2, :])
    out_ref[...] = grad
    low = grad.astype(BF16)
    low_ref[...] = low
    for piece, weight in zip(pieces, weights):
        piece[...] = dot(low, weight[...]).astype(BF16)


def settle_back(terms, weights, grad, stream, gains):
    rows, width = grad.shape
    depth = weights[0].shape[1]
    tile = min(256, rows)
    wide = pl.BlockSpec((tile, width), lambda i: (i, 0))
    weight = pl.BlockSpec((width, depth), lambda i: (0, 0), pipeline_mode=pl.Buffered(1))
    return pl.pallas_call(
        functools.partial(settle_back_kernel, parts=len(terms), count=len(weights)),
        grid=(rows // tile,),
        in_specs=[wide] * len(terms)
        + [weight] * len(weights)
        + [wide, wide, pl.BlockSpec((8, width), lambda i: (0, 0))],
        out_specs=[wide, wide] + [pl.BlockSpec((tile, depth), lambda i: (i, 0))] * len(weights),
        out_shape=[
            jax.ShapeDtypeStruct((rows, width), F32),
            jax.ShapeDtypeStruct((rows, width), BF16),
        ]
        + [jax.ShapeDtypeStruct((rows, depth), BF16)] * len(weights),
        compiler_params=limit(52),
        cost_estimate=declared(2 * len(weights) * rows * width * depth),
    )(*terms, *weights, grad, stream, gains)


def causal(keys, queries):
    key = lax.broadcasted_iota(jnp.int32, (keys, queries), 0)
    return key <= lax.broadcasted_iota(jnp.int32, (keys, queries), 1)


def first_block(bound, offset, block):
    return jnp.where(offset >= bound, lax.div(bound, jnp.int32(block)), 0)


def attend_kernel(order_ref, q_ref, kx_ref, vt_ref, *rest, block):
    out_ref, lse_ref, top_ref, acc_ref = rest[-4:]
    kv = kx_ref.shape[0]
    per = q_ref.shape[1] // LANES // kv
    bound = order_ref[0]
    ones = jnp.ones((16, block), BF16)
    for group in range(kv):

        def q_step(turn, _):
            index = order_ref[1 + turn]
            offset = pl.multiple_of(index * block, block)
            into = pl.ds(pl.multiple_of(turn * block, block), block)
            top_ref[...] = jnp.full(top_ref.shape, MASKED, F32)
            acc_ref[...] = jnp.zeros(acc_ref.shape, F32)

            def tile(step, diagonal):
                keys = pl.ds(pl.multiple_of(step, block), block)
                value_t = jnp.concatenate(
                    [vt_ref[group * HD : (group + 1) * HD, keys], ones], axis=0
                )
                for head in range(2 * per):
                    column = (group * per + head // 2) * LANES
                    query = q_ref[pl.ds(offset, block), column : column + LANES]
                    scores = dot_cols(kx_ref[group, head % 2, keys, :], query)
                    if diagonal:
                        scores = jnp.where(causal(block, block), scores, MASKED)
                    old = top_ref[head, 0:1, :]
                    top = jnp.maximum(old, jnp.max(scores, axis=0, keepdims=True))
                    powered = jnp.exp(scores - top).astype(BF16)
                    acc_ref[head] = acc_ref[head] * jnp.exp(old - top) + dot(value_t, powered)
                    top_ref[head, 0:1, :] = top

            def full_tile(step, carry):
                tile(step * block, False)
                return carry

            lax.fori_loop(first_block(bound, offset, block), index, full_tile, 0)
            tile(offset, True)
            for pair in range(per):
                both = []
                for head in (2 * pair, 2 * pair + 1):
                    total = acc_ref[head, HD : HD + 1, :]
                    both.append(acc_ref[head, :HD, :] / total)
                    place = group * 2 * per + head
                    lse_ref[place : place + 1, into] = top_ref[
                        head, 0:1, :
                    ] + jnp.log(total)
                column = (group * per + pair) * LANES
                out_ref[into, column : column + LANES] = (
                    jnp.concatenate(both, axis=0).T.astype(BF16)
                )
            return _

        lax.fori_loop(0, out_ref.shape[0] // block, q_step, 0)


def attend(bound, order, queries, kx, vt, block, others=()):
    length, width = queries.shape
    heads = width // HD
    kv = kx.shape[0]
    per = heads // kv
    count = len(order)
    cells = heads * count * block * (length + block) // 2
    vmem = pl.BlockSpec(memory_space=pltpu.VMEM)
    return pl.pallas_call(
        functools.partial(attend_kernel, block=block),
        in_specs=[pl.BlockSpec(memory_space=pltpu.SMEM), vmem, vmem, vmem] + [ANYWHERE] * len(others),
        out_specs=[vmem, vmem],
        out_shape=[
            jax.ShapeDtypeStruct((count * block, width), BF16),
            jax.ShapeDtypeStruct((heads, count * block), F32),
        ],
        scratch_shapes=[
            pltpu.VMEM((per, 8, block), F32),
            pltpu.VMEM((per, HD + 16, block), F32),
        ],
        compiler_params=limit(52),
        cost_estimate=declared(2 * 4 * HD * 4 * cells, 16),
    )(jnp.stack([bound, *order]), queries, kx, vt, *others)


def attend_back_kernel(
    order_ref, q_ref, kx_ref, vx_ref, kt_ref, lse_ref, out_ref, grad_ref, cos_ref, sin_ref,
    *rest, block
):
    dqkv_ref, dk_ref, dv_ref, dq_ref = rest[-4:]
    length = q_ref.shape[0]
    kv = kx_ref.shape[0]
    heads = q_ref.shape[1] // HD
    per = heads // 2 // kv
    bound = order_ref[0]
    dk_ref[...] = jnp.zeros(dk_ref.shape, F32)
    dv_ref[...] = jnp.zeros(dv_ref.shape, F32)
    lane = lax.broadcasted_iota(jnp.int32, (8, LANES), 1)
    row = lax.broadcasted_iota(jnp.int32, (8, LANES), 0)
    chosen = ((lane // HD) == row).astype(F32)

    def turn_back(values, rows):
        return values * cos_ref[rows, :] - swap_halves(values) * sin_ref[rows, :]

    for group in range(kv):

        def q_step(turn, _):
            index = order_ref[1 + turn]
            offset = pl.multiple_of(index * block, block)
            rows = pl.ds(offset, block)
            given = pl.ds(pl.multiple_of(turn * block, block), block)
            dq_ref[...] = jnp.zeros(dq_ref.shape, F32)
            deltas = []
            for pair in range(per):
                column = (group * per + pair) * LANES
                product = grad_ref[given, column : column + LANES].astype(F32) * out_ref[
                    given, column : column + LANES
                ].astype(F32)
                deltas.append(
                    lax.dot_general(
                        chosen, product, OVER_COLS, precision=lax.Precision.HIGHEST,
                        preferred_element_type=F32,
                    )
                )

            def tile(step, size, skip, diagonal):
                keys = pl.ds(pl.multiple_of(step, size), size)
                key_t = kt_ref[group * HD : (group + 1) * HD, keys]
                mine = pl.ds(offset + skip, block - skip)
                theirs = pl.ds(turn * block + skip, block - skip)
                for parity in range(2):
                    key_add, value_add = 0.0, 0.0
                    for pair in range(per):
                        head = 2 * pair + parity
                        place = group * 2 * per + head
                        column = (group * per + pair) * LANES
                        query = q_ref[mine, column : column + LANES]
                        grad = grad_ref[theirs, column : column + LANES]
                        scores = dot_cols(kx_ref[group, parity, keys, :], query)
                        if diagonal:
                            scores = jnp.where(causal(size, block - skip), scores, MASKED)
                        probs = jnp.exp(scores - lse_ref[place : place + 1, given][:, skip:])
                        dprobs = dot_cols(vx_ref[group, parity, keys, :], grad)
                        delta = deltas[pair][parity : parity + 1, skip:]
                        dscores = (probs * (dprobs - delta)).astype(BF16)
                        value_add = value_add + dot(probs.astype(BF16), grad)
                        key_add = key_add + dot(dscores, query)
                        dq_ref[head * HD : (head + 1) * HD, skip:] += dot(key_t, dscores)
                    dk_ref[group, parity, keys, :] += key_add
                    dv_ref[group, parity, keys, :] += value_add

            def full_tile(step, carry):
                tile(step * block, block, 0, False)
                return carry

            lax.fori_loop(first_block(bound, offset, block), index, full_tile, 0)
            tile(offset, block // 2, 0, True)
            tile(offset + block // 2, block // 2, block // 2, True)
            for pair in range(per):
                column = (group * per + pair) * LANES
                grad_q = dq_ref[pair * LANES : (pair + 1) * LANES, :].T * (1.0 / math.sqrt(HD))
                dqkv_ref[rows, column : column + LANES] = turn_back(grad_q, rows).astype(BF16)
            return _

        lax.fori_loop(0, length // block, q_step, 0)

    def finish(index, _):
        rows = pl.ds(pl.multiple_of(index * block, block), block)
        lanes = lax.broadcasted_iota(jnp.int32, (block, LANES), 1)

        def placed(part, half):
            ref = dk_ref if part < kv else dv_ref
            even, odd = ref[part % kv, 0, rows, :], ref[part % kv, 1, rows, :]
            return even + pltpu.roll(odd, HD, 1) if half == 0 else pltpu.roll(even, HD, 1) + odd

        for chunk in range(kv):
            values = jnp.where(lanes < HD, placed(2 * chunk, 0), placed(2 * chunk + 1, 1))
            if 2 * chunk + 1 < kv:
                values = turn_back(values, rows)
            elif 2 * chunk < kv:
                values = jnp.where(lanes < HD, turn_back(values, rows), values)
            column = heads * HD + chunk * LANES
            dqkv_ref[rows, column : column + LANES] = values.astype(BF16)
        return _

    lax.fori_loop(0, length // block, finish, 0)


def attend_back(
    bound, order, queries, kx, vx, kt, log_sums, attended, grad, cosine, sine, block, others
):
    length, width = queries.shape
    heads = width // HD
    kv = kx.shape[0]
    cells = heads * length * (length + block) // 2
    vmem = pl.BlockSpec(memory_space=pltpu.VMEM)
    return pl.pallas_call(
        functools.partial(attend_back_kernel, block=block),
        in_specs=[pl.BlockSpec(memory_space=pltpu.SMEM)] + [vmem] * 9 + [ANYWHERE] * len(others),
        out_specs=vmem,
        out_shape=jax.ShapeDtypeStruct((length, width + 2 * kv * HD), BF16),
        scratch_shapes=[
            pltpu.VMEM((kv, 2, length, LANES), F32),
            pltpu.VMEM((kv, 2, length, LANES), F32),
            pltpu.VMEM((heads // kv * HD, block), F32),
        ],
        compiler_params=limit(52),
        cost_estimate=declared(2 * 10 * HD * 4 * cells),
    )(jnp.stack([bound, *order]), queries, kx, vx, kt, log_sums, attended, grad, cosine, sine, *others)


def local(
    inputs,
    segment_ids,
    attn_gain,
    query_weight,
    key_weight,
    value_weight,
    output_weight,
    mlp_gain,
    gate_weight,
    up_weight,
    down_weight,
    cotangent,
    *,
    sizes,
):
    rows = inputs.shape[0]
    length = segment_ids.shape[0]
    query_cols = query_weight.shape[1]
    key_cols = key_weight.shape[1]
    heads, kv = query_cols // HD, key_cols // HD
    columns = query_cols + 2 * key_cols
    slots = slots_of(sizes["tensor"])
    tensor = sizes["tensor"]
    space = (-columns) % query_cols or query_cols
    gains = jnp.pad(jnp.stack([attn_gain, mlp_gain], axis=1), ((0, 0), (0, space - 2)))
    bundle = lax.all_gather(
        jnp.concatenate([query_weight, key_weight, value_weight, gains, output_weight.T], axis=1),
        "dp", axis=0, tiled=True,
    )
    out_own = bundle[:, columns + space :]
    hop = first_hop(inputs, tensor)
    gate_up = lax.all_gather(
        hold(jnp.concatenate([gate_weight, up_weight], axis=1), *(hop or ())),
        "dp", axis=0, tiled=True,
    )

    bound, cosine, sine = rope_tables(segment_ids)
    blocks = second_hop(inputs, hop, tensor)
    stream = inputs.astype(F32)
    arrays = project(slots, blocks, bundle, cosine, sine, heads, kv, length)
    block_a, queries, kx, vx, kt, vt, gains = arrays
    down_t = lax.all_gather(turn(down_weight, [queries]), "dp", axis=0, tiled=True)

    if tensor == 4:
        out_own = hold(out_own, blocks[3])
        out_hop = first_hop(out_own, tensor)
        far, far_sums = attend(bound, slots[3:], queries, kx, vt, rows)
        from_far = lax.ppermute(far, "tensor", pairs(tensor, 3))
        first, first_sums = attend(bound, slots[1:2], queries, kx, vt, rows, [far])
        from_one = lax.ppermute(first, "tensor", pairs(tensor, 1))
        halves = hold_halves(out_hop, first)
        out_all = second_hop(out_own, out_hop, tensor, halves)
        second, second_sums = attend(bound, slots[2:3], queries, kx, vt, rows, halves)
        from_two = lax.ppermute(second, "tensor", pairs(tensor, 2))
        own, own_sums = attend(bound, slots[:1], queries, kx, vt, rows, [second])
        stream_one, low_m = settle(own, 0, [from_one, from_two, from_far], out_all, inputs, gains)
        order = [slots[1], slots[2], slots[0], slots[3]]
        attended = jnp.concatenate([first, second, own, far], axis=0)
        log_sums = jnp.concatenate([first_sums, second_sums, own_sums, far_sums], axis=1)
    else:
        order = slots
        out_all = gather(out_own, tensor)
        attended, log_sums = attend(bound, order, queries, kx, vt, rows)
        given = trade([attended[k * rows : (k + 1) * rows] for k in range(tensor)], tensor)
        stream_one, low_m = settle(given[0], 0, given[1:], out_all, inputs, gains)
        cotangent_sent = cotangent
    parts_m = [low_m]
    units = gate_weight.shape[1]

    def feed_at(place, wanted, fed, others=()):
        return feed(
            feed_kernel, place, tensor, [parts_m[k] for k in wanted], [gate_up] * 2, [0, 1], [],
            units, 3, True, 512, fed, others,
        )

    def back_m(places, fed, into=None, others=(), split=False):
        return back(places, rows, fed[:2], [gate_up] * 2, [0, 1], into, others, split)

    def back_out(places, into=None, others=(), split=False):
        return back(places, rows, [hidden], [down_t], [0], into, others, split)

    def reduce_rows(term, *others):
        if others and tensor == 4:
            term = hold(term, *others)
        return lax.psum_scatter(term, "dp", scatter_dimension=0, tiled=True)

    if tensor == 4:
        hop = first_hop(parts_m[0], tensor)
        cotangent_sent = hold(cotangent, *hop)
        cotangent_hop = first_hop(cotangent_sent, tensor)
        fed = feed_at(3, [0], None)
        parts_m = second_hop(parts_m[0], hop, tensor)
        fed = feed_at(0, [1, 2], fed)
        halves = hold_halves(cotangent_hop, fed[0])
        grad_parts = second_hop(cotangent_sent, cotangent_hop, tensor, halves)
        fed = feed_at(2, [3], fed, halves)
    else:
        grad_parts = second_hop(cotangent_sent, None, tensor)
        parts_m = gather(parts_m[0], tensor)
        fed = None
        for place in range(tensor):
            fed = feed_at(place, [place], fed)
    hidden, silu, slope, block_m = fed
    places = [1, 2, 3, 0] if tensor == 4 else list(range(tensor))
    grad_parts = [grad_parts[k] for k in places]

    def feed_back(others=()):
        return feed(
            feed_back_kernel, 0, tensor, grad_parts, [down_t], [0], [silu, slope], units, 2, False, 512,
            None, others,
        )

    if tensor == 4:
        three_out = back_out([2], None, [fed[0]], True)
        out_one, out_two = out_halves = send_half(three_out, tensor)
        down_t_wgrad = weigh(grad_parts, hidden, three_out[:1])
        one_out, two_out, own_out = back_out(
            [0, 1, 3], [(out_one, False), (out_two, True), None]
        )
        out_parts = [
            own_out,
            lax.ppermute(one_out, "tensor", pairs(tensor, 1)),
            lax.ppermute(two_out, "tensor", pairs(tensor, 2)),
        ]
        fed = feed_back([one_out])
        three_m = back_m([2], fed, None, (), True)
        m_one, m_two = m_halves = send_half(three_m, tensor)
        gate_wgrad = weigh([block_m], fed[0], [three_m[0], *out_parts[1:]])
        one_m, two_m = back_m([0, 1], fed, [(m_one, False), (m_two, True)])
        (own_m,) = back_m([3], fed, None, [one_m])
        up_wgrad = weigh([block_m], fed[1], [own_m])
        grad_m_parts = [
            own_m,
            lax.ppermute(one_m, "tensor", pairs(tensor, 1)),
            lax.ppermute(two_m, "tensor", pairs(tensor, 2)),
        ]
    else:
        down_t_wgrad = weigh(grad_parts, hidden)
        fed = feed_back()
        grad_m_parts = sum_whole(back_m(list(range(tensor)), fed))
        gate_wgrad, up_wgrad = weigh([block_m], fed[0]), weigh([block_m], fed[1])
        out_parts = sum_whole(back_out(list(range(tensor))))
    layer_out = (stream_one + total(out_parts)).astype(BF16)
    if tensor != 4:
        out_halves = m_halves = ()
    down_t_low = reduce_rows(down_t_wgrad, *out_halves)
    gate_low = reduce_rows(gate_wgrad, *m_halves)
    up_low = reduce_rows(up_wgrad, *grad_m_parts[1:])

    grad_stream_one, grad_stream_low, *pieces = settle_back(
        grad_m_parts, out_all, cotangent, stream_one, gains
    )
    given = trade(pieces, tensor)
    places = [1, 2, 0, 3] if tensor == 4 else list(range(tensor))
    grad_attended = jnp.concatenate([given[k] for k in places], axis=0)
    grad_qkv = attend_back(
        bound, order, queries, kx, vx, kt, log_sums, attended, grad_attended, cosine, sine, rows,
        [down_t_low],
    )
    if tensor == 4:
        sent = hold(grad_stream_low, grad_attended)
        grad_stream_parts = trade([sent] * 4, tensor)
    else:
        grad_stream_parts = gather(grad_stream_low, tensor)
    grad_stream_parts = [grad_stream_parts[k] for k in places]

    def back_a(places, others=(), split=False):
        return back(places, rows, [grad_qkv], [bundle], [0], None, others, split)

    if tensor == 4:
        three = back_a(slots[3:], [gate_low], True)
        halves = send_half(three, tensor)
        block_a = hold(block_a, three[0])
    attention_wgrad = weigh_both(block_a, grad_qkv, grad_stream_parts, attended)
    gate_sum, up_sum, down_t_sum = [low.astype(F32) for low in (gate_low, up_low, down_t_low)]
    if tensor == 4:
        attention_wgrad = hold(attention_wgrad, *halves)
    attention_sum = reduce_rows(attention_wgrad).astype(F32)
    if tensor == 4:
        one, two, own = back_a([slots[1], slots[2], slots[0]], three[:1])
        grad_a_parts = [own, *send_whole(one, two, halves, tensor)]
    else:
        grad_a_parts = sum_whole(back_a(slots))
    grad_normed_a = total(grad_a_parts)

    product = attention_wgrad[:, :columns].astype(F32) * bundle[:, :columns].astype(F32)
    attn_term = sum_tensor(jnp.sum(product, axis=1)[None, :], tensor)
    width = attn_gain.shape[0]
    attn_term = lax.dynamic_slice_in_dim(
        sum_blocks(attn_term, sizes["dp"]), lax.axis_index("dp") * width, width, 1
    )

    def gain_term(gain, weights):
        term = sum(jnp.sum(weight.astype(F32) * grad, axis=1) for weight, grad in weights)
        return term / gain.astype(F32)

    query_sum = attention_sum[:, :query_cols]
    key_sum = attention_sum[:, query_cols : query_cols + key_cols]
    value_sum = attention_sum[:, query_cols + key_cols : columns]
    mlp_term = sum_tensor(
        gain_term(mlp_gain, [(gate_weight, gate_sum), (up_weight, up_sum)])[None, :], tensor
    )
    input_grad = (grad_stream_one + norm_back(grad_normed_a, stream, gains[0:1])).astype(BF16)
    return (
        layer_out,
        input_grad,
        attn_term[0] / attn_gain.astype(F32),
        query_sum,
        key_sum,
        value_sum,
        attention_sum[:, columns:].T,
        mlp_term[0],
        gate_sum,
        up_sum,
        down_t_sum.T,
    )


def solution(mesh):
    tokens = P(("dp", "tensor"), None)
    in_specs = (
        tokens,
        P("dp"),
        P("dp"),
        P("dp", "tensor"),
        P("dp", "tensor"),
        P("dp", "tensor"),
        P("tensor", "dp"),
        P("dp"),
        P("dp", "tensor"),
        P("dp", "tensor"),
        P("tensor", "dp"),
        tokens,
    )
    out_specs = (
        tokens,
        tokens,
        P("dp"),
        P("dp", "tensor"),
        P("dp", "tensor"),
        P("dp", "tensor"),
        P("tensor", "dp"),
        P("dp"),
        P("dp", "tensor"),
        P("dp", "tensor"),
        P("tensor", "dp"),
    )
    return jax.shard_map(
        functools.partial(local, sizes={axis: mesh.shape[axis] for axis in ("tensor", "dp")}),
        mesh=mesh, in_specs=in_specs, out_specs=out_specs, check_vma=False,
    )
```

```python
import functools
import math

import jax
import jax.numpy as jnp
from jax import lax
from jax.experimental import pallas as pl
from jax.experimental.pallas import tpu as pltpu
from jax.sharding import PartitionSpec as P

HD = 64
LANES = 128
EPSILON = 1e-05
ROPE_BASE = 500000.0
MASKED = -1e30
OVER_ROWS = (((0,), (0,)), ((), ()))
OVER_COLS = (((1,), (1,)), ((), ()))


def limit(size):
    return pltpu.CompilerParams(vmem_limit_bytes=size * 2**20)


SHORT = 0.0625


def declared(flops, scale=SHORT):
    return pl.CostEstimate(flops=int(flops * scale), bytes_accessed=0, transcendentals=0)


F32 = jnp.float32
BF16 = jnp.bfloat16


def dot_cols(left, right):
    return lax.dot_general(left, right, OVER_COLS, preferred_element_type=F32)


def dot_rows(left, right):
    return lax.dot_general(left, right, OVER_ROWS, preferred_element_type=F32)


def dot(left, right):
    return jnp.dot(left, right, preferred_element_type=F32)


def pairs(size, bit):
    return [(index, index ^ bit) for index in range(size)]


def slots_of(size):
    if size == 4:
        return [lax.axis_index("tensor") ^ step for step in range(size)]
    return [jnp.int32(step) for step in range(size)]


ANYWHERE = pl.BlockSpec(memory_space=pl.ANY)


def nothing_kernel(*refs):
    pass


def hold(value, *others):
    return pl.pallas_call(
        nothing_kernel,
        in_specs=[ANYWHERE] * (1 + len(others)),
        out_specs=ANYWHERE,
        out_shape=jax.ShapeDtypeStruct(value.shape, value.dtype),
        input_output_aliases={0: 0},
        cost_estimate=declared(0),
    )(value, *others)


def first_hop(shard, size):
    if size != 4:
        return None
    return [lax.ppermute(shard, "tensor", pairs(size, bit)) for bit in (1, 2)]


def copy_kernel(value_ref, *rest):
    rest[-1][...] = value_ref[...]


def half_of(value, which, *others):
    rows, width = value.shape
    tile = rows // 4
    return pl.pallas_call(
        copy_kernel,
        grid=(2,),
        in_specs=[pl.BlockSpec((tile, width), lambda i: (2 * which + i, 0))]
        + [ANYWHERE] * len(others),
        out_specs=pl.BlockSpec((tile, width), lambda i: (i, 0)),
        out_shape=jax.ShapeDtypeStruct((rows // 2, width), value.dtype),
        compiler_params=limit(52),
        cost_estimate=declared(0),
    )(value, *others)


def add_kernel(value_ref, extra_ref, out_ref, *, which):
    out_ref[...] = value_ref[...]

    @pl.when(pl.program_id(0) == which)
    def _():
        out_ref[...] = (value_ref[...].astype(F32) + extra_ref[...].astype(F32)).astype(BF16)


def add_half(value, extra, which):
    rows, width = value.shape
    half = pl.BlockSpec((rows // 2, width), lambda i: (i, 0))
    return pl.pallas_call(
        functools.partial(add_kernel, which=which),
        grid=(2,),
        in_specs=[half, pl.BlockSpec((rows // 2, width), lambda i: (0, 0))],
        out_specs=half,
        out_shape=jax.ShapeDtypeStruct((rows, width), value.dtype),
        compiler_params=limit(52),
        cost_estimate=declared(0),
    )(value, extra)


def hold_halves(hop, *others):
    return half_of(hop[0], 0, *others), half_of(hop[1], 1, *others)


def second_hop(shard, hop, size, halves=None):
    if size != 4:
        whole = lax.all_gather(shard, "tensor", axis=0)
        return [whole[step] for step in range(size)]
    one, two = hop
    upper, lower = halves or hold_halves(hop)
    three_a = lax.ppermute(upper, "tensor", pairs(size, 2))
    three_b = lax.ppermute(lower, "tensor", pairs(size, 1))
    return [shard, one, two, jnp.concatenate([three_a, three_b], axis=0)]


def gather(shard, size):
    return second_hop(shard, first_hop(shard, size), size)


def send_half(three, size):
    into_two = lax.ppermute(three[0], "tensor", pairs(size, 1))
    into_one = lax.ppermute(three[1], "tensor", pairs(size, 2))
    return into_one, into_two


def send_whole(one, two, into, size):
    return [
        lax.ppermute(add_half(one, into[0], 1), "tensor", pairs(size, 1)),
        lax.ppermute(add_half(two, into[1], 0), "tensor", pairs(size, 2)),
    ]


def sum_whole(terms):
    return [
        lax.psum_scatter(
            jnp.concatenate(terms, axis=0), "tensor", scatter_dimension=0, tiled=True
        )
    ]


def trade(pieces, size):
    if size != 4:
        whole = lax.all_to_all(jnp.stack(pieces), "tensor", split_axis=0, concat_axis=0, tiled=True)
        return [whole[step] for step in range(size)]
    return [pieces[0]] + [
        lax.ppermute(pieces[step], "tensor", pairs(size, step)) for step in (1, 2, 3)
    ]


def total(parts):
    return functools.reduce(jnp.add, [part.astype(F32) for part in parts])


def sum_tensor(value, size):
    if size & (size - 1):
        return lax.psum(value, "tensor")
    return value + sum(lax.ppermute(value, "tensor", pairs(size, bit)) for bit in range(1, size))


def sum_blocks(value, size):
    if size & (size - 1):
        return lax.psum(value, "dp")
    bit = 1
    while bit < size:
        value = value + lax.ppermute(value, "dp", pairs(size, bit))
        bit *= 2
    return value


def rope_tables(segment):
    length = segment.shape[0]
    bound = jnp.sum((segment == 0).astype(jnp.int32))
    place = lax.broadcasted_iota(jnp.int32, (length, LANES), 0)
    place = place - jnp.where(place >= bound, bound, 0)
    lane = lax.broadcasted_iota(jnp.int32, (length, LANES), 1)
    freqs = jnp.exp(
        (lane % (HD // 2)).astype(F32) * (-2.0 * math.log(ROPE_BASE) / HD)
    )
    angles = place.astype(F32) * freqs
    sine = jnp.sin(angles)
    return bound, jnp.cos(angles), jnp.where(lane % HD < HD // 2, -sine, sine)


def swap_halves(values):
    lane = lax.broadcasted_iota(jnp.int32, values.shape, 1)
    after = pltpu.roll(values, LANES - HD // 2, 1)
    before = pltpu.roll(values, HD // 2, 1)
    return jnp.where(lane % HD < HD // 2, after, before)


def normalize(stream):
    scale_r = lax.rsqrt(jnp.mean(stream * stream, axis=-1, keepdims=True) + EPSILON)
    return (stream * scale_r, scale_r)


def project_kernel(slot_ref, *refs, count, steps, heads, kv):
    gains_ref, w_ref, cos_ref, sin_ref = refs[count : count + 4]
    h_ref, q_ref, kx_ref, vx_ref, kt_ref, vt_ref, gain_ref = refs[-7:]

    @pl.when(pl.program_id(0) == 0)
    def _():
        gain_ref[...] = gains_ref[...].astype(F32).T[:8]

    which = pl.program_id(0) // steps
    rows = h_ref.shape[0]
    part_rows = min(256, rows)
    lane = lax.broadcasted_iota(jnp.int32, (part_rows, LANES), 1)
    for start in range(0, rows, part_rows):
        at = slice(start, start + part_rows)
        tokens = refs[0][at, :]
        for block in range(1, count):
            tokens = jnp.where(which == block, refs[block][at, :], tokens)
        normed, _ = normalize(tokens.astype(F32))
        low = (normed * gain_ref[0:1, :]).astype(BF16)
        h_ref[at, :] = low
        pre = dot(low, w_ref[...])
        cosine, sine = cos_ref[at, :], sin_ref[at, :]
        chunks = []
        for chunk in range(pre.shape[1] // LANES):
            columns = slice(chunk * LANES, (chunk + 1) * LANES)
            part = pre[:, columns]
            first = 2 * chunk
            if first < heads + kv:
                turned = part * cosine + swap_halves(part) * sine
                part = turned if first + 1 < heads + kv else jnp.where(lane < HD, turned, part)
            chunks.append(part)
            if first < heads:
                q_ref[at, columns] = (part * (1.0 / math.sqrt(HD))).astype(BF16)
        flipped = {}
        for head in range(2 * kv):
            place = heads + head
            part = chunks[place // 2]
            moved = pltpu.roll(part, HD, 1)
            wide = [part, moved] if place % 2 == 0 else [moved, part]
            out = kx_ref if head < kv else vx_ref
            out[head % kv, 0, at, :] = jnp.where(lane < HD, wide[0], 0.0).astype(BF16)
            out[head % kv, 1, at, :] = jnp.where(lane < HD, 0.0, wide[1]).astype(BF16)
            if place // 2 not in flipped:
                flipped[place // 2] = part.T
            turn = flipped[place // 2][(place % 2) * HD : (place % 2 + 1) * HD]
            out_t = kt_ref if head < kv else vt_ref
            out_t[(head % kv) * HD : (head % kv + 1) * HD, at] = turn.astype(BF16)


def project(slots, blocks, bundle, cosine, sine, heads, kv, length):
    rows, width = blocks[0].shape
    count = len(blocks)
    tile = rows
    steps = rows // tile
    columns = (heads + 2 * kv) * HD

    def at(i, slot):
        return slot[i // steps] * steps + i % steps

    shapes = [
        jax.ShapeDtypeStruct((length, width), BF16),
        jax.ShapeDtypeStruct((length, heads * HD), BF16),
        jax.ShapeDtypeStruct((kv, 2, length, LANES), BF16),
        jax.ShapeDtypeStruct((kv, 2, length, LANES), BF16),
        jax.ShapeDtypeStruct((kv * HD, length), BF16),
        jax.ShapeDtypeStruct((kv * HD, length), BF16),
        jax.ShapeDtypeStruct((8, width), F32),
    ]
    out_specs = [
        pl.BlockSpec((tile, width), lambda i, s: (at(i, s), 0)),
        pl.BlockSpec((tile, heads * HD), lambda i, s: (at(i, s), 0)),
        pl.BlockSpec((kv, 2, tile, LANES), lambda i, s: (0, 0, at(i, s), 0)),
        pl.BlockSpec((kv, 2, tile, LANES), lambda i, s: (0, 0, at(i, s), 0)),
        pl.BlockSpec((kv * HD, tile), lambda i, s: (0, at(i, s))),
        pl.BlockSpec((kv * HD, tile), lambda i, s: (0, at(i, s))),
        pl.BlockSpec((8, width), lambda i, s: (0, 0)),
    ]
    in_specs = [
        pl.BlockSpec((tile, width), lambda i, s, b=block: (jnp.clip(i - b * steps, 0, steps - 1), 0))
        for block in range(count)
    ]
    in_specs += [
        pl.BlockSpec((width, LANES), lambda i, s: (0, columns // LANES)),
        pl.BlockSpec((width, columns), lambda i, s: (0, 0)),
        pl.BlockSpec((tile, LANES), lambda i, s: (at(i, s), 0)),
        pl.BlockSpec((tile, LANES), lambda i, s: (at(i, s), 0)),
    ]
    operands = [jnp.stack(slots), *blocks, bundle, bundle, cosine, sine]
    return pl.pallas_call(
        functools.partial(
            project_kernel, count=count, steps=steps, heads=heads, kv=kv
        ),
        grid_spec=pltpu.PrefetchScalarGridSpec(
            num_scalar_prefetch=1,
            grid=(count * steps,),
            in_specs=in_specs,
            out_specs=out_specs,
        ),
        out_shape=shapes,
        compiler_params=limit(52),
        cost_estimate=declared(2 * count * rows * width * columns),
    )(*operands)


def feed_kernel(*refs, count):
    tokens = refs[:count]
    gate_ref, up_ref = refs[count : count + 2]
    hidden_ref, silu_ref, slope_ref, h_out = refs[-4:]
    rows = tokens[0].shape[0]
    wide = h_out.shape[1]
    tile = min(256, gate_ref.shape[1])
    lanes = pl.ds(pl.multiple_of(pl.program_id(0) * wide, wide), wide)
    for block in range(count):
        h_out[block * rows : (block + 1) * rows, :] = tokens[block][:, lanes]
    for part in range(gate_ref.shape[1] // tile):
        columns = slice(part * tile, (part + 1) * tile)
        for block in range(count):
            where = slice(block * rows, (block + 1) * rows)
            gate = dot(tokens[block][...], gate_ref[:, columns])
            up = dot(tokens[block][...], up_ref[:, columns])
            sigmoid = 0.5 * jnp.tanh(0.5 * gate) + 0.5
            silu = gate * sigmoid
            hidden_ref[where, columns] = (silu * up).astype(BF16)
            silu_ref[where, columns] = silu.astype(BF16)
            slope_ref[where, columns] = (up * (sigmoid + silu * (1.0 - sigmoid))).astype(BF16)


def feed_back_kernel(*refs, count):
    grads = refs[:count]
    down_ref, silu_ref, slope_ref = refs[count : count + 3]
    dgate_ref, dup_ref = refs[-2:]
    rows = grads[0].shape[0]
    for block in range(count):
        where = slice(block * rows, (block + 1) * rows)
        dhidden = dot(grads[block][...], down_ref[...])
        dup_ref[where, :] = (dhidden * silu_ref[where, :].astype(F32)).astype(BF16)
        dgate_ref[where, :] = (dhidden * slope_ref[where, :].astype(F32)).astype(BF16)


def feed(kernel, place, blocks, tokens, weights, places, kept, units, outs, copy, tile, prev, others):
    rows, width = tokens[0].shape
    count = len(tokens)
    steps = max(units // tile, 1)
    tile, wide = units // steps, width // steps
    shapes = [jax.ShapeDtypeStruct((blocks * rows, units), BF16)] * outs
    in_specs = [pl.BlockSpec((rows, width), lambda i: (0, 0), pipeline_mode=pl.Buffered(1))] * count
    in_specs += [
        pl.BlockSpec((width, tile), lambda i, w=which: (0, w * steps + i)) for which in places
    ]
    cell = pl.BlockSpec((count * rows, tile), lambda i: (place, i))
    in_specs += [cell] * len(kept)
    out_specs = [cell] * outs
    if copy:
        shapes.append(jax.ShapeDtypeStruct((blocks * rows, width), BF16))
        out_specs.append(pl.BlockSpec((count * rows, wide), lambda i: (place, i)))
    operands = [*tokens, *weights, *kept]
    aliases = {}
    if prev is not None:
        for index, array in enumerate(prev):
            aliases[len(operands)] = index
            operands.append(array)
            in_specs.append(ANYWHERE)
    operands += others
    in_specs += [ANYWHERE] * len(others)
    return pl.pallas_call(
        functools.partial(kernel, count=count),
        grid=(steps,),
        in_specs=in_specs,
        out_specs=out_specs,
        out_shape=shapes,
        input_output_aliases=aliases,
        compiler_params=limit(52),
        cost_estimate=declared(2 * len(weights) * count * rows * width * units),
    )(*operands)


def back_kernel(slot_ref, *refs, count, terms, added, split):
    outs = refs[-2:] if split else refs[-count:]
    weights = refs[count * terms : (count + 1) * terms]
    into = list(refs[(count + 1) * terms :])
    for block in range(count):
        value = dot_cols(refs[block * terms][...], weights[0][...])
        for term in range(1, terms):
            value = value + dot_cols(refs[block * terms + term][...], weights[term][...])
        half = value.shape[0] // 2
        if split:
            outs[0][...] = value[:half].astype(BF16)
            outs[1][...] = value[half:].astype(BF16)
            continue
        if added[block] is None:
            outs[block][...] = value.astype(BF16)
            continue
        extra = into.pop(0)[...].astype(F32)
        top, bottom = value[:half], value[half:]
        if added[block]:
            top = top + extra
        else:
            bottom = bottom + extra
        outs[block][:half, :] = top.astype(BF16)
        outs[block][half:, :] = bottom.astype(BF16)


def back(slots, rows, lefts, weights, places, into=None, others=(), split=False):
    depth = lefts[0].shape[1]
    width = weights[0].shape[0]
    tile = min(512, width)
    terms, count = len(lefts), len(slots)
    outs, tall = (2, rows // 2) if split else (count, rows)
    into = into or [None] * count
    in_specs, operands = [], [jnp.stack([jnp.asarray(slot, jnp.int32) for slot in slots])]
    for block in range(count):
        in_specs += [pl.BlockSpec((rows, depth), lambda i, s, b=block: (s[b], 0))] * terms
        operands += lefts
    in_specs += [pl.BlockSpec((tile, depth), lambda i, s, p=place: (i, p)) for place in places]
    operands += weights
    for extra in into:
        if extra is not None:
            in_specs.append(pl.BlockSpec((rows // 2, tile), lambda i, s: (0, i)))
            operands.append(extra[0])
    operands += others
    in_specs += [ANYWHERE] * len(others)
    return pl.pallas_call(
        functools.partial(
            back_kernel,
            count=count,
            terms=terms,
            added=[None if extra is None else extra[1] for extra in into],
            split=split,
        ),
        grid_spec=pltpu.PrefetchScalarGridSpec(
            num_scalar_prefetch=1,
            grid=(width // tile,),
            in_specs=in_specs,
            out_specs=[pl.BlockSpec((tall, tile), lambda i, s: (0, i))] * outs,
        ),
        out_shape=[jax.ShapeDtypeStruct((tall, width), BF16)] * outs,
        compiler_params=limit(52),
        cost_estimate=declared(2 * count * terms * rows * width * depth),
    )(*operands)


def turn_kernel(value_ref, *rest):
    rest[-1][...] = value_ref[...].T


def turn(value, others=()):
    rows, columns = value.shape
    tile = min(512, rows)
    return pl.pallas_call(
        turn_kernel,
        grid=(rows // tile,),
        in_specs=[pl.BlockSpec((tile, columns), lambda i: (i, 0))] + [ANYWHERE] * len(others),
        out_specs=pl.BlockSpec((columns, tile), lambda i: (0, i)),
        out_shape=jax.ShapeDtypeStruct((columns, rows), value.dtype),
        compiler_params=limit(52),
        cost_estimate=declared(0),
    )(value, *others)


def turn_blocks(lefts, turned_ref):
    rows = lefts[0].shape[0]
    for block, left in enumerate(lefts):
        turned_ref[:, block * rows : (block + 1) * rows] = left[...].T


def weigh_kernel(*refs, count):
    lefts, right_ref = refs[:count], refs[count]
    out_ref, *turned = refs[-3:]
    i, j = pl.program_id(0), pl.program_id(1)
    last = j == pl.num_programs(1) - 1

    @pl.when((i == 0) & (j == 0))
    def _():
        turn_blocks(lefts, turned[0])

    for parity in range(2):

        @pl.when((i % 2 == parity) & jnp.logical_not(last))
        def _():
            out_ref[...] = dot(turned[parity][...], right_ref[...]).astype(BF16)

        @pl.when((i % 2 == parity) & last)
        def _():
            out_ref[...] = dot(turned[parity][...], right_ref[...]).astype(BF16)
            turn_blocks(lefts, turned[1 - parity])


def weigh(lefts, right, others=()):
    tokens, columns = right.shape
    rows, width = lefts[0].shape
    tall, wide = min(512, width), min(1024, columns // 2)
    tiles, steps = width // tall, columns // wide

    def ahead(i, j):
        return 0, jnp.minimum(i + jnp.where(j == steps - 1, 1, 0), tiles - 1)

    return pl.pallas_call(
        functools.partial(weigh_kernel, count=len(lefts)),
        grid=(tiles, steps),
        in_specs=[pl.BlockSpec((rows, tall), ahead)] * len(lefts)
        + [pl.BlockSpec((tokens, wide), lambda i, j: (0, j))]
        + [ANYWHERE] * len(others),
        out_specs=pl.BlockSpec((tall, wide), lambda i, j: (i, j)),
        out_shape=jax.ShapeDtypeStruct((width, columns), BF16),
        scratch_shapes=[pltpu.VMEM((tall, tokens), BF16)] * 2,
        compiler_params=limit(52),
        cost_estimate=declared(2 * tokens * width * columns),
    )(*lefts, right, *others)


def weigh_both_kernel(*refs, count):
    one_ref, others = refs[0], refs[1 : 1 + count]
    right_ref, other_ref, out_ref, turned_ref, other_turned_ref = refs[1 + count :]
    columns = right_ref.shape[1]
    turn_blocks([one_ref], turned_ref)
    out_ref[:, :columns] = dot(turned_ref[...], right_ref[...]).astype(BF16)
    turn_blocks(others, other_turned_ref)
    out_ref[:, columns:] = dot(other_turned_ref[...], other_ref[...]).astype(BF16)


def weigh_both(one, right, others, other_right):
    tokens, width = one.shape
    rows = others[0].shape[0]
    columns, more = right.shape[1], other_right.shape[1]
    tall = min(512, width)
    whole = [pl.BlockSpec((tokens, columns), lambda i: (0, 0))]
    whole += [pl.BlockSpec((tokens, more), lambda i: (0, 0))]
    return pl.pallas_call(
        functools.partial(weigh_both_kernel, count=len(others)),
        grid=(width // tall,),
        in_specs=[pl.BlockSpec((tokens, tall), lambda i: (0, i))]
        + [pl.BlockSpec((rows, tall), lambda i: (0, i))] * len(others)
        + whole,
        out_specs=pl.BlockSpec((tall, columns + more), lambda i: (i, 0)),
        out_shape=jax.ShapeDtypeStruct((width, columns + more), BF16),
        scratch_shapes=[pltpu.VMEM((tall, tokens), BF16)] * 2,
        compiler_params=limit(52),
        cost_estimate=declared(2 * tokens * width * (columns + more)),
    )(one, *others, right, other_right)


def settle_kernel(*refs, count):
    pieces, weights = refs[:count], refs[count : 2 * count]
    x_ref, gains_ref = refs[2 * count : 2 * count + 2]
    stream_ref, h_ref = refs[-2:]
    stream = x_ref[...].astype(F32)
    for piece, weight in zip(pieces, weights):
        stream = stream + dot_cols(piece[...], weight[...])
    stream_ref[...] = stream
    normed, _ = normalize(stream)
    h_ref[...] = (normed * gains_ref[1:2, :]).astype(BF16)


def settle(own, place, pieces, weights, tokens, gains, others=()):
    rows, width = tokens.shape
    depth = weights[0].shape[1]
    tile = min(256, rows)
    steps = rows // tile
    wide = pl.BlockSpec((tile, width), lambda i: (i, 0))
    piece = pl.BlockSpec((tile, depth), lambda i: (i, 0))
    weight = pl.BlockSpec((width, depth), lambda i: (0, 0), pipeline_mode=pl.Buffered(1))
    return pl.pallas_call(
        functools.partial(settle_kernel, count=len(weights)),
        grid=(steps,),
        in_specs=[pl.BlockSpec((tile, depth), lambda i: (place * steps + i, 0))]
        + [piece] * len(pieces)
        + [weight] * len(weights)
        + [wide, pl.BlockSpec((8, width), lambda i: (0, 0))]
        + [ANYWHERE] * len(others),
        out_specs=[wide, wide],
        out_shape=[
            jax.ShapeDtypeStruct((rows, width), F32),
            jax.ShapeDtypeStruct((rows, width), BF16),
        ],
        compiler_params=limit(52),
        cost_estimate=declared(2 * len(weights) * rows * width * depth),
    )(own, *pieces, *weights, tokens, gains, *others)


def norm_back(grad_in, stream, gain):
    normed, scale_r = normalize(stream)
    scaled = grad_in * gain
    return scale_r * (scaled - normed * jnp.mean(scaled * normed, axis=-1, keepdims=True))


def settle_back_kernel(*refs, parts, count):
    terms, weights = refs[:parts], refs[parts : parts + count]
    grad_ref, stream_ref, gains_ref, out_ref, low_ref = refs[parts + count : parts + count + 5]
    pieces = refs[parts + count + 5 :]
    grad_in = terms[0][...].astype(F32)
    for term in terms[1:]:
        grad_in = grad_in + term[...].astype(F32)
    grad = grad_ref[...].astype(F32) + norm_back(grad_in, stream_ref[...], gains_ref[1:2, :])
    out_ref[...] = grad
    low = grad.astype(BF16)
    low_ref[...] = low
    for piece, weight in zip(pieces, weights):
        piece[...] = dot(low, weight[...]).astype(BF16)


def settle_back(terms, weights, grad, stream, gains):
    rows, width = grad.shape
    depth = weights[0].shape[1]
    tile = min(256, rows)
    wide = pl.BlockSpec((tile, width), lambda i: (i, 0))
    weight = pl.BlockSpec((width, depth), lambda i: (0, 0), pipeline_mode=pl.Buffered(1))
    return pl.pallas_call(
        functools.partial(settle_back_kernel, parts=len(terms), count=len(weights)),
        grid=(rows // tile,),
        in_specs=[wide] * len(terms)
        + [weight] * len(weights)
        + [wide, wide, pl.BlockSpec((8, width), lambda i: (0, 0))],
        out_specs=[wide, wide] + [pl.BlockSpec((tile, depth), lambda i: (i, 0))] * len(weights),
        out_shape=[
            jax.ShapeDtypeStruct((rows, width), F32),
            jax.ShapeDtypeStruct((rows, width), BF16),
        ]
        + [jax.ShapeDtypeStruct((rows, depth), BF16)] * len(weights),
        compiler_params=limit(52),
        cost_estimate=declared(2 * len(weights) * rows * width * depth),
    )(*terms, *weights, grad, stream, gains)


def settle_last_kernel(*refs):
    grad_ref, x_ref, gains_ref, out_ref = refs[-4:]
    grad_in = refs[0][...].astype(F32)
    for term in refs[1:-4]:
        grad_in = grad_in + term[...].astype(F32)
    back_a = norm_back(grad_in, x_ref[...].astype(F32), gains_ref[0:1, :])
    out_ref[...] = (grad_ref[...] + back_a).astype(BF16)


def settle_last(terms, grad, tokens, gains):
    rows, width = tokens.shape
    tile = min(128, rows)
    wide = pl.BlockSpec((tile, width), lambda i: (i, 0))
    return pl.pallas_call(
        settle_last_kernel,
        grid=(rows // tile,),
        in_specs=[wide] * (len(terms) + 2) + [pl.BlockSpec((8, width), lambda i: (0, 0))],
        out_specs=wide,
        out_shape=jax.ShapeDtypeStruct((rows, width), BF16),
        compiler_params=limit(52),
        cost_estimate=declared(rows * width),
    )(*terms, grad, tokens, gains)


def causal(keys, queries):
    key = lax.broadcasted_iota(jnp.int32, (keys, queries), 0)
    return key <= lax.broadcasted_iota(jnp.int32, (keys, queries), 1)


def first_block(bound, offset, block):
    return jnp.where(offset >= bound, lax.div(bound, jnp.int32(block)), 0)


def attend_kernel(order_ref, q_ref, kx_ref, vt_ref, *rest, block):
    out_ref, lse_ref, top_ref, acc_ref = rest[-4:]
    kv = kx_ref.shape[0]
    per = q_ref.shape[1] // LANES // kv
    bound = order_ref[0]
    ones = jnp.ones((16, block), BF16)
    for group in range(kv):

        def q_step(turn, _):
            index = order_ref[1 + turn]
            offset = pl.multiple_of(index * block, block)
            into = pl.ds(pl.multiple_of(turn * block, block), block)
            top_ref[...] = jnp.full(top_ref.shape, MASKED, F32)
            acc_ref[...] = jnp.zeros(acc_ref.shape, F32)

            def tile(step, diagonal):
                keys = pl.ds(pl.multiple_of(step, block), block)
                value_t = jnp.concatenate(
                    [vt_ref[group * HD : (group + 1) * HD, keys], ones], axis=0
                )
                for head in range(2 * per):
                    column = (group * per + head // 2) * LANES
                    query = q_ref[pl.ds(offset, block), column : column + LANES]
                    scores = dot_cols(kx_ref[group, head % 2, keys, :], query)
                    if diagonal:
                        scores = jnp.where(causal(block, block), scores, MASKED)
                    old = top_ref[head, 0:1, :]
                    top = jnp.maximum(old, jnp.max(scores, axis=0, keepdims=True))
                    powered = jnp.exp(scores - top).astype(BF16)
                    acc_ref[head] = acc_ref[head] * jnp.exp(old - top) + dot(value_t, powered)
                    top_ref[head, 0:1, :] = top

            def full_tile(step, carry):
                tile(step * block, False)
                return carry

            lax.fori_loop(first_block(bound, offset, block), index, full_tile, 0)
            tile(offset, True)
            for pair in range(per):
                both = []
                for head in (2 * pair, 2 * pair + 1):
                    total = acc_ref[head, HD : HD + 1, :]
                    both.append(acc_ref[head, :HD, :] / total)
                    place = group * 2 * per + head
                    lse_ref[place : place + 1, into] = top_ref[
                        head, 0:1, :
                    ] + jnp.log(total)
                column = (group * per + pair) * LANES
                out_ref[into, column : column + LANES] = (
                    jnp.concatenate(both, axis=0).T.astype(BF16)
                )
            return _

        lax.fori_loop(0, out_ref.shape[0] // block, q_step, 0)


def attend(bound, order, queries, kx, vt, block, others=()):
    length, width = queries.shape
    heads = width // HD
    kv = kx.shape[0]
    per = heads // kv
    count = len(order)
    cells = heads * count * block * (length + block) // 2
    vmem = pl.BlockSpec(memory_space=pltpu.VMEM)
    return pl.pallas_call(
        functools.partial(attend_kernel, block=block),
        in_specs=[pl.BlockSpec(memory_space=pltpu.SMEM), vmem, vmem, vmem] + [ANYWHERE] * len(others),
        out_specs=[vmem, vmem],
        out_shape=[
            jax.ShapeDtypeStruct((count * block, width), BF16),
            jax.ShapeDtypeStruct((heads, count * block), F32),
        ],
        scratch_shapes=[
            pltpu.VMEM((per, 8, block), F32),
            pltpu.VMEM((per, HD + 16, block), F32),
        ],
        compiler_params=limit(52),
        cost_estimate=declared(2 * 4 * HD * 4 * cells, 16),
    )(jnp.stack([bound, *order]), queries, kx, vt, *others)


def sort_kernel(order_ref, *refs):
    parts, out_refs = refs[:2], refs[2:]
    block = out_refs[0].shape[0]
    for turn, out_ref in enumerate(out_refs):
        index = order_ref[turn]
        rows = pl.ds(pl.multiple_of(lax.div(index, 2) * block, block), block)
        out_ref[...] = jnp.where(lax.rem(index, 2) == 0, parts[0][rows, :], parts[1][rows, :])


def sort_blocks(order, even, odd):
    rows, width = even.shape[0] // 2, even.shape[1]
    vmem = pl.BlockSpec(memory_space=pltpu.VMEM)
    return pl.pallas_call(
        sort_kernel,
        in_specs=[pl.BlockSpec(memory_space=pltpu.SMEM), vmem, vmem],
        out_specs=[vmem] * len(order),
        out_shape=[jax.ShapeDtypeStruct((rows, width), even.dtype)] * len(order),
        compiler_params=limit(20),
        cost_estimate=declared(0),
    )(jnp.stack(order), even, odd)


def attend_back_kernel(
    order_ref, q_ref, kx_ref, vx_ref, kt_ref, lse_ref, out_ref, grad_ref, cos_ref, sin_ref,
    *rest, block
):
    dqkv_ref, dk_ref, dv_ref, dq_ref = rest[-4:]
    length = q_ref.shape[0]
    kv = kx_ref.shape[0]
    heads = q_ref.shape[1] // HD
    per = heads // 2 // kv
    bound = order_ref[0]
    dk_ref[...] = jnp.zeros(dk_ref.shape, F32)
    dv_ref[...] = jnp.zeros(dv_ref.shape, F32)
    lane = lax.broadcasted_iota(jnp.int32, (8, LANES), 1)
    row = lax.broadcasted_iota(jnp.int32, (8, LANES), 0)
    chosen = ((lane // HD) == row).astype(F32)

    def turn_back(values, rows):
        return values * cos_ref[rows, :] - swap_halves(values) * sin_ref[rows, :]

    for group in range(kv):

        def q_step(turn, _):
            index = order_ref[1 + turn]
            offset = pl.multiple_of(index * block, block)
            rows = pl.ds(offset, block)
            given = pl.ds(pl.multiple_of(turn * block, block), block)
            dq_ref[...] = jnp.zeros(dq_ref.shape, F32)
            deltas = []
            for pair in range(per):
                column = (group * per + pair) * LANES
                product = grad_ref[given, column : column + LANES].astype(F32) * out_ref[
                    given, column : column + LANES
                ].astype(F32)
                deltas.append(
                    lax.dot_general(
                        chosen, product, OVER_COLS, precision=lax.Precision.HIGHEST,
                        preferred_element_type=F32,
                    )
                )

            def tile(step, size, skip, diagonal):
                keys = pl.ds(pl.multiple_of(step, size), size)
                key_t = kt_ref[group * HD : (group + 1) * HD, keys]
                mine = pl.ds(offset + skip, block - skip)
                theirs = pl.ds(turn * block + skip, block - skip)
                for parity in range(2):
                    key_add, value_add = 0.0, 0.0
                    for pair in range(per):
                        head = 2 * pair + parity
                        place = group * 2 * per + head
                        column = (group * per + pair) * LANES
                        query = q_ref[mine, column : column + LANES]
                        grad = grad_ref[theirs, column : column + LANES]
                        scores = dot_cols(kx_ref[group, parity, keys, :], query)
                        if diagonal:
                            scores = jnp.where(causal(size, block - skip), scores, MASKED)
                        probs = jnp.exp(scores - lse_ref[place : place + 1, rows][:, skip:])
                        dprobs = dot_cols(vx_ref[group, parity, keys, :], grad)
                        delta = deltas[pair][parity : parity + 1, skip:]
                        dscores = (probs * (dprobs - delta)).astype(BF16)
                        value_add = value_add + dot(probs.astype(BF16), grad)
                        key_add = key_add + dot(dscores, query)
                        dq_ref[head * HD : (head + 1) * HD, skip:] += dot(key_t, dscores)
                    dk_ref[group, parity, keys, :] += key_add
                    dv_ref[group, parity, keys, :] += value_add

            def full_tile(step, carry):
                tile(step * block, block, 0, False)
                return carry

            lax.fori_loop(first_block(bound, offset, block), index, full_tile, 0)
            tile(offset, block // 2, 0, True)
            tile(offset + block // 2, block // 2, block // 2, True)
            for pair in range(per):
                column = (group * per + pair) * LANES
                grad_q = dq_ref[pair * LANES : (pair + 1) * LANES, :].T * (1.0 / math.sqrt(HD))
                dqkv_ref[rows, column : column + LANES] = turn_back(grad_q, rows).astype(BF16)
            return _

        lax.fori_loop(0, length // block, q_step, 0)

    def finish(index, _):
        rows = pl.ds(pl.multiple_of(index * block, block), block)
        lanes = lax.broadcasted_iota(jnp.int32, (block, LANES), 1)

        def placed(part, half):
            ref = dk_ref if part < kv else dv_ref
            even, odd = ref[part % kv, 0, rows, :], ref[part % kv, 1, rows, :]
            return even + pltpu.roll(odd, HD, 1) if half == 0 else pltpu.roll(even, HD, 1) + odd

        for chunk in range(kv):
            values = jnp.where(lanes < HD, placed(2 * chunk, 0), placed(2 * chunk + 1, 1))
            if 2 * chunk + 1 < kv:
                values = turn_back(values, rows)
            elif 2 * chunk < kv:
                values = jnp.where(lanes < HD, turn_back(values, rows), values)
            column = heads * HD + chunk * LANES
            dqkv_ref[rows, column : column + LANES] = values.astype(BF16)
        return _

    lax.fori_loop(0, length // block, finish, 0)


def attend_back(
    bound, order, queries, kx, vx, kt, log_sums, attended, grad, cosine, sine, block, others
):
    length, width = queries.shape
    heads = width // HD
    kv = kx.shape[0]
    cells = heads * length * (length + block) // 2
    vmem = pl.BlockSpec(memory_space=pltpu.VMEM)
    return pl.pallas_call(
        functools.partial(attend_back_kernel, block=block),
        in_specs=[pl.BlockSpec(memory_space=pltpu.SMEM)] + [vmem] * 9 + [ANYWHERE] * len(others),
        out_specs=vmem,
        out_shape=jax.ShapeDtypeStruct((length, width + 2 * kv * HD), BF16),
        scratch_shapes=[
            pltpu.VMEM((kv, 2, length, LANES), F32),
            pltpu.VMEM((kv, 2, length, LANES), F32),
            pltpu.VMEM((heads // kv * HD, block), F32),
        ],
        compiler_params=limit(52),
        cost_estimate=declared(2 * 10 * HD * 4 * cells),
    )(jnp.stack([bound, *order]), queries, kx, vx, kt, log_sums, attended, grad, cosine, sine, *others)


def local(
    inputs,
    segment_ids,
    attn_gain,
    query_weight,
    key_weight,
    value_weight,
    output_weight,
    mlp_gain,
    gate_weight,
    up_weight,
    down_weight,
    cotangent,
    *,
    sizes,
):
    rows = inputs.shape[0]
    length = segment_ids.shape[0]
    query_cols = query_weight.shape[1]
    key_cols = key_weight.shape[1]
    heads, kv = query_cols // HD, key_cols // HD
    columns = query_cols + 2 * key_cols
    slots = slots_of(sizes["tensor"])
    tensor = sizes["tensor"]
    space = (-columns) % query_cols or query_cols
    gains = jnp.pad(jnp.stack([attn_gain, mlp_gain], axis=1), ((0, 0), (0, space - 2)))
    bundle = lax.all_gather(
        jnp.concatenate([query_weight, key_weight, value_weight, gains, output_weight.T], axis=1),
        "dp", axis=0, tiled=True,
    )
    out_own = bundle[:, columns + space :]
    hop = first_hop(inputs, tensor)
    gate_up = lax.all_gather(
        hold(jnp.concatenate([gate_weight, up_weight], axis=1), *(hop or ())),
        "dp", axis=0, tiled=True,
    )

    bound, cosine, sine = rope_tables(segment_ids)
    blocks = second_hop(inputs, hop, tensor)
    arrays = project(slots, blocks, bundle, cosine, sine, heads, kv, length)
    block_a, queries, kx, vx, kt, vt, gains = arrays
    down_t = lax.all_gather(turn(down_weight, [queries]), "dp", axis=0, tiled=True)

    if tensor == 4:
        out_own = hold(out_own, blocks[3])
        out_hop = first_hop(out_own, tensor)
        odd, odd_sums = attend(bound, [jnp.int32(k) for k in (1, 3)], queries, kx, vt, rows)
        halves = hold_halves(out_hop, odd)
        out_all = second_hop(out_own, out_hop, tensor, halves)
        even, even_sums = attend(bound, [jnp.int32(k) for k in (0, 2)], queries, kx, vt, rows, halves)
        order = [slots[1], slots[2], slots[0], slots[3]]
        first, second, own, far = sort_blocks(order, even, odd)
        from_one = lax.ppermute(first, "tensor", pairs(tensor, 1))
        from_two = lax.ppermute(second, "tensor", pairs(tensor, 2))
        from_far = lax.ppermute(far, "tensor", pairs(tensor, 3))
        stream_one, low_m = settle(own, 0, [from_one, from_two, from_far], out_all, inputs, gains)
        attended = jnp.concatenate([first, second, own, far], axis=0)
        log_sums = jnp.concatenate(
            [part[:, at : at + rows] for at in (0, rows) for part in (even_sums, odd_sums)], axis=1
        )
    else:
        order = slots
        out_all = gather(out_own, tensor)
        attended, log_sums = attend(bound, order, queries, kx, vt, rows)
        given = trade([attended[k * rows : (k + 1) * rows] for k in range(tensor)], tensor)
        stream_one, low_m = settle(given[0], 0, given[1:], out_all, inputs, gains)
        cotangent_sent = cotangent
    parts_m = [low_m]
    units = gate_weight.shape[1]

    def feed_at(place, wanted, fed, others=()):
        return feed(
            feed_kernel, place, tensor, [parts_m[k] for k in wanted], [gate_up] * 2, [0, 1], [],
            units, 3, True, 512, fed, others,
        )

    def back_m(places, fed, into=None, others=(), split=False):
        return back(places, rows, fed[:2], [gate_up] * 2, [0, 1], into, others, split)

    def back_out(places, into=None, others=(), split=False):
        return back(places, rows, [hidden], [down_t], [0], into, others, split)

    def reduce_rows(term, *others):
        if others and tensor == 4:
            term = hold(term, *others)
        return lax.psum_scatter(term, "dp", scatter_dimension=0, tiled=True)

    if tensor == 4:
        hop = first_hop(parts_m[0], tensor)
        fed = feed_at(3, [0], None)
        cotangent_sent = hold(cotangent, fed[0])
        cotangent_hop = first_hop(cotangent_sent, tensor)
        parts_m = second_hop(parts_m[0], hop, tensor)
        fed = feed_at(0, [1, 2], fed, [cotangent_sent])
        halves = hold_halves(cotangent_hop, fed[0])
        grad_parts = second_hop(cotangent_sent, cotangent_hop, tensor, halves)
        grad_parts = grad_parts[1:] + grad_parts[:1]
        fed = feed_at(2, [3], fed, halves)
    else:
        grad_parts = second_hop(cotangent_sent, None, tensor)
        parts_m = gather(parts_m[0], tensor)
        fed = None
        for place in range(tensor):
            fed = feed_at(place, [place], fed)
    hidden, silu, slope, block_m = fed

    def feed_back(others=()):
        return feed(
            feed_back_kernel, 0, tensor, grad_parts, [down_t], [0], [silu, slope], units, 2, False, 512,
            None, others,
        )

    if tensor == 4:
        three_out = back_out([2], None, [fed[0]], True)
        out_one, out_two = out_halves = send_half(three_out, tensor)
        one_out, two_out, own_out = back_out([0, 1, 3], None, three_out[:1])
        down_t_wgrad = weigh(grad_parts, hidden, [one_out])
        one_out, two_out = add_half(one_out, out_one, 1), add_half(two_out, out_two, 0)
        out_parts = [
            own_out,
            lax.ppermute(one_out, "tensor", pairs(tensor, 1)),
            lax.ppermute(two_out, "tensor", pairs(tensor, 2)),
        ]
        fed = feed_back([one_out])
        three_m = back_m([2], fed, None, (), True)
        m_one, m_two = m_halves = send_half(three_m, tensor)
        gate_wgrad = weigh([block_m], fed[0], [three_m[0], *out_parts[1:]])
        one_m, two_m = back_m([0, 1], fed, [(m_one, False), (m_two, True)])
        (own_m,) = back_m([3], fed, None, [one_m])
        up_wgrad = weigh([block_m], fed[1], [own_m])
        grad_m_parts = [
            own_m,
            lax.ppermute(one_m, "tensor", pairs(tensor, 1)),
            lax.ppermute(two_m, "tensor", pairs(tensor, 2)),
        ]
    else:
        down_t_wgrad = weigh(grad_parts, hidden)
        fed = feed_back()
        grad_m_parts = sum_whole(back_m(list(range(tensor)), fed))
        gate_wgrad, up_wgrad = weigh([block_m], fed[0]), weigh([block_m], fed[1])
        out_parts = sum_whole(back_out(list(range(tensor))))
    layer_out = (stream_one + total(out_parts)).astype(BF16)
    if tensor != 4:
        out_halves = m_halves = ()
    down_t_low = reduce_rows(down_t_wgrad, *out_halves)
    gate_low = reduce_rows(gate_wgrad, *m_halves)
    up_low = reduce_rows(up_wgrad, *grad_m_parts[1:])

    grad_stream_one, grad_stream_low, *pieces = settle_back(
        grad_m_parts, out_all, cotangent, stream_one, gains
    )
    given = trade(pieces, tensor)
    places = [1, 2, 0, 3] if tensor == 4 else list(range(tensor))
    grad_attended = jnp.concatenate([given[k] for k in places], axis=0)
    grad_qkv = attend_back(
        bound, order, queries, kx, vx, kt, log_sums, attended, grad_attended, cosine, sine, rows,
        [down_t_low, layer_out],
    )
    if tensor == 4:
        sent = hold(grad_stream_low, grad_attended)
        grad_stream_parts = trade([sent] * 4, tensor)
    else:
        grad_stream_parts = gather(grad_stream_low, tensor)
    grad_stream_parts = [grad_stream_parts[k] for k in places]

    def back_a(places, others=(), split=False):
        return back(places, rows, [grad_qkv], [bundle], [0], None, others, split)

    if tensor == 4:
        three = back_a(slots[3:], [gate_low], True)
        halves = send_half(three, tensor)
        one, two, own = back_a([slots[1], slots[2], slots[0]], three[:1])
        block_a = hold(block_a, one)
    attention_wgrad = weigh_both(block_a, grad_qkv, grad_stream_parts, attended)
    gate_sum, up_sum, down_t_sum = [low.astype(F32) for low in (gate_low, up_low, down_t_low)]
    if tensor == 4:
        attention_wgrad = hold(attention_wgrad, *halves)
    attention_sum = reduce_rows(attention_wgrad).astype(F32)
    if tensor == 4:
        grad_a_parts = [own, *send_whole(one, two, halves, tensor)]
    else:
        grad_a_parts = sum_whole(back_a(slots))

    product = attention_wgrad[:, :columns].astype(F32) * bundle[:, :columns].astype(F32)
    attn_term = sum_tensor(jnp.sum(product, axis=1)[None, :], tensor)
    width = attn_gain.shape[0]
    attn_term = lax.dynamic_slice_in_dim(
        sum_blocks(attn_term, sizes["dp"]), lax.axis_index("dp") * width, width, 1
    )

    def gain_term(gain, weights):
        term = sum(jnp.sum(weight.astype(F32) * grad, axis=1) for weight, grad in weights)
        return term / gain.astype(F32)

    query_sum = attention_sum[:, :query_cols]
    key_sum = attention_sum[:, query_cols : query_cols + key_cols]
    value_sum = attention_sum[:, query_cols + key_cols : columns]
    mlp_term = sum_tensor(
        gain_term(mlp_gain, [(gate_weight, gate_sum), (up_weight, up_sum)])[None, :], tensor
    )
    input_grad = settle_last(grad_a_parts, grad_stream_one, inputs, gains)
    return (
        layer_out,
        input_grad,
        attn_term[0] / attn_gain.astype(F32),
        query_sum,
        key_sum,
        value_sum,
        attention_sum[:, columns:].T,
        mlp_term[0],
        gate_sum,
        up_sum,
        down_t_sum.T,
    )


def solution(mesh):
    tokens = P(("dp", "tensor"), None)
    in_specs = (
        tokens,
        P("dp"),
        P("dp"),
        P("dp", "tensor"),
        P("dp", "tensor"),
        P("dp", "tensor"),
        P("tensor", "dp"),
        P("dp"),
        P("dp", "tensor"),
        P("dp", "tensor"),
        P("tensor", "dp"),
        tokens,
    )
    out_specs = (
        tokens,
        tokens,
        P("dp"),
        P("dp", "tensor"),
        P("dp", "tensor"),
        P("dp", "tensor"),
        P("tensor", "dp"),
        P("dp"),
        P("dp", "tensor"),
        P("dp", "tensor"),
        P("tensor", "dp"),
    )
    return jax.shard_map(
        functools.partial(local, sizes={axis: mesh.shape[axis] for axis in ("tensor", "dp")}),
        mesh=mesh, in_specs=in_specs, out_specs=out_specs, check_vma=False,
    )
```

```python
import functools
import math

import jax
import jax.numpy as jnp
from jax import lax
from jax.experimental import pallas as pl
from jax.experimental.pallas import tpu as pltpu
from jax.sharding import PartitionSpec as P

HD = 64
LANES = 128
EPSILON = 1e-05
ROPE_BASE = 500000.0
MASKED = -1e30
OVER_ROWS = (((0,), (0,)), ((), ()))
OVER_COLS = (((1,), (1,)), ((), ()))


def limit(size):
    return pltpu.CompilerParams(vmem_limit_bytes=size * 2**20)


SHORT = 0.0625


def declared(flops, scale=SHORT):
    return pl.CostEstimate(flops=int(flops * scale), bytes_accessed=0, transcendentals=0)


F32 = jnp.float32
BF16 = jnp.bfloat16


def dot_cols(left, right):
    return lax.dot_general(left, right, OVER_COLS, preferred_element_type=F32)


def dot_rows(left, right):
    return lax.dot_general(left, right, OVER_ROWS, preferred_element_type=F32)


def dot(left, right):
    return jnp.dot(left, right, preferred_element_type=F32)


def pairs(size, bit):
    return [(index, index ^ bit) for index in range(size)]


def slots_of(size):
    if size == 4:
        return [lax.axis_index("tensor") ^ step for step in range(size)]
    return [jnp.int32(step) for step in range(size)]


ANYWHERE = pl.BlockSpec(memory_space=pl.ANY)


def nothing_kernel(*refs):
    pass


def hold(value, *others):
    return pl.pallas_call(
        nothing_kernel,
        in_specs=[ANYWHERE] * (1 + len(others)),
        out_specs=ANYWHERE,
        out_shape=jax.ShapeDtypeStruct(value.shape, value.dtype),
        input_output_aliases={0: 0},
        cost_estimate=declared(0),
    )(value, *others)


def first_hop(shard, size):
    if size != 4:
        return None
    return [lax.ppermute(shard, "tensor", pairs(size, bit)) for bit in (1, 2)]


def copy_kernel(value_ref, *rest):
    rest[-1][...] = value_ref[...]


def half_of(value, which, *others):
    rows, width = value.shape
    tile = rows // 4
    return pl.pallas_call(
        copy_kernel,
        grid=(2,),
        in_specs=[pl.BlockSpec((tile, width), lambda i: (2 * which + i, 0))]
        + [ANYWHERE] * len(others),
        out_specs=pl.BlockSpec((tile, width), lambda i: (i, 0)),
        out_shape=jax.ShapeDtypeStruct((rows // 2, width), value.dtype),
        compiler_params=limit(52),
        cost_estimate=declared(0),
    )(value, *others)


def add_kernel(value_ref, extra_ref, out_ref, *, which):
    out_ref[...] = value_ref[...]

    @pl.when(pl.program_id(0) == which)
    def _():
        out_ref[...] = (value_ref[...].astype(F32) + extra_ref[...].astype(F32)).astype(BF16)


def add_half(value, extra, which):
    rows, width = value.shape
    half = pl.BlockSpec((rows // 2, width), lambda i: (i, 0))
    return pl.pallas_call(
        functools.partial(add_kernel, which=which),
        grid=(2,),
        in_specs=[half, pl.BlockSpec((rows // 2, width), lambda i: (0, 0))],
        out_specs=half,
        out_shape=jax.ShapeDtypeStruct((rows, width), value.dtype),
        compiler_params=limit(52),
        cost_estimate=declared(0),
    )(value, extra)


def hold_halves(hop, *others):
    return half_of(hop[0], 0, *others), half_of(hop[1], 1, *others)


def second_hop(shard, hop, size, halves=None):
    if size != 4:
        whole = lax.all_gather(shard, "tensor", axis=0)
        return [whole[step] for step in range(size)]
    one, two = hop
    upper, lower = halves or hold_halves(hop)
    three_a = lax.ppermute(upper, "tensor", pairs(size, 2))
    three_b = lax.ppermute(lower, "tensor", pairs(size, 1))
    return [shard, one, two, jnp.concatenate([three_a, three_b], axis=0)]


def gather(shard, size):
    return second_hop(shard, first_hop(shard, size), size)


def send_half(three, size):
    into_two = lax.ppermute(three[0], "tensor", pairs(size, 1))
    into_one = lax.ppermute(three[1], "tensor", pairs(size, 2))
    return into_one, into_two


def sum_whole(terms):
    return [
        lax.psum_scatter(
            jnp.concatenate(terms, axis=0), "tensor", scatter_dimension=0, tiled=True
        )
    ]


def trade(pieces, size):
    if size != 4:
        whole = lax.all_to_all(jnp.stack(pieces), "tensor", split_axis=0, concat_axis=0, tiled=True)
        return [whole[step] for step in range(size)]
    return [pieces[0]] + [
        lax.ppermute(pieces[step], "tensor", pairs(size, step)) for step in (1, 2, 3)
    ]


def total(parts):
    return functools.reduce(jnp.add, [part.astype(F32) for part in parts])


def sum_tensor(value, size):
    if size & (size - 1):
        return lax.psum(value, "tensor")
    return value + sum(lax.ppermute(value, "tensor", pairs(size, bit)) for bit in range(1, size))


def sum_blocks(value, size):
    if size & (size - 1):
        return lax.psum(value, "dp")
    bit = 1
    while bit < size:
        value = value + lax.ppermute(value, "dp", pairs(size, bit))
        bit *= 2
    return value


def rope_tables(segment):
    length = segment.shape[0]
    bound = jnp.sum((segment == 0).astype(jnp.int32))
    place = lax.broadcasted_iota(jnp.int32, (length, LANES), 0)
    place = place - jnp.where(place >= bound, bound, 0)
    lane = lax.broadcasted_iota(jnp.int32, (length, LANES), 1)
    freqs = jnp.exp(
        (lane % (HD // 2)).astype(F32) * (-2.0 * math.log(ROPE_BASE) / HD)
    )
    angles = place.astype(F32) * freqs
    sine = jnp.sin(angles)
    return bound, jnp.cos(angles), jnp.where(lane % HD < HD // 2, -sine, sine)


def swap_halves(values):
    lane = lax.broadcasted_iota(jnp.int32, values.shape, 1)
    after = pltpu.roll(values, LANES - HD // 2, 1)
    before = pltpu.roll(values, HD // 2, 1)
    return jnp.where(lane % HD < HD // 2, after, before)


def normalize(stream):
    scale_r = lax.rsqrt(jnp.mean(stream * stream, axis=-1, keepdims=True) + EPSILON)
    return (stream * scale_r, scale_r)


def project_kernel(slot_ref, *refs, count, steps, heads, kv):
    gains_ref, w_ref, cos_ref, sin_ref = refs[count : count + 4]
    h_ref, q_ref, kx_ref, vx_ref, kt_ref, vt_ref, gain_ref = refs[-7:]

    @pl.when(pl.program_id(0) == 0)
    def _():
        gain_ref[...] = gains_ref[...].astype(F32).T[:8]

    which = pl.program_id(0) // steps
    rows = h_ref.shape[0]
    part_rows = min(256, rows)
    lane = lax.broadcasted_iota(jnp.int32, (part_rows, LANES), 1)
    for start in range(0, rows, part_rows):
        at = slice(start, start + part_rows)
        tokens = refs[0][at, :]
        for block in range(1, count):
            tokens = jnp.where(which == block, refs[block][at, :], tokens)
        normed, _ = normalize(tokens.astype(F32))
        low = (normed * gain_ref[0:1, :]).astype(BF16)
        h_ref[at, :] = low
        pre = dot(low, w_ref[...])
        cosine, sine = cos_ref[at, :], sin_ref[at, :]
        chunks = []
        for chunk in range(pre.shape[1] // LANES):
            columns = slice(chunk * LANES, (chunk + 1) * LANES)
            part = pre[:, columns]
            first = 2 * chunk
            if first < heads + kv:
                turned = part * cosine + swap_halves(part) * sine
                part = turned if first + 1 < heads + kv else jnp.where(lane < HD, turned, part)
            chunks.append(part)
            if first < heads:
                q_ref[at, columns] = (part * (1.0 / math.sqrt(HD))).astype(BF16)
        flipped = {}
        for head in range(2 * kv):
            place = heads + head
            part = chunks[place // 2]
            moved = pltpu.roll(part, HD, 1)
            wide = [part, moved] if place % 2 == 0 else [moved, part]
            out = kx_ref if head < kv else vx_ref
            out[head % kv, 0, at, :] = jnp.where(lane < HD, wide[0], 0.0).astype(BF16)
            out[head % kv, 1, at, :] = jnp.where(lane < HD, 0.0, wide[1]).astype(BF16)
            if place // 2 not in flipped:
                flipped[place // 2] = part.T
            turn = flipped[place // 2][(place % 2) * HD : (place % 2 + 1) * HD]
            out_t = kt_ref if head < kv else vt_ref
            out_t[(head % kv) * HD : (head % kv + 1) * HD, at] = turn.astype(BF16)


def project(slots, blocks, bundle, cosine, sine, heads, kv, length):
    rows, width = blocks[0].shape
    count = len(blocks)
    tile = rows
    steps = rows // tile
    columns = (heads + 2 * kv) * HD

    def at(i, slot):
        return slot[i // steps] * steps + i % steps

    shapes = [
        jax.ShapeDtypeStruct((length, width), BF16),
        jax.ShapeDtypeStruct((length, heads * HD), BF16),
        jax.ShapeDtypeStruct((kv, 2, length, LANES), BF16),
        jax.ShapeDtypeStruct((kv, 2, length, LANES), BF16),
        jax.ShapeDtypeStruct((kv * HD, length), BF16),
        jax.ShapeDtypeStruct((kv * HD, length), BF16),
        jax.ShapeDtypeStruct((8, width), F32),
    ]
    out_specs = [
        pl.BlockSpec((tile, width), lambda i, s: (at(i, s), 0)),
        pl.BlockSpec((tile, heads * HD), lambda i, s: (at(i, s), 0)),
        pl.BlockSpec((kv, 2, tile, LANES), lambda i, s: (0, 0, at(i, s), 0)),
        pl.BlockSpec((kv, 2, tile, LANES), lambda i, s: (0, 0, at(i, s), 0)),
        pl.BlockSpec((kv * HD, tile), lambda i, s: (0, at(i, s))),
        pl.BlockSpec((kv * HD, tile), lambda i, s: (0, at(i, s))),
        pl.BlockSpec((8, width), lambda i, s: (0, 0)),
    ]
    in_specs = [
        pl.BlockSpec((tile, width), lambda i, s, b=block: (jnp.clip(i - b * steps, 0, steps - 1), 0))
        for block in range(count)
    ]
    in_specs += [
        pl.BlockSpec((width, LANES), lambda i, s: (0, columns // LANES)),
        pl.BlockSpec((width, columns), lambda i, s: (0, 0)),
        pl.BlockSpec((tile, LANES), lambda i, s: (at(i, s), 0)),
        pl.BlockSpec((tile, LANES), lambda i, s: (at(i, s), 0)),
    ]
    operands = [jnp.stack(slots), *blocks, bundle, bundle, cosine, sine]
    return pl.pallas_call(
        functools.partial(
            project_kernel, count=count, steps=steps, heads=heads, kv=kv
        ),
        grid_spec=pltpu.PrefetchScalarGridSpec(
            num_scalar_prefetch=1,
            grid=(count * steps,),
            in_specs=in_specs,
            out_specs=out_specs,
        ),
        out_shape=shapes,
        compiler_params=limit(52),
        cost_estimate=declared(2 * count * rows * width * columns),
    )(*operands)


def feed_kernel(*refs, count):
    tokens = refs[:count]
    gate_ref, up_ref = refs[count : count + 2]
    hidden_ref, silu_ref, slope_ref, h_out = refs[-4:]
    rows = tokens[0].shape[0]
    wide = h_out.shape[1]
    tile = min(256, gate_ref.shape[1])
    lanes = pl.ds(pl.multiple_of(pl.program_id(0) * wide, wide), wide)
    for block in range(count):
        h_out[block * rows : (block + 1) * rows, :] = tokens[block][:, lanes]
    for part in range(gate_ref.shape[1] // tile):
        columns = slice(part * tile, (part + 1) * tile)
        for block in range(count):
            where = slice(block * rows, (block + 1) * rows)
            gate = dot(tokens[block][...], gate_ref[:, columns])
            up = dot(tokens[block][...], up_ref[:, columns])
            sigmoid = 0.5 * jnp.tanh(0.5 * gate) + 0.5
            silu = gate * sigmoid
            hidden_ref[where, columns] = (silu * up).astype(BF16)
            silu_ref[where, columns] = silu.astype(BF16)
            slope_ref[where, columns] = (up * (sigmoid + silu * (1.0 - sigmoid))).astype(BF16)


def feed_back_kernel(*refs, count):
    grads = refs[:count]
    down_ref, silu_ref, slope_ref = refs[count : count + 3]
    dgate_ref, dup_ref = refs[-2:]
    rows = grads[0].shape[0]
    for block in range(count):
        where = slice(block * rows, (block + 1) * rows)
        dhidden = dot(grads[block][...], down_ref[...])
        dup_ref[where, :] = (dhidden * silu_ref[where, :].astype(F32)).astype(BF16)
        dgate_ref[where, :] = (dhidden * slope_ref[where, :].astype(F32)).astype(BF16)


def feed(kernel, place, blocks, tokens, weights, places, kept, units, outs, copy, tile, prev, others):
    rows, width = tokens[0].shape
    count = len(tokens)
    steps = max(units // tile, 1)
    tile, wide = units // steps, width // steps
    shapes = [jax.ShapeDtypeStruct((blocks * rows, units), BF16)] * outs
    in_specs = [pl.BlockSpec((rows, width), lambda i: (0, 0), pipeline_mode=pl.Buffered(1))] * count
    in_specs += [
        pl.BlockSpec((width, tile), lambda i, w=which: (0, w * steps + i)) for which in places
    ]
    cell = pl.BlockSpec((count * rows, tile), lambda i: (place, i))
    in_specs += [cell] * len(kept)
    out_specs = [cell] * outs
    if copy:
        shapes.append(jax.ShapeDtypeStruct((blocks * rows, width), BF16))
        out_specs.append(pl.BlockSpec((count * rows, wide), lambda i: (place, i)))
    operands = [*tokens, *weights, *kept]
    aliases = {}
    if prev is not None:
        for index, array in enumerate(prev):
            aliases[len(operands)] = index
            operands.append(array)
            in_specs.append(ANYWHERE)
    operands += others
    in_specs += [ANYWHERE] * len(others)
    return pl.pallas_call(
        functools.partial(kernel, count=count),
        grid=(steps,),
        in_specs=in_specs,
        out_specs=out_specs,
        out_shape=shapes,
        input_output_aliases=aliases,
        compiler_params=limit(52),
        cost_estimate=declared(2 * len(weights) * count * rows * width * units),
    )(*operands)


def back_kernel(slot_ref, *refs, count, terms, added, split):
    outs = refs[-2:] if split else refs[-count:]
    weights = refs[count * terms : (count + 1) * terms]
    into = list(refs[(count + 1) * terms :])
    for block in range(count):
        value = dot_cols(refs[block * terms][...], weights[0][...])
        for term in range(1, terms):
            value = value + dot_cols(refs[block * terms + term][...], weights[term][...])
        half = value.shape[0] // 2
        if split:
            outs[0][...] = value[:half].astype(BF16)
            outs[1][...] = value[half:].astype(BF16)
            continue
        if added[block] is None:
            outs[block][...] = value.astype(BF16)
            continue
        extra = into.pop(0)[...].astype(F32)
        top, bottom = value[:half], value[half:]
        if added[block]:
            top = top + extra
        else:
            bottom = bottom + extra
        outs[block][:half, :] = top.astype(BF16)
        outs[block][half:, :] = bottom.astype(BF16)


def back(slots, rows, lefts, weights, places, into=None, others=(), split=False):
    depth = lefts[0].shape[1]
    width = weights[0].shape[0]
    tile = min(512, width)
    terms, count = len(lefts), len(slots)
    outs, tall = (2, rows // 2) if split else (count, rows)
    into = into or [None] * count
    in_specs, operands = [], [jnp.stack([jnp.asarray(slot, jnp.int32) for slot in slots])]
    for block in range(count):
        in_specs += [pl.BlockSpec((rows, depth), lambda i, s, b=block: (s[b], 0))] * terms
        operands += lefts
    in_specs += [pl.BlockSpec((tile, depth), lambda i, s, p=place: (i, p)) for place in places]
    operands += weights
    for extra in into:
        if extra is not None:
            in_specs.append(pl.BlockSpec((rows // 2, tile), lambda i, s: (0, i)))
            operands.append(extra[0])
    operands += others
    in_specs += [ANYWHERE] * len(others)
    return pl.pallas_call(
        functools.partial(
            back_kernel,
            count=count,
            terms=terms,
            added=[None if extra is None else extra[1] for extra in into],
            split=split,
        ),
        grid_spec=pltpu.PrefetchScalarGridSpec(
            num_scalar_prefetch=1,
            grid=(width // tile,),
            in_specs=in_specs,
            out_specs=[pl.BlockSpec((tall, tile), lambda i, s: (0, i))] * outs,
        ),
        out_shape=[jax.ShapeDtypeStruct((tall, width), BF16)] * outs,
        compiler_params=limit(52),
        cost_estimate=declared(2 * count * terms * rows * width * depth),
    )(*operands)


def turn_kernel(value_ref, *rest):
    rest[-1][...] = value_ref[...].T


def turn(value, others=()):
    rows, columns = value.shape
    tile = min(512, rows)
    return pl.pallas_call(
        turn_kernel,
        grid=(rows // tile,),
        in_specs=[pl.BlockSpec((tile, columns), lambda i: (i, 0))] + [ANYWHERE] * len(others),
        out_specs=pl.BlockSpec((columns, tile), lambda i: (0, i)),
        out_shape=jax.ShapeDtypeStruct((columns, rows), value.dtype),
        compiler_params=limit(52),
        cost_estimate=declared(0),
    )(value, *others)


def turn_blocks(lefts, turned_ref):
    rows = lefts[0].shape[0]
    for block, left in enumerate(lefts):
        turned_ref[:, block * rows : (block + 1) * rows] = left[...].T


def weigh_kernel(*refs, count):
    lefts, right_ref = refs[:count], refs[count]
    out_ref, *turned = refs[-3:]
    i, j = pl.program_id(0), pl.program_id(1)
    last = j == pl.num_programs(1) - 1

    @pl.when((i == 0) & (j == 0))
    def _():
        turn_blocks(lefts, turned[0])

    for parity in range(2):

        @pl.when((i % 2 == parity) & jnp.logical_not(last))
        def _():
            out_ref[...] = dot(turned[parity][...], right_ref[...]).astype(BF16)

        @pl.when((i % 2 == parity) & last)
        def _():
            out_ref[...] = dot(turned[parity][...], right_ref[...]).astype(BF16)
            turn_blocks(lefts, turned[1 - parity])


def weigh(lefts, right, others=()):
    tokens, columns = right.shape
    rows, width = lefts[0].shape
    tall, wide = min(512, width), min(1024, columns // 2)
    tiles, steps = width // tall, columns // wide

    def ahead(i, j):
        return 0, jnp.minimum(i + jnp.where(j == steps - 1, 1, 0), tiles - 1)

    return pl.pallas_call(
        functools.partial(weigh_kernel, count=len(lefts)),
        grid=(tiles, steps),
        in_specs=[pl.BlockSpec((rows, tall), ahead)] * len(lefts)
        + [pl.BlockSpec((tokens, wide), lambda i, j: (0, j))]
        + [ANYWHERE] * len(others),
        out_specs=pl.BlockSpec((tall, wide), lambda i, j: (i, j)),
        out_shape=jax.ShapeDtypeStruct((width, columns), BF16),
        scratch_shapes=[pltpu.VMEM((tall, tokens), BF16)] * 2,
        compiler_params=limit(52),
        cost_estimate=declared(2 * tokens * width * columns),
    )(*lefts, right, *others)


def weigh_both_kernel(*refs, count):
    one_ref, others = refs[0], refs[1 : 1 + count]
    right_ref, other_ref, out_ref, turned_ref, other_turned_ref = refs[1 + count :]
    columns = right_ref.shape[1]
    turn_blocks([one_ref], turned_ref)
    out_ref[:, :columns] = dot(turned_ref[...], right_ref[...]).astype(BF16)
    turn_blocks(others, other_turned_ref)
    out_ref[:, columns:] = dot(other_turned_ref[...], other_ref[...]).astype(BF16)


def weigh_both(one, right, others, other_right):
    tokens, width = one.shape
    rows = others[0].shape[0]
    columns, more = right.shape[1], other_right.shape[1]
    tall = min(512, width)
    whole = [pl.BlockSpec((tokens, columns), lambda i: (0, 0))]
    whole += [pl.BlockSpec((tokens, more), lambda i: (0, 0))]
    return pl.pallas_call(
        functools.partial(weigh_both_kernel, count=len(others)),
        grid=(width // tall,),
        in_specs=[pl.BlockSpec((tokens, tall), lambda i: (0, i))]
        + [pl.BlockSpec((rows, tall), lambda i: (0, i))] * len(others)
        + whole,
        out_specs=pl.BlockSpec((tall, columns + more), lambda i: (i, 0)),
        out_shape=jax.ShapeDtypeStruct((width, columns + more), BF16),
        scratch_shapes=[pltpu.VMEM((tall, tokens), BF16)] * 2,
        compiler_params=limit(52),
        cost_estimate=declared(2 * tokens * width * (columns + more)),
    )(one, *others, right, other_right)


def settle_kernel(*refs, count):
    pieces, weights = refs[:count], refs[count : 2 * count]
    x_ref, gains_ref = refs[2 * count : 2 * count + 2]
    stream_ref, h_ref = refs[-2:]
    stream = x_ref[...].astype(F32)
    for piece, weight in zip(pieces, weights):
        stream = stream + dot_cols(piece[...], weight[...])
    stream_ref[...] = stream
    normed, _ = normalize(stream)
    h_ref[...] = (normed * gains_ref[1:2, :]).astype(BF16)


def settle(own, place, pieces, weights, tokens, gains, others=()):
    rows, width = tokens.shape
    depth = weights[0].shape[1]
    tile = min(256, rows)
    steps = rows // tile
    wide = pl.BlockSpec((tile, width), lambda i: (i, 0))
    piece = pl.BlockSpec((tile, depth), lambda i: (i, 0))
    weight = pl.BlockSpec((width, depth), lambda i: (0, 0), pipeline_mode=pl.Buffered(1))
    return pl.pallas_call(
        functools.partial(settle_kernel, count=len(weights)),
        grid=(steps,),
        in_specs=[pl.BlockSpec((tile, depth), lambda i: (place * steps + i, 0))]
        + [piece] * len(pieces)
        + [weight] * len(weights)
        + [wide, pl.BlockSpec((8, width), lambda i: (0, 0))]
        + [ANYWHERE] * len(others),
        out_specs=[wide, wide],
        out_shape=[
            jax.ShapeDtypeStruct((rows, width), F32),
            jax.ShapeDtypeStruct((rows, width), BF16),
        ],
        compiler_params=limit(52),
        cost_estimate=declared(2 * len(weights) * rows * width * depth),
    )(own, *pieces, *weights, tokens, gains, *others)


def norm_back(grad_in, stream, gain):
    normed, scale_r = normalize(stream)
    scaled = grad_in * gain
    return scale_r * (scaled - normed * jnp.mean(scaled * normed, axis=-1, keepdims=True))


def settle_back_kernel(*refs, parts, count):
    terms, weights = refs[:parts], refs[parts : parts + count]
    grad_ref, stream_ref, gains_ref, out_ref, low_ref = refs[parts + count : parts + count + 5]
    pieces = refs[parts + count + 5 :]
    grad_in = terms[0][...].astype(F32)
    for term in terms[1:]:
        grad_in = grad_in + term[...].astype(F32)
    grad = grad_ref[...].astype(F32) + norm_back(grad_in, stream_ref[...], gains_ref[1:2, :])
    out_ref[...] = grad
    low = grad.astype(BF16)
    low_ref[...] = low
    for piece, weight in zip(pieces, weights):
        piece[...] = dot(low, weight[...]).astype(BF16)


def settle_back(terms, weights, grad, stream, gains):
    rows, width = grad.shape
    depth = weights[0].shape[1]
    tile = min(256, rows)
    wide = pl.BlockSpec((tile, width), lambda i: (i, 0))
    weight = pl.BlockSpec((width, depth), lambda i: (0, 0), pipeline_mode=pl.Buffered(1))
    return pl.pallas_call(
        functools.partial(settle_back_kernel, parts=len(terms), count=len(weights)),
        grid=(rows // tile,),
        in_specs=[wide] * len(terms)
        + [weight] * len(weights)
        + [wide, wide, pl.BlockSpec((8, width), lambda i: (0, 0))],
        out_specs=[wide, wide] + [pl.BlockSpec((tile, depth), lambda i: (i, 0))] * len(weights),
        out_shape=[
            jax.ShapeDtypeStruct((rows, width), F32),
            jax.ShapeDtypeStruct((rows, width), BF16),
        ]
        + [jax.ShapeDtypeStruct((rows, depth), BF16)] * len(weights),
        compiler_params=limit(52),
        cost_estimate=declared(2 * len(weights) * rows * width * depth),
    )(*terms, *weights, grad, stream, gains)


def settle_last_kernel(*refs):
    grad_ref, x_ref, gains_ref, out_ref = refs[-4:]
    grad_in = refs[0][...].astype(F32)
    for term in refs[1:-4]:
        grad_in = grad_in + term[...].astype(F32)
    back_a = norm_back(grad_in, x_ref[...].astype(F32), gains_ref[0:1, :])
    out_ref[...] = (grad_ref[...] + back_a).astype(BF16)


def settle_last(terms, grad, tokens, gains):
    rows, width = tokens.shape
    tile = min(128, rows)
    wide = pl.BlockSpec((tile, width), lambda i: (i, 0))
    return pl.pallas_call(
        settle_last_kernel,
        grid=(rows // tile,),
        in_specs=[wide] * (len(terms) + 2) + [pl.BlockSpec((8, width), lambda i: (0, 0))],
        out_specs=wide,
        out_shape=jax.ShapeDtypeStruct((rows, width), BF16),
        compiler_params=limit(52),
        cost_estimate=declared(rows * width),
    )(*terms, grad, tokens, gains)


def finish_kernel(*refs, count):
    value = refs[count][...]
    for term in refs[:count]:
        value = value + term[...].astype(F32)
    refs[-1][...] = value.astype(BF16)


def finish(terms, stream, others=()):
    rows, width = stream.shape
    wide = pl.BlockSpec((rows // 4, width), lambda i: (i, 0))
    return pl.pallas_call(
        functools.partial(finish_kernel, count=len(terms)),
        grid=(4,),
        in_specs=[wide] * (len(terms) + 1) + [ANYWHERE] * len(others),
        out_specs=wide,
        out_shape=jax.ShapeDtypeStruct((rows, width), BF16),
        compiler_params=limit(52),
        cost_estimate=declared(rows * width),
    )(*terms, stream, *others)


def causal(keys, queries):
    key = lax.broadcasted_iota(jnp.int32, (keys, queries), 0)
    return key <= lax.broadcasted_iota(jnp.int32, (keys, queries), 1)


def first_block(bound, offset, block):
    return jnp.where(offset >= bound, lax.div(bound, jnp.int32(block)), 0)


def attend_kernel(order_ref, q_ref, kx_ref, vt_ref, *rest, block):
    out_ref, lse_ref, top_ref, acc_ref = rest[-4:]
    kv = kx_ref.shape[0]
    per = q_ref.shape[1] // LANES // kv
    bound = order_ref[0]
    ones = jnp.ones((16, block), BF16)
    for group in range(kv):

        def q_step(turn, _):
            index = order_ref[1 + turn]
            offset = pl.multiple_of(index * block, block)
            into = pl.ds(pl.multiple_of(turn * block, block), block)
            top_ref[...] = jnp.full(top_ref.shape, MASKED, F32)
            acc_ref[...] = jnp.zeros(acc_ref.shape, F32)

            def tile(step, diagonal):
                keys = pl.ds(pl.multiple_of(step, block), block)
                value_t = jnp.concatenate(
                    [vt_ref[group * HD : (group + 1) * HD, keys], ones], axis=0
                )
                for head in range(2 * per):
                    column = (group * per + head // 2) * LANES
                    query = q_ref[pl.ds(offset, block), column : column + LANES]
                    scores = dot_cols(kx_ref[group, head % 2, keys, :], query)
                    if diagonal:
                        scores = jnp.where(causal(block, block), scores, MASKED)
                    old = top_ref[head, 0:1, :]
                    top = jnp.maximum(old, jnp.max(scores, axis=0, keepdims=True))
                    powered = jnp.exp(scores - top).astype(BF16)
                    acc_ref[head] = acc_ref[head] * jnp.exp(old - top) + dot(value_t, powered)
                    top_ref[head, 0:1, :] = top

            def full_tile(step, carry):
                tile(step * block, False)
                return carry

            lax.fori_loop(first_block(bound, offset, block), index, full_tile, 0)
            tile(offset, True)
            for pair in range(per):
                both = []
                for head in (2 * pair, 2 * pair + 1):
                    total = acc_ref[head, HD : HD + 1, :]
                    both.append(acc_ref[head, :HD, :] / total)
                    place = group * 2 * per + head
                    lse_ref[place : place + 1, into] = top_ref[
                        head, 0:1, :
                    ] + jnp.log(total)
                column = (group * per + pair) * LANES
                out_ref[into, column : column + LANES] = (
                    jnp.concatenate(both, axis=0).T.astype(BF16)
                )
            return _

        lax.fori_loop(0, out_ref.shape[0] // block, q_step, 0)


def attend(bound, order, queries, kx, vt, block, others=()):
    length, width = queries.shape
    heads = width // HD
    kv = kx.shape[0]
    per = heads // kv
    count = len(order)
    cells = heads * count * block * (length + block) // 2
    vmem = pl.BlockSpec(memory_space=pltpu.VMEM)
    return pl.pallas_call(
        functools.partial(attend_kernel, block=block),
        in_specs=[pl.BlockSpec(memory_space=pltpu.SMEM), vmem, vmem, vmem] + [ANYWHERE] * len(others),
        out_specs=[vmem, vmem],
        out_shape=[
            jax.ShapeDtypeStruct((count * block, width), BF16),
            jax.ShapeDtypeStruct((heads, count * block), F32),
        ],
        scratch_shapes=[
            pltpu.VMEM((per, 8, block), F32),
            pltpu.VMEM((per, HD + 16, block), F32),
        ],
        compiler_params=limit(52),
        cost_estimate=declared(2 * 4 * HD * 4 * cells, 16),
    )(jnp.stack([bound, *order]), queries, kx, vt, *others)


def sort_kernel(order_ref, *refs):
    parts, out_refs = refs[:2], refs[2:]
    block = out_refs[0].shape[0]
    for turn, out_ref in enumerate(out_refs):
        index = order_ref[turn]
        rows = pl.ds(pl.multiple_of(lax.div(index, 2) * block, block), block)
        out_ref[...] = jnp.where(lax.rem(index, 2) == 0, parts[0][rows, :], parts[1][rows, :])


def sort_blocks(order, even, odd):
    rows, width = even.shape[0] // 2, even.shape[1]
    vmem = pl.BlockSpec(memory_space=pltpu.VMEM)
    return pl.pallas_call(
        sort_kernel,
        in_specs=[pl.BlockSpec(memory_space=pltpu.SMEM), vmem, vmem],
        out_specs=[vmem] * len(order),
        out_shape=[jax.ShapeDtypeStruct((rows, width), even.dtype)] * len(order),
        compiler_params=limit(20),
        cost_estimate=declared(0),
    )(jnp.stack(order), even, odd)


def attend_back_kernel(
    order_ref, q_ref, kx_ref, vx_ref, kt_ref, lse_ref, out_ref, grad_ref, cos_ref, sin_ref,
    *rest, block
):
    dqkv_ref, dk_ref, dv_ref, dq_ref = rest[-4:]
    length = q_ref.shape[0]
    kv = kx_ref.shape[0]
    heads = q_ref.shape[1] // HD
    per = heads // 2 // kv
    bound = order_ref[0]
    dk_ref[...] = jnp.zeros(dk_ref.shape, F32)
    dv_ref[...] = jnp.zeros(dv_ref.shape, F32)
    lane = lax.broadcasted_iota(jnp.int32, (8, LANES), 1)
    row = lax.broadcasted_iota(jnp.int32, (8, LANES), 0)
    chosen = ((lane // HD) == row).astype(F32)

    def turn_back(values, rows):
        return values * cos_ref[rows, :] - swap_halves(values) * sin_ref[rows, :]

    for group in range(kv):

        def q_step(turn, _):
            index = order_ref[1 + turn]
            offset = pl.multiple_of(index * block, block)
            rows = pl.ds(offset, block)
            given = pl.ds(pl.multiple_of(turn * block, block), block)
            dq_ref[...] = jnp.zeros(dq_ref.shape, F32)
            deltas = []
            for pair in range(per):
                column = (group * per + pair) * LANES
                product = grad_ref[given, column : column + LANES].astype(F32) * out_ref[
                    given, column : column + LANES
                ].astype(F32)
                deltas.append(
                    lax.dot_general(
                        chosen, product, OVER_COLS, precision=lax.Precision.HIGHEST,
                        preferred_element_type=F32,
                    )
                )

            def tile(step, size, skip, diagonal):
                keys = pl.ds(pl.multiple_of(step, size), size)
                key_t = kt_ref[group * HD : (group + 1) * HD, keys]
                mine = pl.ds(offset + skip, block - skip)
                theirs = pl.ds(turn * block + skip, block - skip)
                for parity in range(2):
                    key_add, value_add = 0.0, 0.0
                    for pair in range(per):
                        head = 2 * pair + parity
                        place = group * 2 * per + head
                        column = (group * per + pair) * LANES
                        query = q_ref[mine, column : column + LANES]
                        grad = grad_ref[theirs, column : column + LANES]
                        scores = dot_cols(kx_ref[group, parity, keys, :], query)
                        if diagonal:
                            scores = jnp.where(causal(size, block - skip), scores, MASKED)
                        probs = jnp.exp(scores - lse_ref[place : place + 1, rows][:, skip:])
                        dprobs = dot_cols(vx_ref[group, parity, keys, :], grad)
                        delta = deltas[pair][parity : parity + 1, skip:]
                        dscores = (probs * (dprobs - delta)).astype(BF16)
                        value_add = value_add + dot(probs.astype(BF16), grad)
                        key_add = key_add + dot(dscores, query)
                        dq_ref[head * HD : (head + 1) * HD, skip:] += dot(key_t, dscores)
                    dk_ref[group, parity, keys, :] += key_add
                    dv_ref[group, parity, keys, :] += value_add

            def full_tile(step, carry):
                tile(step * block, block, 0, False)
                return carry

            lax.fori_loop(first_block(bound, offset, block), index, full_tile, 0)
            tile(offset, block // 2, 0, True)
            tile(offset + block // 2, block // 2, block // 2, True)
            for pair in range(per):
                column = (group * per + pair) * LANES
                grad_q = dq_ref[pair * LANES : (pair + 1) * LANES, :].T * (1.0 / math.sqrt(HD))
                dqkv_ref[rows, column : column + LANES] = turn_back(grad_q, rows).astype(BF16)
            return _

        lax.fori_loop(0, length // block, q_step, 0)

    def finish(index, _):
        rows = pl.ds(pl.multiple_of(index * block, block), block)
        lanes = lax.broadcasted_iota(jnp.int32, (block, LANES), 1)

        def placed(part, half):
            ref = dk_ref if part < kv else dv_ref
            even, odd = ref[part % kv, 0, rows, :], ref[part % kv, 1, rows, :]
            return even + pltpu.roll(odd, HD, 1) if half == 0 else pltpu.roll(even, HD, 1) + odd

        for chunk in range(kv):
            values = jnp.where(lanes < HD, placed(2 * chunk, 0), placed(2 * chunk + 1, 1))
            if 2 * chunk + 1 < kv:
                values = turn_back(values, rows)
            elif 2 * chunk < kv:
                values = jnp.where(lanes < HD, turn_back(values, rows), values)
            column = heads * HD + chunk * LANES
            dqkv_ref[rows, column : column + LANES] = values.astype(BF16)
        return _

    lax.fori_loop(0, length // block, finish, 0)


def attend_back(
    bound, order, queries, kx, vx, kt, log_sums, attended, grad, cosine, sine, block, others
):
    length, width = queries.shape
    heads = width // HD
    kv = kx.shape[0]
    cells = heads * length * (length + block) // 2
    vmem = pl.BlockSpec(memory_space=pltpu.VMEM)
    return pl.pallas_call(
        functools.partial(attend_back_kernel, block=block),
        in_specs=[pl.BlockSpec(memory_space=pltpu.SMEM)] + [vmem] * 9 + [ANYWHERE] * len(others),
        out_specs=vmem,
        out_shape=jax.ShapeDtypeStruct((length, width + 2 * kv * HD), BF16),
        scratch_shapes=[
            pltpu.VMEM((kv, 2, length, LANES), F32),
            pltpu.VMEM((kv, 2, length, LANES), F32),
            pltpu.VMEM((heads // kv * HD, block), F32),
        ],
        compiler_params=limit(52),
        cost_estimate=declared(2 * 10 * HD * 4 * cells),
    )(jnp.stack([bound, *order]), queries, kx, vx, kt, log_sums, attended, grad, cosine, sine, *others)


def local(
    inputs,
    segment_ids,
    attn_gain,
    query_weight,
    key_weight,
    value_weight,
    output_weight,
    mlp_gain,
    gate_weight,
    up_weight,
    down_weight,
    cotangent,
    *,
    sizes,
):
    rows = inputs.shape[0]
    length = segment_ids.shape[0]
    query_cols = query_weight.shape[1]
    key_cols = key_weight.shape[1]
    heads, kv = query_cols // HD, key_cols // HD
    columns = query_cols + 2 * key_cols
    slots = slots_of(sizes["tensor"])
    tensor = sizes["tensor"]
    space = (-columns) % query_cols or query_cols
    gains = jnp.pad(jnp.stack([attn_gain, mlp_gain], axis=1), ((0, 0), (0, space - 2)))
    bundle = lax.all_gather(
        jnp.concatenate([query_weight, key_weight, value_weight, gains, output_weight.T], axis=1),
        "dp", axis=0, tiled=True,
    )
    out_own = bundle[:, columns + space :]
    hop = first_hop(inputs, tensor)
    gate_up = lax.all_gather(
        hold(jnp.concatenate([gate_weight, up_weight], axis=1), *(hop or ())),
        "dp", axis=0, tiled=True,
    )

    bound, cosine, sine = rope_tables(segment_ids)
    blocks = second_hop(inputs, hop, tensor)
    arrays = project(slots, blocks, bundle, cosine, sine, heads, kv, length)
    block_a, queries, kx, vx, kt, vt, gains = arrays
    down_t = lax.all_gather(turn(down_weight, [queries]), "dp", axis=0, tiled=True)

    if tensor == 4:
        out_own = hold(out_own, blocks[3])
        out_hop = first_hop(out_own, tensor)
        odd, odd_sums = attend(bound, [jnp.int32(k) for k in (1, 3)], queries, kx, vt, rows)
        halves = hold_halves(out_hop, odd)
        out_all = second_hop(out_own, out_hop, tensor, halves)
        even, even_sums = attend(bound, [jnp.int32(k) for k in (0, 2)], queries, kx, vt, rows, halves)
        order = [slots[1], slots[2], slots[0], slots[3]]
        first, second, own, far = sort_blocks(order, even, odd)
        from_one = lax.ppermute(first, "tensor", pairs(tensor, 1))
        from_two = lax.ppermute(second, "tensor", pairs(tensor, 2))
        from_far = lax.ppermute(far, "tensor", pairs(tensor, 3))
        cotangent_sent = hold(cotangent, first, out_all[3])
        cotangent_hop = first_hop(cotangent_sent, tensor)
        stream_one, low_m = settle(
            own, 0, [from_one, from_two, from_far], out_all, inputs, gains, [cotangent_sent]
        )
        attended = jnp.concatenate([first, second, own, far], axis=0)
        log_sums = jnp.concatenate(
            [part[:, at : at + rows] for at in (0, rows) for part in (even_sums, odd_sums)], axis=1
        )
    else:
        order = slots
        out_all = gather(out_own, tensor)
        attended, log_sums = attend(bound, order, queries, kx, vt, rows)
        given = trade([attended[k * rows : (k + 1) * rows] for k in range(tensor)], tensor)
        stream_one, low_m = settle(given[0], 0, given[1:], out_all, inputs, gains)
        cotangent_sent = cotangent
    parts_m = [low_m]
    units = gate_weight.shape[1]

    def feed_at(place, wanted, fed, others=()):
        return feed(
            feed_kernel, place, tensor, [parts_m[k] for k in wanted], [gate_up] * 2, [0, 1], [],
            units, 3, True, 512, fed, others,
        )

    def back_m(places, fed, into=None, others=(), split=False):
        return back(places, rows, fed[:2], [gate_up] * 2, [0, 1], into, others, split)

    def back_out(places, into=None, others=(), split=False):
        return back(places, rows, [hidden], [down_t], [0], into, others, split)

    def reduce_rows(term, *others):
        if others and tensor == 4:
            term = hold(term, *others)
        return lax.psum_scatter(term, "dp", scatter_dimension=0, tiled=True)

    if tensor == 4:
        fed = feed_at(3, [0], None)
        sent = hold(parts_m[0], fed[0], *cotangent_hop)
        hop = first_hop(sent, tensor)
        parts_m = second_hop(sent, hop, tensor)
        fed = feed_at(0, [1, 2], fed, [sent])
        halves = hold_halves(cotangent_hop, fed[0])
        grad_parts = second_hop(cotangent_sent, cotangent_hop, tensor, halves)
        grad_parts = grad_parts[1:] + grad_parts[:1]
        fed = feed_at(2, [3], fed, halves)
    else:
        grad_parts = second_hop(cotangent_sent, None, tensor)
        parts_m = gather(parts_m[0], tensor)
        fed = None
        for place in range(tensor):
            fed = feed_at(place, [place], fed)
    hidden, silu, slope, block_m = fed

    def feed_back(others=()):
        return feed(
            feed_back_kernel, 0, tensor, grad_parts, [down_t], [0], [silu, slope], units, 2, False, 512,
            None, others,
        )

    if tensor == 4:
        three_out = back_out([2], None, [fed[0]], True)
        out_one, out_two = out_halves = send_half(three_out, tensor)
        down_t_wgrad = weigh(grad_parts, hidden, three_out[:1])
        one_out, two_out, own_out = back_out([0, 1, 3], [(out_one, False), (out_two, True), None])
        out_parts = [
            own_out,
            lax.ppermute(one_out, "tensor", pairs(tensor, 1)),
            lax.ppermute(two_out, "tensor", pairs(tensor, 2)),
        ]
        fed = feed_back([one_out])
        three_m = back_m([2], fed, None, (), True)
        m_one, m_two = m_halves = send_half(three_m, tensor)
        gate_wgrad = weigh([block_m], fed[0], [three_m[0], *out_parts[1:]])
        one_m, two_m = back_m([0, 1], fed, [(m_one, False), (m_two, True)])
        (own_m,) = back_m([3], fed, None, [one_m])
        up_wgrad = weigh([block_m], fed[1], [own_m])
        grad_m_parts = [
            own_m,
            lax.ppermute(one_m, "tensor", pairs(tensor, 1)),
            lax.ppermute(two_m, "tensor", pairs(tensor, 2)),
        ]
    else:
        down_t_wgrad = weigh(grad_parts, hidden)
        fed = feed_back()
        grad_m_parts = sum_whole(back_m(list(range(tensor)), fed))
        gate_wgrad, up_wgrad = weigh([block_m], fed[0]), weigh([block_m], fed[1])
        out_parts = sum_whole(back_out(list(range(tensor))))
    if tensor != 4:
        out_halves = m_halves = ()
    down_t_low = reduce_rows(down_t_wgrad, *out_halves)
    gate_low = reduce_rows(gate_wgrad, *m_halves)
    up_low = reduce_rows(up_wgrad, *grad_m_parts[1:])

    grad_stream_one, grad_stream_low, *pieces = settle_back(
        grad_m_parts, out_all, cotangent, stream_one, gains
    )
    given = trade(pieces, tensor)
    places = [1, 2, 0, 3] if tensor == 4 else list(range(tensor))
    grad_attended = jnp.concatenate([given[k] for k in places], axis=0)
    grad_qkv = attend_back(
        bound, order, queries, kx, vx, kt, log_sums, attended, grad_attended, cosine, sine, rows,
        [down_t_low],
    )
    if tensor == 4:
        sent = hold(grad_stream_low, grad_attended)
        grad_stream_parts = trade([sent] * 4, tensor)
    else:
        grad_stream_parts = gather(grad_stream_low, tensor)
    grad_stream_parts = [grad_stream_parts[k] for k in places]

    def back_a(places, others=(), split=False):
        return back(places, rows, [grad_qkv], [bundle], [0], None, others, split)

    if tensor == 4:
        three = back_a(slots[3:], [gate_low], True)
        halves = send_half(three, tensor)
        one, two = back_a([slots[1], slots[2]], three[:1])
        block_a = hold(block_a, one)
    attention_wgrad = weigh_both(block_a, grad_qkv, grad_stream_parts, attended)
    gate_sum, up_sum, down_t_sum = [low.astype(F32) for low in (gate_low, up_low, down_t_low)]
    if tensor == 4:
        attention_wgrad = hold(attention_wgrad, *halves)
    attention_sum = reduce_rows(attention_wgrad).astype(F32)
    if tensor == 4:
        one, two = add_half(one, halves[0], 1), add_half(two, halves[1], 0)
        sent = [
            lax.ppermute(one, "tensor", pairs(tensor, 1)),
            lax.ppermute(two, "tensor", pairs(tensor, 2)),
        ]
        grad_a_parts = [*back_a([slots[0]], [one, two]), *sent]
        layer_out = finish(out_parts, stream_one, grad_a_parts[:1])
    else:
        grad_a_parts = sum_whole(back_a(slots))
        layer_out = finish(out_parts, stream_one)

    product = attention_wgrad[:, :columns].astype(F32) * bundle[:, :columns].astype(F32)
    attn_term = sum_tensor(jnp.sum(product, axis=1)[None, :], tensor)
    width = attn_gain.shape[0]
    attn_term = lax.dynamic_slice_in_dim(
        sum_blocks(attn_term, sizes["dp"]), lax.axis_index("dp") * width, width, 1
    )

    def gain_term(gain, weights):
        term = sum(jnp.sum(weight.astype(F32) * grad, axis=1) for weight, grad in weights)
        return term / gain.astype(F32)

    query_sum = attention_sum[:, :query_cols]
    key_sum = attention_sum[:, query_cols : query_cols + key_cols]
    value_sum = attention_sum[:, query_cols + key_cols : columns]
    mlp_term = sum_tensor(
        gain_term(mlp_gain, [(gate_weight, gate_sum), (up_weight, up_sum)])[None, :], tensor
    )
    input_grad = settle_last(grad_a_parts, grad_stream_one, inputs, gains)
    return (
        layer_out,
        input_grad,
        attn_term[0] / attn_gain.astype(F32),
        query_sum,
        key_sum,
        value_sum,
        attention_sum[:, columns:].T,
        mlp_term[0],
        gate_sum,
        up_sum,
        down_t_sum.T,
    )


def solution(mesh):
    tokens = P(("dp", "tensor"), None)
    in_specs = (
        tokens,
        P("dp"),
        P("dp"),
        P("dp", "tensor"),
        P("dp", "tensor"),
        P("dp", "tensor"),
        P("tensor", "dp"),
        P("dp"),
        P("dp", "tensor"),
        P("dp", "tensor"),
        P("tensor", "dp"),
        tokens,
    )
    out_specs = (
        tokens,
        tokens,
        P("dp"),
        P("dp", "tensor"),
        P("dp", "tensor"),
        P("dp", "tensor"),
        P("tensor", "dp"),
        P("dp"),
        P("dp", "tensor"),
        P("dp", "tensor"),
        P("tensor", "dp"),
    )
    return jax.shard_map(
        functools.partial(local, sizes={axis: mesh.shape[axis] for axis in ("tensor", "dp")}),
        mesh=mesh, in_specs=in_specs, out_specs=out_specs, check_vma=False,
    )
```

```python
import functools
import math

import jax
import jax.numpy as jnp
from jax import lax
from jax.experimental import pallas as pl
from jax.experimental.pallas import tpu as pltpu
from jax.sharding import PartitionSpec as P

HD = 64
LANES = 128
EPSILON = 1e-05
ROPE_BASE = 500000.0
MASKED = -1e30
OVER_ROWS = (((0,), (0,)), ((), ()))
OVER_COLS = (((1,), (1,)), ((), ()))


def limit(size):
    return pltpu.CompilerParams(vmem_limit_bytes=size * 2**20)


SHORT = 0.0625


def declared(flops, scale=SHORT):
    return pl.CostEstimate(flops=int(flops * scale), bytes_accessed=0, transcendentals=0)


F32 = jnp.float32
BF16 = jnp.bfloat16


def dot_cols(left, right):
    return lax.dot_general(left, right, OVER_COLS, preferred_element_type=F32)


def dot_rows(left, right):
    return lax.dot_general(left, right, OVER_ROWS, preferred_element_type=F32)


def dot(left, right):
    return jnp.dot(left, right, preferred_element_type=F32)


def pairs(size, bit):
    return [(index, index ^ bit) for index in range(size)]


def slots_of(size):
    if size == 4:
        return [lax.axis_index("tensor") ^ step for step in range(size)]
    return [jnp.int32(step) for step in range(size)]


ANYWHERE = pl.BlockSpec(memory_space=pl.ANY)


def nothing_kernel(*refs):
    pass


def hold(value, *others):
    return pl.pallas_call(
        nothing_kernel,
        in_specs=[ANYWHERE] * (1 + len(others)),
        out_specs=ANYWHERE,
        out_shape=jax.ShapeDtypeStruct(value.shape, value.dtype),
        input_output_aliases={0: 0},
        cost_estimate=declared(0),
    )(value, *others)


def first_hop(shard, size):
    if size != 4:
        return None
    return [lax.ppermute(shard, "tensor", pairs(size, bit)) for bit in (1, 2)]


def copy_kernel(value_ref, *rest):
    rest[-1][...] = value_ref[...]


def half_of(value, which, *others):
    rows, width = value.shape
    tile = rows // 4
    return pl.pallas_call(
        copy_kernel,
        grid=(2,),
        in_specs=[pl.BlockSpec((tile, width), lambda i: (2 * which + i, 0))]
        + [ANYWHERE] * len(others),
        out_specs=pl.BlockSpec((tile, width), lambda i: (i, 0)),
        out_shape=jax.ShapeDtypeStruct((rows // 2, width), value.dtype),
        compiler_params=limit(52),
        cost_estimate=declared(0),
    )(value, *others)


def add_kernel(value_ref, extra_ref, out_ref, *, which):
    out_ref[...] = value_ref[...]

    @pl.when(pl.program_id(0) == which)
    def _():
        out_ref[...] = (value_ref[...].astype(F32) + extra_ref[...].astype(F32)).astype(BF16)


def add_half(value, extra, which):
    rows, width = value.shape
    half = pl.BlockSpec((rows // 2, width), lambda i: (i, 0))
    return pl.pallas_call(
        functools.partial(add_kernel, which=which),
        grid=(2,),
        in_specs=[half, pl.BlockSpec((rows // 2, width), lambda i: (0, 0))],
        out_specs=half,
        out_shape=jax.ShapeDtypeStruct((rows, width), value.dtype),
        compiler_params=limit(52),
        cost_estimate=declared(0),
    )(value, extra)


def hold_halves(hop, *others):
    return half_of(hop[0], 0, *others), half_of(hop[1], 1, *others)


def second_hop(shard, hop, size, halves=None):
    if size != 4:
        whole = lax.all_gather(shard, "tensor", axis=0)
        return [whole[step] for step in range(size)]
    one, two = hop
    upper, lower = halves or hold_halves(hop)
    three_a = lax.ppermute(upper, "tensor", pairs(size, 2))
    three_b = lax.ppermute(lower, "tensor", pairs(size, 1))
    return [shard, one, two, jnp.concatenate([three_a, three_b], axis=0)]


def gather(shard, size):
    return second_hop(shard, first_hop(shard, size), size)


def send_half(three, size):
    into_two = lax.ppermute(three[0], "tensor", pairs(size, 1))
    into_one = lax.ppermute(three[1], "tensor", pairs(size, 2))
    return into_one, into_two


def sum_whole(terms):
    return [
        lax.psum_scatter(
            jnp.concatenate(terms, axis=0), "tensor", scatter_dimension=0, tiled=True
        )
    ]


def trade(pieces, size):
    if size != 4:
        whole = lax.all_to_all(jnp.stack(pieces), "tensor", split_axis=0, concat_axis=0, tiled=True)
        return [whole[step] for step in range(size)]
    return [pieces[0]] + [
        lax.ppermute(pieces[step], "tensor", pairs(size, step)) for step in (1, 2, 3)
    ]


def total(parts):
    return functools.reduce(jnp.add, [part.astype(F32) for part in parts])


def sum_tensor(value, size):
    if size & (size - 1):
        return lax.psum(value, "tensor")
    return value + sum(lax.ppermute(value, "tensor", pairs(size, bit)) for bit in range(1, size))


def sum_blocks(value, size):
    if size & (size - 1):
        return lax.psum(value, "dp")
    bit = 1
    while bit < size:
        value = value + lax.ppermute(value, "dp", pairs(size, bit))
        bit *= 2
    return value


def rope_tables(segment):
    length = segment.shape[0]
    bound = jnp.sum((segment == 0).astype(jnp.int32))
    place = lax.broadcasted_iota(jnp.int32, (length, LANES), 0)
    place = place - jnp.where(place >= bound, bound, 0)
    lane = lax.broadcasted_iota(jnp.int32, (length, LANES), 1)
    freqs = jnp.exp(
        (lane % (HD // 2)).astype(F32) * (-2.0 * math.log(ROPE_BASE) / HD)
    )
    angles = place.astype(F32) * freqs
    sine = jnp.sin(angles)
    return bound, jnp.cos(angles), jnp.where(lane % HD < HD // 2, -sine, sine)


def swap_halves(values):
    lane = lax.broadcasted_iota(jnp.int32, values.shape, 1)
    after = pltpu.roll(values, LANES - HD // 2, 1)
    before = pltpu.roll(values, HD // 2, 1)
    return jnp.where(lane % HD < HD // 2, after, before)


def normalize(stream):
    scale_r = lax.rsqrt(jnp.mean(stream * stream, axis=-1, keepdims=True) + EPSILON)
    return (stream * scale_r, scale_r)


def project_kernel(slot_ref, *refs, count, steps, heads, kv):
    gains_ref, w_ref, cos_ref, sin_ref = refs[count : count + 4]
    h_ref, q_ref, kx_ref, vx_ref, kt_ref, vt_ref, gain_ref = refs[-7:]

    @pl.when(pl.program_id(0) == 0)
    def _():
        gain_ref[...] = gains_ref[...].astype(F32).T[:8]

    which = pl.program_id(0) // steps
    rows = h_ref.shape[0]
    part_rows = min(256, rows)
    lane = lax.broadcasted_iota(jnp.int32, (part_rows, LANES), 1)
    for start in range(0, rows, part_rows):
        at = slice(start, start + part_rows)
        tokens = refs[0][at, :]
        for block in range(1, count):
            tokens = jnp.where(which == block, refs[block][at, :], tokens)
        normed, _ = normalize(tokens.astype(F32))
        low = (normed * gain_ref[0:1, :]).astype(BF16)
        h_ref[at, :] = low
        pre = dot(low, w_ref[...])
        cosine, sine = cos_ref[at, :], sin_ref[at, :]
        chunks = []
        for chunk in range(pre.shape[1] // LANES):
            columns = slice(chunk * LANES, (chunk + 1) * LANES)
            part = pre[:, columns]
            first = 2 * chunk
            if first < heads + kv:
                turned = part * cosine + swap_halves(part) * sine
                part = turned if first + 1 < heads + kv else jnp.where(lane < HD, turned, part)
            chunks.append(part)
            if first < heads:
                q_ref[at, columns] = (part * (1.0 / math.sqrt(HD))).astype(BF16)
        flipped = {}
        for head in range(2 * kv):
            place = heads + head
            part = chunks[place // 2]
            moved = pltpu.roll(part, HD, 1)
            wide = [part, moved] if place % 2 == 0 else [moved, part]
            out = kx_ref if head < kv else vx_ref
            out[head % kv, 0, at, :] = jnp.where(lane < HD, wide[0], 0.0).astype(BF16)
            out[head % kv, 1, at, :] = jnp.where(lane < HD, 0.0, wide[1]).astype(BF16)
            if place // 2 not in flipped:
                flipped[place // 2] = part.T
            turn = flipped[place // 2][(place % 2) * HD : (place % 2 + 1) * HD]
            out_t = kt_ref if head < kv else vt_ref
            out_t[(head % kv) * HD : (head % kv + 1) * HD, at] = turn.astype(BF16)


def project(slots, blocks, bundle, cosine, sine, heads, kv, length):
    rows, width = blocks[0].shape
    count = len(blocks)
    tile = rows
    steps = rows // tile
    columns = (heads + 2 * kv) * HD

    def at(i, slot):
        return slot[i // steps] * steps + i % steps

    shapes = [
        jax.ShapeDtypeStruct((length, width), BF16),
        jax.ShapeDtypeStruct((length, heads * HD), BF16),
        jax.ShapeDtypeStruct((kv, 2, length, LANES), BF16),
        jax.ShapeDtypeStruct((kv, 2, length, LANES), BF16),
        jax.ShapeDtypeStruct((kv * HD, length), BF16),
        jax.ShapeDtypeStruct((kv * HD, length), BF16),
        jax.ShapeDtypeStruct((8, width), F32),
    ]
    out_specs = [
        pl.BlockSpec((tile, width), lambda i, s: (at(i, s), 0)),
        pl.BlockSpec((tile, heads * HD), lambda i, s: (at(i, s), 0)),
        pl.BlockSpec((kv, 2, tile, LANES), lambda i, s: (0, 0, at(i, s), 0)),
        pl.BlockSpec((kv, 2, tile, LANES), lambda i, s: (0, 0, at(i, s), 0)),
        pl.BlockSpec((kv * HD, tile), lambda i, s: (0, at(i, s))),
        pl.BlockSpec((kv * HD, tile), lambda i, s: (0, at(i, s))),
        pl.BlockSpec((8, width), lambda i, s: (0, 0)),
    ]
    in_specs = [
        pl.BlockSpec((tile, width), lambda i, s, b=block: (jnp.clip(i - b * steps, 0, steps - 1), 0))
        for block in range(count)
    ]
    in_specs += [
        pl.BlockSpec((width, LANES), lambda i, s: (0, columns // LANES)),
        pl.BlockSpec((width, columns), lambda i, s: (0, 0)),
        pl.BlockSpec((tile, LANES), lambda i, s: (at(i, s), 0)),
        pl.BlockSpec((tile, LANES), lambda i, s: (at(i, s), 0)),
    ]
    operands = [jnp.stack(slots), *blocks, bundle, bundle, cosine, sine]
    return pl.pallas_call(
        functools.partial(
            project_kernel, count=count, steps=steps, heads=heads, kv=kv
        ),
        grid_spec=pltpu.PrefetchScalarGridSpec(
            num_scalar_prefetch=1,
            grid=(count * steps,),
            in_specs=in_specs,
            out_specs=out_specs,
        ),
        out_shape=shapes,
        compiler_params=limit(52),
        cost_estimate=declared(2 * count * rows * width * columns),
    )(*operands)


def feed_kernel(*refs, count):
    tokens = refs[:count]
    gate_ref, up_ref = refs[count : count + 2]
    hidden_ref, silu_ref, slope_ref, h_out = refs[-4:]
    rows = tokens[0].shape[0]
    wide = h_out.shape[1]
    tile = min(256, gate_ref.shape[1])
    lanes = pl.ds(pl.multiple_of(pl.program_id(0) * wide, wide), wide)
    for block in range(count):
        h_out[block * rows : (block + 1) * rows, :] = tokens[block][:, lanes]
    for part in range(gate_ref.shape[1] // tile):
        columns = slice(part * tile, (part + 1) * tile)
        for block in range(count):
            where = slice(block * rows, (block + 1) * rows)
            gate = dot(tokens[block][...], gate_ref[:, columns])
            up = dot(tokens[block][...], up_ref[:, columns])
            sigmoid = 0.5 * jnp.tanh(0.5 * gate) + 0.5
            silu = gate * sigmoid
            hidden_ref[where, columns] = (silu * up).astype(BF16)
            silu_ref[where, columns] = silu.astype(BF16)
            slope_ref[where, columns] = (up * (sigmoid + silu * (1.0 - sigmoid))).astype(BF16)


def feed_back_kernel(*refs, count):
    grads = refs[:count]
    down_ref, silu_ref, slope_ref = refs[count : count + 3]
    dgate_ref, dup_ref = refs[-2:]
    rows = grads[0].shape[0]
    for block in range(count):
        where = slice(block * rows, (block + 1) * rows)
        dhidden = dot(grads[block][...], down_ref[...])
        dup_ref[where, :] = (dhidden * silu_ref[where, :].astype(F32)).astype(BF16)
        dgate_ref[where, :] = (dhidden * slope_ref[where, :].astype(F32)).astype(BF16)


def feed(kernel, place, blocks, tokens, weights, places, kept, units, outs, copy, tile, prev, others):
    rows, width = tokens[0].shape
    count = len(tokens)
    steps = max(units // tile, 1)
    tile, wide = units // steps, width // steps
    shapes = [jax.ShapeDtypeStruct((blocks * rows, units), BF16)] * outs
    in_specs = [pl.BlockSpec((rows, width), lambda i: (0, 0), pipeline_mode=pl.Buffered(1))] * count
    in_specs += [
        pl.BlockSpec((width, tile), lambda i, w=which: (0, w * steps + i)) for which in places
    ]
    cell = pl.BlockSpec((count * rows, tile), lambda i: (place, i))
    in_specs += [cell] * len(kept)
    out_specs = [cell] * outs
    if copy:
        shapes.append(jax.ShapeDtypeStruct((blocks * rows, width), BF16))
        out_specs.append(pl.BlockSpec((count * rows, wide), lambda i: (place, i)))
    operands = [*tokens, *weights, *kept]
    aliases = {}
    if prev is not None:
        for index, array in enumerate(prev):
            aliases[len(operands)] = index
            operands.append(array)
            in_specs.append(ANYWHERE)
    operands += others
    in_specs += [ANYWHERE] * len(others)
    return pl.pallas_call(
        functools.partial(kernel, count=count),
        grid=(steps,),
        in_specs=in_specs,
        out_specs=out_specs,
        out_shape=shapes,
        input_output_aliases=aliases,
        compiler_params=limit(52),
        cost_estimate=declared(2 * len(weights) * count * rows * width * units),
    )(*operands)


def back_kernel(slot_ref, *refs, count, terms, added, split):
    outs = refs[-2:] if split else refs[-count:]
    weights = refs[count * terms : (count + 1) * terms]
    into = list(refs[(count + 1) * terms :])
    for block in range(count):
        value = dot_cols(refs[block * terms][...], weights[0][...])
        for term in range(1, terms):
            value = value + dot_cols(refs[block * terms + term][...], weights[term][...])
        half = value.shape[0] // 2
        if split:
            outs[0][...] = value[:half].astype(BF16)
            outs[1][...] = value[half:].astype(BF16)
            continue
        if added[block] is None:
            outs[block][...] = value.astype(BF16)
            continue
        extra = into.pop(0)[...].astype(F32)
        top, bottom = value[:half], value[half:]
        if added[block]:
            top = top + extra
        else:
            bottom = bottom + extra
        outs[block][:half, :] = top.astype(BF16)
        outs[block][half:, :] = bottom.astype(BF16)


def back(slots, rows, lefts, weights, places, into=None, others=(), split=False):
    depth = lefts[0].shape[1]
    width = weights[0].shape[0]
    tile = min(512, width)
    terms, count = len(lefts), len(slots)
    outs, tall = (2, rows // 2) if split else (count, rows)
    into = into or [None] * count
    in_specs, operands = [], [jnp.stack([jnp.asarray(slot, jnp.int32) for slot in slots])]
    for block in range(count):
        in_specs += [pl.BlockSpec((rows, depth), lambda i, s, b=block: (s[b], 0))] * terms
        operands += lefts
    in_specs += [pl.BlockSpec((tile, depth), lambda i, s, p=place: (i, p)) for place in places]
    operands += weights
    for extra in into:
        if extra is not None:
            in_specs.append(pl.BlockSpec((rows // 2, tile), lambda i, s: (0, i)))
            operands.append(extra[0])
    operands += others
    in_specs += [ANYWHERE] * len(others)
    return pl.pallas_call(
        functools.partial(
            back_kernel,
            count=count,
            terms=terms,
            added=[None if extra is None else extra[1] for extra in into],
            split=split,
        ),
        grid_spec=pltpu.PrefetchScalarGridSpec(
            num_scalar_prefetch=1,
            grid=(width // tile,),
            in_specs=in_specs,
            out_specs=[pl.BlockSpec((tall, tile), lambda i, s: (0, i))] * outs,
        ),
        out_shape=[jax.ShapeDtypeStruct((tall, width), BF16)] * outs,
        compiler_params=limit(52),
        cost_estimate=declared(2 * count * terms * rows * width * depth),
    )(*operands)


def turn_kernel(value_ref, *rest):
    rest[-1][...] = value_ref[...].T


def turn(value, others=()):
    rows, columns = value.shape
    tile = min(512, rows)
    return pl.pallas_call(
        turn_kernel,
        grid=(rows // tile,),
        in_specs=[pl.BlockSpec((tile, columns), lambda i: (i, 0))] + [ANYWHERE] * len(others),
        out_specs=pl.BlockSpec((columns, tile), lambda i: (0, i)),
        out_shape=jax.ShapeDtypeStruct((columns, rows), value.dtype),
        compiler_params=limit(52),
        cost_estimate=declared(0),
    )(value, *others)


def turn_blocks(lefts, turned_ref):
    rows = lefts[0].shape[0]
    for block, left in enumerate(lefts):
        turned_ref[:, block * rows : (block + 1) * rows] = left[...].T


def weigh_kernel(*refs, count):
    lefts, right_ref = refs[:count], refs[count]
    out_ref, *turned = refs[-3:]
    i, j = pl.program_id(0), pl.program_id(1)
    last = j == pl.num_programs(1) - 1

    @pl.when((i == 0) & (j == 0))
    def _():
        turn_blocks(lefts, turned[0])

    for parity in range(2):

        @pl.when((i % 2 == parity) & jnp.logical_not(last))
        def _():
            out_ref[...] = dot(turned[parity][...], right_ref[...]).astype(BF16)

        @pl.when((i % 2 == parity) & last)
        def _():
            out_ref[...] = dot(turned[parity][...], right_ref[...]).astype(BF16)
            turn_blocks(lefts, turned[1 - parity])


def weigh(lefts, right, others=()):
    tokens, columns = right.shape
    rows, width = lefts[0].shape
    tall, wide = min(512, width), min(1024, columns // 2)
    tiles, steps = width // tall, columns // wide

    def ahead(i, j):
        return 0, jnp.minimum(i + jnp.where(j == steps - 1, 1, 0), tiles - 1)

    return pl.pallas_call(
        functools.partial(weigh_kernel, count=len(lefts)),
        grid=(tiles, steps),
        in_specs=[pl.BlockSpec((rows, tall), ahead)] * len(lefts)
        + [pl.BlockSpec((tokens, wide), lambda i, j: (0, j))]
        + [ANYWHERE] * len(others),
        out_specs=pl.BlockSpec((tall, wide), lambda i, j: (i, j)),
        out_shape=jax.ShapeDtypeStruct((width, columns), BF16),
        scratch_shapes=[pltpu.VMEM((tall, tokens), BF16)] * 2,
        compiler_params=limit(52),
        cost_estimate=declared(2 * tokens * width * columns),
    )(*lefts, right, *others)


def weigh_both_kernel(*refs, count):
    one_ref, others = refs[0], refs[1 : 1 + count]
    right_ref, other_ref, out_ref, turned_ref, other_turned_ref = refs[1 + count :]
    columns = right_ref.shape[1]
    turn_blocks([one_ref], turned_ref)
    out_ref[:, :columns] = dot(turned_ref[...], right_ref[...]).astype(BF16)
    turn_blocks(others, other_turned_ref)
    out_ref[:, columns:] = dot(other_turned_ref[...], other_ref[...]).astype(BF16)


def weigh_both(one, right, others, other_right):
    tokens, width = one.shape
    rows = others[0].shape[0]
    columns, more = right.shape[1], other_right.shape[1]
    tall = min(512, width)
    whole = [pl.BlockSpec((tokens, columns), lambda i: (0, 0))]
    whole += [pl.BlockSpec((tokens, more), lambda i: (0, 0))]
    return pl.pallas_call(
        functools.partial(weigh_both_kernel, count=len(others)),
        grid=(width // tall,),
        in_specs=[pl.BlockSpec((tokens, tall), lambda i: (0, i))]
        + [pl.BlockSpec((rows, tall), lambda i: (0, i))] * len(others)
        + whole,
        out_specs=pl.BlockSpec((tall, columns + more), lambda i: (i, 0)),
        out_shape=jax.ShapeDtypeStruct((width, columns + more), BF16),
        scratch_shapes=[pltpu.VMEM((tall, tokens), BF16)] * 2,
        compiler_params=limit(52),
        cost_estimate=declared(2 * tokens * width * (columns + more)),
    )(one, *others, right, other_right)


def settle_kernel(*refs, count):
    pieces, weights = refs[:count], refs[count : 2 * count]
    x_ref, gains_ref = refs[2 * count : 2 * count + 2]
    stream_ref, h_ref = refs[-2:]
    stream = x_ref[...].astype(F32)
    for piece, weight in zip(pieces, weights):
        stream = stream + dot_cols(piece[...], weight[...])
    stream_ref[...] = stream
    normed, _ = normalize(stream)
    h_ref[...] = (normed * gains_ref[1:2, :]).astype(BF16)


def settle(own, place, pieces, weights, tokens, gains, others=()):
    rows, width = tokens.shape
    depth = weights[0].shape[1]
    tile = min(256, rows)
    steps = rows // tile
    wide = pl.BlockSpec((tile, width), lambda i: (i, 0))
    piece = pl.BlockSpec((tile, depth), lambda i: (i, 0))
    weight = pl.BlockSpec((width, depth), lambda i: (0, 0), pipeline_mode=pl.Buffered(1))
    return pl.pallas_call(
        functools.partial(settle_kernel, count=len(weights)),
        grid=(steps,),
        in_specs=[pl.BlockSpec((tile, depth), lambda i: (place * steps + i, 0))]
        + [piece] * len(pieces)
        + [weight] * len(weights)
        + [wide, pl.BlockSpec((8, width), lambda i: (0, 0))]
        + [ANYWHERE] * len(others),
        out_specs=[wide, wide],
        out_shape=[
            jax.ShapeDtypeStruct((rows, width), F32),
            jax.ShapeDtypeStruct((rows, width), BF16),
        ],
        compiler_params=limit(52),
        cost_estimate=declared(2 * len(weights) * rows * width * depth),
    )(own, *pieces, *weights, tokens, gains, *others)


def norm_back(grad_in, stream, gain):
    normed, scale_r = normalize(stream)
    scaled = grad_in * gain
    return scale_r * (scaled - normed * jnp.mean(scaled * normed, axis=-1, keepdims=True))


def settle_back_kernel(*refs, parts, count):
    terms, weights = refs[:parts], refs[parts : parts + count]
    grad_ref, stream_ref, gains_ref, out_ref, low_ref = refs[parts + count : parts + count + 5]
    pieces = refs[parts + count + 5 :]
    grad_in = terms[0][...].astype(F32)
    for term in terms[1:]:
        grad_in = grad_in + term[...].astype(F32)
    grad = grad_ref[...].astype(F32) + norm_back(grad_in, stream_ref[...], gains_ref[1:2, :])
    out_ref[...] = grad
    low = grad.astype(BF16)
    low_ref[...] = low
    for piece, weight in zip(pieces, weights):
        piece[...] = dot(low, weight[...]).astype(BF16)


def settle_back(terms, weights, grad, stream, gains):
    rows, width = grad.shape
    depth = weights[0].shape[1]
    tile = min(256, rows)
    wide = pl.BlockSpec((tile, width), lambda i: (i, 0))
    weight = pl.BlockSpec((width, depth), lambda i: (0, 0), pipeline_mode=pl.Buffered(1))
    return pl.pallas_call(
        functools.partial(settle_back_kernel, parts=len(terms), count=len(weights)),
        grid=(rows // tile,),
        in_specs=[wide] * len(terms)
        + [weight] * len(weights)
        + [wide, wide, pl.BlockSpec((8, width), lambda i: (0, 0))],
        out_specs=[wide, wide] + [pl.BlockSpec((tile, depth), lambda i: (i, 0))] * len(weights),
        out_shape=[
            jax.ShapeDtypeStruct((rows, width), F32),
            jax.ShapeDtypeStruct((rows, width), BF16),
        ]
        + [jax.ShapeDtypeStruct((rows, depth), BF16)] * len(weights),
        compiler_params=limit(52),
        cost_estimate=declared(2 * len(weights) * rows * width * depth),
    )(*terms, *weights, grad, stream, gains)


def settle_last_kernel(*refs):
    grad_ref, x_ref, gains_ref, out_ref = refs[-4:]
    grad_in = refs[0][...].astype(F32)
    for term in refs[1:-4]:
        grad_in = grad_in + term[...].astype(F32)
    back_a = norm_back(grad_in, x_ref[...].astype(F32), gains_ref[0:1, :])
    out_ref[...] = (grad_ref[...] + back_a).astype(BF16)


def settle_last(terms, grad, tokens, gains):
    rows, width = tokens.shape
    tile = min(128, rows)
    wide = pl.BlockSpec((tile, width), lambda i: (i, 0))
    return pl.pallas_call(
        settle_last_kernel,
        grid=(rows // tile,),
        in_specs=[wide] * (len(terms) + 2) + [pl.BlockSpec((8, width), lambda i: (0, 0))],
        out_specs=wide,
        out_shape=jax.ShapeDtypeStruct((rows, width), BF16),
        compiler_params=limit(52),
        cost_estimate=declared(rows * width),
    )(*terms, grad, tokens, gains)


def finish_kernel(*refs, count):
    value = refs[count][...]
    for term in refs[:count]:
        value = value + term[...].astype(F32)
    refs[-1][...] = value.astype(BF16)


def finish(terms, stream, others=()):
    rows, width = stream.shape
    wide = pl.BlockSpec((rows // 4, width), lambda i: (i, 0))
    return pl.pallas_call(
        functools.partial(finish_kernel, count=len(terms)),
        grid=(4,),
        in_specs=[wide] * (len(terms) + 1) + [ANYWHERE] * len(others),
        out_specs=wide,
        out_shape=jax.ShapeDtypeStruct((rows, width), BF16),
        compiler_params=limit(52),
        cost_estimate=declared(rows * width),
    )(*terms, stream, *others)


def causal(keys, queries):
    key = lax.broadcasted_iota(jnp.int32, (keys, queries), 0)
    return key <= lax.broadcasted_iota(jnp.int32, (keys, queries), 1)


def first_block(bound, offset, block):
    return jnp.where(offset >= bound, lax.div(bound, jnp.int32(block)), 0)


def attend_kernel(order_ref, q_ref, kx_ref, vt_ref, *rest, block):
    out_ref, lse_ref, top_ref, acc_ref = rest[-4:]
    kv = kx_ref.shape[0]
    per = q_ref.shape[1] // LANES // kv
    bound = order_ref[0]
    ones = jnp.ones((16, block), BF16)
    for group in range(kv):

        def q_step(turn, _):
            index = order_ref[1 + turn]
            offset = pl.multiple_of(index * block, block)
            into = pl.ds(pl.multiple_of(turn * block, block), block)
            top_ref[...] = jnp.full(top_ref.shape, MASKED, F32)
            acc_ref[...] = jnp.zeros(acc_ref.shape, F32)

            def tile(step, diagonal):
                keys = pl.ds(pl.multiple_of(step, block), block)
                value_t = jnp.concatenate(
                    [vt_ref[group * HD : (group + 1) * HD, keys], ones], axis=0
                )
                for head in range(2 * per):
                    column = (group * per + head // 2) * LANES
                    query = q_ref[pl.ds(offset, block), column : column + LANES]
                    scores = dot_cols(kx_ref[group, head % 2, keys, :], query)
                    if diagonal:
                        scores = jnp.where(causal(block, block), scores, MASKED)
                    old = top_ref[head, 0:1, :]
                    top = jnp.maximum(old, jnp.max(scores, axis=0, keepdims=True))
                    powered = jnp.exp(scores - top).astype(BF16)
                    acc_ref[head] = acc_ref[head] * jnp.exp(old - top) + dot(value_t, powered)
                    top_ref[head, 0:1, :] = top

            def full_tile(step, carry):
                tile(step * block, False)
                return carry

            lax.fori_loop(first_block(bound, offset, block), index, full_tile, 0)
            tile(offset, True)
            for pair in range(per):
                both = []
                for head in (2 * pair, 2 * pair + 1):
                    total = acc_ref[head, HD : HD + 1, :]
                    both.append(acc_ref[head, :HD, :] / total)
                    place = group * 2 * per + head
                    lse_ref[place : place + 1, into] = top_ref[
                        head, 0:1, :
                    ] + jnp.log(total)
                column = (group * per + pair) * LANES
                out_ref[into, column : column + LANES] = (
                    jnp.concatenate(both, axis=0).T.astype(BF16)
                )
            return _

        lax.fori_loop(0, out_ref.shape[0] // block, q_step, 0)


def attend(bound, order, queries, kx, vt, block, others=()):
    length, width = queries.shape
    heads = width // HD
    kv = kx.shape[0]
    per = heads // kv
    count = len(order)
    cells = heads * count * block * (length + block) // 2
    vmem = pl.BlockSpec(memory_space=pltpu.VMEM)
    return pl.pallas_call(
        functools.partial(attend_kernel, block=block),
        in_specs=[pl.BlockSpec(memory_space=pltpu.SMEM), vmem, vmem, vmem] + [ANYWHERE] * len(others),
        out_specs=[vmem, vmem],
        out_shape=[
            jax.ShapeDtypeStruct((count * block, width), BF16),
            jax.ShapeDtypeStruct((heads, count * block), F32),
        ],
        scratch_shapes=[
            pltpu.VMEM((per, 8, block), F32),
            pltpu.VMEM((per, HD + 16, block), F32),
        ],
        compiler_params=limit(52),
        cost_estimate=declared(2 * 4 * HD * 4 * cells, 16),
    )(jnp.stack([bound, *order]), queries, kx, vt, *others)


def sort_kernel(order_ref, *refs):
    parts, out_refs = refs[:2], refs[2:]
    block = out_refs[0].shape[0]
    for turn, out_ref in enumerate(out_refs):
        index = order_ref[turn]
        rows = pl.ds(pl.multiple_of(lax.div(index, 2) * block, block), block)
        out_ref[...] = jnp.where(lax.rem(index, 2) == 0, parts[0][rows, :], parts[1][rows, :])


def sort_blocks(order, even, odd):
    rows, width = even.shape[0] // 2, even.shape[1]
    vmem = pl.BlockSpec(memory_space=pltpu.VMEM)
    return pl.pallas_call(
        sort_kernel,
        in_specs=[pl.BlockSpec(memory_space=pltpu.SMEM), vmem, vmem],
        out_specs=[vmem] * len(order),
        out_shape=[jax.ShapeDtypeStruct((rows, width), even.dtype)] * len(order),
        compiler_params=limit(20),
        cost_estimate=declared(0),
    )(jnp.stack(order), even, odd)


def attend_back_kernel(
    order_ref, q_ref, kx_ref, vx_ref, kt_ref, lse_ref, out_ref, grad_ref, cos_ref, sin_ref,
    *rest, block
):
    dqkv_ref, dk_ref, dv_ref, dq_ref = rest[-4:]
    length = q_ref.shape[0]
    kv = kx_ref.shape[0]
    heads = q_ref.shape[1] // HD
    per = heads // 2 // kv
    bound = order_ref[0]
    dk_ref[...] = jnp.zeros(dk_ref.shape, F32)
    dv_ref[...] = jnp.zeros(dv_ref.shape, F32)
    lane = lax.broadcasted_iota(jnp.int32, (8, LANES), 1)
    row = lax.broadcasted_iota(jnp.int32, (8, LANES), 0)
    chosen = ((lane // HD) == row).astype(F32)

    def turn_back(values, rows):
        return values * cos_ref[rows, :] - swap_halves(values) * sin_ref[rows, :]

    for group in range(kv):

        def q_step(turn, _):
            index = order_ref[1 + turn]
            offset = pl.multiple_of(index * block, block)
            rows = pl.ds(offset, block)
            given = pl.ds(pl.multiple_of(turn * block, block), block)
            dq_ref[...] = jnp.zeros(dq_ref.shape, F32)
            deltas = []
            for pair in range(per):
                column = (group * per + pair) * LANES
                product = grad_ref[given, column : column + LANES].astype(F32) * out_ref[
                    given, column : column + LANES
                ].astype(F32)
                deltas.append(
                    lax.dot_general(
                        chosen, product, OVER_COLS, precision=lax.Precision.HIGHEST,
                        preferred_element_type=F32,
                    )
                )

            def tile(step, size, skip, diagonal):
                keys = pl.ds(pl.multiple_of(step, size), size)
                key_t = kt_ref[group * HD : (group + 1) * HD, keys]
                mine = pl.ds(offset + skip, block - skip)
                theirs = pl.ds(turn * block + skip, block - skip)
                for parity in range(2):
                    key_add, value_add = 0.0, 0.0
                    for pair in range(per):
                        head = 2 * pair + parity
                        place = group * 2 * per + head
                        column = (group * per + pair) * LANES
                        query = q_ref[mine, column : column + LANES]
                        grad = grad_ref[theirs, column : column + LANES]
                        scores = dot_cols(kx_ref[group, parity, keys, :], query)
                        if diagonal:
                            scores = jnp.where(causal(size, block - skip), scores, MASKED)
                        probs = jnp.exp(scores - lse_ref[place : place + 1, rows][:, skip:])
                        dprobs = dot_cols(vx_ref[group, parity, keys, :], grad)
                        delta = deltas[pair][parity : parity + 1, skip:]
                        dscores = (probs * (dprobs - delta)).astype(BF16)
                        value_add = value_add + dot(probs.astype(BF16), grad)
                        key_add = key_add + dot(dscores, query)
                        dq_ref[head * HD : (head + 1) * HD, skip:] += dot(key_t, dscores)
                    dk_ref[group, parity, keys, :] += key_add
                    dv_ref[group, parity, keys, :] += value_add

            def full_tile(step, carry):
                tile(step * block, block, 0, False)
                return carry

            lax.fori_loop(first_block(bound, offset, block), index, full_tile, 0)
            tile(offset, block // 2, 0, True)
            tile(offset + block // 2, block // 2, block // 2, True)
            for pair in range(per):
                column = (group * per + pair) * LANES
                grad_q = dq_ref[pair * LANES : (pair + 1) * LANES, :].T * (1.0 / math.sqrt(HD))
                dqkv_ref[rows, column : column + LANES] = turn_back(grad_q, rows).astype(BF16)
            return _

        lax.fori_loop(0, length // block, q_step, 0)

    def finish(index, _):
        rows = pl.ds(pl.multiple_of(index * block, block), block)
        lanes = lax.broadcasted_iota(jnp.int32, (block, LANES), 1)

        def placed(part, half):
            ref = dk_ref if part < kv else dv_ref
            even, odd = ref[part % kv, 0, rows, :], ref[part % kv, 1, rows, :]
            return even + pltpu.roll(odd, HD, 1) if half == 0 else pltpu.roll(even, HD, 1) + odd

        for chunk in range(kv):
            values = jnp.where(lanes < HD, placed(2 * chunk, 0), placed(2 * chunk + 1, 1))
            if 2 * chunk + 1 < kv:
                values = turn_back(values, rows)
            elif 2 * chunk < kv:
                values = jnp.where(lanes < HD, turn_back(values, rows), values)
            column = heads * HD + chunk * LANES
            dqkv_ref[rows, column : column + LANES] = values.astype(BF16)
        return _

    lax.fori_loop(0, length // block, finish, 0)


def attend_back(
    bound, order, queries, kx, vx, kt, log_sums, attended, grad, cosine, sine, block, others
):
    length, width = queries.shape
    heads = width // HD
    kv = kx.shape[0]
    cells = heads * length * (length + block) // 2
    vmem = pl.BlockSpec(memory_space=pltpu.VMEM)
    return pl.pallas_call(
        functools.partial(attend_back_kernel, block=block),
        in_specs=[pl.BlockSpec(memory_space=pltpu.SMEM)] + [vmem] * 9 + [ANYWHERE] * len(others),
        out_specs=vmem,
        out_shape=jax.ShapeDtypeStruct((length, width + 2 * kv * HD), BF16),
        scratch_shapes=[
            pltpu.VMEM((kv, 2, length, LANES), F32),
            pltpu.VMEM((kv, 2, length, LANES), F32),
            pltpu.VMEM((heads // kv * HD, block), F32),
        ],
        compiler_params=limit(52),
        cost_estimate=declared(2 * 10 * HD * 4 * cells),
    )(jnp.stack([bound, *order]), queries, kx, vx, kt, log_sums, attended, grad, cosine, sine, *others)


def local(
    inputs,
    segment_ids,
    attn_gain,
    query_weight,
    key_weight,
    value_weight,
    output_weight,
    mlp_gain,
    gate_weight,
    up_weight,
    down_weight,
    cotangent,
    *,
    sizes,
):
    rows = inputs.shape[0]
    length = segment_ids.shape[0]
    query_cols = query_weight.shape[1]
    key_cols = key_weight.shape[1]
    heads, kv = query_cols // HD, key_cols // HD
    columns = query_cols + 2 * key_cols
    slots = slots_of(sizes["tensor"])
    tensor = sizes["tensor"]
    space = (-columns) % query_cols or query_cols
    gains = jnp.pad(jnp.stack([attn_gain, mlp_gain], axis=1), ((0, 0), (0, space - 2)))
    bundle = lax.all_gather(
        jnp.concatenate([query_weight, key_weight, value_weight, gains, output_weight.T], axis=1),
        "dp", axis=0, tiled=True,
    )
    out_own = bundle[:, columns + space :]
    hop = first_hop(inputs, tensor)
    gate_up = lax.all_gather(
        hold(jnp.concatenate([gate_weight, up_weight], axis=1), *(hop or ())),
        "dp", axis=0, tiled=True,
    )

    bound, cosine, sine = rope_tables(segment_ids)
    blocks = second_hop(inputs, hop, tensor)
    arrays = project(slots, blocks, bundle, cosine, sine, heads, kv, length)
    block_a, queries, kx, vx, kt, vt, gains = arrays

    if tensor == 4:
        out_hop = first_hop(out_own, tensor)
        odd, odd_sums = attend(bound, [jnp.int32(k) for k in (1, 3)], queries, kx, vt, rows)
        halves = hold_halves(out_hop, odd)
        out_all = second_hop(out_own, out_hop, tensor, halves)
        even, even_sums = attend(bound, [jnp.int32(k) for k in (0, 2)], queries, kx, vt, rows, halves)
        order = [slots[1], slots[2], slots[0], slots[3]]
        first, second, own, far = sort_blocks(order, even, odd)
        from_one = lax.ppermute(first, "tensor", pairs(tensor, 1))
        from_two = lax.ppermute(second, "tensor", pairs(tensor, 2))
        from_far = lax.ppermute(far, "tensor", pairs(tensor, 3))
        stream_one, low_m = settle(own, 0, [from_one, from_two, from_far], out_all, inputs, gains)
        attended = jnp.concatenate([first, second, own, far], axis=0)
        log_sums = jnp.concatenate(
            [part[:, at : at + rows] for at in (0, rows) for part in (even_sums, odd_sums)], axis=1
        )
    else:
        order = slots
        out_all = gather(out_own, tensor)
        attended, log_sums = attend(bound, order, queries, kx, vt, rows)
        given = trade([attended[k * rows : (k + 1) * rows] for k in range(tensor)], tensor)
        stream_one, low_m = settle(given[0], 0, given[1:], out_all, inputs, gains)
        cotangent_sent = cotangent
    down_t = lax.all_gather(turn(down_weight, [low_m]), "dp", axis=0, tiled=True)
    parts_m = [low_m]
    units = gate_weight.shape[1]

    def feed_at(place, wanted, fed, others=()):
        return feed(
            feed_kernel, place, tensor, [parts_m[k] for k in wanted], [gate_up] * 2, [0, 1], [],
            units, 3, True, 512, fed, others,
        )

    def back_m(places, fed, into=None, others=(), split=False):
        return back(places, rows, fed[:2], [gate_up] * 2, [0, 1], into, others, split)

    def back_out(places, into=None, others=(), split=False):
        return back(places, rows, [hidden], [down_t], [0], into, others, split)

    def reduce_rows(term, *others):
        if others and tensor == 4:
            term = hold(term, *others)
        return lax.psum_scatter(term, "dp", scatter_dimension=0, tiled=True)

    if tensor == 4:
        hop = first_hop(parts_m[0], tensor)
        fed = feed_at(3, [0], None)
        cotangent_sent = hold(cotangent, fed[0])
        cotangent_hop = first_hop(cotangent_sent, tensor)
        parts_m = second_hop(parts_m[0], hop, tensor)
        fed = feed_at(0, [1, 2], fed, [cotangent_sent])
        halves = hold_halves(cotangent_hop, fed[0])
        grad_parts = second_hop(cotangent_sent, cotangent_hop, tensor, halves)
        grad_parts = grad_parts[1:] + grad_parts[:1]
        fed = feed_at(2, [3], fed, halves)
    else:
        grad_parts = second_hop(cotangent_sent, None, tensor)
        parts_m = gather(parts_m[0], tensor)
        fed = None
        for place in range(tensor):
            fed = feed_at(place, [place], fed)
    hidden, silu, slope, block_m = fed

    def feed_back(others=()):
        return feed(
            feed_back_kernel, 0, tensor, grad_parts, [down_t], [0], [silu, slope], units, 2, False, 512,
            None, others,
        )

    if tensor == 4:
        three_out = back_out([2], None, [fed[0]], True)
        out_one, out_two = out_halves = send_half(three_out, tensor)
        down_t_wgrad = weigh(grad_parts, hidden, three_out[:1])
        one_out, two_out, own_out = back_out([0, 1, 3], [(out_one, False), (out_two, True), None])
        out_parts = [
            own_out,
            lax.ppermute(one_out, "tensor", pairs(tensor, 1)),
            lax.ppermute(two_out, "tensor", pairs(tensor, 2)),
        ]
        fed = feed_back([one_out])
        three_m = back_m([2], fed, None, (), True)
        m_one, m_two = m_halves = send_half(three_m, tensor)
        gate_wgrad = weigh([block_m], fed[0], [three_m[0], *out_parts[1:]])
        one_m, two_m = back_m([0, 1], fed, [(m_one, False), (m_two, True)])
        (own_m,) = back_m([3], fed, None, [one_m])
        up_wgrad = weigh([block_m], fed[1], [own_m])
        grad_m_parts = [
            own_m,
            lax.ppermute(one_m, "tensor", pairs(tensor, 1)),
            lax.ppermute(two_m, "tensor", pairs(tensor, 2)),
        ]
    else:
        down_t_wgrad = weigh(grad_parts, hidden)
        fed = feed_back()
        grad_m_parts = sum_whole(back_m(list(range(tensor)), fed))
        gate_wgrad, up_wgrad = weigh([block_m], fed[0]), weigh([block_m], fed[1])
        out_parts = sum_whole(back_out(list(range(tensor))))
    if tensor != 4:
        out_halves = m_halves = ()
    down_t_low = reduce_rows(down_t_wgrad, *out_halves)
    gate_low = reduce_rows(gate_wgrad, *m_halves)
    up_low = reduce_rows(up_wgrad, *grad_m_parts[1:])

    grad_stream_one, grad_stream_low, *pieces = settle_back(
        grad_m_parts, out_all, cotangent, stream_one, gains
    )
    given = trade(pieces, tensor)
    places = [1, 2, 0, 3] if tensor == 4 else list(range(tensor))
    grad_attended = jnp.concatenate([given[k] for k in places], axis=0)
    grad_qkv = attend_back(
        bound, order, queries, kx, vx, kt, log_sums, attended, grad_attended, cosine, sine, rows,
        [down_t_low],
    )
    if tensor == 4:
        sent = hold(grad_stream_low, grad_attended)
        grad_stream_parts = trade([sent] * 4, tensor)
    else:
        grad_stream_parts = gather(grad_stream_low, tensor)
    grad_stream_parts = [grad_stream_parts[k] for k in places]

    def back_a(places, others=(), split=False):
        return back(places, rows, [grad_qkv], [bundle], [0], None, others, split)

    if tensor == 4:
        three = back_a(slots[3:], [gate_low], True)
        halves = send_half(three, tensor)
        one, two, own = back_a([slots[1], slots[2], slots[0]], three[:1])
        block_a = hold(block_a, one)
    attention_wgrad = weigh_both(block_a, grad_qkv, grad_stream_parts, attended)
    gate_sum, up_sum, down_t_sum = [low.astype(F32) for low in (gate_low, up_low, down_t_low)]
    if tensor == 4:
        attention_wgrad = hold(attention_wgrad, *halves)
    attention_sum = reduce_rows(attention_wgrad).astype(F32)
    if tensor == 4:
        one, two = add_half(one, halves[0], 1), add_half(two, halves[1], 0)
        grad_a_parts = [
            own,
            lax.ppermute(one, "tensor", pairs(tensor, 1)),
            lax.ppermute(two, "tensor", pairs(tensor, 2)),
        ]
        layer_out = finish(out_parts, stream_one, [one, two])
    else:
        grad_a_parts = sum_whole(back_a(slots))
        layer_out = finish(out_parts, stream_one)

    product = attention_wgrad[:, :columns].astype(F32) * bundle[:, :columns].astype(F32)
    attn_term = sum_tensor(hold(jnp.sum(product, axis=1)[None, :], layer_out), tensor)
    width = attn_gain.shape[0]
    attn_term = lax.dynamic_slice_in_dim(
        sum_blocks(attn_term, sizes["dp"]), lax.axis_index("dp") * width, width, 1
    )

    def gain_term(gain, weights):
        term = sum(jnp.sum(weight.astype(F32) * grad, axis=1) for weight, grad in weights)
        return term / gain.astype(F32)

    query_sum = attention_sum[:, :query_cols]
    key_sum = attention_sum[:, query_cols : query_cols + key_cols]
    value_sum = attention_sum[:, query_cols + key_cols : columns]
    mlp_term = sum_tensor(
        gain_term(mlp_gain, [(gate_weight, gate_sum), (up_weight, up_sum)])[None, :], tensor
    )
    input_grad = settle_last(grad_a_parts, grad_stream_one, inputs, gains)
    return (
        layer_out,
        input_grad,
        attn_term[0] / attn_gain.astype(F32),
        query_sum,
        key_sum,
        value_sum,
        attention_sum[:, columns:].T,
        mlp_term[0],
        gate_sum,
        up_sum,
        down_t_sum.T,
    )


def solution(mesh):
    tokens = P(("dp", "tensor"), None)
    in_specs = (
        tokens,
        P("dp"),
        P("dp"),
        P("dp", "tensor"),
        P("dp", "tensor"),
        P("dp", "tensor"),
        P("tensor", "dp"),
        P("dp"),
        P("dp", "tensor"),
        P("dp", "tensor"),
        P("tensor", "dp"),
        tokens,
    )
    out_specs = (
        tokens,
        tokens,
        P("dp"),
        P("dp", "tensor"),
        P("dp", "tensor"),
        P("dp", "tensor"),
        P("tensor", "dp"),
        P("dp"),
        P("dp", "tensor"),
        P("dp", "tensor"),
        P("tensor", "dp"),
    )
    return jax.shard_map(
        functools.partial(local, sizes={axis: mesh.shape[axis] for axis in ("tensor", "dp")}),
        mesh=mesh, in_specs=in_specs, out_specs=out_specs, check_vma=False,
    )
```

```python
import functools
import math

import jax
import jax.numpy as jnp
from jax import lax
from jax.experimental import pallas as pl
from jax.experimental.pallas import tpu as pltpu
from jax.sharding import PartitionSpec as P

HD = 64
LANES = 128
EPSILON = 1e-05
ROPE_BASE = 500000.0
MASKED = -1e30
OVER_ROWS = (((0,), (0,)), ((), ()))
OVER_COLS = (((1,), (1,)), ((), ()))


def limit(size):
    return pltpu.CompilerParams(vmem_limit_bytes=size * 2**20)


SHORT = 0.0625


def declared(flops, scale=SHORT):
    return pl.CostEstimate(flops=int(flops * scale), bytes_accessed=0, transcendentals=0)


F32 = jnp.float32
BF16 = jnp.bfloat16


def dot_cols(left, right):
    return lax.dot_general(left, right, OVER_COLS, preferred_element_type=F32)


def dot_rows(left, right):
    return lax.dot_general(left, right, OVER_ROWS, preferred_element_type=F32)


def dot(left, right):
    return jnp.dot(left, right, preferred_element_type=F32)


def pairs(size, bit):
    return [(index, index ^ bit) for index in range(size)]


def slots_of(size):
    if size == 4:
        return [lax.axis_index("tensor") ^ step for step in range(size)]
    return [jnp.int32(step) for step in range(size)]


ANYWHERE = pl.BlockSpec(memory_space=pl.ANY)


def nothing_kernel(*refs):
    pass


def hold(value, *others):
    return pl.pallas_call(
        nothing_kernel,
        in_specs=[ANYWHERE] * (1 + len(others)),
        out_specs=ANYWHERE,
        out_shape=jax.ShapeDtypeStruct(value.shape, value.dtype),
        input_output_aliases={0: 0},
        cost_estimate=declared(0),
    )(value, *others)


def first_hop(shard, size):
    if size != 4:
        return None
    return [lax.ppermute(shard, "tensor", pairs(size, bit)) for bit in (1, 2)]


def copy_kernel(value_ref, *rest):
    rest[-1][...] = value_ref[...]


def half_of(value, which, *others):
    rows, width = value.shape
    tile = rows // 4
    return pl.pallas_call(
        copy_kernel,
        grid=(2,),
        in_specs=[pl.BlockSpec((tile, width), lambda i: (2 * which + i, 0))]
        + [ANYWHERE] * len(others),
        out_specs=pl.BlockSpec((tile, width), lambda i: (i, 0)),
        out_shape=jax.ShapeDtypeStruct((rows // 2, width), value.dtype),
        compiler_params=limit(52),
        cost_estimate=declared(0),
    )(value, *others)


def add_kernel(value_ref, extra_ref, out_ref, *, which):
    out_ref[...] = value_ref[...]

    @pl.when(pl.program_id(0) == which)
    def _():
        out_ref[...] = (value_ref[...].astype(F32) + extra_ref[...].astype(F32)).astype(BF16)


def add_half(value, extra, which):
    rows, width = value.shape
    half = pl.BlockSpec((rows // 2, width), lambda i: (i, 0))
    return pl.pallas_call(
        functools.partial(add_kernel, which=which),
        grid=(2,),
        in_specs=[half, pl.BlockSpec((rows // 2, width), lambda i: (0, 0))],
        out_specs=half,
        out_shape=jax.ShapeDtypeStruct((rows, width), value.dtype),
        compiler_params=limit(52),
        cost_estimate=declared(0),
    )(value, extra)


def hold_halves(hop, *others):
    return half_of(hop[0], 0, *others), half_of(hop[1], 1, *others)


def second_hop(shard, hop, size, halves=None):
    if size != 4:
        whole = lax.all_gather(shard, "tensor", axis=0)
        return [whole[step] for step in range(size)]
    one, two = hop
    upper, lower = halves or hold_halves(hop)
    three_a = lax.ppermute(upper, "tensor", pairs(size, 2))
    three_b = lax.ppermute(lower, "tensor", pairs(size, 1))
    return [shard, one, two, jnp.concatenate([three_a, three_b], axis=0)]


def gather(shard, size):
    return second_hop(shard, first_hop(shard, size), size)


def send_half(three, size):
    into_two = lax.ppermute(three[0], "tensor", pairs(size, 1))
    into_one = lax.ppermute(three[1], "tensor", pairs(size, 2))
    return into_one, into_two


def sum_whole(terms):
    return [
        lax.psum_scatter(
            jnp.concatenate(terms, axis=0), "tensor", scatter_dimension=0, tiled=True
        )
    ]


def trade(pieces, size):
    if size != 4:
        whole = lax.all_to_all(jnp.stack(pieces), "tensor", split_axis=0, concat_axis=0, tiled=True)
        return [whole[step] for step in range(size)]
    return [pieces[0]] + [
        lax.ppermute(pieces[step], "tensor", pairs(size, step)) for step in (1, 2, 3)
    ]


def total(parts):
    return functools.reduce(jnp.add, [part.astype(F32) for part in parts])


def sum_tensor(value, size):
    if size & (size - 1):
        return lax.psum(value, "tensor")
    return value + sum(lax.ppermute(value, "tensor", pairs(size, bit)) for bit in range(1, size))


def sum_blocks(value, size):
    if size & (size - 1):
        return lax.psum(value, "dp")
    bit = 1
    while bit < size:
        value = value + lax.ppermute(value, "dp", pairs(size, bit))
        bit *= 2
    return value


def rope_tables(segment):
    length = segment.shape[0]
    bound = jnp.sum((segment == 0).astype(jnp.int32))
    place = lax.broadcasted_iota(jnp.int32, (length, LANES), 0)
    place = place - jnp.where(place >= bound, bound, 0)
    lane = lax.broadcasted_iota(jnp.int32, (length, LANES), 1)
    freqs = jnp.exp(
        (lane % (HD // 2)).astype(F32) * (-2.0 * math.log(ROPE_BASE) / HD)
    )
    angles = place.astype(F32) * freqs
    sine = jnp.sin(angles)
    return bound, jnp.cos(angles), jnp.where(lane % HD < HD // 2, -sine, sine)


def swap_halves(values):
    lane = lax.broadcasted_iota(jnp.int32, values.shape, 1)
    after = pltpu.roll(values, LANES - HD // 2, 1)
    before = pltpu.roll(values, HD // 2, 1)
    return jnp.where(lane % HD < HD // 2, after, before)


def normalize(stream):
    scale_r = lax.rsqrt(jnp.mean(stream * stream, axis=-1, keepdims=True) + EPSILON)
    return (stream * scale_r, scale_r)


def project_kernel(slot_ref, *refs, count, steps, heads, kv):
    gains_ref, w_ref, cos_ref, sin_ref = refs[count : count + 4]
    h_ref, q_ref, kx_ref, vx_ref, kt_ref, vt_ref, gain_ref = refs[-7:]

    @pl.when(pl.program_id(0) == 0)
    def _():
        gain_ref[...] = gains_ref[...].astype(F32).T[:8]

    which = pl.program_id(0) // steps
    rows = h_ref.shape[0]
    part_rows = min(256, rows)
    lane = lax.broadcasted_iota(jnp.int32, (part_rows, LANES), 1)
    for start in range(0, rows, part_rows):
        at = slice(start, start + part_rows)
        tokens = refs[0][at, :]
        for block in range(1, count):
            tokens = jnp.where(which == block, refs[block][at, :], tokens)
        normed, _ = normalize(tokens.astype(F32))
        low = (normed * gain_ref[0:1, :]).astype(BF16)
        h_ref[at, :] = low
        pre = dot(low, w_ref[...])
        cosine, sine = cos_ref[at, :], sin_ref[at, :]
        chunks = []
        for chunk in range(pre.shape[1] // LANES):
            columns = slice(chunk * LANES, (chunk + 1) * LANES)
            part = pre[:, columns]
            first = 2 * chunk
            if first < heads + kv:
                turned = part * cosine + swap_halves(part) * sine
                part = turned if first + 1 < heads + kv else jnp.where(lane < HD, turned, part)
            chunks.append(part)
            if first < heads:
                q_ref[at, columns] = (part * (1.0 / math.sqrt(HD))).astype(BF16)
        flipped = {}
        for head in range(2 * kv):
            place = heads + head
            part = chunks[place // 2]
            moved = pltpu.roll(part, HD, 1)
            wide = [part, moved] if place % 2 == 0 else [moved, part]
            out = kx_ref if head < kv else vx_ref
            out[head % kv, 0, at, :] = jnp.where(lane < HD, wide[0], 0.0).astype(BF16)
            out[head % kv, 1, at, :] = jnp.where(lane < HD, 0.0, wide[1]).astype(BF16)
            if place // 2 not in flipped:
                flipped[place // 2] = part.T
            turn = flipped[place // 2][(place % 2) * HD : (place % 2 + 1) * HD]
            out_t = kt_ref if head < kv else vt_ref
            out_t[(head % kv) * HD : (head % kv + 1) * HD, at] = turn.astype(BF16)


def project(slots, blocks, bundle, cosine, sine, heads, kv, length):
    rows, width = blocks[0].shape
    count = len(blocks)
    tile = rows
    steps = rows // tile
    columns = (heads + 2 * kv) * HD

    def at(i, slot):
        return slot[i // steps] * steps + i % steps

    shapes = [
        jax.ShapeDtypeStruct((length, width), BF16),
        jax.ShapeDtypeStruct((length, heads * HD), BF16),
        jax.ShapeDtypeStruct((kv, 2, length, LANES), BF16),
        jax.ShapeDtypeStruct((kv, 2, length, LANES), BF16),
        jax.ShapeDtypeStruct((kv * HD, length), BF16),
        jax.ShapeDtypeStruct((kv * HD, length), BF16),
        jax.ShapeDtypeStruct((8, width), F32),
    ]
    out_specs = [
        pl.BlockSpec((tile, width), lambda i, s: (at(i, s), 0)),
        pl.BlockSpec((tile, heads * HD), lambda i, s: (at(i, s), 0)),
        pl.BlockSpec((kv, 2, tile, LANES), lambda i, s: (0, 0, at(i, s), 0)),
        pl.BlockSpec((kv, 2, tile, LANES), lambda i, s: (0, 0, at(i, s), 0)),
        pl.BlockSpec((kv * HD, tile), lambda i, s: (0, at(i, s))),
        pl.BlockSpec((kv * HD, tile), lambda i, s: (0, at(i, s))),
        pl.BlockSpec((8, width), lambda i, s: (0, 0)),
    ]
    in_specs = [
        pl.BlockSpec((tile, width), lambda i, s, b=block: (jnp.clip(i - b * steps, 0, steps - 1), 0))
        for block in range(count)
    ]
    in_specs += [
        pl.BlockSpec((width, LANES), lambda i, s: (0, columns // LANES)),
        pl.BlockSpec((width, columns), lambda i, s: (0, 0)),
        pl.BlockSpec((tile, LANES), lambda i, s: (at(i, s), 0)),
        pl.BlockSpec((tile, LANES), lambda i, s: (at(i, s), 0)),
    ]
    operands = [jnp.stack(slots), *blocks, bundle, bundle, cosine, sine]
    return pl.pallas_call(
        functools.partial(
            project_kernel, count=count, steps=steps, heads=heads, kv=kv
        ),
        grid_spec=pltpu.PrefetchScalarGridSpec(
            num_scalar_prefetch=1,
            grid=(count * steps,),
            in_specs=in_specs,
            out_specs=out_specs,
        ),
        out_shape=shapes,
        compiler_params=limit(52),
        cost_estimate=declared(2 * count * rows * width * columns),
    )(*operands)


def feed_kernel(*refs, count):
    tokens = refs[:count]
    gate_ref, up_ref = refs[count : count + 2]
    hidden_ref, silu_ref, slope_ref, h_out = refs[-4:]
    rows = tokens[0].shape[0]
    wide = h_out.shape[1]
    tile = min(256, gate_ref.shape[1])
    lanes = pl.ds(pl.multiple_of(pl.program_id(0) * wide, wide), wide)
    for block in range(count):
        h_out[block * rows : (block + 1) * rows, :] = tokens[block][:, lanes]
    for part in range(gate_ref.shape[1] // tile):
        columns = slice(part * tile, (part + 1) * tile)
        for block in range(count):
            where = slice(block * rows, (block + 1) * rows)
            gate = dot(tokens[block][...], gate_ref[:, columns])
            up = dot(tokens[block][...], up_ref[:, columns])
            sigmoid = 0.5 * jnp.tanh(0.5 * gate) + 0.5
            silu = gate * sigmoid
            hidden_ref[where, columns] = (silu * up).astype(BF16)
            silu_ref[where, columns] = silu.astype(BF16)
            slope_ref[where, columns] = (up * (sigmoid + silu * (1.0 - sigmoid))).astype(BF16)


def feed_back_kernel(*refs, count):
    grads = refs[:count]
    down_ref, silu_ref, slope_ref = refs[count : count + 3]
    dgate_ref, dup_ref = refs[-2:]
    rows = grads[0].shape[0]
    for block in range(count):
        where = slice(block * rows, (block + 1) * rows)
        dhidden = dot(grads[block][...], down_ref[...])
        dup_ref[where, :] = (dhidden * silu_ref[where, :].astype(F32)).astype(BF16)
        dgate_ref[where, :] = (dhidden * slope_ref[where, :].astype(F32)).astype(BF16)


def feed(kernel, place, blocks, tokens, weights, places, kept, units, outs, copy, tile, prev, others):
    rows, width = tokens[0].shape
    count = len(tokens)
    steps = max(units // tile, 1)
    tile, wide = units // steps, width // steps
    shapes = [jax.ShapeDtypeStruct((blocks * rows, units), BF16)] * outs
    in_specs = [pl.BlockSpec((rows, width), lambda i: (0, 0), pipeline_mode=pl.Buffered(1))] * count
    in_specs += [
        pl.BlockSpec((width, tile), lambda i, w=which: (0, w * steps + i)) for which in places
    ]
    cell = pl.BlockSpec((count * rows, tile), lambda i: (place, i))
    in_specs += [cell] * len(kept)
    out_specs = [cell] * outs
    if copy:
        shapes.append(jax.ShapeDtypeStruct((blocks * rows, width), BF16))
        out_specs.append(pl.BlockSpec((count * rows, wide), lambda i: (place, i)))
    operands = [*tokens, *weights, *kept]
    aliases = {}
    if prev is not None:
        for index, array in enumerate(prev):
            aliases[len(operands)] = index
            operands.append(array)
            in_specs.append(ANYWHERE)
    operands += others
    in_specs += [ANYWHERE] * len(others)
    return pl.pallas_call(
        functools.partial(kernel, count=count),
        grid=(steps,),
        in_specs=in_specs,
        out_specs=out_specs,
        out_shape=shapes,
        input_output_aliases=aliases,
        compiler_params=limit(52),
        cost_estimate=declared(2 * len(weights) * count * rows * width * units),
    )(*operands)


def back_kernel(slot_ref, *refs, count, terms, added, split):
    outs = refs[-2:] if split else refs[-count:]
    weights = refs[count * terms : (count + 1) * terms]
    into = list(refs[(count + 1) * terms :])
    for block in range(count):
        value = dot_cols(refs[block * terms][...], weights[0][...])
        for term in range(1, terms):
            value = value + dot_cols(refs[block * terms + term][...], weights[term][...])
        half = value.shape[0] // 2
        if split:
            outs[0][...] = value[:half].astype(BF16)
            outs[1][...] = value[half:].astype(BF16)
            continue
        if added[block] is None:
            outs[block][...] = value.astype(BF16)
            continue
        extra = into.pop(0)[...].astype(F32)
        top, bottom = value[:half], value[half:]
        if added[block]:
            top = top + extra
        else:
            bottom = bottom + extra
        outs[block][:half, :] = top.astype(BF16)
        outs[block][half:, :] = bottom.astype(BF16)


def back(slots, rows, lefts, weights, places, into=None, others=(), split=False):
    depth = lefts[0].shape[1]
    width = weights[0].shape[0]
    tile = min(512, width)
    terms, count = len(lefts), len(slots)
    outs, tall = (2, rows // 2) if split else (count, rows)
    into = into or [None] * count
    in_specs, operands = [], [jnp.stack([jnp.asarray(slot, jnp.int32) for slot in slots])]
    for block in range(count):
        in_specs += [pl.BlockSpec((rows, depth), lambda i, s, b=block: (s[b], 0))] * terms
        operands += lefts
    in_specs += [pl.BlockSpec((tile, depth), lambda i, s, p=place: (i, p)) for place in places]
    operands += weights
    for extra in into:
        if extra is not None:
            in_specs.append(pl.BlockSpec((rows // 2, tile), lambda i, s: (0, i)))
            operands.append(extra[0])
    operands += others
    in_specs += [ANYWHERE] * len(others)
    return pl.pallas_call(
        functools.partial(
            back_kernel,
            count=count,
            terms=terms,
            added=[None if extra is None else extra[1] for extra in into],
            split=split,
        ),
        grid_spec=pltpu.PrefetchScalarGridSpec(
            num_scalar_prefetch=1,
            grid=(width // tile,),
            in_specs=in_specs,
            out_specs=[pl.BlockSpec((tall, tile), lambda i, s: (0, i))] * outs,
        ),
        out_shape=[jax.ShapeDtypeStruct((tall, width), BF16)] * outs,
        compiler_params=limit(52),
        cost_estimate=declared(2 * count * terms * rows * width * depth),
    )(*operands)


def turn_kernel(value_ref, *rest):
    rest[-1][...] = value_ref[...].T


def turn(value, others=()):
    rows, columns = value.shape
    tile = min(512, rows)
    return pl.pallas_call(
        turn_kernel,
        grid=(rows // tile,),
        in_specs=[pl.BlockSpec((tile, columns), lambda i: (i, 0))] + [ANYWHERE] * len(others),
        out_specs=pl.BlockSpec((columns, tile), lambda i: (0, i)),
        out_shape=jax.ShapeDtypeStruct((columns, rows), value.dtype),
        compiler_params=limit(52),
        cost_estimate=declared(0),
    )(value, *others)


def turn_blocks(lefts, turned_ref):
    rows = lefts[0].shape[0]
    for block, left in enumerate(lefts):
        turned_ref[:, block * rows : (block + 1) * rows] = left[...].T


def weigh_kernel(*refs, count):
    lefts, right_ref = refs[:count], refs[count]
    out_ref, *turned = refs[-3:]
    i, j = pl.program_id(0), pl.program_id(1)
    last = j == pl.num_programs(1) - 1

    @pl.when((i == 0) & (j == 0))
    def _():
        turn_blocks(lefts, turned[0])

    for parity in range(2):

        @pl.when((i % 2 == parity) & jnp.logical_not(last))
        def _():
            out_ref[...] = dot(turned[parity][...], right_ref[...]).astype(BF16)

        @pl.when((i % 2 == parity) & last)
        def _():
            out_ref[...] = dot(turned[parity][...], right_ref[...]).astype(BF16)
            turn_blocks(lefts, turned[1 - parity])


def weigh(lefts, right, others=()):
    tokens, columns = right.shape
    rows, width = lefts[0].shape
    tall, wide = min(512, width), min(1024, columns // 2)
    tiles, steps = width // tall, columns // wide

    def ahead(i, j):
        return 0, jnp.minimum(i + jnp.where(j == steps - 1, 1, 0), tiles - 1)

    return pl.pallas_call(
        functools.partial(weigh_kernel, count=len(lefts)),
        grid=(tiles, steps),
        in_specs=[pl.BlockSpec((rows, tall), ahead)] * len(lefts)
        + [pl.BlockSpec((tokens, wide), lambda i, j: (0, j))]
        + [ANYWHERE] * len(others),
        out_specs=pl.BlockSpec((tall, wide), lambda i, j: (i, j)),
        out_shape=jax.ShapeDtypeStruct((width, columns), BF16),
        scratch_shapes=[pltpu.VMEM((tall, tokens), BF16)] * 2,
        compiler_params=limit(52),
        cost_estimate=declared(2 * tokens * width * columns),
    )(*lefts, right, *others)


def weigh_both_kernel(*refs, count):
    one_ref, others = refs[0], refs[1 : 1 + count]
    right_ref, other_ref, out_ref, turned_ref, other_turned_ref = refs[1 + count :]
    columns = right_ref.shape[1]
    turn_blocks([one_ref], turned_ref)
    out_ref[:, :columns] = dot(turned_ref[...], right_ref[...]).astype(BF16)
    turn_blocks(others, other_turned_ref)
    out_ref[:, columns:] = dot(other_turned_ref[...], other_ref[...]).astype(BF16)


def weigh_both(one, right, others, other_right):
    tokens, width = one.shape
    rows = others[0].shape[0]
    columns, more = right.shape[1], other_right.shape[1]
    tall = min(512, width)
    whole = [pl.BlockSpec((tokens, columns), lambda i: (0, 0))]
    whole += [pl.BlockSpec((tokens, more), lambda i: (0, 0))]
    return pl.pallas_call(
        functools.partial(weigh_both_kernel, count=len(others)),
        grid=(width // tall,),
        in_specs=[pl.BlockSpec((tokens, tall), lambda i: (0, i))]
        + [pl.BlockSpec((rows, tall), lambda i: (0, i))] * len(others)
        + whole,
        out_specs=pl.BlockSpec((tall, columns + more), lambda i: (i, 0)),
        out_shape=jax.ShapeDtypeStruct((width, columns + more), BF16),
        scratch_shapes=[pltpu.VMEM((tall, tokens), BF16)] * 2,
        compiler_params=limit(52),
        cost_estimate=declared(2 * tokens * width * (columns + more)),
    )(one, *others, right, other_right)


def settle_kernel(*refs, count):
    pieces, weights = refs[:count], refs[count : 2 * count]
    x_ref, gains_ref = refs[2 * count : 2 * count + 2]
    stream_ref, h_ref = refs[-2:]
    stream = x_ref[...].astype(F32)
    for piece, weight in zip(pieces, weights):
        stream = stream + dot_cols(piece[...], weight[...])
    stream_ref[...] = stream
    normed, _ = normalize(stream)
    h_ref[...] = (normed * gains_ref[1:2, :]).astype(BF16)


def settle(own, place, pieces, weights, tokens, gains, others=()):
    rows, width = tokens.shape
    depth = weights[0].shape[1]
    tile = min(256, rows)
    steps = rows // tile
    wide = pl.BlockSpec((tile, width), lambda i: (i, 0))
    piece = pl.BlockSpec((tile, depth), lambda i: (i, 0))
    weight = pl.BlockSpec((width, depth), lambda i: (0, 0), pipeline_mode=pl.Buffered(1))
    return pl.pallas_call(
        functools.partial(settle_kernel, count=len(weights)),
        grid=(steps,),
        in_specs=[pl.BlockSpec((tile, depth), lambda i: (place * steps + i, 0))]
        + [piece] * len(pieces)
        + [weight] * len(weights)
        + [wide, pl.BlockSpec((8, width), lambda i: (0, 0))]
        + [ANYWHERE] * len(others),
        out_specs=[wide, wide],
        out_shape=[
            jax.ShapeDtypeStruct((rows, width), F32),
            jax.ShapeDtypeStruct((rows, width), BF16),
        ],
        compiler_params=limit(52),
        cost_estimate=declared(2 * len(weights) * rows * width * depth),
    )(own, *pieces, *weights, tokens, gains, *others)


def norm_back(grad_in, stream, gain):
    normed, scale_r = normalize(stream)
    scaled = grad_in * gain
    return scale_r * (scaled - normed * jnp.mean(scaled * normed, axis=-1, keepdims=True))


def settle_back_kernel(*refs, parts, count):
    terms, weights = refs[:parts], refs[parts : parts + count]
    grad_ref, stream_ref, gains_ref, out_ref, low_ref = refs[parts + count : parts + count + 5]
    pieces = refs[parts + count + 5 :]
    grad_in = terms[0][...].astype(F32)
    for term in terms[1:]:
        grad_in = grad_in + term[...].astype(F32)
    grad = grad_ref[...].astype(F32) + norm_back(grad_in, stream_ref[...], gains_ref[1:2, :])
    out_ref[...] = grad
    low = grad.astype(BF16)
    low_ref[...] = low
    for piece, weight in zip(pieces, weights):
        piece[...] = dot(low, weight[...]).astype(BF16)


def settle_back(terms, weights, grad, stream, gains):
    rows, width = grad.shape
    depth = weights[0].shape[1]
    tile = min(256, rows)
    wide = pl.BlockSpec((tile, width), lambda i: (i, 0))
    weight = pl.BlockSpec((width, depth), lambda i: (0, 0), pipeline_mode=pl.Buffered(1))
    return pl.pallas_call(
        functools.partial(settle_back_kernel, parts=len(terms), count=len(weights)),
        grid=(rows // tile,),
        in_specs=[wide] * len(terms)
        + [weight] * len(weights)
        + [wide, wide, pl.BlockSpec((8, width), lambda i: (0, 0))],
        out_specs=[wide, wide] + [pl.BlockSpec((tile, depth), lambda i: (i, 0))] * len(weights),
        out_shape=[
            jax.ShapeDtypeStruct((rows, width), F32),
            jax.ShapeDtypeStruct((rows, width), BF16),
        ]
        + [jax.ShapeDtypeStruct((rows, depth), BF16)] * len(weights),
        compiler_params=limit(52),
        cost_estimate=declared(2 * len(weights) * rows * width * depth),
    )(*terms, *weights, grad, stream, gains)


def settle_last_kernel(*refs):
    grad_ref, x_ref, gains_ref, out_ref = refs[-4:]
    grad_in = refs[0][...].astype(F32)
    for term in refs[1:-4]:
        grad_in = grad_in + term[...].astype(F32)
    back_a = norm_back(grad_in, x_ref[...].astype(F32), gains_ref[0:1, :])
    out_ref[...] = (grad_ref[...] + back_a).astype(BF16)


def settle_last(terms, grad, tokens, gains):
    rows, width = tokens.shape
    tile = min(128, rows)
    wide = pl.BlockSpec((tile, width), lambda i: (i, 0))
    return pl.pallas_call(
        settle_last_kernel,
        grid=(rows // tile,),
        in_specs=[wide] * (len(terms) + 2) + [pl.BlockSpec((8, width), lambda i: (0, 0))],
        out_specs=wide,
        out_shape=jax.ShapeDtypeStruct((rows, width), BF16),
        compiler_params=limit(52),
        cost_estimate=declared(rows * width),
    )(*terms, grad, tokens, gains)


def finish_kernel(*refs, count):
    value = refs[count][...]
    for term in refs[:count]:
        value = value + term[...].astype(F32)
    refs[-1][...] = value.astype(BF16)


def finish(terms, stream, others=()):
    rows, width = stream.shape
    wide = pl.BlockSpec((rows // 4, width), lambda i: (i, 0))
    return pl.pallas_call(
        functools.partial(finish_kernel, count=len(terms)),
        grid=(4,),
        in_specs=[wide] * (len(terms) + 1) + [ANYWHERE] * len(others),
        out_specs=wide,
        out_shape=jax.ShapeDtypeStruct((rows, width), BF16),
        compiler_params=limit(52),
        cost_estimate=declared(rows * width),
    )(*terms, stream, *others)


def causal(keys, queries):
    key = lax.broadcasted_iota(jnp.int32, (keys, queries), 0)
    return key <= lax.broadcasted_iota(jnp.int32, (keys, queries), 1)


def first_block(bound, offset, block):
    return jnp.where(offset >= bound, lax.div(bound, jnp.int32(block)), 0)


def attend_kernel(order_ref, q_ref, kx_ref, vt_ref, *rest, block):
    out_ref, lse_ref, top_ref, acc_ref = rest[-4:]
    kv = kx_ref.shape[0]
    per = q_ref.shape[1] // LANES // kv
    bound = order_ref[0]
    ones = jnp.ones((16, block), BF16)
    for group in range(kv):

        def q_step(turn, _):
            index = order_ref[1 + turn]
            offset = pl.multiple_of(index * block, block)
            into = pl.ds(pl.multiple_of(turn * block, block), block)
            top_ref[...] = jnp.full(top_ref.shape, MASKED, F32)
            acc_ref[...] = jnp.zeros(acc_ref.shape, F32)

            def tile(step, diagonal):
                keys = pl.ds(pl.multiple_of(step, block), block)
                value_t = jnp.concatenate(
                    [vt_ref[group * HD : (group + 1) * HD, keys], ones], axis=0
                )
                for head in range(2 * per):
                    column = (group * per + head // 2) * LANES
                    query = q_ref[pl.ds(offset, block), column : column + LANES]
                    scores = dot_cols(kx_ref[group, head % 2, keys, :], query)
                    if diagonal:
                        scores = jnp.where(causal(block, block), scores, MASKED)
                    old = top_ref[head, 0:1, :]
                    top = jnp.maximum(old, jnp.max(scores, axis=0, keepdims=True))
                    powered = jnp.exp(scores - top).astype(BF16)
                    acc_ref[head] = acc_ref[head] * jnp.exp(old - top) + dot(value_t, powered)
                    top_ref[head, 0:1, :] = top

            def full_tile(step, carry):
                tile(step * block, False)
                return carry

            lax.fori_loop(first_block(bound, offset, block), index, full_tile, 0)
            tile(offset, True)
            for pair in range(per):
                both = []
                for head in (2 * pair, 2 * pair + 1):
                    total = acc_ref[head, HD : HD + 1, :]
                    both.append(acc_ref[head, :HD, :] / total)
                    place = group * 2 * per + head
                    lse_ref[place : place + 1, into] = top_ref[
                        head, 0:1, :
                    ] + jnp.log(total)
                column = (group * per + pair) * LANES
                out_ref[into, column : column + LANES] = (
                    jnp.concatenate(both, axis=0).T.astype(BF16)
                )
            return _

        lax.fori_loop(0, out_ref.shape[0] // block, q_step, 0)


def attend(bound, order, queries, kx, vt, block, others=()):
    length, width = queries.shape
    heads = width // HD
    kv = kx.shape[0]
    per = heads // kv
    count = len(order)
    cells = heads * count * block * (length + block) // 2
    vmem = pl.BlockSpec(memory_space=pltpu.VMEM)
    return pl.pallas_call(
        functools.partial(attend_kernel, block=block),
        in_specs=[pl.BlockSpec(memory_space=pltpu.SMEM), vmem, vmem, vmem] + [ANYWHERE] * len(others),
        out_specs=[vmem, vmem],
        out_shape=[
            jax.ShapeDtypeStruct((count * block, width), BF16),
            jax.ShapeDtypeStruct((heads, count * block), F32),
        ],
        scratch_shapes=[
            pltpu.VMEM((per, 8, block), F32),
            pltpu.VMEM((per, HD + 16, block), F32),
        ],
        compiler_params=limit(52),
        cost_estimate=declared(2 * 4 * HD * 4 * cells, 16),
    )(jnp.stack([bound, *order]), queries, kx, vt, *others)


def sort_kernel(order_ref, *refs):
    parts, out_refs = refs[:2], refs[2:]
    block = out_refs[0].shape[0]
    for turn, out_ref in enumerate(out_refs):
        index = order_ref[turn]
        rows = pl.ds(pl.multiple_of(lax.div(index, 2) * block, block), block)
        out_ref[...] = jnp.where(lax.rem(index, 2) == 0, parts[0][rows, :], parts[1][rows, :])


def sort_blocks(order, even, odd):
    rows, width = even.shape[0] // 2, even.shape[1]
    vmem = pl.BlockSpec(memory_space=pltpu.VMEM)
    return pl.pallas_call(
        sort_kernel,
        in_specs=[pl.BlockSpec(memory_space=pltpu.SMEM), vmem, vmem],
        out_specs=[vmem] * len(order),
        out_shape=[jax.ShapeDtypeStruct((rows, width), even.dtype)] * len(order),
        compiler_params=limit(20),
        cost_estimate=declared(0),
    )(jnp.stack(order), even, odd)


def attend_back_kernel(
    order_ref, q_ref, kx_ref, vx_ref, kt_ref, lse_ref, out_ref, grad_ref, cos_ref, sin_ref,
    *rest, block
):
    dqkv_ref, dk_ref, dv_ref, dq_ref = rest[-4:]
    length = q_ref.shape[0]
    kv = kx_ref.shape[0]
    heads = q_ref.shape[1] // HD
    per = heads // 2 // kv
    bound = order_ref[0]
    dk_ref[...] = jnp.zeros(dk_ref.shape, F32)
    dv_ref[...] = jnp.zeros(dv_ref.shape, F32)
    lane = lax.broadcasted_iota(jnp.int32, (8, LANES), 1)
    row = lax.broadcasted_iota(jnp.int32, (8, LANES), 0)
    chosen = ((lane // HD) == row).astype(F32)

    def turn_back(values, rows):
        return values * cos_ref[rows, :] - swap_halves(values) * sin_ref[rows, :]

    for group in range(kv):

        def q_step(turn, _):
            index = order_ref[1 + turn]
            offset = pl.multiple_of(index * block, block)
            rows = pl.ds(offset, block)
            given = pl.ds(pl.multiple_of(turn * block, block), block)
            dq_ref[...] = jnp.zeros(dq_ref.shape, F32)
            deltas = []
            for pair in range(per):
                column = (group * per + pair) * LANES
                product = grad_ref[given, column : column + LANES].astype(F32) * out_ref[
                    given, column : column + LANES
                ].astype(F32)
                deltas.append(
                    lax.dot_general(
                        chosen, product, OVER_COLS, precision=lax.Precision.HIGHEST,
                        preferred_element_type=F32,
                    )
                )

            def tile(step, size, skip, diagonal):
                keys = pl.ds(pl.multiple_of(step, size), size)
                key_t = kt_ref[group * HD : (group + 1) * HD, keys]
                mine = pl.ds(offset + skip, block - skip)
                theirs = pl.ds(turn * block + skip, block - skip)
                for parity in range(2):
                    key_add, value_add = 0.0, 0.0
                    for pair in range(per):
                        head = 2 * pair + parity
                        place = group * 2 * per + head
                        column = (group * per + pair) * LANES
                        query = q_ref[mine, column : column + LANES]
                        grad = grad_ref[theirs, column : column + LANES]
                        scores = dot_cols(kx_ref[group, parity, keys, :], query)
                        if diagonal:
                            scores = jnp.where(causal(size, block - skip), scores, MASKED)
                        probs = jnp.exp(scores - lse_ref[place : place + 1, rows][:, skip:])
                        dprobs = dot_cols(vx_ref[group, parity, keys, :], grad)
                        delta = deltas[pair][parity : parity + 1, skip:]
                        dscores = (probs * (dprobs - delta)).astype(BF16)
                        value_add = value_add + dot(probs.astype(BF16), grad)
                        key_add = key_add + dot(dscores, query)
                        dq_ref[head * HD : (head + 1) * HD, skip:] += dot(key_t, dscores)
                    dk_ref[group, parity, keys, :] += key_add
                    dv_ref[group, parity, keys, :] += value_add

            def full_tile(step, carry):
                tile(step * block, block, 0, False)
                return carry

            lax.fori_loop(first_block(bound, offset, block), index, full_tile, 0)
            tile(offset, block // 2, 0, True)
            tile(offset + block // 2, block // 2, block // 2, True)
            for pair in range(per):
                column = (group * per + pair) * LANES
                grad_q = dq_ref[pair * LANES : (pair + 1) * LANES, :].T * (1.0 / math.sqrt(HD))
                dqkv_ref[rows, column : column + LANES] = turn_back(grad_q, rows).astype(BF16)
            return _

        lax.fori_loop(0, length // block, q_step, 0)

    def finish(index, _):
        rows = pl.ds(pl.multiple_of(index * block, block), block)
        lanes = lax.broadcasted_iota(jnp.int32, (block, LANES), 1)

        def placed(part, half):
            ref = dk_ref if part < kv else dv_ref
            even, odd = ref[part % kv, 0, rows, :], ref[part % kv, 1, rows, :]
            return even + pltpu.roll(odd, HD, 1) if half == 0 else pltpu.roll(even, HD, 1) + odd

        for chunk in range(kv):
            values = jnp.where(lanes < HD, placed(2 * chunk, 0), placed(2 * chunk + 1, 1))
            if 2 * chunk + 1 < kv:
                values = turn_back(values, rows)
            elif 2 * chunk < kv:
                values = jnp.where(lanes < HD, turn_back(values, rows), values)
            column = heads * HD + chunk * LANES
            dqkv_ref[rows, column : column + LANES] = values.astype(BF16)
        return _

    lax.fori_loop(0, length // block, finish, 0)


def attend_back(
    bound, order, queries, kx, vx, kt, log_sums, attended, grad, cosine, sine, block, others
):
    length, width = queries.shape
    heads = width // HD
    kv = kx.shape[0]
    cells = heads * length * (length + block) // 2
    vmem = pl.BlockSpec(memory_space=pltpu.VMEM)
    return pl.pallas_call(
        functools.partial(attend_back_kernel, block=block),
        in_specs=[pl.BlockSpec(memory_space=pltpu.SMEM)] + [vmem] * 9 + [ANYWHERE] * len(others),
        out_specs=vmem,
        out_shape=jax.ShapeDtypeStruct((length, width + 2 * kv * HD), BF16),
        scratch_shapes=[
            pltpu.VMEM((kv, 2, length, LANES), F32),
            pltpu.VMEM((kv, 2, length, LANES), F32),
            pltpu.VMEM((heads // kv * HD, block), F32),
        ],
        compiler_params=limit(52),
        cost_estimate=declared(2 * 10 * HD * 4 * cells),
    )(jnp.stack([bound, *order]), queries, kx, vx, kt, log_sums, attended, grad, cosine, sine, *others)


def local(
    inputs,
    segment_ids,
    attn_gain,
    query_weight,
    key_weight,
    value_weight,
    output_weight,
    mlp_gain,
    gate_weight,
    up_weight,
    down_weight,
    cotangent,
    *,
    sizes,
):
    rows = inputs.shape[0]
    length = segment_ids.shape[0]
    query_cols = query_weight.shape[1]
    key_cols = key_weight.shape[1]
    heads, kv = query_cols // HD, key_cols // HD
    columns = query_cols + 2 * key_cols
    slots = slots_of(sizes["tensor"])
    tensor = sizes["tensor"]
    space = (-columns) % query_cols or query_cols
    gains = jnp.pad(jnp.stack([attn_gain, mlp_gain], axis=1), ((0, 0), (0, space - 2)))
    bundle = lax.all_gather(
        jnp.concatenate([query_weight, key_weight, value_weight, gains, output_weight.T], axis=1),
        "dp", axis=0, tiled=True,
    )
    out_own = bundle[:, columns + space :]
    hop = first_hop(inputs, tensor)
    gate_up = lax.all_gather(
        hold(jnp.concatenate([gate_weight, up_weight], axis=1), *(hop or ())),
        "dp", axis=0, tiled=True,
    )

    bound, cosine, sine = rope_tables(segment_ids)
    blocks = second_hop(inputs, hop, tensor)
    arrays = project(slots, blocks, bundle, cosine, sine, heads, kv, length)
    block_a, queries, kx, vx, kt, vt, gains = arrays

    if tensor == 4:
        out_hop = first_hop(out_own, tensor)
        odd, odd_sums = attend(bound, [jnp.int32(k) for k in (1, 3)], queries, kx, vt, rows)
        halves = hold_halves(out_hop, odd)
        out_all = second_hop(out_own, out_hop, tensor, halves)
        even, even_sums = attend(bound, [jnp.int32(k) for k in (0, 2)], queries, kx, vt, rows, halves)
        order = [slots[1], slots[2], slots[0], slots[3]]
        first, second, own, far = sort_blocks(order, even, odd)
        from_one = lax.ppermute(first, "tensor", pairs(tensor, 1))
        from_two = lax.ppermute(second, "tensor", pairs(tensor, 2))
        from_far = lax.ppermute(far, "tensor", pairs(tensor, 3))
        stream_one, low_m = settle(own, 0, [from_one, from_two, from_far], out_all, inputs, gains)
        attended = jnp.concatenate([first, second, own, far], axis=0)
        log_sums = jnp.concatenate(
            [part[:, at : at + rows] for at in (0, rows) for part in (even_sums, odd_sums)], axis=1
        )
    else:
        order = slots
        out_all = gather(out_own, tensor)
        attended, log_sums = attend(bound, order, queries, kx, vt, rows)
        given = trade([attended[k * rows : (k + 1) * rows] for k in range(tensor)], tensor)
        stream_one, low_m = settle(given[0], 0, given[1:], out_all, inputs, gains)
        cotangent_sent = cotangent
    down_t = lax.all_gather(turn(down_weight, [low_m]), "dp", axis=0, tiled=True)
    parts_m = [low_m]
    units = gate_weight.shape[1]

    def feed_at(place, wanted, fed, others=()):
        return feed(
            feed_kernel, place, tensor, [parts_m[k] for k in wanted], [gate_up] * 2, [0, 1], [],
            units, 3, True, 512, fed, others,
        )

    def back_m(places, fed, into=None, others=(), split=False):
        return back(places, rows, fed[:2], [gate_up] * 2, [0, 1], into, others, split)

    def back_out(places, into=None, others=(), split=False):
        return back(places, rows, [hidden], [down_t], [0], into, others, split)

    def reduce_rows(term, *others):
        if others and tensor == 4:
            term = hold(term, *others)
        return lax.psum_scatter(term, "dp", scatter_dimension=0, tiled=True)

    if tensor == 4:
        hop = first_hop(parts_m[0], tensor)
        fed = feed_at(3, [0], None)
        cotangent_sent = hold(cotangent, fed[0])
        cotangent_hop = first_hop(cotangent_sent, tensor)
        parts_m = second_hop(parts_m[0], hop, tensor)
        fed = feed_at(0, [1, 2], fed, [cotangent_sent])
        halves = hold_halves(cotangent_hop, fed[0])
        grad_parts = second_hop(cotangent_sent, cotangent_hop, tensor, halves)
        grad_parts = grad_parts[1:] + grad_parts[:1]
        fed = feed_at(2, [3], fed, halves)
    else:
        grad_parts = second_hop(cotangent_sent, None, tensor)
        parts_m = gather(parts_m[0], tensor)
        fed = None
        for place in range(tensor):
            fed = feed_at(place, [place], fed)
    hidden, silu, slope, block_m = fed

    def feed_back(others=()):
        return feed(
            feed_back_kernel, 0, tensor, grad_parts, [down_t], [0], [silu, slope], units, 2, False, 512,
            None, others,
        )

    if tensor == 4:
        three_out = back_out([2], None, [fed[0]], True)
        out_one, out_two = out_halves = send_half(three_out, tensor)
        down_t_wgrad = weigh(grad_parts, hidden, three_out[:1])
        one_out, two_out, own_out = back_out([0, 1, 3], [(out_one, False), (out_two, True), None])
        out_parts = [
            own_out,
            lax.ppermute(one_out, "tensor", pairs(tensor, 1)),
            lax.ppermute(two_out, "tensor", pairs(tensor, 2)),
        ]
        fed = feed_back([one_out])
        three_m = back_m([2], fed, None, (), True)
        m_one, m_two = m_halves = send_half(three_m, tensor)
        gate_wgrad = weigh([block_m], fed[0], [three_m[0], *out_parts[1:]])
        one_m, two_m = back_m([0, 1], fed, [(m_one, False), (m_two, True)])
        (own_m,) = back_m([3], fed, None, [one_m])
        up_wgrad = weigh([block_m], fed[1], [own_m])
        grad_m_parts = [
            own_m,
            lax.ppermute(one_m, "tensor", pairs(tensor, 1)),
            lax.ppermute(two_m, "tensor", pairs(tensor, 2)),
        ]
    else:
        down_t_wgrad = weigh(grad_parts, hidden)
        fed = feed_back()
        grad_m_parts = sum_whole(back_m(list(range(tensor)), fed))
        gate_wgrad, up_wgrad = weigh([block_m], fed[0]), weigh([block_m], fed[1])
        out_parts = sum_whole(back_out(list(range(tensor))))
    if tensor != 4:
        out_halves = m_halves = ()
    down_t_low = reduce_rows(down_t_wgrad, *out_halves)
    gate_low = reduce_rows(gate_wgrad, *m_halves)
    up_low = reduce_rows(up_wgrad, *grad_m_parts[1:])

    grad_stream_one, grad_stream_low, *pieces = settle_back(
        grad_m_parts, out_all, cotangent, stream_one, gains
    )
    given = trade(pieces, tensor)
    places = [1, 2, 0, 3] if tensor == 4 else list(range(tensor))
    grad_attended = jnp.concatenate([given[k] for k in places], axis=0)
    grad_qkv = attend_back(
        bound, order, queries, kx, vx, kt, log_sums, attended, grad_attended, cosine, sine, rows,
        [down_t_low],
    )
    if tensor == 4:
        sent = hold(grad_stream_low, grad_attended)
        grad_stream_parts = trade([sent] * 4, tensor)
    else:
        grad_stream_parts = gather(grad_stream_low, tensor)
    grad_stream_parts = [grad_stream_parts[k] for k in places]

    def back_a(places, others=(), split=False):
        return back(places, rows, [grad_qkv], [bundle], [0], None, others, split)

    if tensor == 4:
        three = back_a(slots[3:], [gate_low], True)
        halves = send_half(three, tensor)
        one, two, own = back_a([slots[1], slots[2], slots[0]], three[:1])
        block_a = hold(block_a, one)
    attention_wgrad = weigh_both(block_a, grad_qkv, grad_stream_parts, attended)
    gate_sum, up_sum, down_t_sum = [low.astype(F32) for low in (gate_low, up_low, down_t_low)]
    if tensor == 4:
        attention_wgrad = hold(attention_wgrad, *halves)
    attention_sum = reduce_rows(attention_wgrad).astype(F32)
    if tensor == 4:
        one, two = add_half(one, halves[0], 1), add_half(two, halves[1], 0)
        grad_a_parts = [
            own,
            lax.ppermute(one, "tensor", pairs(tensor, 1)),
            lax.ppermute(two, "tensor", pairs(tensor, 2)),
        ]
    else:
        grad_a_parts = sum_whole(back_a(slots))

    product = attention_wgrad[:, :columns].astype(F32) * bundle[:, :columns].astype(F32)
    attn_term = sum_tensor(jnp.sum(product, axis=1)[None, :], tensor)
    width = attn_gain.shape[0]
    attn_term = lax.dynamic_slice_in_dim(
        sum_blocks(attn_term, sizes["dp"]), lax.axis_index("dp") * width, width, 1
    )

    def gain_term(gain, weights):
        term = sum(jnp.sum(weight.astype(F32) * grad, axis=1) for weight, grad in weights)
        return term / gain.astype(F32)

    query_sum = attention_sum[:, :query_cols]
    key_sum = attention_sum[:, query_cols : query_cols + key_cols]
    value_sum = attention_sum[:, query_cols + key_cols : columns]
    mlp_term = sum_tensor(
        gain_term(mlp_gain, [(gate_weight, gate_sum), (up_weight, up_sum)])[None, :], tensor
    )
    input_grad = settle_last(grad_a_parts, grad_stream_one, inputs, gains)
    layer_out = finish(out_parts, stream_one, [input_grad])
    return (
        layer_out,
        input_grad,
        attn_term[0] / attn_gain.astype(F32),
        query_sum,
        key_sum,
        value_sum,
        attention_sum[:, columns:].T,
        mlp_term[0],
        gate_sum,
        up_sum,
        down_t_sum.T,
    )


def solution(mesh):
    tokens = P(("dp", "tensor"), None)
    in_specs = (
        tokens,
        P("dp"),
        P("dp"),
        P("dp", "tensor"),
        P("dp", "tensor"),
        P("dp", "tensor"),
        P("tensor", "dp"),
        P("dp"),
        P("dp", "tensor"),
        P("dp", "tensor"),
        P("tensor", "dp"),
        tokens,
    )
    out_specs = (
        tokens,
        tokens,
        P("dp"),
        P("dp", "tensor"),
        P("dp", "tensor"),
        P("dp", "tensor"),
        P("tensor", "dp"),
        P("dp"),
        P("dp", "tensor"),
        P("dp", "tensor"),
        P("tensor", "dp"),
    )
    return jax.shard_map(
        functools.partial(local, sizes={axis: mesh.shape[axis] for axis in ("tensor", "dp")}),
        mesh=mesh, in_specs=in_specs, out_specs=out_specs, check_vma=False,
    )
```
